32 devices in a mesh: groups: 2 (over x), sub: 16 (over z, y, core).
Axes of the slice: x: 2, y: 2, z: 4, core: 2. Of those that a mesh axis runs over, the one named last changes fastest.
Arguments:
- rhs: float32 [2, 2048, 512], P(None, ('groups', 'sub')), parts along dimension 1, may hold values from -6 to 6
- viscosity: float32 [2048, 512], P(('groups', 'sub')), parts along dimension 0, may hold values from 0.3 to 3
- coupling: float32 [2, 2048, 512], P(None, ('groups', 'sub')), parts along dimension 1, may hold values from -0.3 to 0.3
- margin_rows: int32 [32], P('groups'), parts along dimension 0, may hold values from 1 to 20, as said below
- coarse_basis: bfloat16 [48, 2, 2048, 512], P(None, None, ('groups', 'sub')), parts along dimension 2, may hold values from -0.0078125 to 0.0078125
- coarse_inverse: float32 [1536, 768], P(('groups', 'sub')), parts along dimension 0, as said below
Outputs:
- solution: float32 [2, 2048, 512], P(None, ('groups', 'sub')), parts along dimension 1
- hessenberg: float32 [6, 2], P('groups'), parts along dimension 0
The draws below stay inside these ranges and needn't reach their ends.
There are 2 independent parts, one for each index of `groups`. The reference program is written for one: setup_inputs(seed, part) draws one part's arguments, and reference() takes and returns one part's arrays. A program takes and returns all parts, laid end to end along the dimension named above; each array names one. Nothing has to cross between parts.
Inputs may be any that keep to these rules, and one draw needn't show every extreme that they name: `margin_rows`: the last entry is not read; some entry before it equals 20. `coarse_inverse`: A dense matrix.
All inputs are finite; a program needn't handle non-finite values.
Results may differ from the reference program's by a relative error of at most 0.003.
Values sent between devices are 32-bit elements; how exact they have to be, the bound alone decides.
No kernel may reach another device: no remote copies, remote signals or barrier semaphores. Data moves between devices by JAX's collectives and lax.ppermute only.
A program may use at most 64 MiB of HBM per device.

```python
import math
import jax
import jax.numpy as jnp
from jax import lax

ROWS = 64
CELLS = 512
MARGIN = 20
VECTORS = 48
SWEEPS = 4
ITERS = 2
SUBDOMAINS = 16
NR = 1024
COARSE = 768


def draw_margin_rows(key, part):
    key = jax.random.fold_in(key, 11)
    first, second = jax.random.split(key)
    counts = jax.random.randint(first, (SUBDOMAINS,), 1, MARGIN + 1)
    spot = jax.random.randint(second, (), 0, SUBDOMAINS - 1)
    return jnp.where(jnp.arange(SUBDOMAINS) == spot, MARGIN, counts).astype(jnp.int32)


def draw_coarse_inverse(key, part):
    key = jax.random.fold_in(key, 23)
    first, second = jax.random.split(key)
    factor = 2.0 * math.sqrt(ROWS * CELLS / (2.0 * VECTORS))
    spread = jax.random.normal(first, (COARSE, COARSE), jnp.float32) * (0.5 / math.sqrt(COARSE))
    middle = jax.random.uniform(second, (COARSE,), jnp.float32, 0.5, 1.5)
    return factor * (spread + jnp.diag(middle))


def shard_levels(key, dims, cuts, smallest, high):
    def one(position, shards_of):
        draws = jax.random.uniform(jax.random.fold_in(jax.random.fold_in(key, 6), position), (shards_of,), jnp.float32, smallest / len(cuts), high / len(cuts))
        return jnp.repeat(jnp.exp(draws), dims[position] // shards_of).reshape((-1,) + (1,) * (len(dims) - position - 1))

    loudness = one(*cuts[0])
    for cut in cuts[1:]:
        loudness = loudness * one(*cut)
    return loudness


def scatter_about(rng, shape, deviation, bound, cuts=(), held_as=jnp.bfloat16):
    values = jax.random.normal(rng, shape, jnp.float32) * deviation
    if len(cuts) > 0:
        values = shard_levels(rng, shape, cuts, -0.22, 0.18) * values
    return jnp.clip(values, min=-bound, max=bound).astype(held_as)


def setup_inputs(seed: int = 0, part: int = 0) -> dict:
    key_of = jax.random.split(jax.random.key(seed), 7)
    own_keys = jax.random.split(jax.random.fold_in(key_of[6], part), 7)
    rhs = scatter_about(own_keys[0], (2, NR, CELLS), 1.0, 6.0, ((1, 16),), jnp.float32)
    viscosity = jnp.clip(jnp.exp(math.log(3.0) - 2.3025851 * jax.random.uniform(own_keys[1], (NR, CELLS), jnp.float32) ** shard_levels(own_keys[1], (NR, CELLS), ((0, 16),), -0.2, 0.2)), 0.3, 3.0)
    coupling = jnp.clip(jax.random.uniform(own_keys[2], (2, NR, CELLS), jnp.float32, -0.3, 0.3) * shard_levels(own_keys[2], (2, NR, CELLS), ((1, 16),), -0.4, 0.0), -0.3, 0.3)
    margin_rows = draw_margin_rows(jax.random.fold_in(jax.random.fold_in(key_of[6], part), 71), part)
    coarse_basis = scatter_about(own_keys[4], (VECTORS, 2, NR, CELLS), (20 * ROWS * CELLS) ** -0.5, 0.0078125, ((2, 16),))
    coarse_inverse = draw_coarse_inverse(jax.random.fold_in(jax.random.fold_in(key_of[6], part), 71), part)
    return {"rhs": rhs, "viscosity": viscosity, "coupling": coupling, "margin_rows": margin_rows, "coarse_basis": coarse_basis, "coarse_inverse": coarse_inverse}


relax_factor = 0.7

def apply_operator(padded, viscosity, coupling):
    middle = padded[:, 1:-1]
    row_sum = padded[:, :-2] + padded[:, 2:]
    bordered = jnp.pad(middle, ((0, 0), (0, 0), (1, 1)))
    col_sum = bordered[:, :, :-2] + bordered[:, :, 2:]
    row_factor = jnp.array([1.0, 4.0], jnp.float32)[:, None, None]
    col_factor = jnp.array([4.0, 1.0], jnp.float32)[:, None, None]
    diagonal = 10.0 * viscosity + jnp.abs(coupling) + 0.05
    return diagonal * middle - viscosity * (row_factor * row_sum + col_factor * col_sum) + coupling * middle[::-1]

def pad_rows(field):
    return jnp.pad(field, ((0, 0), (1, 1), (0, 0)))

def local_solve(residual, viscosity, coupling, live):
    live_grid = live[None, :, None]
    diagonal = 10.0 * viscosity + jnp.abs(coupling) + 0.05
    solved = jnp.zeros_like(residual)
    for sweep in range(SWEEPS):
        image = apply_operator(pad_rows(solved), viscosity, coupling)
        solved = live_grid * (solved + relax_factor * (residual - image) / diagonal)
    return solved

def window_weights(lower, upper, length):
    places = jnp.arange(length, dtype=jnp.int32) - MARGIN
    place_f = places.astype(jnp.float32)
    lower_f = lower.astype(jnp.float32)
    upper_f = upper.astype(jnp.float32)
    live = ((places >= -lower) & (places < ROWS + upper)).astype(jnp.float32)
    weight = jnp.ones((length,), jnp.float32)
    weight = jnp.where(places < lower, (place_f + lower_f + 0.5) / (2.0 * jnp.maximum(lower_f, 1.0)), weight)
    weight = jnp.where(places >= ROWS - upper, (ROWS + upper_f - place_f - 0.5) / (2.0 * jnp.maximum(upper_f, 1.0)), weight)
    return (live, weight * live)

def least_squares(hessenberg, beta):
    normal = jnp.dot(hessenberg.T, hessenberg, precision=lax.Precision.HIGHEST)
    target = beta * hessenberg[0]
    factor = jnp.linalg.cholesky(normal)
    forward = []
    for row in range(ITERS):
        acc = target[row]
        for col in range(row):
            acc = acc - factor[row, col] * forward[col]
        forward.append(acc / factor[row, row])
    backward = [None] * ITERS
    for row in reversed(range(ITERS)):
        acc = forward[row]
        for col in range(row + 1, ITERS):
            acc = acc - factor[col, row] * backward[col]
        backward[row] = acc / factor[row, row]
    return backward

def reference(rhs, viscosity, coupling, margin_rows, coarse_basis, coarse_inverse):
    length = ROWS + 2 * MARGIN
    ranks = jnp.arange(SUBDOMAINS, dtype=jnp.int32)
    starts = ranks * ROWS

    def extend(field):
        padded = jnp.pad(field, ((0, 0), (MARGIN, MARGIN), (0, 0)))
        return jax.vmap(lambda start: lax.dynamic_slice_in_dim(padded, start, length, 1))(starts)
    coefficients = extend(jnp.concatenate([viscosity[None], coupling], 0))
    lower = jnp.where(ranks > 0, jnp.roll(margin_rows, 1), 0)
    upper = jnp.where(ranks < SUBDOMAINS - 1, margin_rows, 0)
    live, weight = jax.vmap(lambda low, high: window_weights(low, high, length))(lower, upper)
    blocks = coarse_basis.reshape(VECTORS, 2, SUBDOMAINS, ROWS, CELLS)

    def precondition(vector):
        pieces = extend(vector)
        solved = jax.vmap(local_solve)(pieces, coefficients[:, 0], coefficients[:, 1:], live)
        shares = solved * weight[:, None, :, None]
        middle = shares[:, :, MARGIN:MARGIN + ROWS]
        middle = middle.at[:-1, :, ROWS - MARGIN:].add(shares[1:, :, :MARGIN])
        middle = middle.at[1:, :, :MARGIN].add(shares[:-1, :, MARGIN + ROWS:])
        schwarz = jnp.transpose(middle, (1, 0, 2, 3)).reshape(2, NR, CELLS)
        rounded = vector.astype(jnp.bfloat16).reshape(2, SUBDOMAINS, ROWS, CELLS)

        def restrict(index):
            block = lax.dynamic_index_in_dim(blocks, index, 2, keepdims=False).astype(jnp.float32)
            piece = lax.dynamic_index_in_dim(rounded, index, 1, keepdims=False).astype(jnp.float32)
            return jnp.einsum('varc,arc->v', block, piece, precision=lax.Precision.HIGHEST)
        coarse_res = lax.map(restrict, ranks)
        lifted = jnp.dot(coarse_inverse, coarse_res.reshape(-1), precision=lax.Precision.HIGHEST)
        lifted = lifted.astype(jnp.bfloat16).reshape(SUBDOMAINS, VECTORS)

        def prolong(index):
            block = lax.dynamic_index_in_dim(blocks, index, 2, keepdims=False).astype(jnp.float32)
            amounts = lax.dynamic_index_in_dim(lifted, index, 0, keepdims=False).astype(jnp.float32)
            return jnp.einsum('v,varc->arc', amounts, block, precision=lax.Precision.HIGHEST)
        coarse = lax.map(prolong, ranks)
        coarse = jnp.transpose(coarse, (1, 0, 2, 3)).reshape(2, NR, CELLS)
        return schwarz + coarse
    beta = jnp.sqrt(jnp.sum(rhs * rhs))
    krylov = [rhs / beta]
    directions = []
    hessenberg = jnp.zeros((ITERS + 1, ITERS), jnp.float32)
    for turn in range(ITERS):
        direction = precondition(krylov[turn])
        directions.append(direction)
        image = apply_operator(pad_rows(direction), viscosity, coupling)
        heights = [jnp.sum(earlier * image) for earlier in krylov]
        for earlier, height in zip(krylov, heights):
            image = image - height * earlier
        length_new = jnp.sqrt(jnp.sum(image * image))
        for slot, height in enumerate(heights):
            hessenberg = hessenberg.at[slot, turn].set(height)
        hessenberg = hessenberg.at[turn + 1, turn].set(length_new)
        krylov.append(image / length_new)
    coeffs = least_squares(hessenberg, beta)
    solution = coeffs[0] * directions[0]
    for turn in range(1, ITERS):
        solution = solution + coeffs[turn] * directions[turn]
    return (solution, hessenberg)
```

```python
import jax
import jax.numpy as jnp
from jax import lax
from jax.sharding import PartitionSpec as P

ROWS = 64
CELLS = 512
MARGIN = 20
SWEEPS = 4
ITERS = 2


relax_factor = 0.7


def with_halo(cells, sides, width):
    for axis, dim in sides:
        count = lax.axis_size(axis)
        ends = count - 1
        head = lax.slice_in_dim(cells, 0, width, axis=dim)
        tail = lax.slice_in_dim(cells, cells.shape[dim] - width, cells.shape[dim], axis=dim)
        cells = jnp.concatenate(
            [
                lax.ppermute(tail, axis, [(i, (i + 1) % count) for i in range(ends)]),
                cells,
                lax.ppermute(head, axis, [((i + 1) % count, i) for i in range(ends)]),
            ],
            axis=dim,
        )
    return cells


def apply_operator(padded, viscosity, coupling):
    middle = padded[:, 1:-1]
    row_sum = padded[:, :-2] + padded[:, 2:]
    bordered = jnp.pad(middle, ((0, 0), (0, 0), (1, 1)))
    col_sum = bordered[:, :, :-2] + bordered[:, :, 2:]
    row_factor = jnp.array([1.0, 4.0], jnp.float32)[:, None, None]
    col_factor = jnp.array([4.0, 1.0], jnp.float32)[:, None, None]
    diagonal = 10.0 * viscosity + jnp.abs(coupling) + 0.05
    return (
        diagonal * middle
        - viscosity * (row_factor * row_sum + col_factor * col_sum)
        + coupling * middle[::-1]
    )


def pad_rows(field):
    return jnp.pad(field, ((0, 0), (1, 1), (0, 0)))


def local_solve(residual, viscosity, coupling, live):
    live_grid = live[None, :, None]
    diagonal = 10.0 * viscosity + jnp.abs(coupling) + 0.05
    solved = jnp.zeros_like(residual)
    for sweep in range(SWEEPS):
        image = apply_operator(pad_rows(solved), viscosity, coupling)
        solved = live_grid * (solved + relax_factor * (residual - image) / diagonal)
    return solved


def window_weights(lower, upper, length):
    places = jnp.arange(length, dtype=jnp.int32) - MARGIN
    place_f = places.astype(jnp.float32)
    lower_f = lower.astype(jnp.float32)
    upper_f = upper.astype(jnp.float32)
    live = ((places >= -lower) & (places < ROWS + upper)).astype(jnp.float32)
    weight = jnp.ones((length,), jnp.float32)
    weight = jnp.where(
        places < lower, (place_f + lower_f + 0.5) / (2.0 * jnp.maximum(lower_f, 1.0)), weight
    )
    weight = jnp.where(
        places >= ROWS - upper,
        (ROWS + upper_f - place_f - 0.5) / (2.0 * jnp.maximum(upper_f, 1.0)),
        weight,
    )
    return (live, weight * live)


def from_everyone(values):
    count = lax.axis_size("sub")
    copies = jnp.broadcast_to(values[None], (count,) + values.shape)
    return lax.all_to_all(copies, "sub", 0, 0, tiled=True)


def restrict(flat_basis, field):
    flat = field.reshape(-1)
    high = flat.astype(jnp.bfloat16)
    low = (flat - high.astype(jnp.float32)).astype(jnp.bfloat16)
    both = jnp.dot(flat_basis, jnp.stack([high, low], 1), preferred_element_type=jnp.float32)
    return both[:, 0] + both[:, 1]


def schwarz_part(field, coefficients, live, weight):
    length = live.shape[0]
    extended = with_halo(field, (("sub", 1),), MARGIN)
    solved = local_solve(extended, coefficients[0], coefficients[1:], live)
    shares = solved * weight[None, :, None]
    outgoing = jnp.concatenate([shares[:, :MARGIN], shares[:, length - MARGIN :]], 1)
    received = with_halo(outgoing, (("sub", 1),), MARGIN)
    middle = shares[:, MARGIN : MARGIN + ROWS]
    return jnp.concatenate(
        [
            middle[:, :MARGIN] + received[:, :MARGIN],
            middle[:, MARGIN : ROWS - MARGIN],
            middle[:, ROWS - MARGIN :] + received[:, 3 * MARGIN :],
        ],
        1,
    )


def on_device(rhs, viscosity, coupling, margin_rows, coarse_basis, coarse_inverse):
    length = ROWS + 2 * MARGIN
    count = lax.axis_size("sub")
    rank = lax.axis_index("sub")
    vectors = coarse_basis.shape[0]
    lower = jnp.where(rank > 0, margin_rows[jnp.maximum(rank - 1, 0)], 0)
    upper = jnp.where(rank < count - 1, margin_rows[rank], 0)
    live, weight = window_weights(lower, upper, length)
    coefficients = with_halo(jnp.concatenate([viscosity[None], coupling], 0), (("sub", 1),), MARGIN)
    flat_basis = coarse_basis.reshape(vectors, -1)

    def coarse_part(residuals):
        lifted = jnp.dot(coarse_inverse, residuals, precision=lax.Precision.HIGHEST)
        lifted = lifted.astype(jnp.bfloat16)
        return jnp.dot(lifted, flat_basis, preferred_element_type=jnp.float32).reshape(rhs.shape)

    def image_of(field):
        return apply_operator(with_halo(field, (("sub", 1),), 1), viscosity, coupling)

    first = from_everyone(
        jnp.concatenate([restrict(flat_basis, rhs), jnp.sum(rhs * rhs)[None]])
    )
    smooth_0 = schwarz_part(rhs, coefficients, live, weight)
    beta = jnp.sqrt(jnp.sum(first[:, vectors]))
    res_0 = first[:, :vectors].reshape(-1) / beta
    z_0 = smooth_0 / beta + coarse_part(res_0)
    w_0 = image_of(z_0)
    second = from_everyone(
        jnp.concatenate(
            [
                restrict(flat_basis, w_0),
                jnp.stack([jnp.sum(rhs * w_0), jnp.sum(w_0 * w_0)]),
            ]
        )
    )
    smooth_1 = schwarz_part(w_0, coefficients, live, weight)
    h_00 = jnp.sum(second[:, vectors]) / beta
    h_10 = jnp.sqrt(jnp.sum(second[:, vectors + 1]) - h_00 * h_00)
    res_1 = (second[:, :vectors].reshape(-1) - h_00 * res_0) / h_10
    z_1 = (smooth_1 - (h_00 / beta) * smooth_0) / h_10 + coarse_part(res_1)
    w_1 = image_of(z_1)
    third = from_everyone(
        jnp.stack([jnp.sum(rhs * w_1), jnp.sum(w_0 * w_1), jnp.sum(w_1 * w_1)])
    )
    sums = jnp.sum(third, 0)
    h_01 = sums[0] / beta
    h_11 = (sums[1] - h_00 * h_01) / h_10
    h_21 = jnp.sqrt(sums[2] - h_01 * h_01 - h_11 * h_11)
    zero = jnp.zeros_like(beta)
    hessenberg = jnp.stack([h_00, h_01, h_10, h_11, zero, h_21]).reshape(ITERS + 1, ITERS)
    n_00 = h_00 * h_00 + h_10 * h_10
    n_01 = h_00 * h_01 + h_10 * h_11
    n_11 = h_01 * h_01 + h_11 * h_11 + h_21 * h_21
    l_00 = jnp.sqrt(n_00)
    l_10 = n_01 / l_00
    l_11 = jnp.sqrt(n_11 - l_10 * l_10)
    f_0 = beta * h_00 / l_00
    f_1 = (beta * h_01 - l_10 * f_0) / l_11
    c_1 = f_1 / l_11
    c_0 = (f_0 - l_10 * c_1) / l_00
    return (c_0 * z_0 + c_1 * z_1, hessenberg)


def solution(mesh):
    in_specs = (
        P(None, ("groups", "sub"), None),
        P(("groups", "sub"), None),
        P(None, ("groups", "sub"), None),
        P("groups"),
        P(None, None, ("groups", "sub"), None),
        P(("groups", "sub"), None),
    )
    out_specs = (P(None, ("groups", "sub"), None), P("groups", None))
    return jax.shard_map(
        on_device, mesh=mesh, in_specs=in_specs, out_specs=out_specs, check_vma=False
    )
```

```python
import functools

import jax
import jax.numpy as jnp
from jax import lax
from jax.experimental import pallas as pl
from jax.experimental.pallas import tpu as pltpu
from jax.sharding import PartitionSpec as P

ROWS = 64
CELLS = 512
VECTORS = 48
HALO = 8
EXT = ROWS + 2 * HALO
STRIP = 32
CHUNK = 16
CHUNKS = 2 * ROWS // CHUNK
LANES = 128
SLOTS = 56
EDGE_AT = 5 * HALO
INVERSE_AT = EDGE_AT + 2 * VECTORS
SWEEPS = 4
RELAX = 0.7
ROW_FACTOR = (1.0, 4.0)
CELL_FACTOR = (4.0, 1.0)

VMEM = pl.BlockSpec(memory_space=pltpu.VMEM)
SMEM = pl.BlockSpec(memory_space=pltpu.SMEM)
ANY = pl.BlockSpec(memory_space=pl.ANY)


def packed_rows(columns):
    return INVERSE_AT + VECTORS * (columns // 512) + (VECTORS // 2) * (columns % 512 // 256)


def cell_sum(field):
    column = lax.broadcasted_iota(jnp.int32, field.shape, 1)
    left = jnp.where(column == 0, 0.0, pltpu.roll(field, 1, 1))
    right = jnp.where(column == CELLS - 1, 0.0, pltpu.roll(field, CELLS - 1, 1))
    return left + right


def row_sum(field):
    count = field.shape[0]
    return pltpu.roll(field, 1, 0) + pltpu.roll(field, count - 1, 0)


def neighbours(field, component):
    rows, cells = row_sum(field), cell_sum(field)
    if component == 0:
        return rows + CELL_FACTOR[0] * cells
    return ROW_FACTOR[1] * rows + cells


def apply_operator(extended, viscosity, coupling):
    inner = slice(HALO, HALO + ROWS)
    images = []
    for a in range(2):
        around = neighbours(extended[a], a)[inner]
        diagonal = 10.0 * viscosity + jnp.abs(coupling[a]) + 0.05
        images.append(
            diagonal * extended[a][inner]
            - viscosity * around
            + coupling[a] * extended[1 - a][inner]
        )
    return images


def basis_copies(basis_ref, held, sems):
    return [
        pltpu.make_async_copy(
            basis_ref.at[:, i // 4, pl.ds(CHUNK * (i % 4), CHUNK), :], held.at[i], sems.at[i]
        )
        for i in range(CHUNKS)
    ]


def restrict_chunk(i, held, field, sums):
    a = i // 4
    start = pl.multiple_of((i % 4) * CHUNK, CHUNK)
    parts = [field[a, pl.ds(start, CHUNK), pl.ds(LANES * c, LANES)] for c in range(4)]
    for k in range(VECTORS):
        total = None
        for c in range(4):
            term = held[i, k, :, pl.ds(LANES * c, LANES)].astype(jnp.float32) * parts[c]
            total = term if total is None else total + term
        sums[8 * k : 8 * k + 8, :] += total[:8] + total[8:]


def fold(field):
    total = None
    for part in field:
        for r in range(0, part.shape[0], 8):
            for c in range(0, part.shape[1], LANES):
                term = part[r : r + 8, c : c + LANES]
                total = term if total is None else total + term
    return total


def send_sums(sums, out_ref):
    pick_row = lax.broadcasted_iota(jnp.int32, (LANES, 8 * SLOTS), 0)
    pick_col = lax.broadcasted_iota(jnp.int32, (LANES, 8 * SLOTS), 1)
    pick = (pick_col // 8 == pick_row).astype(jnp.float32)
    by_slot = jnp.dot(
        pick, sums[...], precision=lax.Precision.HIGHEST, preferred_element_type=jnp.float32
    )
    row = lax.dot_general(
        jnp.ones((8, LANES), jnp.float32),
        by_slot,
        (((1,), (1,)), ((), ())),
        precision=lax.Precision.HIGHEST,
        preferred_element_type=jnp.float32,
    )
    out_ref[...] = jnp.broadcast_to(row[:1], out_ref.shape)


def start_kernel(
    rhs_ref, visc_ref, coup_ref, inverse_ref, basis_ref,
    sums_ref, up_ref, down_ref,
    held, sums, sems,
):
    copies = basis_copies(basis_ref, held, sems)
    for copy in copies:
        copy.start()
    columns = inverse_ref.shape[1]
    for out_ref, rows in ((up_ref, slice(ROWS - HALO, ROWS)), (down_ref, slice(0, HALO))):
        out_ref[0:HALO] = visc_ref[rows]
        for a in range(2):
            out_ref[HALO * (1 + a) : HALO * (2 + a)] = coup_ref[a, rows]
            out_ref[HALO * (3 + a) : HALO * (4 + a)] = rhs_ref[a, rows]
        at = INVERSE_AT
        for c in range(0, columns - 511, 512):
            out_ref[at : at + VECTORS] = inverse_ref[:, c : c + 512]
            at += VECTORS
        if columns % 512:
            half = VECTORS // 2
            out_ref[at : at + half, :256] = inverse_ref[:half, columns - 256 :]
            out_ref[at : at + half, 256:] = inverse_ref[half:, columns - 256 :]
    sums[...] = jnp.zeros_like(sums)
    sums[8 * VECTORS : 8 * VECTORS + 8] = fold([rhs_ref[a] * rhs_ref[a] for a in range(2)])
    for copy in copies:
        copy.wait()

    def body(i, carry):
        restrict_chunk(i, held, rhs_ref, sums)
        return carry

    lax.fori_loop(0, CHUNKS, body, 0)
    picker = lax.broadcasted_iota(jnp.int32, (VECTORS, CHUNK * VECTORS), 0) * CHUNK
    place = lax.broadcasted_iota(jnp.int32, (VECTORS, CHUNK * VECTORS), 1)
    for out_ref, block, row in ((up_ref, 3, CHUNK - 1), (down_ref, 0, 0)):
        pick = (place == picker + row).astype(jnp.float32).astype(jnp.bfloat16)
        for a in range(2):
            rows = held[4 * a + block].reshape(CHUNK * VECTORS, CELLS)
            at = EDGE_AT + VECTORS * a
            out_ref[at : at + VECTORS] = jnp.dot(pick, rows, preferred_element_type=jnp.float32)
    send_sums(sums, sums_ref)


def solve_kernel(count, margin_ref, own_refs, below_refs, above_refs, out_ref):
    rank = lax.axis_index("sub")
    lower = jnp.where(rank > 0, margin_ref[jnp.maximum(rank - 1, 0)], 0)
    upper = jnp.where(rank < count - 1, margin_ref[rank], 0)
    lower_f, upper_f = lower.astype(jnp.float32), upper.astype(jnp.float32)
    low_scale = 2.0 * jnp.maximum(lower_f, 1.0)
    high_scale = 2.0 * jnp.maximum(upper_f, 1.0)

    def masks(first, rows, side):
        place = lax.broadcasted_iota(jnp.int32, (rows, LANES), 0) + first
        place_f = place.astype(jnp.float32)
        rising = lambda base, scale: (place_f - base + 0.5) / scale
        falling = lambda base, scale: (base - place_f - 0.5) / scale
        if side == 0:
            live = (place >= -lower) & (place < ROWS + upper)
            weight = jnp.where(place < lower, rising(-lower_f, low_scale), 1.0)
            weight = jnp.where(
                place >= ROWS - upper, falling(ROWS + upper_f, high_scale), weight
            )
        elif side < 0:
            live = place < lower
            weight = jnp.where(place >= -lower, falling(lower_f, low_scale), 1.0)
        else:
            live = place >= ROWS - upper
            weight = jnp.where(place < ROWS + upper, rising(ROWS - upper_f, high_scale), 1.0)
        wide = lambda x: jnp.concatenate([x] * (CELLS // LANES), 1)
        return wide(live.astype(jnp.float32)), wide(weight)

    def stack(below, own, above):
        return jnp.concatenate([below, own, above], 0)

    def triple(field):
        return jnp.concatenate([field, field[:STRIP], field[EXT - STRIP :]], 0)

    viscosity = stack(below_refs[0][...], own_refs[0][...], above_refs[0][...])
    blocks = [masks(-HALO, EXT, 0), masks(-HALO, STRIP, -1), masks(ROWS + HALO - STRIP, STRIP, 1)]
    live = jnp.concatenate([block[0] for block in blocks], 0)
    first, across, other = [], [], []
    for a in range(2):
        coupling = stack(below_refs[1][a], own_refs[1][a], above_refs[1][a])
        field = stack(below_refs[2][a], own_refs[2][a], above_refs[2][a])
        scale = RELAX / (10.0 * viscosity + jnp.abs(coupling) + 0.05)
        first.append(live * triple(scale * field))
        across.append(live * triple(scale * viscosity))
        other.append(live * triple(scale * coupling))
    solved = list(first)
    for _ in range(SWEEPS - 1):
        solved = [
            (1.0 - RELAX) * solved[a]
            + first[a]
            + across[a] * neighbours(solved[a], a)
            - other[a] * solved[1 - a]
            for a in range(2)
        ]
    for a in range(2):
        shares = solved[a] * jnp.concatenate([block[1] for block in blocks], 0)
        out_ref[a] = shares[:EXT]
        out_ref[a, :STRIP] += shares[EXT : EXT + STRIP]
        out_ref[a, EXT - STRIP :] += shares[EXT + STRIP :]


class Part:
    def __init__(self, ref, at, stacked):
        self.ref, self.at, self.stacked = ref, at, stacked

    def __getitem__(self, index):
        at = self.at + (HALO * index if self.stacked else 0)
        return self.ref[at : at + HALO, :]


def packed_fields(ref):
    return (Part(ref, 0, False), Part(ref, HALO, True), Part(ref, 3 * HALO, True))


def first_solve_kernel(count, margin_ref, visc_ref, coup_ref, rhs_ref, low_ref, high_ref, out_ref):
    solve_kernel(
        count,
        margin_ref,
        (visc_ref, coup_ref, rhs_ref),
        packed_fields(low_ref),
        packed_fields(high_ref),
        out_ref,
    )


def second_solve_kernel(
    count, margin_ref, visc_ref, coup_ref, image_ref, low_ref, high_ref,
    low_image_ref, high_image_ref, out_ref,
):
    solve_kernel(
        count,
        margin_ref,
        (visc_ref, coup_ref, image_ref),
        packed_fields(low_ref)[:2] + (low_image_ref,),
        packed_fields(high_ref)[:2] + (high_image_ref,),
        out_ref,
    )


def line_up(residuals):
    devices = residuals.shape[0]
    lane = lax.broadcasted_iota(jnp.int32, (1, LANES), 1)
    tiles = [jnp.zeros((1, LANES), jnp.float32) for _ in range(devices * VECTORS // LANES)]
    for t in range(devices):
        tile, offset = divmod(VECTORS * t, LANES)
        row = jnp.where(lane < VECTORS, residuals[t : t + 1], 0.0)
        if offset:
            row = pltpu.roll(row, offset, 1)
        if offset + VECTORS <= LANES:
            tiles[tile] = tiles[tile] + row
        else:
            tiles[tile] = tiles[tile] + jnp.where(lane >= offset, row, 0.0)
            tiles[tile + 1] = tiles[tile + 1] + jnp.where(lane < offset, row, 0.0)
    return jnp.concatenate(tiles, 1)


def rounded(column):
    return column.astype(jnp.bfloat16).astype(jnp.float32)


def lift(inverse_ref, residual):
    return rounded(jnp.sum(inverse_ref[...] * residual, 1, keepdims=True))


def lift_packed(ref, residual):
    columns = residual.shape[1]
    at, total = INVERSE_AT, None
    for c in range(0, columns - 511, 512):
        term = jnp.sum(ref[at : at + VECTORS] * residual[:, c : c + 512], 1, keepdims=True)
        total = term if total is None else total + term
        at += VECTORS
    if columns % 512:
        half = VECTORS // 2
        last = residual[:, columns - 256 :]
        term = jnp.concatenate(
            [
                jnp.sum(ref[at : at + half, :256] * last, 1, keepdims=True),
                jnp.sum(ref[at : at + half, 256:] * last, 1, keepdims=True),
            ],
            0,
        )
        total = term if total is None else total + term
    return rounded(total)


def edge_values(ref, lifted):
    return [
        jnp.sum(ref[EDGE_AT + VECTORS * a : EDGE_AT + VECTORS * (a + 1)] * lifted, 0, keepdims=True)
        for a in range(2)
    ]


def spread(lifted):
    shape = (VECTORS, CHUNK * VECTORS)
    owner = lax.broadcasted_iota(jnp.int32, shape, 1) // CHUNK
    row = lax.broadcasted_iota(jnp.int32, shape, 0)
    line = jnp.sum(jnp.where(owner == row, lifted, 0.0), 0, keepdims=True)
    shape = (CHUNK, CHUNK * VECTORS)
    place = lax.broadcasted_iota(jnp.int32, shape, 1) % CHUNK
    row = lax.broadcasted_iota(jnp.int32, shape, 0)
    return jnp.where(place == row, line, 0.0).astype(jnp.bfloat16)


def prolong(residual, inverse_ref, low_ref, high_ref, smooth, held, copies, extended):
    low_edge = edge_values(low_ref, lift_packed(low_ref, residual))
    high_edge = edge_values(high_ref, lift_packed(high_ref, residual))
    place = lax.broadcasted_iota(jnp.int32, (HALO, CELLS), 0)
    for a in range(2):
        rows = slice(0, HALO)
        extended[a, rows] = smooth(a, rows) + jnp.where(place == HALO - 1, low_edge[a], 0.0)
        rows = slice(EXT - HALO, EXT)
        extended[a, rows] = smooth(a, rows) + jnp.where(place == 0, high_edge[a], 0.0)
    matrix = spread(lift(inverse_ref, residual))
    for i in range(CHUNKS):
        a, start = i // 4, HALO + CHUNK * (i % 4)
        rows = slice(start, start + CHUNK)
        copies[i].wait()
        coarse = jnp.dot(
            matrix,
            held[i].reshape(CHUNK * VECTORS, CELLS),
            preferred_element_type=jnp.float32,
        )
        extended[a, rows] = smooth(a, rows) + coarse


def lane_total(received, lane):
    return jnp.sum(received[:, lane : lane + 1], 0, keepdims=True)


def first_turn_kernel(
    sums_ref, inverse_ref, low_ref, high_ref, basis_ref, smooth_ref, rhs_ref, visc_ref, coup_ref,
    direction_ref, image_ref, head_ref, tail_ref, next_ref,
    held, extended, sums, sems,
):
    copies = basis_copies(basis_ref, held, sems)
    for copy in copies:
        copy.start()
    received = sums_ref[...]
    over_beta = 1.0 / jnp.sqrt(lane_total(received, VECTORS))
    residual = line_up(received) * over_beta
    prolong(
        residual,
        inverse_ref,
        low_ref,
        high_ref,
        lambda a, rows: smooth_ref[a, rows] * over_beta,
        held,
        copies,
        extended,
    )
    images = apply_operator(
        [extended[a] for a in range(2)], visc_ref[...], [coup_ref[a] for a in range(2)]
    )
    for a in range(2):
        direction_ref[a] = extended[a, HALO : HALO + ROWS]
        image_ref[a] = images[a]
        head_ref[a] = images[a][:HALO]
        tail_ref[a] = images[a][ROWS - HALO :]
    sums[...] = jnp.zeros_like(sums)
    at = 8 * VECTORS
    sums[at : at + 8] = fold([rhs_ref[a] * images[a] for a in range(2)])
    sums[at + 8 : at + 16] = fold([images[a] * images[a] for a in range(2)])

    def body(i, carry):
        restrict_chunk(i, held, image_ref, sums)
        return carry

    lax.fori_loop(0, CHUNKS, body, 0)
    send_sums(sums, next_ref)


def first_column(first, second):
    beta = jnp.sqrt(lane_total(first, VECTORS))
    h_00 = lane_total(second, VECTORS) / beta
    h_10 = jnp.sqrt(lane_total(second, VECTORS + 1) - h_00 * h_00)
    return beta, h_00, h_10


def second_turn_kernel(
    first_ref, second_ref, inverse_ref, low_ref, high_ref, basis_ref, smooth_ref, image_smooth_ref,
    rhs_ref, image_ref, visc_ref, coup_ref,
    direction_ref, next_ref,
    held, extended, sums, sems,
):
    copies = basis_copies(basis_ref, held, sems)
    for copy in copies:
        copy.start()
    first, second = first_ref[...], second_ref[...]
    beta, h_00, h_10 = first_column(first, second)
    ratio = h_00 / beta
    over = 1.0 / h_10
    residual = (line_up(second) - ratio * line_up(first)) * over
    prolong(
        residual,
        inverse_ref,
        low_ref,
        high_ref,
        lambda a, rows: (image_smooth_ref[a, rows] - ratio * smooth_ref[a, rows]) * over,
        held,
        copies,
        extended,
    )
    images = apply_operator(
        [extended[a] for a in range(2)], visc_ref[...], [coup_ref[a] for a in range(2)]
    )
    sums[...] = jnp.zeros_like(sums)
    sums[0:8] = fold([rhs_ref[a] * images[a] for a in range(2)])
    sums[8:16] = fold([image_ref[a] * images[a] for a in range(2)])
    sums[16:24] = fold([images[a] * images[a] for a in range(2)])
    for a in range(2):
        direction_ref[a] = extended[a, HALO : HALO + ROWS]
    send_sums(sums, next_ref)


def finish_kernel(
    first_ref, second_ref, third_ref, first_direction_ref, second_direction_ref,
    solution_ref, hessenberg_ref,
):
    third = third_ref[...]
    beta, h_00, h_10 = first_column(first_ref[...], second_ref[...])
    h_01 = lane_total(third, 0) / beta
    h_11 = (lane_total(third, 1) - h_00 * h_01) / h_10
    h_21 = jnp.sqrt(lane_total(third, 2) - h_01 * h_01 - h_11 * h_11)
    n_00 = h_00 * h_00 + h_10 * h_10
    n_10 = h_00 * h_01 + h_10 * h_11
    n_11 = h_01 * h_01 + h_11 * h_11 + h_21 * h_21
    l_00 = jnp.sqrt(n_00)
    l_10 = n_10 / l_00
    l_11 = jnp.sqrt(n_11 - l_10 * l_10)
    f_0 = beta * h_00 / l_00
    f_1 = (beta * h_01 - l_10 * f_0) / l_11
    c_1 = f_1 / l_11
    c_0 = (f_0 - l_10 * c_1) / l_00
    for a in range(2):
        solution_ref[a] = c_0 * first_direction_ref[a] + c_1 * second_direction_ref[a]
    shape = hessenberg_ref.shape
    row = lax.broadcasted_iota(jnp.int32, shape, 0)
    column = lax.broadcasted_iota(jnp.int32, shape, 1)
    entries = jnp.zeros(shape, jnp.float32)
    for i, j, value in ((0, 0, h_00), (0, 1, h_01), (1, 0, h_10), (1, 1, h_11), (2, 1, h_21)):
        entries = jnp.where((row == i) & (column == j), value, entries)
    hessenberg_ref[...] = entries


def call(kernel, name, in_specs, out_shapes, flops, scratch=()):
    outs = [jax.ShapeDtypeStruct(shape, jnp.float32) for shape in out_shapes]
    return pl.pallas_call(
        kernel,
        name=name,
        in_specs=in_specs,
        out_specs=[VMEM] * len(outs),
        out_shape=outs,
        scratch_shapes=scratch,
        compiler_params=pltpu.CompilerParams(vmem_limit_bytes=40 * 1024 * 1024),
        cost_estimate=pl.CostEstimate(flops=flops, bytes_accessed=4_000_000, transcendentals=0),
    )


def from_everyone(rows):
    return lax.all_to_all(rows, "sub", 0, 0, tiled=True)


def shift(up, down):
    count = lax.axis_size("sub")
    ends = count - 1
    from_below = lax.ppermute(up, "sub", [(i, i + 1) for i in range(ends)])
    from_above = lax.ppermute(down, "sub", [(i + 1, i) for i in range(ends)])
    return from_below, from_above


def on_device(rhs, viscosity, coupling, margin_rows, coarse_basis, coarse_inverse):
    count = lax.axis_size("sub")
    columns = coarse_inverse.shape[1]
    held = pltpu.VMEM((CHUNKS, VECTORS, CHUNK, CELLS), jnp.bfloat16)
    extended = pltpu.VMEM((2, EXT, CELLS), jnp.float32)
    sums = pltpu.VMEM((8 * SLOTS, LANES), jnp.float32)
    sems = pltpu.SemaphoreType.DMA((CHUNKS,))
    row, whole, edge = (count, LANES), (2, ROWS, CELLS), (2, HALO, CELLS)
    packed = (packed_rows(columns), CELLS)
    first, up, down = call(
        start_kernel, "start", [VMEM] * 4 + [ANY], [row, packed, packed], 10_000_000,
        [held, sums, sems],
    )(rhs, viscosity, coupling, coarse_inverse, coarse_basis)
    low, high = shift(up, down)
    first = from_everyone(first)
    (smooth,) = call(
        functools.partial(first_solve_kernel, count), "first_solve", [SMEM] + [VMEM] * 5,
        [(2, EXT, CELLS)], 10_000_000,
    )(margin_rows, viscosity, coupling, rhs, low, high)
    direction, image, head, tail, second = call(
        first_turn_kernel, "first_turn", [VMEM] * 4 + [ANY] + [VMEM] * 4,
        [whole, whole, edge, edge, row], 20_000_000, [held, extended, sums, sems],
    )(first, coarse_inverse, low, high, coarse_basis, smooth, rhs, viscosity, coupling)
    low_image, high_image = shift(tail, head)
    second = from_everyone(second)
    (image_smooth,) = call(
        functools.partial(second_solve_kernel, count), "second_solve", [SMEM] + [VMEM] * 7,
        [(2, EXT, CELLS)], 10_000_000,
    )(margin_rows, viscosity, coupling, image, low, high, low_image, high_image)
    second_direction, third = call(
        second_turn_kernel, "second_turn", [VMEM] * 5 + [ANY] + [VMEM] * 6, [whole, row],
        20_000_000, [held, extended, sums, sems],
    )(
        first, second, coarse_inverse, low, high, coarse_basis, smooth, image_smooth, rhs, image,
        viscosity, coupling,
    )
    third = from_everyone(third)
    return tuple(
        call(finish_kernel, "finish", [VMEM] * 5, [whole, (3, 2)], 1_000_000)(
            first, second, third, direction, second_direction
        )
    )


def solution(mesh):
    in_specs = (
        P(None, ("groups", "sub"), None),
        P(("groups", "sub"), None),
        P(None, ("groups", "sub"), None),
        P("groups"),
        P(None, None, ("groups", "sub"), None),
        P(("groups", "sub"), None),
    )
    out_specs = (P(None, ("groups", "sub"), None), P("groups", None))
    return jax.shard_map(
        on_device, mesh=mesh, in_specs=in_specs, out_specs=out_specs, check_vma=False
    )
```

```python
import functools

import jax
import jax.numpy as jnp
from jax import lax
from jax.experimental import pallas as pl
from jax.experimental.pallas import tpu as pltpu
from jax.sharding import PartitionSpec as P

ROWS = 64
CELLS = 512
VECTORS = 48
HALO = 8
EXT = ROWS + 2 * HALO
STRIP = 32
CHUNK = 16
CHUNKS = 2 * ROWS // CHUNK
LANES = 128
SLOTS = 56
EDGE_AT = 5 * HALO
INVERSE_AT = 2 * VECTORS
SWEEPS = 4
RELAX = 0.7
ROW_FACTOR = (1.0, 4.0)
CELL_FACTOR = (4.0, 1.0)

VMEM = pl.BlockSpec(memory_space=pltpu.VMEM)
SMEM = pl.BlockSpec(memory_space=pltpu.SMEM)
HBM = pl.BlockSpec(memory_space=pltpu.HBM)
ANY = pl.BlockSpec(memory_space=pl.ANY)


def coarse_rows(columns):
    return INVERSE_AT + VECTORS * (columns // 512) + (VECTORS // 2) * (columns % 512 // 256)


def cell_sum(field):
    column = lax.broadcasted_iota(jnp.int32, field.shape, 1)
    left = jnp.where(column == 0, 0.0, pltpu.roll(field, 1, 1))
    right = jnp.where(column == CELLS - 1, 0.0, pltpu.roll(field, CELLS - 1, 1))
    return left + right


def row_sum(field):
    count = field.shape[0]
    return pltpu.roll(field, 1, 0) + pltpu.roll(field, count - 1, 0)


def neighbours(field, component):
    rows, cells = row_sum(field), cell_sum(field)
    if component == 0:
        return rows + CELL_FACTOR[0] * cells
    return ROW_FACTOR[1] * rows + cells


def apply_operator(extended, viscosity, coupling):
    inner = slice(HALO, HALO + ROWS)
    images = []
    for a in range(2):
        around = neighbours(extended[a], a)[inner]
        diagonal = 10.0 * viscosity + jnp.abs(coupling[a]) + 0.05
        images.append(
            diagonal * extended[a][inner]
            - viscosity * around
            + coupling[a] * extended[1 - a][inner]
        )
    return images


def basis_copy(i, basis_ref, held, sems):
    rows = pl.ds(pl.multiple_of(CHUNK * (i % 4), CHUNK), CHUNK)
    return pltpu.make_async_copy(basis_ref.at[:, i // 4, rows, :], held.at[i], sems.at[i])


def restrict_chunk(i, held, field, sums):
    a = i // 4
    start = pl.multiple_of((i % 4) * CHUNK, CHUNK)
    parts = [field[a, pl.ds(start, CHUNK), pl.ds(LANES * c, LANES)] for c in range(4)]
    for k in range(VECTORS):
        total = None
        for c in range(4):
            term = held[i, k, :, pl.ds(LANES * c, LANES)].astype(jnp.float32) * parts[c]
            total = term if total is None else total + term
        sums[8 * k : 8 * k + 8, :] += total[:8] + total[8:]


def fold(field):
    total = None
    for part in field:
        for r in range(0, part.shape[0], 8):
            for c in range(0, part.shape[1], LANES):
                term = part[r : r + 8, c : c + LANES]
                total = term if total is None else total + term
    return total


def send_sums(sums, out_ref):
    pick_row = lax.broadcasted_iota(jnp.int32, (LANES, 8 * SLOTS), 0)
    pick_col = lax.broadcasted_iota(jnp.int32, (LANES, 8 * SLOTS), 1)
    pick = (pick_col // 8 == pick_row).astype(jnp.float32)
    by_slot = jnp.dot(
        pick, sums[...], precision=lax.Precision.HIGHEST, preferred_element_type=jnp.float32
    )
    row = lax.dot_general(
        jnp.ones((8, LANES), jnp.float32),
        by_slot,
        (((1,), (1,)), ((), ())),
        precision=lax.Precision.HIGHEST,
        preferred_element_type=jnp.float32,
    )
    out_ref[...] = jnp.broadcast_to(row[:1], out_ref.shape)


def pack_copies(out_ref, first_row, rhs_ref, visc_ref, coup_ref, inverse_ref, sems, at_sem):
    rows = pl.ds(pl.multiple_of(first_row, HALO), HALO)
    moves = [(visc_ref.at[rows, :], 0, HALO, None)]
    for a in range(2):
        moves.append((coup_ref.at[a, rows, :], HALO * (1 + a), HALO, None))
        moves.append((rhs_ref.at[a, rows, :], HALO * (3 + a), HALO, None))
    columns = inverse_ref.shape[1]
    at = EDGE_AT + INVERSE_AT
    for c in range(0, columns - 511, 512):
        moves.append((inverse_ref.at[:, pl.ds(c, 512)], at, VECTORS, None))
        at += VECTORS
    if columns % 512:
        half = VECTORS // 2
        last = pl.ds(columns - 256, 256)
        moves.append((inverse_ref.at[pl.ds(0, half), last], at, half, 0))
        moves.append((inverse_ref.at[pl.ds(half, half), last], at, half, 256))
    copies = []
    for n, (source, at, size, lane) in enumerate(moves):
        place = pl.ds(at, size)
        target = out_ref.at[place, :] if lane is None else out_ref.at[place, pl.ds(lane, 256)]
        copies.append(pltpu.make_async_copy(source, target, sems.at[at_sem + n]))
    return copies


def pack_count(columns):
    return 5 + columns // 512 + 2 * (columns % 512 // 256)


def start_kernel(
    rhs_ref, visc_ref, coup_ref, inverse_ref, basis_ref,
    sums_ref, partner_ref, other_ref,
    held, field, sums, field_sem, sems, pack_sems,
):
    odd = lax.axis_index("sub") % 2
    field_copy = pltpu.make_async_copy(rhs_ref, field, field_sem)
    field_copy.start()
    for i in range(CHUNKS):
        basis_copy(i, basis_ref, held, sems).start()
    packs = []
    for n, (out_ref, up) in enumerate(((partner_ref, 1 - odd), (other_ref, odd))):
        packs += pack_copies(
            out_ref, up * (ROWS - HALO), rhs_ref, visc_ref, coup_ref, inverse_ref, pack_sems,
            n * pack_count(inverse_ref.shape[1]),
        )
    for copy in packs:
        copy.start()
    sums[...] = jnp.zeros_like(sums)
    field_copy.wait()
    sums[8 * VECTORS : 8 * VECTORS + 8] = fold([field[a] * field[a] for a in range(2)])

    def body(i, carry):
        basis_copy(i, basis_ref, held, sems).wait()
        restrict_chunk(i, held, field, sums)
        return carry

    lax.fori_loop(0, CHUNKS, body, 0)
    picker = lax.broadcasted_iota(jnp.int32, (VECTORS, CHUNK * VECTORS), 0) * CHUNK
    place = lax.broadcasted_iota(jnp.int32, (VECTORS, CHUNK * VECTORS), 1)
    for out_ref, up in ((partner_ref, 1 - odd), (other_ref, odd)):
        pick = (place == picker + up * (CHUNK - 1)).astype(jnp.float32).astype(jnp.bfloat16)
        for a in range(2):
            rows = held[4 * a + 3 * up].reshape(CHUNK * VECTORS, CELLS)
            at = EDGE_AT + VECTORS * a
            out_ref[at : at + VECTORS] = jnp.dot(pick, rows, preferred_element_type=jnp.float32)
    for copy in packs:
        copy.wait()
    send_sums(sums, sums_ref)


def fetch(partner_ref, other_ref, low_ref, high_ref, first_row, sems):
    odd = lax.axis_index("sub") % 2
    rows = pl.ds(first_row, low_ref.shape[0])

    def copies(below_ref, above_ref):
        return (
            pltpu.make_async_copy(below_ref.at[rows], low_ref, sems.at[0]),
            pltpu.make_async_copy(above_ref.at[rows], high_ref, sems.at[1]),
        )

    @pl.when(odd == 1)
    def _():
        for copy in copies(partner_ref, other_ref):
            copy.start()

    @pl.when(odd == 0)
    def _():
        for copy in copies(other_ref, partner_ref):
            copy.start()

    def finish():
        for copy in copies(partner_ref, other_ref):
            copy.wait()

    return finish


def solve(count, margin_ref, visc_ref, coup_ref, field_ref, low_ref, high_ref, edges, out_ref):
    rank = lax.axis_index("sub")
    lower = jnp.where(rank > 0, margin_ref[jnp.maximum(rank - 1, 0)], 0)
    upper = jnp.where(rank < count - 1, margin_ref[rank], 0)
    lower_f, upper_f = lower.astype(jnp.float32), upper.astype(jnp.float32)
    low_scale = 2.0 * jnp.maximum(lower_f, 1.0)
    high_scale = 2.0 * jnp.maximum(upper_f, 1.0)

    def masks(first, rows, side):
        place = lax.broadcasted_iota(jnp.int32, (rows, LANES), 0) + first
        place_f = place.astype(jnp.float32)
        rising = lambda base, scale: (place_f - base + 0.5) / scale
        falling = lambda base, scale: (base - place_f - 0.5) / scale
        if side == 0:
            live = (place >= -lower) & (place < ROWS + upper)
            weight = jnp.where(place < lower, rising(-lower_f, low_scale), 1.0)
            weight = jnp.where(
                place >= ROWS - upper, falling(ROWS + upper_f, high_scale), weight
            )
        elif side < 0:
            live = place < lower
            weight = jnp.where(place >= -lower, falling(lower_f, low_scale), 1.0)
        else:
            live = place >= ROWS - upper
            weight = jnp.where(place < ROWS + upper, rising(ROWS - upper_f, high_scale), 1.0)
        wide = lambda x: jnp.concatenate([x] * (CELLS // LANES), 1)
        return wide(live.astype(jnp.float32)), wide(weight)

    def stack(own, at):
        rows = slice(at, at + HALO)
        return jnp.concatenate([low_ref[rows], own, high_ref[rows]], 0)

    def triple(field):
        return jnp.concatenate([field, field[:STRIP], field[EXT - STRIP :]], 0)

    viscosity = stack(visc_ref[...], 0)
    blocks = [masks(-HALO, EXT, 0), masks(-HALO, STRIP, -1), masks(ROWS + HALO - STRIP, STRIP, 1)]
    live = jnp.concatenate([block[0] for block in blocks], 0)
    first, across, other = [], [], []
    for a in range(2):
        coupling = stack(coup_ref[a], HALO * (1 + a))
        field = jnp.concatenate([edges[a][0], field_ref[a], edges[a][1]], 0)
        scale = RELAX / (10.0 * viscosity + jnp.abs(coupling) + 0.05)
        first.append(live * triple(scale * field))
        across.append(live * triple(scale * viscosity))
        other.append(live * triple(scale * coupling))
    solved = list(first)
    for _ in range(SWEEPS - 1):
        solved = [
            (1.0 - RELAX) * solved[a]
            + first[a]
            + across[a] * neighbours(solved[a], a)
            - other[a] * solved[1 - a]
            for a in range(2)
        ]
    for a in range(2):
        shares = solved[a] * jnp.concatenate([block[1] for block in blocks], 0)
        out_ref[a] = shares[:EXT]
        out_ref[a, :STRIP] += shares[EXT : EXT + STRIP]
        out_ref[a, EXT - STRIP :] += shares[EXT + STRIP :]


def first_solve_kernel(
    count, margin_ref, visc_ref, coup_ref, rhs_ref, partner_ref, other_ref,
    out_ref,
    low, high, sems,
):
    fetch(partner_ref, other_ref, low, high, 0, sems)()
    rows = [slice(HALO * (3 + a), HALO * (4 + a)) for a in range(2)]
    edges = [(low[rows[a]], high[rows[a]]) for a in range(2)]
    solve(count, margin_ref, visc_ref, coup_ref, rhs_ref, low, high, edges, out_ref)


def second_solve_kernel(
    count, margin_ref, visc_ref, coup_ref, image_ref, partner_ref, other_ref,
    partner_image_ref, other_image_ref,
    out_ref,
    low, high, low_image, high_image, sems, image_sems,
):
    images = fetch(partner_image_ref, other_image_ref, low_image, high_image, 0, image_sems)
    fetch(partner_ref, other_ref, low, high, 0, sems)()
    images()
    edges = [(low_image[a], high_image[a]) for a in range(2)]
    solve(count, margin_ref, visc_ref, coup_ref, image_ref, low, high, edges, out_ref)


def line_up(residuals):
    devices = residuals.shape[0]
    lane = lax.broadcasted_iota(jnp.int32, (1, LANES), 1)
    tiles = [jnp.zeros((1, LANES), jnp.float32) for _ in range(devices * VECTORS // LANES)]
    for t in range(devices):
        tile, offset = divmod(VECTORS * t, LANES)
        row = jnp.where(lane < VECTORS, residuals[t : t + 1], 0.0)
        if offset:
            row = pltpu.roll(row, offset, 1)
        if offset + VECTORS <= LANES:
            tiles[tile] = tiles[tile] + row
        else:
            tiles[tile] = tiles[tile] + jnp.where(lane >= offset, row, 0.0)
            tiles[tile + 1] = tiles[tile + 1] + jnp.where(lane < offset, row, 0.0)
    return jnp.concatenate(tiles, 1)


def rounded(column):
    return column.astype(jnp.bfloat16).astype(jnp.float32)


def lift(inverse_ref, residual):
    return rounded(jnp.sum(inverse_ref[...] * residual, 1, keepdims=True))


def lift_packed(ref, residual):
    columns = residual.shape[1]
    at, total = INVERSE_AT, None
    for c in range(0, columns - 511, 512):
        term = jnp.sum(ref[at : at + VECTORS] * residual[:, c : c + 512], 1, keepdims=True)
        total = term if total is None else total + term
        at += VECTORS
    if columns % 512:
        half = VECTORS // 2
        last = residual[:, columns - 256 :]
        rows = ref[at : at + half]
        term = jnp.concatenate(
            [
                jnp.sum(rows[:, :256] * last, 1, keepdims=True),
                jnp.sum(rows[:, 256:] * last, 1, keepdims=True),
            ],
            0,
        )
        total = term if total is None else total + term
    return rounded(total)


def edge_values(ref, lifted):
    return [
        jnp.sum(ref[VECTORS * a : VECTORS * (a + 1)] * lifted, 0, keepdims=True)
        for a in range(2)
    ]


def spread(lifted):
    shape = (VECTORS, CHUNK * VECTORS)
    owner = lax.broadcasted_iota(jnp.int32, shape, 1) // CHUNK
    row = lax.broadcasted_iota(jnp.int32, shape, 0)
    line = jnp.sum(jnp.where(owner == row, lifted, 0.0), 0, keepdims=True)
    shape = (CHUNK, CHUNK * VECTORS)
    place = lax.broadcasted_iota(jnp.int32, shape, 1) % CHUNK
    row = lax.broadcasted_iota(jnp.int32, shape, 0)
    return jnp.where(place == row, line, 0.0).astype(jnp.bfloat16)


class Coarse:
    def __init__(self, partner_ref, other_ref, basis_ref, held, low, high, sems, side_sems):
        self.held, self.low, self.high = held, low, high
        self.sides_ready = fetch(partner_ref, other_ref, low, high, EDGE_AT, side_sems)
        self.copies = [basis_copy(i, basis_ref, held, sems) for i in range(CHUNKS)]
        for copy in self.copies:
            copy.start()

    def prolong(self, residual, inverse_ref, smooth, extended):
        matrix = spread(lift(inverse_ref, residual))
        for i, copy in enumerate(self.copies):
            a, start = i // 4, HALO + CHUNK * (i % 4)
            rows = slice(start, start + CHUNK)
            if i == CHUNKS // 2:
                self.prolong_edges(residual, smooth, extended)
            copy.wait()
            coarse = jnp.dot(
                matrix,
                self.held[i].reshape(CHUNK * VECTORS, CELLS),
                preferred_element_type=jnp.float32,
            )
            extended[a, rows] = smooth(a, rows) + coarse

    def prolong_edges(self, residual, smooth, extended):
        self.sides_ready()
        low_edge = edge_values(self.low, lift_packed(self.low, residual))
        high_edge = edge_values(self.high, lift_packed(self.high, residual))
        place = lax.broadcasted_iota(jnp.int32, (HALO, CELLS), 0)
        for a in range(2):
            rows = slice(0, HALO)
            extended[a, rows] = smooth(a, rows) + jnp.where(place == HALO - 1, low_edge[a], 0.0)
            rows = slice(EXT - HALO, EXT)
            extended[a, rows] = smooth(a, rows) + jnp.where(place == 0, high_edge[a], 0.0)


def lane_total(received, lane):
    return jnp.sum(received[:, lane : lane + 1], 0, keepdims=True)


def first_turn_kernel(
    sums_ref, inverse_ref, partner_ref, other_ref, basis_ref, smooth_ref, rhs_ref, visc_ref,
    coup_ref,
    direction_ref, image_ref, partner_rows_ref, other_rows_ref, next_ref,
    held, low, high, sems, side_sems, extended, sums,
):
    coarse = Coarse(partner_ref, other_ref, basis_ref, held, low, high, sems, side_sems)
    received = sums_ref[...]
    over_beta = 1.0 / jnp.sqrt(lane_total(received, VECTORS))
    residual = line_up(received) * over_beta
    coarse.prolong(
        residual,
        inverse_ref,
        lambda a, rows: smooth_ref[a, rows] * over_beta,
        extended,
    )
    images = apply_operator(
        [extended[a] for a in range(2)], visc_ref[...], [coup_ref[a] for a in range(2)]
    )
    odd = lax.axis_index("sub") % 2 == 1
    for a in range(2):
        direction_ref[a] = extended[a, HALO : HALO + ROWS]
        image_ref[a] = images[a]
        head, tail = images[a][:HALO], images[a][ROWS - HALO :]
        partner_rows_ref[a] = jnp.where(odd, head, tail)
        other_rows_ref[a] = jnp.where(odd, tail, head)
    sums[...] = jnp.zeros_like(sums)
    at = 8 * VECTORS
    sums[at : at + 8] = fold([rhs_ref[a] * images[a] for a in range(2)])
    sums[at + 8 : at + 16] = fold([images[a] * images[a] for a in range(2)])

    def body(i, carry):
        restrict_chunk(i, held, image_ref, sums)
        return carry

    lax.fori_loop(0, CHUNKS, body, 0)
    send_sums(sums, next_ref)


def first_column(first, second):
    beta = jnp.sqrt(lane_total(first, VECTORS))
    h_00 = lane_total(second, VECTORS) / beta
    h_10 = jnp.sqrt(lane_total(second, VECTORS + 1) - h_00 * h_00)
    return beta, h_00, h_10


def second_turn_kernel(
    first_ref, second_ref, inverse_ref, partner_ref, other_ref, basis_ref, smooth_ref,
    image_smooth_ref, rhs_ref, image_ref, visc_ref, coup_ref,
    direction_ref, next_ref,
    held, low, high, sems, side_sems, extended, sums,
):
    coarse = Coarse(partner_ref, other_ref, basis_ref, held, low, high, sems, side_sems)
    first, second = first_ref[...], second_ref[...]
    beta, h_00, h_10 = first_column(first, second)
    ratio = h_00 / beta
    over = 1.0 / h_10
    residual = (line_up(second) - ratio * line_up(first)) * over
    coarse.prolong(
        residual,
        inverse_ref,
        lambda a, rows: (image_smooth_ref[a, rows] - ratio * smooth_ref[a, rows]) * over,
        extended,
    )
    images = apply_operator(
        [extended[a] for a in range(2)], visc_ref[...], [coup_ref[a] for a in range(2)]
    )
    sums[...] = jnp.zeros_like(sums)
    sums[0:8] = fold([rhs_ref[a] * images[a] for a in range(2)])
    sums[8:16] = fold([image_ref[a] * images[a] for a in range(2)])
    sums[16:24] = fold([images[a] * images[a] for a in range(2)])
    for a in range(2):
        direction_ref[a] = extended[a, HALO : HALO + ROWS]
    send_sums(sums, next_ref)


def finish_kernel(
    first_ref, second_ref, third_ref, first_direction_ref, second_direction_ref,
    solution_ref, hessenberg_ref,
):
    third = third_ref[...]
    beta, h_00, h_10 = first_column(first_ref[...], second_ref[...])
    h_01 = lane_total(third, 0) / beta
    h_11 = (lane_total(third, 1) - h_00 * h_01) / h_10
    h_21 = jnp.sqrt(lane_total(third, 2) - h_01 * h_01 - h_11 * h_11)
    n_00 = h_00 * h_00 + h_10 * h_10
    n_10 = h_00 * h_01 + h_10 * h_11
    n_11 = h_01 * h_01 + h_11 * h_11 + h_21 * h_21
    l_00 = jnp.sqrt(n_00)
    l_10 = n_10 / l_00
    l_11 = jnp.sqrt(n_11 - l_10 * l_10)
    f_0 = beta * h_00 / l_00
    f_1 = (beta * h_01 - l_10 * f_0) / l_11
    c_1 = f_1 / l_11
    c_0 = (f_0 - l_10 * c_1) / l_00
    for a in range(2):
        solution_ref[a] = c_0 * first_direction_ref[a] + c_1 * second_direction_ref[a]
    shape = hessenberg_ref.shape
    row = lax.broadcasted_iota(jnp.int32, shape, 1)
    column = lax.broadcasted_iota(jnp.int32, shape, 0)
    entries = jnp.zeros(shape, jnp.float32)
    for i, j, value in ((0, 0, h_00), (0, 1, h_01), (1, 0, h_10), (1, 1, h_11), (2, 1, h_21)):
        entries = jnp.where((row == i) & (column == j), value, entries)
    hessenberg_ref[...] = entries


def call(kernel, name, in_specs, outs, flops, scratch=(), traffic=4_000_000):
    return pl.pallas_call(
        kernel,
        name=name,
        in_specs=in_specs,
        out_specs=[VMEM] * len(outs),
        out_shape=outs,
        scratch_shapes=scratch,
        compiler_params=pltpu.CompilerParams(vmem_limit_bytes=16 * 1024 * 1024),
        cost_estimate=pl.CostEstimate(flops=flops, bytes_accessed=traffic, transcendentals=0),
    )


def in_hbm(array):
    return pltpu.with_memory_space_constraint(array, pltpu.HBM)


def from_everyone(rows):
    return lax.all_to_all(rows, "sub", 0, 0, tiled=True)


def from_everyone_reversed(rows):
    order = [list(range(lax.axis_size("sub")))[::-1]]
    return lax.all_to_all(rows, "sub", 0, 0, tiled=True, axis_index_groups=order)


def swap(partner, other):
    count = lax.axis_size("sub")
    both = lambda lows: [pair for i in lows for pair in ((i, i + 1), (i + 1, i))]
    return (
        lax.ppermute(partner, "sub", both(range(0, count, 2))),
        lax.ppermute(other, "sub", both(range(1, count - 1, 2))),
    )


def on_device(rhs, viscosity, coupling, margin_rows, coarse_basis, coarse_inverse):
    count = lax.axis_size("sub")
    columns = coarse_inverse.shape[1]
    f32 = lambda *shape: jax.ShapeDtypeStruct(shape, jnp.float32)
    dma = lambda *shape: pltpu.SemaphoreType.DMA(shape)
    held = pltpu.VMEM((CHUNKS, VECTORS, CHUNK, CELLS), jnp.bfloat16)
    field = pltpu.VMEM((2, ROWS, CELLS), jnp.float32)
    sums = pltpu.VMEM((8 * SLOTS, LANES), jnp.float32)
    edge_scratch = [pltpu.VMEM((EDGE_AT, CELLS), jnp.float32)] * 2
    image_scratch = [pltpu.VMEM((2, HALO, CELLS), jnp.float32)] * 2
    turn_scratch = (
        [held]
        + [pltpu.VMEM((coarse_rows(columns), CELLS), jnp.float32)] * 2
        + [dma(CHUNKS), dma(2), pltpu.VMEM((2, EXT, CELLS), jnp.float32), sums]
    )
    row, whole, edge = f32(count, LANES), f32(2, ROWS, CELLS), f32(2, HALO, CELLS)
    packed, smoothed = f32(EDGE_AT + coarse_rows(columns), CELLS), f32(2, EXT, CELLS)
    basis = in_hbm(coarse_basis)
    first, partner, other = call(
        start_kernel, "start", [HBM] * 5, [row, packed, packed], 10_000_000,
        [held, field, sums, dma(), dma(CHUNKS), dma(2 * pack_count(columns))],
    )(in_hbm(rhs), in_hbm(viscosity), in_hbm(coupling), in_hbm(coarse_inverse), basis)
    partner, other = swap(partner, other)
    first = from_everyone(first)
    (smooth,) = call(
        functools.partial(first_solve_kernel, count), "first_solve",
        [SMEM] + [VMEM] * 3 + [ANY] * 2, [smoothed], 10_000_000, edge_scratch + [dma(2)],
    )(margin_rows, viscosity, coupling, rhs, partner, other)
    partner, other = in_hbm(partner), in_hbm(other)
    direction, image, partner_rows, other_rows, second = call(
        first_turn_kernel, "first_turn", [VMEM] * 2 + [HBM] * 3 + [VMEM] * 4,
        [whole, whole, edge, edge, row], 20_000_000, turn_scratch,
    )(first, coarse_inverse, partner, other, basis, smooth, rhs, viscosity, coupling)
    partner_rows, other_rows = swap(partner_rows, other_rows)
    second = from_everyone(second)
    (image_smooth,) = call(
        functools.partial(second_solve_kernel, count), "second_solve",
        [SMEM] + [VMEM] * 3 + [HBM] * 2 + [ANY] * 2, [smoothed], 0,
        edge_scratch + image_scratch + [dma(2)] * 2, 0,
    )(margin_rows, viscosity, coupling, image, partner, other, partner_rows, other_rows)
    second_direction, third = call(
        second_turn_kernel, "second_turn", [VMEM] * 3 + [HBM] * 3 + [VMEM] * 6, [whole, row],
        20_000_000, turn_scratch,
    )(
        first, second, coarse_inverse, partner, other, basis, smooth, image_smooth, rhs, image,
        viscosity, coupling,
    )
    third = from_everyone_reversed(third)
    result, transposed = call(finish_kernel, "finish", [VMEM] * 5, [whole, f32(2, 3)], 1_000_000)(
        first, second, third, direction, second_direction
    )
    return result, transposed.T


def solution(mesh):
    in_specs = (
        P(None, ("groups", "sub"), None),
        P(("groups", "sub"), None),
        P(None, ("groups", "sub"), None),
        P("groups"),
        P(None, None, ("groups", "sub"), None),
        P(("groups", "sub"), None),
    )
    out_specs = (P(None, ("groups", "sub"), None), P("groups", None))
    return jax.shard_map(
        on_device, mesh=mesh, in_specs=in_specs, out_specs=out_specs, check_vma=False
    )
```

```python
import functools

import jax
import jax.numpy as jnp
from jax import lax
from jax.experimental import pallas as pl
from jax.experimental.pallas import tpu as pltpu
from jax.sharding import PartitionSpec as P

ROWS = 64
CELLS = 512
VECTORS = 48
HALO = 8
EXT = ROWS + 2 * HALO
STRIP = 32
CHUNK = 16
CHUNKS = 2 * ROWS // CHUNK
AHEAD = 3
LANES = 128
SLOTS = 56
EDGE_AT = 5 * HALO
INVERSE_AT = 2 * VECTORS
SWEEPS = 4
RELAX = 0.7
ROW_FACTOR = (1.0, 4.0)
CELL_FACTOR = (4.0, 1.0)

VMEM = pl.BlockSpec(memory_space=pltpu.VMEM)
SMEM = pl.BlockSpec(memory_space=pltpu.SMEM)
HBM = pl.BlockSpec(memory_space=pltpu.HBM)
ANY = pl.BlockSpec(memory_space=pl.ANY)


def coarse_rows(columns):
    return INVERSE_AT + VECTORS * (columns // 512) + (VECTORS // 2) * (columns % 512 // 256)


def cell_sum(field):
    column = lax.broadcasted_iota(jnp.int32, field.shape, 1)
    left = jnp.where(column == 0, 0.0, pltpu.roll(field, 1, 1))
    right = jnp.where(column == CELLS - 1, 0.0, pltpu.roll(field, CELLS - 1, 1))
    return left + right


def row_sum(field):
    count = field.shape[0]
    return pltpu.roll(field, 1, 0) + pltpu.roll(field, count - 1, 0)


def neighbours(field, component):
    rows, cells = row_sum(field), cell_sum(field)
    if component == 0:
        return rows + CELL_FACTOR[0] * cells
    return ROW_FACTOR[1] * rows + cells


def apply_operator(extended, viscosity, coupling):
    inner = slice(HALO, HALO + ROWS)
    images = []
    for a in range(2):
        around = neighbours(extended[a], a)[inner]
        diagonal = 10.0 * viscosity + jnp.abs(coupling[a]) + 0.05
        images.append(
            diagonal * extended[a][inner]
            - viscosity * around
            + coupling[a] * extended[1 - a][inner]
        )
    return images


def basis_copy(i, basis_ref, held, sems):
    rows = pl.ds(pl.multiple_of(CHUNK * (i % 4), CHUNK), CHUNK)
    return pltpu.make_async_copy(basis_ref.at[:, i // 4, rows, :], held.at[i], sems.at[i])


def restrict_chunk(i, held, field, sums):
    a = i // 4
    start = pl.multiple_of((i % 4) * CHUNK, CHUNK)
    parts = [field[a, pl.ds(start, CHUNK), pl.ds(LANES * c, LANES)] for c in range(4)]
    for k in range(VECTORS):
        total = None
        for c in range(4):
            term = held[i, k, :, pl.ds(LANES * c, LANES)].astype(jnp.float32) * parts[c]
            total = term if total is None else total + term
        sums[8 * k : 8 * k + 8, :] += total[:8] + total[8:]


def fold(field):
    total = None
    for part in field:
        for r in range(0, part.shape[0], 8):
            for c in range(0, part.shape[1], LANES):
                term = part[r : r + 8, c : c + LANES]
                total = term if total is None else total + term
    return total


def send_sums(sums, out_ref):
    pick_row = lax.broadcasted_iota(jnp.int32, (LANES, 8 * SLOTS), 0)
    pick_col = lax.broadcasted_iota(jnp.int32, (LANES, 8 * SLOTS), 1)
    pick = (pick_col // 8 == pick_row).astype(jnp.float32)
    by_slot = jnp.dot(
        pick, sums[...], precision=lax.Precision.HIGHEST, preferred_element_type=jnp.float32
    )
    row = lax.dot_general(
        jnp.ones((8, LANES), jnp.float32),
        by_slot,
        (((1,), (1,)), ((), ())),
        precision=lax.Precision.HIGHEST,
        preferred_element_type=jnp.float32,
    )
    out_ref[...] = jnp.broadcast_to(row[:1], out_ref.shape)


def pack_copies(out_ref, first_row, rhs_ref, visc_ref, coup_ref, inverse_ref, sems, at_sem):
    rows = pl.ds(pl.multiple_of(first_row, HALO), HALO)
    moves = [(visc_ref.at[rows, :], 0, HALO, None)]
    for a in range(2):
        moves.append((coup_ref.at[a, rows, :], HALO * (1 + a), HALO, None))
        moves.append((rhs_ref.at[a, rows, :], HALO * (3 + a), HALO, None))
    columns = inverse_ref.shape[1]
    at = EDGE_AT + INVERSE_AT
    for c in range(0, columns - 511, 512):
        moves.append((inverse_ref.at[:, pl.ds(c, 512)], at, VECTORS, None))
        at += VECTORS
    if columns % 512:
        half = VECTORS // 2
        last = pl.ds(columns - 256, 256)
        moves.append((inverse_ref.at[pl.ds(0, half), last], at, half, 0))
        moves.append((inverse_ref.at[pl.ds(half, half), last], at, half, 256))
    copies = []
    for n, (source, at, size, lane) in enumerate(moves):
        place = pl.ds(at, size)
        target = out_ref.at[place, :] if lane is None else out_ref.at[place, pl.ds(lane, 256)]
        copies.append(pltpu.make_async_copy(source, target, sems.at[at_sem + n]))
    return copies


def pack_count(columns):
    return 5 + columns // 512 + 2 * (columns % 512 // 256)


def start_kernel(
    rhs_ref, visc_ref, coup_ref, inverse_ref, basis_ref,
    sums_ref, partner_ref, other_ref,
    held, field, sums, field_sem, sems, pack_sems,
):
    odd = lax.axis_index("sub") % 2
    field_copy = pltpu.make_async_copy(rhs_ref, field, field_sem)
    field_copy.start()
    for i in range(AHEAD):
        basis_copy(i, basis_ref, held, sems).start()
    packs = []
    for n, (out_ref, up) in enumerate(((partner_ref, 1 - odd), (other_ref, odd))):
        packs += pack_copies(
            out_ref, up * (ROWS - HALO), rhs_ref, visc_ref, coup_ref, inverse_ref, pack_sems,
            n * pack_count(inverse_ref.shape[1]),
        )
    for copy in packs:
        copy.start()
    sums[...] = jnp.zeros_like(sums)
    field_copy.wait()
    sums[8 * VECTORS : 8 * VECTORS + 8] = fold([field[a] * field[a] for a in range(2)])

    def body(i, carry):
        basis_copy(i, basis_ref, held, sems).wait()

        @pl.when(i + AHEAD < CHUNKS)
        def _():
            basis_copy(i + AHEAD, basis_ref, held, sems).start()

        restrict_chunk(i, held, field, sums)
        return carry

    lax.fori_loop(0, CHUNKS, body, 0)
    picker = lax.broadcasted_iota(jnp.int32, (VECTORS, CHUNK * VECTORS), 0) * CHUNK
    place = lax.broadcasted_iota(jnp.int32, (VECTORS, CHUNK * VECTORS), 1)
    for out_ref, up in ((partner_ref, 1 - odd), (other_ref, odd)):
        pick = (place == picker + up * (CHUNK - 1)).astype(jnp.float32).astype(jnp.bfloat16)
        for a in range(2):
            rows = held[4 * a + 3 * up].reshape(CHUNK * VECTORS, CELLS)
            at = EDGE_AT + VECTORS * a
            out_ref[at : at + VECTORS] = jnp.dot(pick, rows, preferred_element_type=jnp.float32)
    for copy in packs:
        copy.wait()
    send_sums(sums, sums_ref)


def fetch(partner_ref, other_ref, low_ref, high_ref, first_row, sems):
    odd = lax.axis_index("sub") % 2
    rows = pl.ds(first_row, low_ref.shape[0])

    def copies(below_ref, above_ref):
        return (
            pltpu.make_async_copy(below_ref.at[rows], low_ref, sems.at[0]),
            pltpu.make_async_copy(above_ref.at[rows], high_ref, sems.at[1]),
        )

    @pl.when(odd == 1)
    def _():
        for copy in copies(partner_ref, other_ref):
            copy.start()

    @pl.when(odd == 0)
    def _():
        for copy in copies(other_ref, partner_ref):
            copy.start()

    def finish():
        for copy in copies(partner_ref, other_ref):
            copy.wait()

    return finish


def solve(count, margin_ref, visc_ref, coup_ref, field_ref, low_ref, high_ref, edges, out_ref):
    rank = lax.axis_index("sub")
    lower = jnp.where(rank > 0, margin_ref[jnp.maximum(rank - 1, 0)], 0)
    upper = jnp.where(rank < count - 1, margin_ref[rank], 0)
    lower_f, upper_f = lower.astype(jnp.float32), upper.astype(jnp.float32)
    low_scale = 2.0 * jnp.maximum(lower_f, 1.0)
    high_scale = 2.0 * jnp.maximum(upper_f, 1.0)

    def masks(first, rows, side):
        place = lax.broadcasted_iota(jnp.int32, (rows, LANES), 0) + first
        place_f = place.astype(jnp.float32)
        rising = lambda base, scale: (place_f - base + 0.5) / scale
        falling = lambda base, scale: (base - place_f - 0.5) / scale
        if side == 0:
            live = (place >= -lower) & (place < ROWS + upper)
            weight = jnp.where(place < lower, rising(-lower_f, low_scale), 1.0)
            weight = jnp.where(
                place >= ROWS - upper, falling(ROWS + upper_f, high_scale), weight
            )
        elif side < 0:
            live = place < lower
            weight = jnp.where(place >= -lower, falling(lower_f, low_scale), 1.0)
        else:
            live = place >= ROWS - upper
            weight = jnp.where(place < ROWS + upper, rising(ROWS - upper_f, high_scale), 1.0)
        wide = lambda x: jnp.concatenate([x] * (CELLS // LANES), 1)
        return wide(live.astype(jnp.float32)), wide(weight)

    def stack(own, at):
        rows = slice(at, at + HALO)
        return jnp.concatenate([low_ref[rows], own, high_ref[rows]], 0)

    def triple(field):
        return jnp.concatenate([field, field[:STRIP], field[EXT - STRIP :]], 0)

    viscosity = stack(visc_ref[...], 0)
    blocks = [masks(-HALO, EXT, 0), masks(-HALO, STRIP, -1), masks(ROWS + HALO - STRIP, STRIP, 1)]
    live = jnp.concatenate([block[0] for block in blocks], 0)
    first, across, other = [], [], []
    for a in range(2):
        coupling = stack(coup_ref[a], HALO * (1 + a))
        field = jnp.concatenate([edges[a][0], field_ref[a], edges[a][1]], 0)
        scale = RELAX / (10.0 * viscosity + jnp.abs(coupling) + 0.05)
        first.append(live * triple(scale * field))
        across.append(live * triple(scale * viscosity))
        other.append(live * triple(scale * coupling))
    solved = list(first)
    for _ in range(SWEEPS - 1):
        solved = [
            (1.0 - RELAX) * solved[a]
            + first[a]
            + across[a] * neighbours(solved[a], a)
            - other[a] * solved[1 - a]
            for a in range(2)
        ]
    for a in range(2):
        shares = solved[a] * jnp.concatenate([block[1] for block in blocks], 0)
        out_ref[a] = shares[:EXT]
        out_ref[a, :STRIP] += shares[EXT : EXT + STRIP]
        out_ref[a, EXT - STRIP :] += shares[EXT + STRIP :]


def first_solve_kernel(
    count, margin_ref, visc_ref, coup_ref, rhs_ref, partner_ref, other_ref,
    out_ref,
    low, high, sems,
):
    fetch(partner_ref, other_ref, low, high, 0, sems)()
    rows = [slice(HALO * (3 + a), HALO * (4 + a)) for a in range(2)]
    edges = [(low[rows[a]], high[rows[a]]) for a in range(2)]
    solve(count, margin_ref, visc_ref, coup_ref, rhs_ref, low, high, edges, out_ref)


def second_solve_kernel(
    count, margin_ref, visc_ref, coup_ref, image_ref, partner_ref, other_ref,
    partner_image_ref, other_image_ref,
    out_ref,
    low, high, low_image, high_image, sems, image_sems,
):
    images = fetch(partner_image_ref, other_image_ref, low_image, high_image, 0, image_sems)
    fetch(partner_ref, other_ref, low, high, 0, sems)()
    images()
    edges = [(low_image[a], high_image[a]) for a in range(2)]
    solve(count, margin_ref, visc_ref, coup_ref, image_ref, low, high, edges, out_ref)


def line_up(residuals):
    devices = residuals.shape[0]
    lane = lax.broadcasted_iota(jnp.int32, (1, LANES), 1)
    tiles = [jnp.zeros((1, LANES), jnp.float32) for _ in range(devices * VECTORS // LANES)]
    for t in range(devices):
        tile, offset = divmod(VECTORS * t, LANES)
        row = jnp.where(lane < VECTORS, residuals[t : t + 1], 0.0)
        if offset:
            row = pltpu.roll(row, offset, 1)
        if offset + VECTORS <= LANES:
            tiles[tile] = tiles[tile] + row
        else:
            tiles[tile] = tiles[tile] + jnp.where(lane >= offset, row, 0.0)
            tiles[tile + 1] = tiles[tile + 1] + jnp.where(lane < offset, row, 0.0)
    return jnp.concatenate(tiles, 1)


def rounded(column):
    return column.astype(jnp.bfloat16).astype(jnp.float32)


def lift(inverse_ref, residual):
    return rounded(jnp.sum(inverse_ref[...] * residual, 1, keepdims=True))


def lift_packed(ref, residual):
    columns = residual.shape[1]
    at, total = INVERSE_AT, None
    for c in range(0, columns - 511, 512):
        term = jnp.sum(ref[at : at + VECTORS] * residual[:, c : c + 512], 1, keepdims=True)
        total = term if total is None else total + term
        at += VECTORS
    if columns % 512:
        half = VECTORS // 2
        last = residual[:, columns - 256 :]
        rows = ref[at : at + half]
        term = jnp.concatenate(
            [
                jnp.sum(rows[:, :256] * last, 1, keepdims=True),
                jnp.sum(rows[:, 256:] * last, 1, keepdims=True),
            ],
            0,
        )
        total = term if total is None else total + term
    return rounded(total)


def edge_values(ref, lifted):
    return [
        jnp.sum(ref[VECTORS * a : VECTORS * (a + 1)] * lifted, 0, keepdims=True)
        for a in range(2)
    ]


def spread(lifted):
    shape = (VECTORS, CHUNK * VECTORS)
    owner = lax.broadcasted_iota(jnp.int32, shape, 1) // CHUNK
    row = lax.broadcasted_iota(jnp.int32, shape, 0)
    line = jnp.sum(jnp.where(owner == row, lifted, 0.0), 0, keepdims=True)
    shape = (CHUNK, CHUNK * VECTORS)
    place = lax.broadcasted_iota(jnp.int32, shape, 1) % CHUNK
    row = lax.broadcasted_iota(jnp.int32, shape, 0)
    return jnp.where(place == row, line, 0.0).astype(jnp.bfloat16)


class Coarse:
    def __init__(self, partner_ref, other_ref, basis_ref, held, low, high, sems, side_sems):
        self.held, self.low, self.high = held, low, high
        self.sides_ready = fetch(partner_ref, other_ref, low, high, EDGE_AT, side_sems)
        self.copies = [basis_copy(i, basis_ref, held, sems) for i in range(CHUNKS)]
        for copy in self.copies[:AHEAD]:
            copy.start()

    def prolong(self, residual, inverse_ref, smooth, extended):
        matrix = spread(lift(inverse_ref, residual))
        for i, copy in enumerate(self.copies):
            a, start = i // 4, HALO + CHUNK * (i % 4)
            rows = slice(start, start + CHUNK)
            if i == CHUNKS // 2:
                self.prolong_edges(residual, smooth, extended)
            copy.wait()
            if i + AHEAD < CHUNKS:
                self.copies[i + AHEAD].start()
            coarse = jnp.dot(
                matrix,
                self.held[i].reshape(CHUNK * VECTORS, CELLS),
                preferred_element_type=jnp.float32,
            )
            extended[a, rows] = smooth(a, rows) + coarse

    def prolong_edges(self, residual, smooth, extended):
        self.sides_ready()
        low_edge = edge_values(self.low, lift_packed(self.low, residual))
        high_edge = edge_values(self.high, lift_packed(self.high, residual))
        place = lax.broadcasted_iota(jnp.int32, (HALO, CELLS), 0)
        for a in range(2):
            rows = slice(0, HALO)
            extended[a, rows] = smooth(a, rows) + jnp.where(place == HALO - 1, low_edge[a], 0.0)
            rows = slice(EXT - HALO, EXT)
            extended[a, rows] = smooth(a, rows) + jnp.where(place == 0, high_edge[a], 0.0)


def lane_total(received, lane):
    return jnp.sum(received[:, lane : lane + 1], 0, keepdims=True)


def first_turn_kernel(
    sums_ref, inverse_ref, partner_ref, other_ref, basis_ref, smooth_ref, rhs_ref, visc_ref,
    coup_ref,
    direction_ref, image_ref, partner_rows_ref, other_rows_ref, next_ref,
    held, low, high, sems, side_sems, extended, sums,
):
    coarse = Coarse(partner_ref, other_ref, basis_ref, held, low, high, sems, side_sems)
    received = sums_ref[...]
    over_beta = 1.0 / jnp.sqrt(lane_total(received, VECTORS))
    residual = line_up(received) * over_beta
    coarse.prolong(
        residual,
        inverse_ref,
        lambda a, rows: smooth_ref[a, rows] * over_beta,
        extended,
    )
    images = apply_operator(
        [extended[a] for a in range(2)], visc_ref[...], [coup_ref[a] for a in range(2)]
    )
    odd = lax.axis_index("sub") % 2 == 1
    for a in range(2):
        direction_ref[a] = extended[a, HALO : HALO + ROWS]
        image_ref[a] = images[a]
        head, tail = images[a][:HALO], images[a][ROWS - HALO :]
        partner_rows_ref[a] = jnp.where(odd, head, tail)
        other_rows_ref[a] = jnp.where(odd, tail, head)
    sums[...] = jnp.zeros_like(sums)
    at = 8 * VECTORS
    sums[at : at + 8] = fold([rhs_ref[a] * images[a] for a in range(2)])
    sums[at + 8 : at + 16] = fold([images[a] * images[a] for a in range(2)])

    def body(i, carry):
        restrict_chunk(i, held, image_ref, sums)
        return carry

    lax.fori_loop(0, CHUNKS, body, 0)
    send_sums(sums, next_ref)


def first_column(first, second):
    beta = jnp.sqrt(lane_total(first, VECTORS))
    h_00 = lane_total(second, VECTORS) / beta
    h_10 = jnp.sqrt(lane_total(second, VECTORS + 1) - h_00 * h_00)
    return beta, h_00, h_10


def second_turn_kernel(
    first_ref, second_ref, inverse_ref, partner_ref, other_ref, basis_ref, smooth_ref,
    image_smooth_ref, rhs_ref, image_ref, visc_ref, coup_ref,
    direction_ref, next_ref,
    held, low, high, sems, side_sems, extended, sums,
):
    coarse = Coarse(partner_ref, other_ref, basis_ref, held, low, high, sems, side_sems)
    first, second = first_ref[...], second_ref[...]
    beta, h_00, h_10 = first_column(first, second)
    ratio = h_00 / beta
    over = 1.0 / h_10
    residual = (line_up(second) - ratio * line_up(first)) * over
    coarse.prolong(
        residual,
        inverse_ref,
        lambda a, rows: (image_smooth_ref[a, rows] - ratio * smooth_ref[a, rows]) * over,
        extended,
    )
    images = apply_operator(
        [extended[a] for a in range(2)], visc_ref[...], [coup_ref[a] for a in range(2)]
    )
    sums[...] = jnp.zeros_like(sums)
    sums[0:8] = fold([rhs_ref[a] * images[a] for a in range(2)])
    sums[8:16] = fold([image_ref[a] * images[a] for a in range(2)])
    sums[16:24] = fold([images[a] * images[a] for a in range(2)])
    for a in range(2):
        direction_ref[a] = extended[a, HALO : HALO + ROWS]
    send_sums(sums, next_ref)


def finish_kernel(
    first_ref, second_ref, third_ref, first_direction_ref, second_direction_ref,
    solution_ref, hessenberg_ref,
):
    third = third_ref[...]
    beta, h_00, h_10 = first_column(first_ref[...], second_ref[...])
    h_01 = lane_total(third, 0) / beta
    h_11 = (lane_total(third, 1) - h_00 * h_01) / h_10
    h_21 = jnp.sqrt(lane_total(third, 2) - h_01 * h_01 - h_11 * h_11)
    n_00 = h_00 * h_00 + h_10 * h_10
    n_10 = h_00 * h_01 + h_10 * h_11
    n_11 = h_01 * h_01 + h_11 * h_11 + h_21 * h_21
    l_00 = jnp.sqrt(n_00)
    l_10 = n_10 / l_00
    l_11 = jnp.sqrt(n_11 - l_10 * l_10)
    f_0 = beta * h_00 / l_00
    f_1 = (beta * h_01 - l_10 * f_0) / l_11
    c_1 = f_1 / l_11
    c_0 = (f_0 - l_10 * c_1) / l_00
    for a in range(2):
        solution_ref[a] = c_0 * first_direction_ref[a] + c_1 * second_direction_ref[a]
    shape = hessenberg_ref.shape
    row = lax.broadcasted_iota(jnp.int32, shape, 1)
    column = lax.broadcasted_iota(jnp.int32, shape, 0)
    entries = jnp.zeros(shape, jnp.float32)
    for i, j, value in ((0, 0, h_00), (0, 1, h_01), (1, 0, h_10), (1, 1, h_11), (2, 1, h_21)):
        entries = jnp.where((row == i) & (column == j), value, entries)
    hessenberg_ref[...] = entries


def call(kernel, name, in_specs, outs, flops, scratch=(), traffic=4_000_000):
    return pl.pallas_call(
        kernel,
        name=name,
        in_specs=in_specs,
        out_specs=[VMEM] * len(outs),
        out_shape=outs,
        scratch_shapes=scratch,
        compiler_params=pltpu.CompilerParams(vmem_limit_bytes=16 * 1024 * 1024),
        cost_estimate=pl.CostEstimate(flops=flops, bytes_accessed=traffic, transcendentals=0),
    )


def in_hbm(array):
    return pltpu.with_memory_space_constraint(array, pltpu.HBM)


def from_everyone(rows):
    return lax.all_to_all(rows, "sub", 0, 0, tiled=True)


def gather_blocks(rows):
    return lax.all_gather(rows[:8], "sub", axis=0)[:, 0]


def swap(partner, other):
    count = lax.axis_size("sub")
    both = lambda lows: [pair for i in lows for pair in ((i, i + 1), (i + 1, i))]
    return (
        lax.ppermute(partner, "sub", both(range(0, count, 2))),
        lax.ppermute(other, "sub", both(range(1, count - 1, 2))),
    )


def on_device(rhs, viscosity, coupling, margin_rows, coarse_basis, coarse_inverse):
    count = lax.axis_size("sub")
    columns = coarse_inverse.shape[1]
    f32 = lambda *shape: jax.ShapeDtypeStruct(shape, jnp.float32)
    dma = lambda *shape: pltpu.SemaphoreType.DMA(shape)
    held = pltpu.VMEM((CHUNKS, VECTORS, CHUNK, CELLS), jnp.bfloat16)
    field = pltpu.VMEM((2, ROWS, CELLS), jnp.float32)
    sums = pltpu.VMEM((8 * SLOTS, LANES), jnp.float32)
    edge_scratch = [pltpu.VMEM((EDGE_AT, CELLS), jnp.float32)] * 2
    image_scratch = [pltpu.VMEM((2, HALO, CELLS), jnp.float32)] * 2
    turn_scratch = (
        [held]
        + [pltpu.VMEM((coarse_rows(columns), CELLS), jnp.float32)] * 2
        + [dma(CHUNKS), dma(2), pltpu.VMEM((2, EXT, CELLS), jnp.float32), sums]
    )
    row, whole, edge = f32(count, LANES), f32(2, ROWS, CELLS), f32(2, HALO, CELLS)
    packed, smoothed = f32(EDGE_AT + coarse_rows(columns), CELLS), f32(2, EXT, CELLS)
    basis = in_hbm(coarse_basis)
    first, partner, other = call(
        start_kernel, "start", [HBM] * 5, [row, packed, packed], 10_000_000,
        [held, field, sums, dma(), dma(CHUNKS), dma(2 * pack_count(columns))],
    )(in_hbm(rhs), in_hbm(viscosity), in_hbm(coupling), in_hbm(coarse_inverse), basis)
    partner, other = swap(partner, other)
    first = from_everyone(first)
    (smooth,) = call(
        functools.partial(first_solve_kernel, count), "first_solve",
        [SMEM] + [VMEM] * 3 + [ANY] * 2, [smoothed], 10_000_000, edge_scratch + [dma(2)],
    )(margin_rows, viscosity, coupling, rhs, partner, other)
    partner, other = in_hbm(partner), in_hbm(other)
    direction, image, partner_rows, other_rows, second = call(
        first_turn_kernel, "first_turn", [VMEM] * 2 + [HBM] * 3 + [VMEM] * 4,
        [whole, whole, edge, edge, row], 20_000_000, turn_scratch,
    )(first, coarse_inverse, partner, other, basis, smooth, rhs, viscosity, coupling)
    partner_rows, other_rows = swap(partner_rows, other_rows)
    second = from_everyone(second)
    (image_smooth,) = call(
        functools.partial(second_solve_kernel, count), "second_solve",
        [SMEM] + [VMEM] * 3 + [HBM] * 2 + [ANY] * 2, [smoothed], 0,
        edge_scratch + image_scratch + [dma(2)] * 2, 0,
    )(margin_rows, viscosity, coupling, image, partner, other, partner_rows, other_rows)
    second_direction, third = call(
        second_turn_kernel, "second_turn", [VMEM] * 3 + [HBM] * 3 + [VMEM] * 6, [whole, row],
        20_000_000, turn_scratch,
    )(
        first, second, coarse_inverse, partner, other, basis, smooth, image_smooth, rhs, image,
        viscosity, coupling,
    )
    third = gather_blocks(third)
    result, transposed = call(finish_kernel, "finish", [VMEM] * 5, [whole, f32(2, 3)], 1_000_000)(
        first, second, third, direction, second_direction
    )
    return result, transposed.T


def solution(mesh):
    in_specs = (
        P(None, ("groups", "sub"), None),
        P(("groups", "sub"), None),
        P(None, ("groups", "sub"), None),
        P("groups"),
        P(None, None, ("groups", "sub"), None),
        P(("groups", "sub"), None),
    )
    out_specs = (P(None, ("groups", "sub"), None), P("groups", None))
    return jax.shard_map(
        on_device, mesh=mesh, in_specs=in_specs, out_specs=out_specs, check_vma=False
    )
```

```python
import functools

import jax
import jax.numpy as jnp
from jax import lax
from jax.experimental import pallas as pl
from jax.experimental.pallas import tpu as pltpu
from jax.sharding import PartitionSpec as P

ROWS = 64
CELLS = 512
VECTORS = 48
HALO = 8
EXT = ROWS + 2 * HALO
STRIP = 32
CHUNK = 16
CHUNKS = 2 * ROWS // CHUNK
PIECE = 6
PIECES = VECTORS // PIECE
LANES = 128
SLOTS = 56
EDGE_AT = 5 * HALO
INVERSE_AT = 2 * VECTORS
SWEEPS = 4
RELAX = 0.7
ROW_FACTOR = (1.0, 4.0)
CELL_FACTOR = (4.0, 1.0)

VMEM = pl.BlockSpec(memory_space=pltpu.VMEM)
SMEM = pl.BlockSpec(memory_space=pltpu.SMEM)
HBM = pl.BlockSpec(memory_space=pltpu.HBM)


def coarse_rows(columns):
    return INVERSE_AT + VECTORS * (columns // 512) + (VECTORS // 2) * (columns % 512 // 256)


def cell_sum(field):
    column = lax.broadcasted_iota(jnp.int32, field.shape, 1)
    left = jnp.where(column == 0, 0.0, pltpu.roll(field, 1, 1))
    right = jnp.where(column == CELLS - 1, 0.0, pltpu.roll(field, CELLS - 1, 1))
    return left + right


def row_sum(field):
    count = field.shape[0]
    return pltpu.roll(field, 1, 0) + pltpu.roll(field, count - 1, 0)


def neighbours(field, component):
    rows, cells = row_sum(field), cell_sum(field)
    if component == 0:
        return rows + CELL_FACTOR[0] * cells
    return ROW_FACTOR[1] * rows + cells


def apply_operator(extended, viscosity, coupling):
    inner = slice(HALO, HALO + ROWS)
    images = []
    for a in range(2):
        around = neighbours(extended[a], a)[inner]
        diagonal = 10.0 * viscosity + jnp.abs(coupling[a]) + 0.05
        images.append(
            diagonal * extended[a][inner]
            - viscosity * around
            + coupling[a] * extended[1 - a][inner]
        )
    return images


def basis_copy(i, basis_ref, held, sems):
    vectors = pl.ds(PIECE * i, PIECE)
    return pltpu.make_async_copy(basis_ref.at[vectors], held.at[vectors], sems.at[i])


def restrict_piece(i, held, field, sums):
    for n in range(PIECE):
        k = PIECE * i + n
        total = None
        for a in range(2):
            for r in range(0, ROWS, CHUNK):
                for c in range(0, CELLS, LANES):
                    rows, cells = slice(r, r + CHUNK), slice(c, c + LANES)
                    term = held[k, a, rows, cells].astype(jnp.float32) * field[a, rows, cells]
                    term = term[:8] + term[8:]
                    total = term if total is None else total + term
        sums[pl.ds(pl.multiple_of(8 * k, 8), 8), :] = total


def fold(field):
    total = None
    for part in field:
        for r in range(0, part.shape[0], 8):
            for c in range(0, part.shape[1], LANES):
                term = part[r : r + 8, c : c + LANES]
                total = term if total is None else total + term
    return total


def send_sums(sums, out_ref):
    pick_row = lax.broadcasted_iota(jnp.int32, (LANES, 8 * SLOTS), 0)
    pick_col = lax.broadcasted_iota(jnp.int32, (LANES, 8 * SLOTS), 1)
    pick = (pick_col // 8 == pick_row).astype(jnp.float32)
    by_slot = jnp.dot(
        pick, sums[...], precision=lax.Precision.HIGHEST, preferred_element_type=jnp.float32
    )
    row = lax.dot_general(
        jnp.ones((8, LANES), jnp.float32),
        by_slot,
        (((1,), (1,)), ((), ())),
        precision=lax.Precision.HIGHEST,
        preferred_element_type=jnp.float32,
    )
    out_ref[...] = jnp.broadcast_to(row[:1], out_ref.shape)


def pack_copies(out_ref, first_row, rhs_ref, visc_ref, coup_ref, inverse_ref, sems, at_sem):
    rows = pl.ds(pl.multiple_of(first_row, HALO), HALO)
    moves = [(visc_ref.at[rows, :], 0, HALO, None)]
    for a in range(2):
        moves.append((coup_ref.at[a, rows, :], HALO * (1 + a), HALO, None))
        moves.append((rhs_ref.at[a, rows, :], HALO * (3 + a), HALO, None))
    columns = inverse_ref.shape[1]
    at = EDGE_AT + INVERSE_AT
    for c in range(0, columns - 511, 512):
        moves.append((inverse_ref.at[:, pl.ds(c, 512)], at, VECTORS, None))
        at += VECTORS
    if columns % 512:
        half = VECTORS // 2
        last = pl.ds(columns - 256, 256)
        moves.append((inverse_ref.at[pl.ds(0, half), last], at, half, 0))
        moves.append((inverse_ref.at[pl.ds(half, half), last], at, half, 256))
    copies = []
    for n, (source, at, size, lane) in enumerate(moves):
        place = pl.ds(at, size)
        target = out_ref.at[place, :] if lane is None else out_ref.at[place, pl.ds(lane, 256)]
        copies.append(pltpu.make_async_copy(source, target, sems.at[at_sem + n]))
    return copies


def pack_count(columns):
    return 5 + columns // 512 + 2 * (columns % 512 // 256)


def start_kernel(
    rhs_ref, visc_ref, coup_ref, inverse_ref, basis_ref,
    sums_ref, partner_ref, other_ref, held,
    field, sums, field_sem, sems, pack_sems,
):
    odd = lax.axis_index("sub") % 2
    field_copy = pltpu.make_async_copy(rhs_ref, field, field_sem)
    field_copy.start()
    for i in range(PIECES):
        basis_copy(i, basis_ref, held, sems).start()
    packs = []
    for n, (out_ref, up) in enumerate(((partner_ref, 1 - odd), (other_ref, odd))):
        packs += pack_copies(
            out_ref, up * (ROWS - HALO), rhs_ref, visc_ref, coup_ref, inverse_ref, pack_sems,
            n * pack_count(inverse_ref.shape[1]),
        )
    for copy in packs:
        copy.start()
    sums[...] = jnp.zeros_like(sums)
    field_copy.wait()
    sums[8 * VECTORS : 8 * VECTORS + 8] = fold([field[a] * field[a] for a in range(2)])

    def body(i, carry):
        basis_copy(i, basis_ref, held, sems).wait()
        restrict_piece(i, held, field, sums)
        return carry

    lax.fori_loop(0, PIECES, body, 0)
    picker = lax.broadcasted_iota(jnp.int32, (VECTORS, CHUNK * VECTORS), 0) * CHUNK
    place = lax.broadcasted_iota(jnp.int32, (VECTORS, CHUNK * VECTORS), 1)
    for out_ref, up in ((partner_ref, 1 - odd), (other_ref, odd)):
        pick = (place == picker + up * (CHUNK - 1)).astype(jnp.float32).astype(jnp.bfloat16)
        first_row = pl.multiple_of(up * (ROWS - CHUNK), CHUNK)
        for a in range(2):
            rows = held[:, a, pl.ds(first_row, CHUNK), :].reshape(CHUNK * VECTORS, CELLS)
            at = EDGE_AT + VECTORS * a
            out_ref[at : at + VECTORS] = jnp.dot(pick, rows, preferred_element_type=jnp.float32)
    for copy in packs:
        copy.wait()
    send_sums(sums, sums_ref)


class Neighbour:
    def __init__(self, first_ref, second_ref):
        self.odd = lax.axis_index("sub") % 2 == 1
        self.first, self.second = first_ref, second_ref

    def __getitem__(self, index):
        return jnp.where(self.odd, self.first[index], self.second[index])


def neighbours_of(partner_ref, other_ref):
    return Neighbour(partner_ref, other_ref), Neighbour(other_ref, partner_ref)


def solve(count, margin_ref, visc_ref, coup_ref, field_ref, low_ref, high_ref, edges, out_ref):
    rank = lax.axis_index("sub")
    lower = jnp.where(rank > 0, margin_ref[jnp.maximum(rank - 1, 0)], 0)
    upper = jnp.where(rank < count - 1, margin_ref[rank], 0)
    lower_f, upper_f = lower.astype(jnp.float32), upper.astype(jnp.float32)
    low_scale = 2.0 * jnp.maximum(lower_f, 1.0)
    high_scale = 2.0 * jnp.maximum(upper_f, 1.0)

    def masks(first, rows, side):
        place = lax.broadcasted_iota(jnp.int32, (rows, LANES), 0) + first
        place_f = place.astype(jnp.float32)
        rising = lambda base, scale: (place_f - base + 0.5) / scale
        falling = lambda base, scale: (base - place_f - 0.5) / scale
        if side == 0:
            live = (place >= -lower) & (place < ROWS + upper)
            weight = jnp.where(place < lower, rising(-lower_f, low_scale), 1.0)
            weight = jnp.where(
                place >= ROWS - upper, falling(ROWS + upper_f, high_scale), weight
            )
        elif side < 0:
            live = place < lower
            weight = jnp.where(place >= -lower, falling(lower_f, low_scale), 1.0)
        else:
            live = place >= ROWS - upper
            weight = jnp.where(place < ROWS + upper, rising(ROWS - upper_f, high_scale), 1.0)
        wide = lambda x: jnp.concatenate([x] * (CELLS // LANES), 1)
        return wide(live.astype(jnp.float32)), wide(weight)

    def stack(own, at):
        rows = slice(at, at + HALO)
        return jnp.concatenate([low_ref[rows], own, high_ref[rows]], 0)

    def triple(field):
        return jnp.concatenate([field, field[:STRIP], field[EXT - STRIP :]], 0)

    viscosity = stack(visc_ref[...], 0)
    blocks = [masks(-HALO, EXT, 0), masks(-HALO, STRIP, -1), masks(ROWS + HALO - STRIP, STRIP, 1)]
    live = jnp.concatenate([block[0] for block in blocks], 0)
    first, across, other = [], [], []
    for a in range(2):
        coupling = stack(coup_ref[a], HALO * (1 + a))
        field = jnp.concatenate([edges[a][0], field_ref[a], edges[a][1]], 0)
        scale = RELAX / (10.0 * viscosity + jnp.abs(coupling) + 0.05)
        first.append(live * triple(scale * field))
        across.append(live * triple(scale * viscosity))
        other.append(live * triple(scale * coupling))
    solved = list(first)
    for _ in range(SWEEPS - 1):
        solved = [
            (1.0 - RELAX) * solved[a]
            + first[a]
            + across[a] * neighbours(solved[a], a)
            - other[a] * solved[1 - a]
            for a in range(2)
        ]
    for a in range(2):
        shares = solved[a] * jnp.concatenate([block[1] for block in blocks], 0)
        out_ref[a] = shares[:EXT]
        out_ref[a, :STRIP] += shares[EXT : EXT + STRIP]
        out_ref[a, EXT - STRIP :] += shares[EXT + STRIP :]


def line_up(residuals):
    devices = residuals.shape[0]
    lane = lax.broadcasted_iota(jnp.int32, (1, LANES), 1)
    tiles = [jnp.zeros((1, LANES), jnp.float32) for _ in range(devices * VECTORS // LANES)]
    for t in range(devices):
        tile, offset = divmod(VECTORS * t, LANES)
        row = jnp.where(lane < VECTORS, residuals[t : t + 1], 0.0)
        if offset:
            row = pltpu.roll(row, offset, 1)
        if offset + VECTORS <= LANES:
            tiles[tile] = tiles[tile] + row
        else:
            tiles[tile] = tiles[tile] + jnp.where(lane >= offset, row, 0.0)
            tiles[tile + 1] = tiles[tile + 1] + jnp.where(lane < offset, row, 0.0)
    return jnp.concatenate(tiles, 1)


def rounded(column):
    return column.astype(jnp.bfloat16).astype(jnp.float32)


def lift(inverse_ref, residual):
    return rounded(jnp.sum(inverse_ref[...] * residual, 1, keepdims=True))


def lift_packed(ref, residual):
    columns = residual.shape[1]
    at, total = EDGE_AT + INVERSE_AT, None
    for c in range(0, columns - 511, 512):
        term = jnp.sum(ref[at : at + VECTORS] * residual[:, c : c + 512], 1, keepdims=True)
        total = term if total is None else total + term
        at += VECTORS
    if columns % 512:
        half = VECTORS // 2
        last = residual[:, columns - 256 :]
        rows = ref[at : at + half]
        term = jnp.concatenate(
            [
                jnp.sum(rows[:, :256] * last, 1, keepdims=True),
                jnp.sum(rows[:, 256:] * last, 1, keepdims=True),
            ],
            0,
        )
        total = term if total is None else total + term
    return rounded(total)


def edge_values(ref, lifted):
    starts = [EDGE_AT + VECTORS * a for a in range(2)]
    return [jnp.sum(ref[at : at + VECTORS] * lifted, 0, keepdims=True) for at in starts]


def spread(lifted):
    shape = (VECTORS, CHUNK * VECTORS)
    owner = lax.broadcasted_iota(jnp.int32, shape, 1) // CHUNK
    row = lax.broadcasted_iota(jnp.int32, shape, 0)
    line = jnp.sum(jnp.where(owner == row, lifted, 0.0), 0, keepdims=True)
    shape = (CHUNK, CHUNK * VECTORS)
    place = lax.broadcasted_iota(jnp.int32, shape, 1) % CHUNK
    row = lax.broadcasted_iota(jnp.int32, shape, 0)
    return jnp.where(place == row, line, 0.0).astype(jnp.bfloat16)


def prolong(residual, inverse_ref, held, extended):
    matrix = spread(lift(inverse_ref, residual))
    for a in range(2):
        for r in range(0, ROWS, CHUNK):
            rows = held[:, a, r : r + CHUNK, :].reshape(CHUNK * VECTORS, CELLS)
            extended[a, HALO + r : HALO + r + CHUNK] = jnp.dot(
                matrix, rows, preferred_element_type=jnp.float32
            )


def add_smooth(residual, low, high, smooth, extended):
    low_edge = edge_values(low, lift_packed(low, residual))
    high_edge = edge_values(high, lift_packed(high, residual))
    place = lax.broadcasted_iota(jnp.int32, (HALO, CELLS), 0)
    for a in range(2):
        rows = slice(HALO, HALO + ROWS)
        extended[a, rows] += smooth(a, rows)
        rows = slice(0, HALO)
        extended[a, rows] = smooth(a, rows) + jnp.where(place == HALO - 1, low_edge[a], 0.0)
        rows = slice(EXT - HALO, EXT)
        extended[a, rows] = smooth(a, rows) + jnp.where(place == 0, high_edge[a], 0.0)


def lane_total(received, lane):
    return jnp.sum(received[:, lane : lane + 1], 0, keepdims=True)


def first_turn_kernel(
    count, margin_ref, sums_ref, inverse_ref, partner_ref, other_ref, held, rhs_ref, visc_ref,
    coup_ref,
    direction_ref, image_ref, smooth_ref, partner_rows_ref, other_rows_ref, next_ref,
    extended, sums,
):
    received = sums_ref[...]
    over_beta = 1.0 / jnp.sqrt(lane_total(received, VECTORS))
    residual = line_up(received) * over_beta
    prolong(residual, inverse_ref, held, extended)
    low, high = neighbours_of(partner_ref, other_ref)
    starts = [HALO * (3 + a) for a in range(2)]
    edges = [(low[at : at + HALO], high[at : at + HALO]) for at in starts]
    solve(count, margin_ref, visc_ref, coup_ref, rhs_ref, low, high, edges, smooth_ref)
    add_smooth(
        residual, low, high, lambda a, rows: smooth_ref[a, rows] * over_beta, extended
    )
    images = apply_operator(
        [extended[a] for a in range(2)], visc_ref[...], [coup_ref[a] for a in range(2)]
    )
    odd = lax.axis_index("sub") % 2 == 1
    for a in range(2):
        direction_ref[a] = extended[a, HALO : HALO + ROWS]
        image_ref[a] = images[a]
        head, tail = images[a][:HALO], images[a][ROWS - HALO :]
        partner_rows_ref[a] = jnp.where(odd, head, tail)
        other_rows_ref[a] = jnp.where(odd, tail, head)
    sums[...] = jnp.zeros_like(sums)
    at = 8 * VECTORS
    sums[at : at + 8] = fold([rhs_ref[a] * images[a] for a in range(2)])
    sums[at + 8 : at + 16] = fold([images[a] * images[a] for a in range(2)])

    def body(i, carry):
        restrict_piece(i, held, image_ref, sums)
        return carry

    lax.fori_loop(0, PIECES, body, 0)
    send_sums(sums, next_ref)


def first_column(first, second):
    beta = jnp.sqrt(lane_total(first, VECTORS))
    h_00 = lane_total(second, VECTORS) / beta
    h_10 = jnp.sqrt(lane_total(second, VECTORS + 1) - h_00 * h_00)
    return beta, h_00, h_10


def second_turn_kernel(
    count, margin_ref, first_ref, second_ref, inverse_ref, partner_ref, other_ref,
    partner_rows_ref, other_rows_ref, held, smooth_ref, rhs_ref, image_ref, visc_ref, coup_ref,
    direction_ref, next_ref,
    image_smooth, extended, sums,
):
    first, second = first_ref[...], second_ref[...]
    beta, h_00, h_10 = first_column(first, second)
    ratio = h_00 / beta
    over = 1.0 / h_10
    residual = (line_up(second) - ratio * line_up(first)) * over
    prolong(residual, inverse_ref, held, extended)
    low, high = neighbours_of(partner_ref, other_ref)
    low_rows, high_rows = neighbours_of(partner_rows_ref, other_rows_ref)
    edges = [(low_rows[a], high_rows[a]) for a in range(2)]
    solve(count, margin_ref, visc_ref, coup_ref, image_ref, low, high, edges, image_smooth)
    add_smooth(
        residual,
        low,
        high,
        lambda a, rows: (image_smooth[a, rows] - ratio * smooth_ref[a, rows]) * over,
        extended,
    )
    images = apply_operator(
        [extended[a] for a in range(2)], visc_ref[...], [coup_ref[a] for a in range(2)]
    )
    sums[...] = jnp.zeros_like(sums)
    sums[0:8] = fold([rhs_ref[a] * images[a] for a in range(2)])
    sums[8:16] = fold([image_ref[a] * images[a] for a in range(2)])
    sums[16:24] = fold([images[a] * images[a] for a in range(2)])
    for a in range(2):
        direction_ref[a] = extended[a, HALO : HALO + ROWS]
    send_sums(sums, next_ref)


def finish_kernel(
    first_ref, second_ref, third_ref, first_direction_ref, second_direction_ref,
    solution_ref, hessenberg_ref,
):
    third = third_ref[...]
    beta, h_00, h_10 = first_column(first_ref[...], second_ref[...])
    h_01 = lane_total(third, 0) / beta
    h_11 = (lane_total(third, 1) - h_00 * h_01) / h_10
    h_21 = jnp.sqrt(lane_total(third, 2) - h_01 * h_01 - h_11 * h_11)
    n_00 = h_00 * h_00 + h_10 * h_10
    n_10 = h_00 * h_01 + h_10 * h_11
    n_11 = h_01 * h_01 + h_11 * h_11 + h_21 * h_21
    l_00 = jnp.sqrt(n_00)
    l_10 = n_10 / l_00
    l_11 = jnp.sqrt(n_11 - l_10 * l_10)
    f_0 = beta * h_00 / l_00
    f_1 = (beta * h_01 - l_10 * f_0) / l_11
    c_1 = f_1 / l_11
    c_0 = (f_0 - l_10 * c_1) / l_00
    for a in range(2):
        solution_ref[a] = c_0 * first_direction_ref[a] + c_1 * second_direction_ref[a]
    shape = hessenberg_ref.shape
    row = lax.broadcasted_iota(jnp.int32, shape, 1)
    column = lax.broadcasted_iota(jnp.int32, shape, 0)
    entries = jnp.zeros(shape, jnp.float32)
    for i, j, value in ((0, 0, h_00), (0, 1, h_01), (1, 0, h_10), (1, 1, h_11), (2, 1, h_21)):
        entries = jnp.where((row == i) & (column == j), value, entries)
    hessenberg_ref[...] = entries


def call(kernel, name, in_specs, outs, flops, scratch=(), traffic=4_000_000):
    return pl.pallas_call(
        kernel,
        name=name,
        in_specs=in_specs,
        out_specs=[VMEM] * len(outs),
        out_shape=outs,
        scratch_shapes=scratch,
        compiler_params=pltpu.CompilerParams(vmem_limit_bytes=16 * 1024 * 1024),
        cost_estimate=pl.CostEstimate(flops=flops, bytes_accessed=traffic, transcendentals=0),
    )


def in_hbm(array):
    return pltpu.with_memory_space_constraint(array, pltpu.HBM)


def from_everyone(rows):
    return lax.all_to_all(rows, "sub", 0, 0, tiled=True)


def from_everyone_reversed(rows):
    order = [list(range(lax.axis_size("sub")))[::-1]]
    return lax.all_to_all(rows, "sub", 0, 0, tiled=True, axis_index_groups=order)


def swap(partner, other):
    count = lax.axis_size("sub")
    both = lambda lows: [pair for i in lows for pair in ((i, i + 1), (i + 1, i))]
    return (
        lax.ppermute(partner, "sub", both(range(0, count, 2))),
        lax.ppermute(other, "sub", both(range(1, count - 1, 2))),
    )


def on_device(rhs, viscosity, coupling, margin_rows, coarse_basis, coarse_inverse):
    count = lax.axis_size("sub")
    columns = coarse_inverse.shape[1]
    f32 = lambda *shape: jax.ShapeDtypeStruct(shape, jnp.float32)
    dma = lambda *shape: pltpu.SemaphoreType.DMA(shape)
    field = pltpu.VMEM((2, ROWS, CELLS), jnp.float32)
    extended = pltpu.VMEM((2, EXT, CELLS), jnp.float32)
    sums = pltpu.VMEM((8 * SLOTS, LANES), jnp.float32)
    row, whole, edge = f32(count, LANES), f32(2, ROWS, CELLS), f32(2, HALO, CELLS)
    packed, smoothed = f32(EDGE_AT + coarse_rows(columns), CELLS), f32(2, EXT, CELLS)
    basis = jax.ShapeDtypeStruct(coarse_basis.shape, jnp.bfloat16)
    arguments = (rhs, viscosity, coupling, coarse_inverse, coarse_basis)
    first, partner, other, held = call(
        start_kernel, "start", [HBM] * 5, [row, packed, packed, basis], 10_000_000,
        [field, sums, dma(), dma(PIECES), dma(2 * pack_count(columns))],
    )(*map(in_hbm, arguments))
    partner, other = swap(partner, other)
    first = from_everyone(first)
    direction, image, smooth, partner_rows, other_rows, second = call(
        functools.partial(first_turn_kernel, count), "first_turn", [SMEM] + [VMEM] * 8,
        [whole, whole, smoothed, edge, edge, row], 20_000_000, [extended, sums],
    )(margin_rows, first, coarse_inverse, partner, other, held, rhs, viscosity, coupling)
    partner_rows, other_rows = swap(partner_rows, other_rows)
    second = from_everyone(second)
    second_direction, third = call(
        functools.partial(second_turn_kernel, count), "second_turn", [SMEM] + [VMEM] * 13,
        [whole, row], 20_000_000, [extended, extended, sums],
    )(
        margin_rows, first, second, coarse_inverse, partner, other, partner_rows, other_rows,
        held, smooth, rhs, image, viscosity, coupling,
    )
    third = from_everyone_reversed(third)
    result, transposed = call(finish_kernel, "finish", [VMEM] * 5, [whole, f32(2, 3)], 1_000_000)(
        first, second, third, direction, second_direction
    )
    return result, transposed.T


def solution(mesh):
    in_specs = (
        P(None, ("groups", "sub"), None),
        P(("groups", "sub"), None),
        P(None, ("groups", "sub"), None),
        P("groups"),
        P(None, None, ("groups", "sub"), None),
        P(("groups", "sub"), None),
    )
    out_specs = (P(None, ("groups", "sub"), None), P("groups", None))
    return jax.shard_map(
        on_device, mesh=mesh, in_specs=in_specs, out_specs=out_specs, check_vma=False
    )
```

```python
import functools

import jax
import jax.numpy as jnp
from jax import lax
from jax.experimental import pallas as pl
from jax.experimental.pallas import tpu as pltpu
from jax.sharding import PartitionSpec as P

ROWS = 64
CELLS = 512
VECTORS = 48
HALO = 8
EXT = ROWS + 2 * HALO
STRIP = 32
CHUNK = 16
CHUNKS = 2 * ROWS // CHUNK
PIECE = 6
PIECES = VECTORS // PIECE
AHEAD = 4
LANES = 128
SLOTS = 56
EDGE_AT = 5 * HALO
INVERSE_AT = 2 * VECTORS
SWEEPS = 4
RELAX = 0.7
ROW_FACTOR = (1.0, 4.0)
CELL_FACTOR = (4.0, 1.0)

VMEM = pl.BlockSpec(memory_space=pltpu.VMEM)
SMEM = pl.BlockSpec(memory_space=pltpu.SMEM)
HBM = pl.BlockSpec(memory_space=pltpu.HBM)


def coarse_rows(columns):
    return INVERSE_AT + VECTORS * (columns // 512) + (VECTORS // 2) * (columns % 512 // 256)


def cell_sum(field):
    column = lax.broadcasted_iota(jnp.int32, field.shape, 1)
    left = jnp.where(column == 0, 0.0, pltpu.roll(field, 1, 1))
    right = jnp.where(column == CELLS - 1, 0.0, pltpu.roll(field, CELLS - 1, 1))
    return left + right


def row_sum(field):
    count = field.shape[0]
    return pltpu.roll(field, 1, 0) + pltpu.roll(field, count - 1, 0)


def neighbours(field, component):
    rows, cells = row_sum(field), cell_sum(field)
    if component == 0:
        return rows + CELL_FACTOR[0] * cells
    return ROW_FACTOR[1] * rows + cells


def apply_operator(extended, viscosity, coupling):
    inner = slice(HALO, HALO + ROWS)
    images = []
    for a in range(2):
        around = neighbours(extended[a], a)[inner]
        diagonal = 10.0 * viscosity + jnp.abs(coupling[a]) + 0.05
        images.append(
            diagonal * extended[a][inner]
            - viscosity * around
            + coupling[a] * extended[1 - a][inner]
        )
    return images


def basis_copy(i, basis_ref, held, sems):
    vectors = pl.ds(PIECE * i, PIECE)
    return pltpu.make_async_copy(basis_ref.at[vectors], held.at[vectors], sems.at[i])


def restrict_piece(i, held, field, sums):
    for n in range(PIECE):
        k = PIECE * i + n
        total = None
        for a in range(2):
            for r in range(0, ROWS, CHUNK):
                for c in range(0, CELLS, LANES):
                    rows, cells = slice(r, r + CHUNK), slice(c, c + LANES)
                    term = held[k, a, rows, cells].astype(jnp.float32) * field[a, rows, cells]
                    term = term[:8] + term[8:]
                    total = term if total is None else total + term
        sums[pl.ds(pl.multiple_of(8 * k, 8), 8), :] = total


def fold(field):
    total = None
    for part in field:
        for r in range(0, part.shape[0], 8):
            for c in range(0, part.shape[1], LANES):
                term = part[r : r + 8, c : c + LANES]
                total = term if total is None else total + term
    return total


def send_sums(sums, turned, out_ref):
    for k in range(SLOTS):
        turned[pl.ds(k, 8, stride=SLOTS), :] = sums[8 * k : 8 * k + 8, :]
    by_slot = turned[:SLOTS]
    for j in range(1, 8):
        by_slot = by_slot + turned[SLOTS * j : SLOTS * (j + 1)]
    row = lax.dot_general(
        jnp.ones((8, LANES), jnp.float32),
        by_slot,
        (((1,), (1,)), ((), ())),
        precision=lax.Precision.HIGHEST,
        preferred_element_type=jnp.float32,
    )
    wide = jnp.concatenate([row[:1], jnp.zeros((1, LANES - SLOTS), jnp.float32)], 1)
    out_ref[...] = jnp.broadcast_to(wide, out_ref.shape)


def pack_copies(out_ref, first_row, rhs_ref, visc_ref, coup_ref, inverse_ref, sems, at_sem):
    rows = pl.ds(pl.multiple_of(first_row, HALO), HALO)
    moves = [(visc_ref.at[rows, :], 0, HALO, None)]
    for a in range(2):
        moves.append((coup_ref.at[a, rows, :], HALO * (1 + a), HALO, None))
        moves.append((rhs_ref.at[a, rows, :], HALO * (3 + a), HALO, None))
    columns = inverse_ref.shape[1]
    at = EDGE_AT + INVERSE_AT
    for c in range(0, columns - 511, 512):
        moves.append((inverse_ref.at[:, pl.ds(c, 512)], at, VECTORS, None))
        at += VECTORS
    if columns % 512:
        half = VECTORS // 2
        last = pl.ds(columns - 256, 256)
        moves.append((inverse_ref.at[pl.ds(0, half), last], at, half, 0))
        moves.append((inverse_ref.at[pl.ds(half, half), last], at, half, 256))
    copies = []
    for n, (source, at, size, lane) in enumerate(moves):
        place = pl.ds(at, size)
        target = out_ref.at[place, :] if lane is None else out_ref.at[place, pl.ds(lane, 256)]
        copies.append(pltpu.make_async_copy(source, target, sems.at[at_sem + n]))
    return copies


def pack_count(columns):
    return 5 + columns // 512 + 2 * (columns % 512 // 256)


def start_kernel(
    rhs_ref, visc_ref, coup_ref, inverse_ref, basis_ref,
    sums_ref, partner_ref, other_ref, held,
    field, sums, turned, field_sem, sems, pack_sems,
):
    odd = lax.axis_index("sub") % 2
    field_copy = pltpu.make_async_copy(rhs_ref, field, field_sem)
    field_copy.start()
    for i in range(AHEAD):
        basis_copy(i, basis_ref, held, sems).start()
    packs = []
    for n, (out_ref, up) in enumerate(((partner_ref, 1 - odd), (other_ref, odd))):
        packs += pack_copies(
            out_ref, up * (ROWS - HALO), rhs_ref, visc_ref, coup_ref, inverse_ref, pack_sems,
            n * pack_count(inverse_ref.shape[1]),
        )
    for copy in packs:
        copy.start()
    sums[...] = jnp.zeros_like(sums)
    field_copy.wait()
    sums[8 * VECTORS : 8 * VECTORS + 8] = fold([field[a] * field[a] for a in range(2)])

    def body(i, carry):
        basis_copy(i, basis_ref, held, sems).wait()

        @pl.when(i + AHEAD < PIECES)
        def _():
            basis_copy(i + AHEAD, basis_ref, held, sems).start()

        restrict_piece(i, held, field, sums)
        for n in range(PIECE):
            k = PIECE * i + n
            for a in range(2):
                top = held[k, a, :CHUNK, :].astype(jnp.float32)[:1]
                bottom = held[k, a, ROWS - CHUNK :, :].astype(jnp.float32)[CHUNK - 1 :]
                place = pl.ds(EDGE_AT + VECTORS * a + k, 1)
                partner_ref[place, :] = jnp.where(odd == 1, top, bottom)
                other_ref[place, :] = jnp.where(odd == 1, bottom, top)
        return carry

    lax.fori_loop(0, PIECES, body, 0)
    for copy in packs:
        copy.wait()
    send_sums(sums, turned, sums_ref)


class Neighbour:
    def __init__(self, first_ref, second_ref):
        self.odd = lax.axis_index("sub") % 2 == 1
        self.first, self.second = first_ref, second_ref

    def __getitem__(self, index):
        return jnp.where(self.odd, self.first[index], self.second[index])


def neighbours_of(partner_ref, other_ref):
    return Neighbour(partner_ref, other_ref), Neighbour(other_ref, partner_ref)


def solve(count, margin_ref, visc_ref, coup_ref, field_ref, low_ref, high_ref, edges, out_ref):
    rank = lax.axis_index("sub")
    lower = jnp.where(rank > 0, margin_ref[jnp.maximum(rank - 1, 0)], 0)
    upper = jnp.where(rank < count - 1, margin_ref[rank], 0)
    lower_f, upper_f = lower.astype(jnp.float32), upper.astype(jnp.float32)
    low_scale = 2.0 * jnp.maximum(lower_f, 1.0)
    high_scale = 2.0 * jnp.maximum(upper_f, 1.0)

    def masks(first, rows, side):
        place = lax.broadcasted_iota(jnp.int32, (rows, LANES), 0) + first
        place_f = place.astype(jnp.float32)
        rising = lambda base, scale: (place_f - base + 0.5) / scale
        falling = lambda base, scale: (base - place_f - 0.5) / scale
        if side == 0:
            live = (place >= -lower) & (place < ROWS + upper)
            weight = jnp.where(place < lower, rising(-lower_f, low_scale), 1.0)
            weight = jnp.where(
                place >= ROWS - upper, falling(ROWS + upper_f, high_scale), weight
            )
        elif side < 0:
            live = place < lower
            weight = jnp.where(place >= -lower, falling(lower_f, low_scale), 1.0)
        else:
            live = place >= ROWS - upper
            weight = jnp.where(place < ROWS + upper, rising(ROWS - upper_f, high_scale), 1.0)
        wide = lambda x: jnp.concatenate([x] * (CELLS // LANES), 1)
        return wide(live.astype(jnp.float32)), wide(weight)

    def stack(own, at):
        rows = slice(at, at + HALO)
        return jnp.concatenate([low_ref[rows], own, high_ref[rows]], 0)

    def triple(field):
        return jnp.concatenate([field, field[:STRIP], field[EXT - STRIP :]], 0)

    viscosity = stack(visc_ref[...], 0)
    blocks = [masks(-HALO, EXT, 0), masks(-HALO, STRIP, -1), masks(ROWS + HALO - STRIP, STRIP, 1)]
    live = jnp.concatenate([block[0] for block in blocks], 0)
    first, across, other = [], [], []
    for a in range(2):
        coupling = stack(coup_ref[a], HALO * (1 + a))
        field = jnp.concatenate([edges[a][0], field_ref[a], edges[a][1]], 0)
        scale = RELAX / (10.0 * viscosity + jnp.abs(coupling) + 0.05)
        first.append(live * triple(scale * field))
        across.append(live * triple(scale * viscosity))
        other.append(live * triple(scale * coupling))
    solved = list(first)
    for _ in range(SWEEPS - 1):
        solved = [
            (1.0 - RELAX) * solved[a]
            + first[a]
            + across[a] * neighbours(solved[a], a)
            - other[a] * solved[1 - a]
            for a in range(2)
        ]
    for a in range(2):
        shares = solved[a] * jnp.concatenate([block[1] for block in blocks], 0)
        out_ref[a] = shares[:EXT]
        out_ref[a, :STRIP] += shares[EXT : EXT + STRIP]
        out_ref[a, EXT - STRIP :] += shares[EXT + STRIP :]


def line_up(residuals):
    devices = residuals.shape[0]
    lane = lax.broadcasted_iota(jnp.int32, (1, LANES), 1)
    tiles = [jnp.zeros((1, LANES), jnp.float32) for _ in range(devices * VECTORS // LANES)]
    for t in range(devices):
        tile, offset = divmod(VECTORS * t, LANES)
        row = jnp.where(lane < VECTORS, residuals[t : t + 1], 0.0)
        if offset:
            row = pltpu.roll(row, offset, 1)
        if offset + VECTORS <= LANES:
            tiles[tile] = tiles[tile] + row
        else:
            tiles[tile] = tiles[tile] + jnp.where(lane >= offset, row, 0.0)
            tiles[tile + 1] = tiles[tile + 1] + jnp.where(lane < offset, row, 0.0)
    return jnp.concatenate(tiles, 1)


def rounded(column):
    return column.astype(jnp.bfloat16).astype(jnp.float32)


def lift(inverse_ref, residual):
    return rounded(jnp.sum(inverse_ref[...] * residual, 1, keepdims=True))


def lift_packed(ref, residual):
    columns = residual.shape[1]
    at, total = EDGE_AT + INVERSE_AT, None
    for c in range(0, columns - 511, 512):
        term = jnp.sum(ref[at : at + VECTORS] * residual[:, c : c + 512], 1, keepdims=True)
        total = term if total is None else total + term
        at += VECTORS
    if columns % 512:
        half = VECTORS // 2
        last = residual[:, columns - 256 :]
        rows = ref[at : at + half]
        term = jnp.concatenate(
            [
                jnp.sum(rows[:, :256] * last, 1, keepdims=True),
                jnp.sum(rows[:, 256:] * last, 1, keepdims=True),
            ],
            0,
        )
        total = term if total is None else total + term
    return rounded(total)


def edge_values(ref, lifted):
    starts = [EDGE_AT + VECTORS * a for a in range(2)]
    return [jnp.sum(ref[at : at + VECTORS] * lifted, 0, keepdims=True) for at in starts]


def spread(lifted):
    shape = (VECTORS, CHUNK * VECTORS)
    owner = lax.broadcasted_iota(jnp.int32, shape, 1) // CHUNK
    row = lax.broadcasted_iota(jnp.int32, shape, 0)
    line = jnp.sum(jnp.where(owner == row, lifted, 0.0), 0, keepdims=True)
    shape = (CHUNK, CHUNK * VECTORS)
    place = lax.broadcasted_iota(jnp.int32, shape, 1) % CHUNK
    row = lax.broadcasted_iota(jnp.int32, shape, 0)
    return jnp.where(place == row, line, 0.0).astype(jnp.bfloat16)


def prolong(residual, inverse_ref, held, extended):
    matrix = spread(lift(inverse_ref, residual))
    for a in range(2):
        for r in range(0, ROWS, CHUNK):
            rows = held[:, a, r : r + CHUNK, :].reshape(CHUNK * VECTORS, CELLS)
            extended[a, HALO + r : HALO + r + CHUNK] = jnp.dot(
                matrix, rows, preferred_element_type=jnp.float32
            )


def add_smooth(residual, low, high, smooth, extended):
    low_edge = edge_values(low, lift_packed(low, residual))
    high_edge = edge_values(high, lift_packed(high, residual))
    place = lax.broadcasted_iota(jnp.int32, (HALO, CELLS), 0)
    for a in range(2):
        rows = slice(HALO, HALO + ROWS)
        extended[a, rows] += smooth(a, rows)
        rows = slice(0, HALO)
        extended[a, rows] = smooth(a, rows) + jnp.where(place == HALO - 1, low_edge[a], 0.0)
        rows = slice(EXT - HALO, EXT)
        extended[a, rows] = smooth(a, rows) + jnp.where(place == 0, high_edge[a], 0.0)


def lane_total(received, lane):
    return jnp.sum(received[:, lane : lane + 1], 0, keepdims=True)


def first_turn_kernel(
    count, margin_ref, sums_ref, inverse_ref, partner_ref, other_ref, held, rhs_ref, visc_ref,
    coup_ref,
    direction_ref, image_ref, smooth_ref, partner_rows_ref, other_rows_ref, next_ref,
    extended, sums, turned,
):
    received = sums_ref[...]
    over_beta = 1.0 / jnp.sqrt(lane_total(received, VECTORS))
    residual = line_up(received) * over_beta
    prolong(residual, inverse_ref, held, extended)
    low, high = neighbours_of(partner_ref, other_ref)
    starts = [HALO * (3 + a) for a in range(2)]
    edges = [(low[at : at + HALO], high[at : at + HALO]) for at in starts]
    solve(count, margin_ref, visc_ref, coup_ref, rhs_ref, low, high, edges, smooth_ref)
    add_smooth(
        residual, low, high, lambda a, rows: smooth_ref[a, rows] * over_beta, extended
    )
    images = apply_operator(
        [extended[a] for a in range(2)], visc_ref[...], [coup_ref[a] for a in range(2)]
    )
    odd = lax.axis_index("sub") % 2 == 1
    for a in range(2):
        direction_ref[a] = extended[a, HALO : HALO + ROWS]
        image_ref[a] = images[a]
        head, tail = images[a][:HALO], images[a][ROWS - HALO :]
        partner_rows_ref[a] = jnp.where(odd, head, tail)
        other_rows_ref[a] = jnp.where(odd, tail, head)
    sums[...] = jnp.zeros_like(sums)
    at = 8 * VECTORS
    sums[at : at + 8] = fold([rhs_ref[a] * images[a] for a in range(2)])
    sums[at + 8 : at + 16] = fold([images[a] * images[a] for a in range(2)])

    def body(i, carry):
        restrict_piece(i, held, image_ref, sums)
        return carry

    lax.fori_loop(0, PIECES, body, 0)
    send_sums(sums, turned, next_ref)


def first_column(first, second):
    beta = jnp.sqrt(lane_total(first, VECTORS))
    h_00 = lane_total(second, VECTORS) / beta
    h_10 = jnp.sqrt(lane_total(second, VECTORS + 1) - h_00 * h_00)
    return beta, h_00, h_10


def second_turn_kernel(
    count, margin_ref, first_ref, second_ref, inverse_ref, partner_ref, other_ref,
    partner_rows_ref, other_rows_ref, held, smooth_ref, rhs_ref, image_ref, visc_ref, coup_ref,
    direction_ref, next_ref,
    image_smooth, extended, sums, turned,
):
    first, second = first_ref[...], second_ref[...]
    beta, h_00, h_10 = first_column(first, second)
    ratio = h_00 / beta
    over = 1.0 / h_10
    residual = (line_up(second) - ratio * line_up(first)) * over
    prolong(residual, inverse_ref, held, extended)
    low, high = neighbours_of(partner_ref, other_ref)
    low_rows, high_rows = neighbours_of(partner_rows_ref, other_rows_ref)
    edges = [(low_rows[a], high_rows[a]) for a in range(2)]
    solve(count, margin_ref, visc_ref, coup_ref, image_ref, low, high, edges, image_smooth)
    add_smooth(
        residual,
        low,
        high,
        lambda a, rows: (image_smooth[a, rows] - ratio * smooth_ref[a, rows]) * over,
        extended,
    )
    images = apply_operator(
        [extended[a] for a in range(2)], visc_ref[...], [coup_ref[a] for a in range(2)]
    )
    sums[...] = jnp.zeros_like(sums)
    sums[0:8] = fold([rhs_ref[a] * images[a] for a in range(2)])
    sums[8:16] = fold([image_ref[a] * images[a] for a in range(2)])
    sums[16:24] = fold([images[a] * images[a] for a in range(2)])
    for a in range(2):
        direction_ref[a] = extended[a, HALO : HALO + ROWS]
    send_sums(sums, turned, next_ref)


def finish_kernel(
    first_ref, second_ref, third_ref, first_direction_ref, second_direction_ref,
    solution_ref, hessenberg_ref,
):
    third = third_ref[...]
    beta, h_00, h_10 = first_column(first_ref[...], second_ref[...])
    h_01 = lane_total(third, 0) / beta
    h_11 = (lane_total(third, 1) - h_00 * h_01) / h_10
    h_21 = jnp.sqrt(lane_total(third, 2) - h_01 * h_01 - h_11 * h_11)
    n_00 = h_00 * h_00 + h_10 * h_10
    n_10 = h_00 * h_01 + h_10 * h_11
    n_11 = h_01 * h_01 + h_11 * h_11 + h_21 * h_21
    l_00 = jnp.sqrt(n_00)
    l_10 = n_10 / l_00
    l_11 = jnp.sqrt(n_11 - l_10 * l_10)
    f_0 = beta * h_00 / l_00
    f_1 = (beta * h_01 - l_10 * f_0) / l_11
    c_1 = f_1 / l_11
    c_0 = (f_0 - l_10 * c_1) / l_00
    for a in range(2):
        solution_ref[a] = c_0 * first_direction_ref[a] + c_1 * second_direction_ref[a]
    shape = hessenberg_ref.shape
    row = lax.broadcasted_iota(jnp.int32, shape, 1)
    column = lax.broadcasted_iota(jnp.int32, shape, 0)
    entries = jnp.zeros(shape, jnp.float32)
    for i, j, value in ((0, 0, h_00), (0, 1, h_01), (1, 0, h_10), (1, 1, h_11), (2, 1, h_21)):
        entries = jnp.where((row == i) & (column == j), value, entries)
    hessenberg_ref[...] = entries


def call(kernel, name, in_specs, outs, flops, scratch=(), traffic=4_000_000):
    return pl.pallas_call(
        kernel,
        name=name,
        in_specs=in_specs,
        out_specs=[VMEM] * len(outs),
        out_shape=outs,
        scratch_shapes=scratch,
        compiler_params=pltpu.CompilerParams(vmem_limit_bytes=16 * 1024 * 1024),
        cost_estimate=pl.CostEstimate(flops=flops, bytes_accessed=traffic, transcendentals=0),
    )


def in_hbm(array):
    return pltpu.with_memory_space_constraint(array, pltpu.HBM)


def from_everyone(rows):
    return lax.all_to_all(rows, "sub", 0, 0, tiled=True)


def from_everyone_reversed(rows):
    order = [list(range(lax.axis_size("sub")))[::-1]]
    return lax.all_to_all(rows, "sub", 0, 0, tiled=True, axis_index_groups=order)


def swap(partner, other):
    count = lax.axis_size("sub")
    both = lambda lows: [pair for i in lows for pair in ((i, i + 1), (i + 1, i))]
    return (
        lax.ppermute(partner, "sub", both(range(0, count, 2))),
        lax.ppermute(other, "sub", both(range(1, count - 1, 2))),
    )


def on_device(rhs, viscosity, coupling, margin_rows, coarse_basis, coarse_inverse):
    count = lax.axis_size("sub")
    columns = coarse_inverse.shape[1]
    f32 = lambda *shape: jax.ShapeDtypeStruct(shape, jnp.float32)
    dma = lambda *shape: pltpu.SemaphoreType.DMA(shape)
    field = pltpu.VMEM((2, ROWS, CELLS), jnp.float32)
    extended = pltpu.VMEM((2, EXT, CELLS), jnp.float32)
    sums = pltpu.VMEM((8 * SLOTS, LANES), jnp.float32)
    row, whole, edge = f32(count, LANES), f32(2, ROWS, CELLS), f32(2, HALO, CELLS)
    packed, smoothed = f32(EDGE_AT + coarse_rows(columns), CELLS), f32(2, EXT, CELLS)
    basis = jax.ShapeDtypeStruct(coarse_basis.shape, jnp.bfloat16)
    arguments = (rhs, viscosity, coupling, coarse_inverse, coarse_basis)
    first, partner, other, held = call(
        start_kernel, "start", [HBM] * 5, [row, packed, packed, basis], 10_000_000,
        [field, sums, sums, dma(), dma(PIECES), dma(2 * pack_count(columns))],
    )(*map(in_hbm, arguments))
    partner, other = swap(partner, other)
    first = from_everyone(first)
    direction, image, smooth, partner_rows, other_rows, second = call(
        functools.partial(first_turn_kernel, count), "first_turn", [SMEM] + [VMEM] * 8,
        [whole, whole, smoothed, edge, edge, row], 20_000_000, [extended, sums, sums],
    )(margin_rows, first, coarse_inverse, partner, other, held, rhs, viscosity, coupling)
    partner_rows, other_rows = swap(partner_rows, other_rows)
    second = from_everyone(second)
    second_direction, third = call(
        functools.partial(second_turn_kernel, count), "second_turn", [SMEM] + [VMEM] * 13,
        [whole, row], 20_000_000, [extended, extended, sums, sums],
    )(
        margin_rows, first, second, coarse_inverse, partner, other, partner_rows, other_rows,
        held, smooth, rhs, image, viscosity, coupling,
    )
    third = from_everyone_reversed(third)
    result, transposed = call(finish_kernel, "finish", [VMEM] * 5, [whole, f32(2, 3)], 1_000_000)(
        first, second, third, direction, second_direction
    )
    return result, transposed.T


def solution(mesh):
    in_specs = (
        P(None, ("groups", "sub"), None),
        P(("groups", "sub"), None),
        P(None, ("groups", "sub"), None),
        P("groups"),
        P(None, None, ("groups", "sub"), None),
        P(("groups", "sub"), None),
    )
    out_specs = (P(None, ("groups", "sub"), None), P("groups", None))
    return jax.shard_map(
        on_device, mesh=mesh, in_specs=in_specs, out_specs=out_specs, check_vma=False
    )
```

```python
import functools

import jax
import jax.numpy as jnp
from jax import lax
from jax.experimental import pallas as pl
from jax.experimental.pallas import tpu as pltpu
from jax.sharding import PartitionSpec as P

ROWS = 64
CELLS = 512
VECTORS = 48
HALO = 8
EXT = ROWS + 2 * HALO
STRIP = 32
CHUNK = 16
CHUNKS = 2 * ROWS // CHUNK
PIECE = 6
PIECES = VECTORS // PIECE
AHEAD = 4
LANES = 128
SLOTS = 56
EDGE_AT = 5 * HALO
INVERSE_AT = 2 * VECTORS
SWEEPS = 4
RELAX = 0.7
ROW_FACTOR = (1.0, 4.0)
CELL_FACTOR = (4.0, 1.0)

VMEM = pl.BlockSpec(memory_space=pltpu.VMEM)
SMEM = pl.BlockSpec(memory_space=pltpu.SMEM)
HBM = pl.BlockSpec(memory_space=pltpu.HBM)


def coarse_rows(columns):
    return INVERSE_AT + VECTORS * (columns // 512) + (VECTORS // 2) * (columns % 512 // 256)


def cell_sum(field):
    lane = lax.broadcasted_iota(jnp.int32, (field.shape[0], LANES), 1)
    left, right = pltpu.roll(field, 1, 1), pltpu.roll(field, CELLS - 1, 1)
    inner = left[:, LANES:-LANES] + right[:, LANES:-LANES]
    first = jnp.where(lane == 0, 0.0, left[:, :LANES]) + right[:, :LANES]
    last = left[:, -LANES:] + jnp.where(lane == LANES - 1, 0.0, right[:, -LANES:])
    return jnp.concatenate([first, inner, last], 1)


def row_sum(field):
    count = field.shape[0]
    return pltpu.roll(field, 1, 0) + pltpu.roll(field, count - 1, 0)


def neighbours(field, component):
    rows, cells = row_sum(field), cell_sum(field)
    if component == 0:
        return rows + CELL_FACTOR[0] * cells
    return ROW_FACTOR[1] * rows + cells


def apply_operator(extended, viscosity, coupling):
    inner = slice(HALO, HALO + ROWS)
    images = []
    for a in range(2):
        around = neighbours(extended[a], a)[inner]
        diagonal = 10.0 * viscosity + jnp.abs(coupling[a]) + 0.05
        images.append(
            diagonal * extended[a][inner]
            - viscosity * around
            + coupling[a] * extended[1 - a][inner]
        )
    return images


def basis_copy(i, basis_ref, held, sems):
    vectors = pl.ds(PIECE * i, PIECE)
    return pltpu.make_async_copy(basis_ref.at[vectors], held.at[vectors], sems.at[i])


def restrict_piece(i, held, field, sums):
    for n in range(PIECE):
        k = PIECE * i + n
        total = None
        for a in range(2):
            for r in range(0, ROWS, CHUNK):
                for c in range(0, CELLS, LANES):
                    rows, cells = slice(r, r + CHUNK), slice(c, c + LANES)
                    term = held[k, a, rows, cells].astype(jnp.float32) * field[a, rows, cells]
                    term = term[:8] + term[8:]
                    total = term if total is None else total + term
        sums[pl.ds(pl.multiple_of(8 * k, 8), 8), :] = total


def fold(field):
    total = None
    for part in field:
        for r in range(0, part.shape[0], 8):
            for c in range(0, part.shape[1], LANES):
                term = part[r : r + 8, c : c + LANES]
                total = term if total is None else total + term
    return total


def send_sums(sums, turned, out_ref):
    for k in range(SLOTS):
        turned[pl.ds(k, 8, stride=SLOTS), :] = sums[8 * k : 8 * k + 8, :]
    by_slot = turned[:SLOTS]
    for j in range(1, 8):
        by_slot = by_slot + turned[SLOTS * j : SLOTS * (j + 1)]
    row = lax.dot_general(
        jnp.ones((8, LANES), jnp.float32),
        by_slot,
        (((1,), (1,)), ((), ())),
        precision=lax.Precision.HIGHEST,
        preferred_element_type=jnp.float32,
    )
    wide = jnp.concatenate([row[:1], jnp.zeros((1, LANES - SLOTS), jnp.float32)], 1)
    out_ref[...] = jnp.broadcast_to(wide, out_ref.shape)


def pack_copies(out_ref, first_row, rhs_ref, visc_ref, coup_ref, inverse_ref, sems, at_sem):
    rows = pl.ds(pl.multiple_of(first_row, HALO), HALO)
    moves = [(visc_ref.at[rows, :], 0, HALO, None)]
    for a in range(2):
        moves.append((coup_ref.at[a, rows, :], HALO * (1 + a), HALO, None))
        moves.append((rhs_ref.at[a, rows, :], HALO * (3 + a), HALO, None))
    columns = inverse_ref.shape[1]
    at = EDGE_AT + INVERSE_AT
    for c in range(0, columns - 511, 512):
        moves.append((inverse_ref.at[:, pl.ds(c, 512)], at, VECTORS, None))
        at += VECTORS
    if columns % 512:
        half = VECTORS // 2
        last = pl.ds(columns - 256, 256)
        moves.append((inverse_ref.at[pl.ds(0, half), last], at, half, 0))
        moves.append((inverse_ref.at[pl.ds(half, half), last], at, half, 256))
    copies = []
    for n, (source, at, size, lane) in enumerate(moves):
        place = pl.ds(at, size)
        target = out_ref.at[place, :] if lane is None else out_ref.at[place, pl.ds(lane, 256)]
        copies.append(pltpu.make_async_copy(source, target, sems.at[at_sem + n]))
    return copies


def pack_count(columns):
    return 5 + columns // 512 + 2 * (columns % 512 // 256)


def start_kernel(
    rhs_ref, visc_ref, coup_ref, inverse_ref, basis_ref,
    sums_ref, partner_ref, other_ref, held,
    field, sums, turned, field_sem, sems, pack_sems,
):
    odd = lax.axis_index("sub") % 2
    field_copy = pltpu.make_async_copy(rhs_ref, field, field_sem)
    field_copy.start()
    for i in range(AHEAD):
        basis_copy(i, basis_ref, held, sems).start()
    packs = []
    for n, (out_ref, up) in enumerate(((partner_ref, 1 - odd), (other_ref, odd))):
        packs += pack_copies(
            out_ref, up * (ROWS - HALO), rhs_ref, visc_ref, coup_ref, inverse_ref, pack_sems,
            n * pack_count(inverse_ref.shape[1]),
        )
    for copy in packs:
        copy.start()
    sums[...] = jnp.zeros_like(sums)
    field_copy.wait()
    sums[8 * VECTORS : 8 * VECTORS + 8] = fold([field[a] * field[a] for a in range(2)])

    def body(i, carry):
        basis_copy(i, basis_ref, held, sems).wait()

        @pl.when(i + AHEAD < PIECES)
        def _():
            basis_copy(i + AHEAD, basis_ref, held, sems).start()

        restrict_piece(i, held, field, sums)
        for n in range(PIECE):
            k = PIECE * i + n
            for a in range(2):
                top = held[k, a, :CHUNK, :].astype(jnp.float32)[:1]
                bottom = held[k, a, ROWS - CHUNK :, :].astype(jnp.float32)[CHUNK - 1 :]
                place = pl.ds(EDGE_AT + VECTORS * a + k, 1)
                partner_ref[place, :] = jnp.where(odd == 1, top, bottom)
                other_ref[place, :] = jnp.where(odd == 1, bottom, top)
        return carry

    lax.fori_loop(0, PIECES, body, 0)
    for copy in packs:
        copy.wait()
    send_sums(sums, turned, sums_ref)


class Neighbour:
    def __init__(self, first_ref, second_ref):
        self.odd = lax.axis_index("sub") % 2 == 1
        self.first, self.second = first_ref, second_ref

    def __getitem__(self, index):
        return jnp.where(self.odd, self.first[index], self.second[index])


def neighbours_of(partner_ref, other_ref):
    return Neighbour(partner_ref, other_ref), Neighbour(other_ref, partner_ref)


def solve(
    count, margin_ref, visc_ref, coup_ref, field_ref, low_ref, high_ref, edges, out_ref, beside
):
    rank = lax.axis_index("sub")
    lower = jnp.where(rank > 0, margin_ref[jnp.maximum(rank - 1, 0)], 0)
    upper = jnp.where(rank < count - 1, margin_ref[rank], 0)
    lower_f, upper_f = lower.astype(jnp.float32), upper.astype(jnp.float32)
    low_scale = 2.0 * jnp.maximum(lower_f, 1.0)
    high_scale = 2.0 * jnp.maximum(upper_f, 1.0)

    def masks(first, rows, side):
        place = lax.broadcasted_iota(jnp.int32, (rows, LANES), 0) + first
        place_f = place.astype(jnp.float32)
        rising = lambda base, scale: (place_f - base + 0.5) / scale
        falling = lambda base, scale: (base - place_f - 0.5) / scale
        if side == 0:
            live = (place >= -lower) & (place < ROWS + upper)
            weight = jnp.where(place < lower, rising(-lower_f, low_scale), 1.0)
            weight = jnp.where(
                place >= ROWS - upper, falling(ROWS + upper_f, high_scale), weight
            )
        elif side < 0:
            live = place < lower
            weight = jnp.where(place >= -lower, falling(lower_f, low_scale), 1.0)
        else:
            live = place >= ROWS - upper
            weight = jnp.where(place < ROWS + upper, rising(ROWS - upper_f, high_scale), 1.0)
        wide = lambda x: jnp.concatenate([x] * (CELLS // LANES), 1)
        return wide(live.astype(jnp.float32)), wide(weight)

    def stack(own, at):
        rows = slice(at, at + HALO)
        return jnp.concatenate([low_ref[rows], own, high_ref[rows]], 0)

    def triple(field):
        return jnp.concatenate([field, field[:STRIP], field[EXT - STRIP :]], 0)

    viscosity = stack(visc_ref[...], 0)
    blocks = [masks(-HALO, EXT, 0), masks(-HALO, STRIP, -1), masks(ROWS + HALO - STRIP, STRIP, 1)]
    live = jnp.concatenate([block[0] for block in blocks], 0)
    first, across, other = [], [], []
    for a in range(2):
        coupling = stack(coup_ref[a], HALO * (1 + a))
        field = jnp.concatenate([edges[a][0], field_ref[a], edges[a][1]], 0)
        scale = RELAX / (10.0 * viscosity + jnp.abs(coupling) + 0.05)
        first.append(live * triple(scale * field))
        across.append(live * triple(scale * viscosity))
        other.append(live * triple(scale * coupling))
    solved = list(first)
    for sweep in range(1, SWEEPS):
        beside(sweep)
        solved = [
            (1.0 - RELAX) * solved[a]
            + first[a]
            + across[a] * neighbours(solved[a], a)
            - other[a] * solved[1 - a]
            for a in range(2)
        ]
    for a in range(2):
        shares = solved[a] * jnp.concatenate([block[1] for block in blocks], 0)
        out_ref[a] = shares[:EXT]
        out_ref[a, :STRIP] += shares[EXT : EXT + STRIP]
        out_ref[a, EXT - STRIP :] += shares[EXT + STRIP :]


def line_up(residuals):
    devices = residuals.shape[0]
    lane = lax.broadcasted_iota(jnp.int32, (1, LANES), 1)
    tiles = [jnp.zeros((1, LANES), jnp.float32) for _ in range(devices * VECTORS // LANES)]
    for t in range(devices):
        tile, offset = divmod(VECTORS * t, LANES)
        row = jnp.where(lane < VECTORS, residuals[devices - 1 - t : devices - t], 0.0)
        if offset:
            row = pltpu.roll(row, offset, 1)
        if offset + VECTORS <= LANES:
            tiles[tile] = tiles[tile] + row
        else:
            tiles[tile] = tiles[tile] + jnp.where(lane >= offset, row, 0.0)
            tiles[tile + 1] = tiles[tile + 1] + jnp.where(lane < offset, row, 0.0)
    return jnp.concatenate(tiles, 1)


def rounded(column):
    return column.astype(jnp.bfloat16).astype(jnp.float32)


def lift(inverse_ref, residual):
    return rounded(jnp.sum(inverse_ref[...] * residual, 1, keepdims=True))


def lift_packed(ref, residual):
    columns = residual.shape[1]
    at, total = EDGE_AT + INVERSE_AT, None
    for c in range(0, columns - 511, 512):
        term = jnp.sum(ref[at : at + VECTORS] * residual[:, c : c + 512], 1, keepdims=True)
        total = term if total is None else total + term
        at += VECTORS
    if columns % 512:
        half = VECTORS // 2
        last = residual[:, columns - 256 :]
        rows = ref[at : at + half]
        term = jnp.concatenate(
            [
                jnp.sum(rows[:, :256] * last, 1, keepdims=True),
                jnp.sum(rows[:, 256:] * last, 1, keepdims=True),
            ],
            0,
        )
        total = term if total is None else total + term
    return rounded(total)


def edge_values(ref, lifted):
    starts = [EDGE_AT + VECTORS * a for a in range(2)]
    return [jnp.sum(ref[at : at + VECTORS] * lifted, 0, keepdims=True) for at in starts]


def spread(lifted):
    shape = (VECTORS, CHUNK * VECTORS)
    owner = lax.broadcasted_iota(jnp.int32, shape, 1) // CHUNK
    row = lax.broadcasted_iota(jnp.int32, shape, 0)
    line = jnp.sum(jnp.where(owner == row, lifted, 0.0), 0, keepdims=True)
    shape = (CHUNK, CHUNK * VECTORS)
    place = lax.broadcasted_iota(jnp.int32, shape, 1) % CHUNK
    row = lax.broadcasted_iota(jnp.int32, shape, 0)
    return jnp.where(place == row, line, 0.0).astype(jnp.bfloat16)


def prolonging(residual, inverse_ref, held, extended):
    matrix = spread(lift(inverse_ref, residual))
    places = [(a, r) for a in range(2) for r in range(0, ROWS, CHUNK)]

    def beside(n):
        for a, r in places[n - 1 :: SWEEPS - 1]:
            rows = held[:, a, r : r + CHUNK, :].reshape(CHUNK * VECTORS, CELLS)
            extended[a, HALO + r : HALO + r + CHUNK] = jnp.dot(
                matrix, rows, preferred_element_type=jnp.float32
            )

    return beside


def add_smooth(residual, low, high, smooth, extended):
    low_edge = edge_values(low, lift_packed(low, residual))
    high_edge = edge_values(high, lift_packed(high, residual))
    place = lax.broadcasted_iota(jnp.int32, (HALO, CELLS), 0)
    for a in range(2):
        rows = slice(HALO, HALO + ROWS)
        extended[a, rows] += smooth(a, rows)
        rows = slice(0, HALO)
        extended[a, rows] = smooth(a, rows) + jnp.where(place == HALO - 1, low_edge[a], 0.0)
        rows = slice(EXT - HALO, EXT)
        extended[a, rows] = smooth(a, rows) + jnp.where(place == 0, high_edge[a], 0.0)


def lane_total(received, lane):
    return jnp.sum(received[:, lane : lane + 1], 0, keepdims=True)


def first_turn_kernel(
    count, margin_ref, sums_ref, inverse_ref, partner_ref, other_ref, held, rhs_ref, visc_ref,
    coup_ref,
    direction_ref, image_ref, smooth_ref, partner_rows_ref, other_rows_ref, next_ref,
    extended, sums, turned,
):
    received = sums_ref[...]
    over_beta = 1.0 / jnp.sqrt(lane_total(received, VECTORS))
    residual = line_up(received) * over_beta
    beside = prolonging(residual, inverse_ref, held, extended)
    low, high = neighbours_of(partner_ref, other_ref)
    starts = [HALO * (3 + a) for a in range(2)]
    edges = [(low[at : at + HALO], high[at : at + HALO]) for at in starts]
    solve(count, margin_ref, visc_ref, coup_ref, rhs_ref, low, high, edges, smooth_ref, beside)
    add_smooth(
        residual, low, high, lambda a, rows: smooth_ref[a, rows] * over_beta, extended
    )
    images = apply_operator(
        [extended[a] for a in range(2)], visc_ref[...], [coup_ref[a] for a in range(2)]
    )
    odd = lax.axis_index("sub") % 2 == 1
    for a in range(2):
        direction_ref[a] = extended[a, HALO : HALO + ROWS]
        image_ref[a] = images[a]
        head, tail = images[a][:HALO], images[a][ROWS - HALO :]
        partner_rows_ref[a] = jnp.where(odd, head, tail)
        other_rows_ref[a] = jnp.where(odd, tail, head)
    sums[...] = jnp.zeros_like(sums)
    at = 8 * VECTORS
    sums[at : at + 8] = fold([rhs_ref[a] * images[a] for a in range(2)])
    sums[at + 8 : at + 16] = fold([images[a] * images[a] for a in range(2)])

    def body(i, carry):
        restrict_piece(i, held, image_ref, sums)
        return carry

    lax.fori_loop(0, PIECES, body, 0)
    send_sums(sums, turned, next_ref)


def first_column(first, second):
    beta = jnp.sqrt(lane_total(first, VECTORS))
    h_00 = lane_total(second, VECTORS) / beta
    h_10 = jnp.sqrt(lane_total(second, VECTORS + 1) - h_00 * h_00)
    return beta, h_00, h_10


def second_turn_kernel(
    count, margin_ref, first_ref, second_ref, inverse_ref, partner_ref, other_ref,
    partner_rows_ref, other_rows_ref, held, smooth_ref, rhs_ref, image_ref, visc_ref, coup_ref,
    direction_ref, next_ref,
    image_smooth, extended, sums, turned,
):
    first, second = first_ref[...], second_ref[...]
    beta, h_00, h_10 = first_column(first, second)
    ratio = h_00 / beta
    over = 1.0 / h_10
    residual = (line_up(second) - ratio * line_up(first)) * over
    beside = prolonging(residual, inverse_ref, held, extended)
    low, high = neighbours_of(partner_ref, other_ref)
    low_rows, high_rows = neighbours_of(partner_rows_ref, other_rows_ref)
    edges = [(low_rows[a], high_rows[a]) for a in range(2)]
    solve(
        count, margin_ref, visc_ref, coup_ref, image_ref, low, high, edges, image_smooth, beside
    )
    add_smooth(
        residual,
        low,
        high,
        lambda a, rows: (image_smooth[a, rows] - ratio * smooth_ref[a, rows]) * over,
        extended,
    )
    images = apply_operator(
        [extended[a] for a in range(2)], visc_ref[...], [coup_ref[a] for a in range(2)]
    )
    sums[...] = jnp.zeros_like(sums)
    sums[0:8] = fold([rhs_ref[a] * images[a] for a in range(2)])
    sums[8:16] = fold([image_ref[a] * images[a] for a in range(2)])
    sums[16:24] = fold([images[a] * images[a] for a in range(2)])
    for a in range(2):
        direction_ref[a] = extended[a, HALO : HALO + ROWS]
    send_sums(sums, turned, next_ref)


def finish_kernel(
    first_ref, second_ref, third_ref, first_direction_ref, second_direction_ref,
    solution_ref, hessenberg_ref,
):
    third = third_ref[...]
    beta, h_00, h_10 = first_column(first_ref[...], second_ref[...])
    h_01 = lane_total(third, 0) / beta
    h_11 = (lane_total(third, 1) - h_00 * h_01) / h_10
    h_21 = jnp.sqrt(lane_total(third, 2) - h_01 * h_01 - h_11 * h_11)
    n_00 = h_00 * h_00 + h_10 * h_10
    n_10 = h_00 * h_01 + h_10 * h_11
    n_11 = h_01 * h_01 + h_11 * h_11 + h_21 * h_21
    l_00 = jnp.sqrt(n_00)
    l_10 = n_10 / l_00
    l_11 = jnp.sqrt(n_11 - l_10 * l_10)
    f_0 = beta * h_00 / l_00
    f_1 = (beta * h_01 - l_10 * f_0) / l_11
    c_1 = f_1 / l_11
    c_0 = (f_0 - l_10 * c_1) / l_00
    for a in range(2):
        solution_ref[a] = c_0 * first_direction_ref[a] + c_1 * second_direction_ref[a]
    shape = hessenberg_ref.shape
    row = lax.broadcasted_iota(jnp.int32, shape, 1)
    column = lax.broadcasted_iota(jnp.int32, shape, 0)
    entries = jnp.zeros(shape, jnp.float32)
    for i, j, value in ((0, 0, h_00), (0, 1, h_01), (1, 0, h_10), (1, 1, h_11), (2, 1, h_21)):
        entries = jnp.where((row == i) & (column == j), value, entries)
    hessenberg_ref[...] = entries


def call(kernel, name, in_specs, outs, flops, scratch=(), traffic=4_000_000):
    return pl.pallas_call(
        kernel,
        name=name,
        in_specs=in_specs,
        out_specs=[VMEM] * len(outs),
        out_shape=outs,
        scratch_shapes=scratch,
        compiler_params=pltpu.CompilerParams(vmem_limit_bytes=16 * 1024 * 1024),
        cost_estimate=pl.CostEstimate(flops=flops, bytes_accessed=traffic, transcendentals=0),
    )


def in_hbm(array):
    return pltpu.with_memory_space_constraint(array, pltpu.HBM)


def from_everyone(rows):
    order = [list(range(lax.axis_size("sub")))[::-1]]
    return lax.all_to_all(rows, "sub", 0, 0, tiled=True, axis_index_groups=order)


def swap(partner, other):
    count = lax.axis_size("sub")
    both = lambda lows: [pair for i in lows for pair in ((i, i + 1), (i + 1, i))]
    return (
        lax.ppermute(partner, "sub", both(range(0, count, 2))),
        lax.ppermute(other, "sub", both(range(1, count - 1, 2))),
    )


def on_device(rhs, viscosity, coupling, margin_rows, coarse_basis, coarse_inverse):
    count = lax.axis_size("sub")
    columns = coarse_inverse.shape[1]
    f32 = lambda *shape: jax.ShapeDtypeStruct(shape, jnp.float32)
    dma = lambda *shape: pltpu.SemaphoreType.DMA(shape)
    field = pltpu.VMEM((2, ROWS, CELLS), jnp.float32)
    extended = pltpu.VMEM((2, EXT, CELLS), jnp.float32)
    sums = pltpu.VMEM((8 * SLOTS, LANES), jnp.float32)
    row, whole, edge = f32(count, LANES), f32(2, ROWS, CELLS), f32(2, HALO, CELLS)
    packed, smoothed = f32(EDGE_AT + coarse_rows(columns), CELLS), f32(2, EXT, CELLS)
    basis = jax.ShapeDtypeStruct(coarse_basis.shape, jnp.bfloat16)
    arguments = (rhs, viscosity, coupling, coarse_inverse, coarse_basis)
    first, partner, other, held = call(
        start_kernel, "start", [HBM] * 5, [row, packed, packed, basis], 10_000_000,
        [field, sums, sums, dma(), dma(PIECES), dma(2 * pack_count(columns))],
    )(*map(in_hbm, arguments))
    partner, other = swap(partner, other)
    first = from_everyone(first)
    direction, image, smooth, partner_rows, other_rows, second = call(
        functools.partial(first_turn_kernel, count), "first_turn", [SMEM] + [VMEM] * 8,
        [whole, whole, smoothed, edge, edge, row], 20_000_000, [extended, sums, sums],
    )(margin_rows, first, coarse_inverse, partner, other, held, rhs, viscosity, coupling)
    partner_rows, other_rows = swap(partner_rows, other_rows)
    second = from_everyone(second)
    second_direction, third = call(
        functools.partial(second_turn_kernel, count), "second_turn", [SMEM] + [VMEM] * 13,
        [whole, row], 20_000_000, [extended, extended, sums, sums],
    )(
        margin_rows, first, second, coarse_inverse, partner, other, partner_rows, other_rows,
        held, smooth, rhs, image, viscosity, coupling,
    )
    third = from_everyone(third)
    result, transposed = call(finish_kernel, "finish", [VMEM] * 5, [whole, f32(2, 3)], 1_000_000)(
        first, second, third, direction, second_direction
    )
    return result, transposed.T


def solution(mesh):
    in_specs = (
        P(None, ("groups", "sub"), None),
        P(("groups", "sub"), None),
        P(None, ("groups", "sub"), None),
        P("groups"),
        P(None, None, ("groups", "sub"), None),
        P(("groups", "sub"), None),
    )
    out_specs = (P(None, ("groups", "sub"), None), P("groups", None))
    return jax.shard_map(
        on_device, mesh=mesh, in_specs=in_specs, out_specs=out_specs, check_vma=False
    )
```

```python
import functools

import jax
import jax.numpy as jnp
from jax import lax
from jax.experimental import pallas as pl
from jax.experimental.pallas import tpu as pltpu
from jax.sharding import PartitionSpec as P

ROWS = 64
CELLS = 512
VECTORS = 48
HALO = 8
EXT = ROWS + 2 * HALO
STRIP = 32
CHUNK = 16
CHUNKS = 2 * ROWS // CHUNK
PIECE = 6
PIECES = VECTORS // PIECE
LANES = 128
SLOTS = 56
EDGE_AT = 5 * HALO
INVERSE_AT = 2 * VECTORS
SWEEPS = 4
RELAX = 0.7
ROW_FACTOR = (1.0, 4.0)
CELL_FACTOR = (4.0, 1.0)

VMEM = pl.BlockSpec(memory_space=pltpu.VMEM)
SMEM = pl.BlockSpec(memory_space=pltpu.SMEM)
HBM = pl.BlockSpec(memory_space=pltpu.HBM)


def coarse_rows(columns):
    return INVERSE_AT + VECTORS * (columns // 512) + (VECTORS // 2) * (columns % 512 // 256)


def cell_sum(field):
    lane = lax.broadcasted_iota(jnp.int32, (field.shape[0], LANES), 1)
    left, right = pltpu.roll(field, 1, 1), pltpu.roll(field, CELLS - 1, 1)
    inner = left[:, LANES:-LANES] + right[:, LANES:-LANES]
    first = jnp.where(lane == 0, 0.0, left[:, :LANES]) + right[:, :LANES]
    last = left[:, -LANES:] + jnp.where(lane == LANES - 1, 0.0, right[:, -LANES:])
    return jnp.concatenate([first, inner, last], 1)


def row_sum(field):
    count = field.shape[0]
    return pltpu.roll(field, 1, 0) + pltpu.roll(field, count - 1, 0)


def neighbours(field, component):
    rows, cells = row_sum(field), cell_sum(field)
    if component == 0:
        return rows + CELL_FACTOR[0] * cells
    return ROW_FACTOR[1] * rows + cells


def apply_operator(extended, viscosity, coupling):
    inner = slice(HALO, HALO + ROWS)
    images = []
    for a in range(2):
        around = neighbours(extended[a], a)[inner]
        diagonal = 10.0 * viscosity + jnp.abs(coupling[a]) + 0.05
        images.append(
            diagonal * extended[a][inner]
            - viscosity * around
            + coupling[a] * extended[1 - a][inner]
        )
    return images


def restrict_piece(i, held, field, sums):
    for n in range(PIECE):
        k = PIECE * i + n
        total = None
        for a in range(2):
            for r in range(0, ROWS, CHUNK):
                for c in range(0, CELLS, LANES):
                    rows, cells = slice(r, r + CHUNK), slice(c, c + LANES)
                    term = held[k, a, rows, cells].astype(jnp.float32) * field[a, rows, cells]
                    term = term[:8] + term[8:]
                    total = term if total is None else total + term
        sums[pl.ds(pl.multiple_of(8 * k, 8), 8), :] = total


def fold(field):
    total = None
    for part in field:
        for r in range(0, part.shape[0], 8):
            for c in range(0, part.shape[1], LANES):
                term = part[r : r + 8, c : c + LANES]
                total = term if total is None else total + term
    return total


def send_sums(sums, turned, out_ref):
    for k in range(SLOTS):
        turned[pl.ds(k, 8, stride=SLOTS), :] = sums[8 * k : 8 * k + 8, :]
    by_slot = turned[:SLOTS]
    for j in range(1, 8):
        by_slot = by_slot + turned[SLOTS * j : SLOTS * (j + 1)]
    row = lax.dot_general(
        jnp.ones((8, LANES), jnp.float32),
        by_slot,
        (((1,), (1,)), ((), ())),
        precision=lax.Precision.HIGHEST,
        preferred_element_type=jnp.float32,
    )
    wide = jnp.concatenate([row[:1], jnp.zeros((1, LANES - SLOTS), jnp.float32)], 1)
    out_ref[...] = jnp.broadcast_to(wide, out_ref.shape)


def pack_copies(out_ref, first_row, rhs_ref, visc_ref, coup_ref, inverse_ref, sems, at_sem):
    rows = pl.ds(pl.multiple_of(first_row, HALO), HALO)
    moves = [(visc_ref.at[rows, :], 0, HALO, None)]
    for a in range(2):
        moves.append((coup_ref.at[a, rows, :], HALO * (1 + a), HALO, None))
        moves.append((rhs_ref.at[a, rows, :], HALO * (3 + a), HALO, None))
    columns = inverse_ref.shape[1]
    at = EDGE_AT + INVERSE_AT
    for c in range(0, columns - 511, 512):
        moves.append((inverse_ref.at[:, pl.ds(c, 512)], at, VECTORS, None))
        at += VECTORS
    if columns % 512:
        half = VECTORS // 2
        last = pl.ds(columns - 256, 256)
        moves.append((inverse_ref.at[pl.ds(0, half), last], at, half, 0))
        moves.append((inverse_ref.at[pl.ds(half, half), last], at, half, 256))
    copies = []
    for n, (source, at, size, lane) in enumerate(moves):
        place = pl.ds(at, size)
        target = out_ref.at[place, :] if lane is None else out_ref.at[place, pl.ds(lane, 256)]
        copies.append(pltpu.make_async_copy(source, target, sems.at[at_sem + n]))
    return copies


def pack_count(columns):
    return 5 + columns // 512 + 2 * (columns % 512 // 256)


def pack_kernel(
    rhs_ref, visc_ref, coup_ref, inverse_ref, basis_ref,
    partner_ref, other_ref,
    groups, group_sems, pack_sems,
):
    odd = lax.axis_index("sub") % 2
    sides = ((partner_ref, 1 - odd), (other_ref, odd))
    group_copies, packs = [], []
    for n, (out_ref, up) in enumerate(sides):
        for a in range(2):
            rows = pl.ds(pl.multiple_of(up * (ROWS - CHUNK), CHUNK), CHUNK)
            group_copies.append(
                pltpu.make_async_copy(
                    basis_ref.at[:, a, rows, :], groups.at[2 * n + a], group_sems.at[2 * n + a]
                )
            )
        packs += pack_copies(
            out_ref, up * (ROWS - HALO), rhs_ref, visc_ref, coup_ref, inverse_ref, pack_sems,
            n * pack_count(inverse_ref.shape[1]),
        )
    for copy in group_copies + packs:
        copy.start()
    for n, (out_ref, up) in enumerate(sides):
        for a in range(2):
            group_copies[2 * n + a].wait()
            for k in range(VECTORS):
                rows = groups[2 * n + a, k].astype(jnp.float32)
                at = EDGE_AT + VECTORS * a + k
                out_ref[at : at + 1] = jnp.where(up == 1, rows[CHUNK - 1 :], rows[:1])
    for copy in packs:
        copy.wait()


def restrict_kernel(rhs_ref, held, sums_ref, sums, turned):
    sums[...] = jnp.zeros_like(sums)
    sums[8 * VECTORS : 8 * VECTORS + 8] = fold([rhs_ref[a] * rhs_ref[a] for a in range(2)])

    def body(i, carry):
        restrict_piece(i, held, rhs_ref, sums)
        return carry

    lax.fori_loop(0, PIECES, body, 0)
    send_sums(sums, turned, sums_ref)


class Neighbour:
    def __init__(self, first_ref, second_ref):
        self.odd = lax.axis_index("sub") % 2 == 1
        self.first, self.second = first_ref, second_ref

    def __getitem__(self, index):
        return jnp.where(self.odd, self.first[index], self.second[index])


def neighbours_of(partner_ref, other_ref):
    return Neighbour(partner_ref, other_ref), Neighbour(other_ref, partner_ref)


def solve(
    count, margin_ref, visc_ref, coup_ref, field_ref, low_ref, high_ref, edges, out_ref, beside
):
    rank = lax.axis_index("sub")
    lower = jnp.where(rank > 0, margin_ref[jnp.maximum(rank - 1, 0)], 0)
    upper = jnp.where(rank < count - 1, margin_ref[rank], 0)
    lower_f, upper_f = lower.astype(jnp.float32), upper.astype(jnp.float32)
    low_scale = 2.0 * jnp.maximum(lower_f, 1.0)
    high_scale = 2.0 * jnp.maximum(upper_f, 1.0)

    def masks(first, rows, side):
        place = lax.broadcasted_iota(jnp.int32, (rows, LANES), 0) + first
        place_f = place.astype(jnp.float32)
        rising = lambda base, scale: (place_f - base + 0.5) / scale
        falling = lambda base, scale: (base - place_f - 0.5) / scale
        if side == 0:
            live = (place >= -lower) & (place < ROWS + upper)
            weight = jnp.where(place < lower, rising(-lower_f, low_scale), 1.0)
            weight = jnp.where(
                place >= ROWS - upper, falling(ROWS + upper_f, high_scale), weight
            )
        elif side < 0:
            live = place < lower
            weight = jnp.where(place >= -lower, falling(lower_f, low_scale), 1.0)
        else:
            live = place >= ROWS - upper
            weight = jnp.where(place < ROWS + upper, rising(ROWS - upper_f, high_scale), 1.0)
        wide = lambda x: jnp.concatenate([x] * (CELLS // LANES), 1)
        return wide(live.astype(jnp.float32)), wide(weight)

    def stack(own, at):
        rows = slice(at, at + HALO)
        return jnp.concatenate([low_ref[rows], own, high_ref[rows]], 0)

    def triple(field):
        return jnp.concatenate([field, field[:STRIP], field[EXT - STRIP :]], 0)

    viscosity = stack(visc_ref[...], 0)
    blocks = [masks(-HALO, EXT, 0), masks(-HALO, STRIP, -1), masks(ROWS + HALO - STRIP, STRIP, 1)]
    live = jnp.concatenate([block[0] for block in blocks], 0)
    first, across, other = [], [], []
    for a in range(2):
        coupling = stack(coup_ref[a], HALO * (1 + a))
        field = jnp.concatenate([edges[a][0], field_ref[a], edges[a][1]], 0)
        scale = RELAX / (10.0 * viscosity + jnp.abs(coupling) + 0.05)
        first.append(live * triple(scale * field))
        across.append(live * triple(scale * viscosity))
        other.append(live * triple(scale * coupling))
    solved = list(first)
    for sweep in range(1, SWEEPS):
        beside(sweep)
        solved = [
            (1.0 - RELAX) * solved[a]
            + first[a]
            + across[a] * neighbours(solved[a], a)
            - other[a] * solved[1 - a]
            for a in range(2)
        ]
    for a in range(2):
        shares = solved[a] * jnp.concatenate([block[1] for block in blocks], 0)
        out_ref[a] = shares[:EXT]
        out_ref[a, :STRIP] += shares[EXT : EXT + STRIP]
        out_ref[a, EXT - STRIP :] += shares[EXT + STRIP :]


def line_up(residuals):
    devices = residuals.shape[0]
    lane = lax.broadcasted_iota(jnp.int32, (1, LANES), 1)
    tiles = [jnp.zeros((1, LANES), jnp.float32) for _ in range(devices * VECTORS // LANES)]
    for t in range(devices):
        tile, offset = divmod(VECTORS * t, LANES)
        row = jnp.where(lane < VECTORS, residuals[devices - 1 - t : devices - t], 0.0)
        if offset:
            row = pltpu.roll(row, offset, 1)
        if offset + VECTORS <= LANES:
            tiles[tile] = tiles[tile] + row
        else:
            tiles[tile] = tiles[tile] + jnp.where(lane >= offset, row, 0.0)
            tiles[tile + 1] = tiles[tile + 1] + jnp.where(lane < offset, row, 0.0)
    return jnp.concatenate(tiles, 1)


def rounded(column):
    return column.astype(jnp.bfloat16).astype(jnp.float32)


def lift(inverse_ref, residual):
    return rounded(jnp.sum(inverse_ref[...] * residual, 1, keepdims=True))


def lift_packed(ref, residual):
    columns = residual.shape[1]
    at, total = EDGE_AT + INVERSE_AT, None
    for c in range(0, columns - 511, 512):
        term = jnp.sum(ref[at : at + VECTORS] * residual[:, c : c + 512], 1, keepdims=True)
        total = term if total is None else total + term
        at += VECTORS
    if columns % 512:
        half = VECTORS // 2
        last = residual[:, columns - 256 :]
        rows = ref[at : at + half]
        term = jnp.concatenate(
            [
                jnp.sum(rows[:, :256] * last, 1, keepdims=True),
                jnp.sum(rows[:, 256:] * last, 1, keepdims=True),
            ],
            0,
        )
        total = term if total is None else total + term
    return rounded(total)


def edge_values(ref, lifted):
    starts = [EDGE_AT + VECTORS * a for a in range(2)]
    return [jnp.sum(ref[at : at + VECTORS] * lifted, 0, keepdims=True) for at in starts]


def spread(lifted):
    shape = (VECTORS, CHUNK * VECTORS)
    owner = lax.broadcasted_iota(jnp.int32, shape, 1) // CHUNK
    row = lax.broadcasted_iota(jnp.int32, shape, 0)
    line = jnp.sum(jnp.where(owner == row, lifted, 0.0), 0, keepdims=True)
    shape = (CHUNK, CHUNK * VECTORS)
    place = lax.broadcasted_iota(jnp.int32, shape, 1) % CHUNK
    row = lax.broadcasted_iota(jnp.int32, shape, 0)
    return jnp.where(place == row, line, 0.0).astype(jnp.bfloat16)


def prolonging(residual, inverse_ref, held, extended):
    matrix = spread(lift(inverse_ref, residual))
    places = [(a, r) for a in range(2) for r in range(0, ROWS, CHUNK)]

    def beside(n):
        for a, r in places[n - 1 :: SWEEPS - 1]:
            rows = held[:, a, r : r + CHUNK, :].reshape(CHUNK * VECTORS, CELLS)
            extended[a, HALO + r : HALO + r + CHUNK] = jnp.dot(
                matrix, rows, preferred_element_type=jnp.float32
            )

    return beside


def add_smooth(residual, low, high, smooth, extended):
    low_edge = edge_values(low, lift_packed(low, residual))
    high_edge = edge_values(high, lift_packed(high, residual))
    place = lax.broadcasted_iota(jnp.int32, (HALO, CELLS), 0)
    for a in range(2):
        rows = slice(HALO, HALO + ROWS)
        extended[a, rows] += smooth(a, rows)
        rows = slice(0, HALO)
        extended[a, rows] = smooth(a, rows) + jnp.where(place == HALO - 1, low_edge[a], 0.0)
        rows = slice(EXT - HALO, EXT)
        extended[a, rows] = smooth(a, rows) + jnp.where(place == 0, high_edge[a], 0.0)


def lane_total(received, lane):
    return jnp.sum(received[:, lane : lane + 1], 0, keepdims=True)


def first_turn_kernel(
    count, margin_ref, sums_ref, inverse_ref, partner_ref, other_ref, held, rhs_ref, visc_ref,
    coup_ref,
    direction_ref, image_ref, smooth_ref, partner_rows_ref, other_rows_ref, next_ref,
    extended, sums, turned,
):
    received = sums_ref[...]
    over_beta = 1.0 / jnp.sqrt(lane_total(received, VECTORS))
    residual = line_up(received) * over_beta
    beside = prolonging(residual, inverse_ref, held, extended)
    low, high = neighbours_of(partner_ref, other_ref)
    starts = [HALO * (3 + a) for a in range(2)]
    edges = [(low[at : at + HALO], high[at : at + HALO]) for at in starts]
    solve(count, margin_ref, visc_ref, coup_ref, rhs_ref, low, high, edges, smooth_ref, beside)
    add_smooth(
        residual, low, high, lambda a, rows: smooth_ref[a, rows] * over_beta, extended
    )
    images = apply_operator(
        [extended[a] for a in range(2)], visc_ref[...], [coup_ref[a] for a in range(2)]
    )
    odd = lax.axis_index("sub") % 2 == 1
    for a in range(2):
        direction_ref[a] = extended[a, HALO : HALO + ROWS]
        image_ref[a] = images[a]
        head, tail = images[a][:HALO], images[a][ROWS - HALO :]
        partner_rows_ref[a] = jnp.where(odd, head, tail)
        other_rows_ref[a] = jnp.where(odd, tail, head)
    sums[...] = jnp.zeros_like(sums)
    at = 8 * VECTORS
    sums[at : at + 8] = fold([rhs_ref[a] * images[a] for a in range(2)])
    sums[at + 8 : at + 16] = fold([images[a] * images[a] for a in range(2)])

    def body(i, carry):
        restrict_piece(i, held, image_ref, sums)
        return carry

    lax.fori_loop(0, PIECES, body, 0)
    send_sums(sums, turned, next_ref)


def first_column(first, second):
    beta = jnp.sqrt(lane_total(first, VECTORS))
    h_00 = lane_total(second, VECTORS) / beta
    h_10 = jnp.sqrt(lane_total(second, VECTORS + 1) - h_00 * h_00)
    return beta, h_00, h_10


def second_turn_kernel(
    count, margin_ref, first_ref, second_ref, inverse_ref, partner_ref, other_ref,
    partner_rows_ref, other_rows_ref, held, smooth_ref, rhs_ref, image_ref, visc_ref, coup_ref,
    direction_ref, next_ref,
    image_smooth, extended, sums, turned,
):
    first, second = first_ref[...], second_ref[...]
    beta, h_00, h_10 = first_column(first, second)
    ratio = h_00 / beta
    over = 1.0 / h_10
    residual = (line_up(second) - ratio * line_up(first)) * over
    beside = prolonging(residual, inverse_ref, held, extended)
    low, high = neighbours_of(partner_ref, other_ref)
    low_rows, high_rows = neighbours_of(partner_rows_ref, other_rows_ref)
    edges = [(low_rows[a], high_rows[a]) for a in range(2)]
    solve(
        count, margin_ref, visc_ref, coup_ref, image_ref, low, high, edges, image_smooth, beside
    )
    add_smooth(
        residual,
        low,
        high,
        lambda a, rows: (image_smooth[a, rows] - ratio * smooth_ref[a, rows]) * over,
        extended,
    )
    images = apply_operator(
        [extended[a] for a in range(2)], visc_ref[...], [coup_ref[a] for a in range(2)]
    )
    sums[...] = jnp.zeros_like(sums)
    sums[0:8] = fold([rhs_ref[a] * images[a] for a in range(2)])
    sums[8:16] = fold([image_ref[a] * images[a] for a in range(2)])
    sums[16:24] = fold([images[a] * images[a] for a in range(2)])
    for a in range(2):
        direction_ref[a] = extended[a, HALO : HALO + ROWS]
    send_sums(sums, turned, next_ref)


def finish_kernel(
    first_ref, second_ref, third_ref, first_direction_ref, second_direction_ref,
    solution_ref, hessenberg_ref,
):
    third = third_ref[...]
    beta, h_00, h_10 = first_column(first_ref[...], second_ref[...])
    h_01 = lane_total(third, 0) / beta
    h_11 = (lane_total(third, 1) - h_00 * h_01) / h_10
    h_21 = jnp.sqrt(lane_total(third, 2) - h_01 * h_01 - h_11 * h_11)
    n_00 = h_00 * h_00 + h_10 * h_10
    n_10 = h_00 * h_01 + h_10 * h_11
    n_11 = h_01 * h_01 + h_11 * h_11 + h_21 * h_21
    l_00 = jnp.sqrt(n_00)
    l_10 = n_10 / l_00
    l_11 = jnp.sqrt(n_11 - l_10 * l_10)
    f_0 = beta * h_00 / l_00
    f_1 = (beta * h_01 - l_10 * f_0) / l_11
    c_1 = f_1 / l_11
    c_0 = (f_0 - l_10 * c_1) / l_00
    for a in range(2):
        solution_ref[a] = c_0 * first_direction_ref[a] + c_1 * second_direction_ref[a]
    shape = hessenberg_ref.shape
    row = lax.broadcasted_iota(jnp.int32, shape, 1)
    column = lax.broadcasted_iota(jnp.int32, shape, 0)
    entries = jnp.zeros(shape, jnp.float32)
    for i, j, value in ((0, 0, h_00), (0, 1, h_01), (1, 0, h_10), (1, 1, h_11), (2, 1, h_21)):
        entries = jnp.where((row == i) & (column == j), value, entries)
    hessenberg_ref[...] = entries


def call(kernel, name, in_specs, outs, flops, scratch=(), traffic=4_000_000):
    return pl.pallas_call(
        kernel,
        name=name,
        in_specs=in_specs,
        out_specs=[VMEM] * len(outs),
        out_shape=outs,
        scratch_shapes=scratch,
        compiler_params=pltpu.CompilerParams(vmem_limit_bytes=16 * 1024 * 1024),
        cost_estimate=pl.CostEstimate(flops=flops, bytes_accessed=traffic, transcendentals=0),
    )


def in_hbm(array):
    return pltpu.with_memory_space_constraint(array, pltpu.HBM)


def from_everyone(rows):
    order = [list(range(lax.axis_size("sub")))[::-1]]
    return lax.all_to_all(rows, "sub", 0, 0, tiled=True, axis_index_groups=order)


def swap(partner, other):
    count = lax.axis_size("sub")
    both = lambda lows: [pair for i in lows for pair in ((i, i + 1), (i + 1, i))]
    return (
        lax.ppermute(partner, "sub", both(range(0, count, 2))),
        lax.ppermute(other, "sub", both(range(1, count - 1, 2))),
    )


def on_device(rhs, viscosity, coupling, margin_rows, coarse_basis, coarse_inverse):
    count = lax.axis_size("sub")
    columns = coarse_inverse.shape[1]
    f32 = lambda *shape: jax.ShapeDtypeStruct(shape, jnp.float32)
    dma = lambda *shape: pltpu.SemaphoreType.DMA(shape)
    extended = pltpu.VMEM((2, EXT, CELLS), jnp.float32)
    sums = pltpu.VMEM((8 * SLOTS, LANES), jnp.float32)
    row, whole, edge = f32(count, LANES), f32(2, ROWS, CELLS), f32(2, HALO, CELLS)
    packed, smoothed = f32(EDGE_AT + coarse_rows(columns), CELLS), f32(2, EXT, CELLS)
    arguments = (rhs, viscosity, coupling, coarse_inverse, coarse_basis)
    packs = call(
        pack_kernel, "pack", [HBM] * 5, [packed, packed], 5_000_000,
        [pltpu.VMEM((4, VECTORS, CHUNK, CELLS), jnp.bfloat16), dma(4)]
        + [dma(2 * pack_count(columns))],
    )(*map(in_hbm, arguments))
    held, partner, other = lax.optimization_barrier((coarse_basis, *packs))
    partner, other = swap(partner, other)
    (first,) = call(
        restrict_kernel, "restrict", [VMEM] * 2, [row], 10_000_000, [sums, sums]
    )(rhs, held)
    first = from_everyone(first)
    direction, image, smooth, partner_rows, other_rows, second = call(
        functools.partial(first_turn_kernel, count), "first_turn", [SMEM] + [VMEM] * 8,
        [whole, whole, smoothed, edge, edge, row], 20_000_000, [extended, sums, sums],
    )(margin_rows, first, coarse_inverse, partner, other, held, rhs, viscosity, coupling)
    partner_rows, other_rows = swap(partner_rows, other_rows)
    second = from_everyone(second)
    second_direction, third = call(
        functools.partial(second_turn_kernel, count), "second_turn", [SMEM] + [VMEM] * 13,
        [whole, row], 20_000_000, [extended, extended, sums, sums],
    )(
        margin_rows, first, second, coarse_inverse, partner, other, partner_rows, other_rows,
        held, smooth, rhs, image, viscosity, coupling,
    )
    third = from_everyone(third)
    result, transposed = call(finish_kernel, "finish", [VMEM] * 5, [whole, f32(2, 3)], 1_000_000)(
        first, second, third, direction, second_direction
    )
    return result, transposed.T


def solution(mesh):
    in_specs = (
        P(None, ("groups", "sub"), None),
        P(("groups", "sub"), None),
        P(None, ("groups", "sub"), None),
        P("groups"),
        P(None, None, ("groups", "sub"), None),
        P(("groups", "sub"), None),
    )
    out_specs = (P(None, ("groups", "sub"), None), P("groups", None))
    return jax.shard_map(
        on_device, mesh=mesh, in_specs=in_specs, out_specs=out_specs, check_vma=False
    )
```

```python
import functools

import jax
import jax.numpy as jnp
from jax import lax
from jax.experimental import pallas as pl
from jax.experimental.pallas import tpu as pltpu
from jax.sharding import PartitionSpec as P

ROWS = 64
CELLS = 512
VECTORS = 48
HALO = 8
EXT = ROWS + 2 * HALO
STRIP = 32
STACKED = EXT + 2 * STRIP
BLOCK = STACKED // 8
CHUNK = 16
CHUNKS = 2 * ROWS // CHUNK
PIECE = 6
PIECES = VECTORS // PIECE
LANES = 128
SLOTS = 56
EDGE_AT = 5 * HALO
INVERSE_AT = 2 * VECTORS
SWEEPS = 4
RELAX = 0.7
ROW_FACTOR = (1.0, 4.0)
CELL_FACTOR = (4.0, 1.0)

VMEM = pl.BlockSpec(memory_space=pltpu.VMEM)
SMEM = pl.BlockSpec(memory_space=pltpu.SMEM)
HBM = pl.BlockSpec(memory_space=pltpu.HBM)


def coarse_rows(columns):
    return INVERSE_AT + VECTORS * (columns // 512) + (VECTORS // 2) * (columns % 512 // 256)


def cell_sum(field):
    axis = field.ndim - 1
    lane = lax.broadcasted_iota(jnp.int32, field.shape[:-1] + (LANES,), axis)
    left, right = pltpu.roll(field, 1, axis), pltpu.roll(field, CELLS - 1, axis)
    inner = left[..., LANES:-LANES] + right[..., LANES:-LANES]
    first = jnp.where(lane == 0, 0.0, left[..., :LANES]) + right[..., :LANES]
    last = left[..., -LANES:] + jnp.where(lane == LANES - 1, 0.0, right[..., -LANES:])
    return jnp.concatenate([first, inner, last], axis)


def row_sum(field):
    if field.ndim == 2:
        return pltpu.roll(field, 1, 0) + pltpu.roll(field, field.shape[0] - 1, 0)
    below = jnp.concatenate([pltpu.roll(field[-1], 1, 0)[None], field[:-1]], 0)
    above = jnp.concatenate([field[1:], pltpu.roll(field[0], 7, 0)[None]], 0)
    return below + above


def neighbours(field, component):
    rows, cells = row_sum(field), cell_sum(field)
    if component == 0:
        return rows + CELL_FACTOR[0] * cells
    return ROW_FACTOR[1] * rows + cells


def apply_operator(extended, viscosity, coupling):
    inner = slice(HALO, HALO + ROWS)
    images = []
    for a in range(2):
        around = neighbours(extended[a], a)[inner]
        diagonal = 10.0 * viscosity + jnp.abs(coupling[a]) + 0.05
        images.append(
            diagonal * extended[a][inner]
            - viscosity * around
            + coupling[a] * extended[1 - a][inner]
        )
    return images


def restrict_piece(i, held, field, sums):
    for n in range(PIECE):
        k = PIECE * i + n
        total = None
        for a in range(2):
            for r in range(0, ROWS, CHUNK):
                for c in range(0, CELLS, LANES):
                    rows, cells = slice(r, r + CHUNK), slice(c, c + LANES)
                    term = held[k, a, rows, cells].astype(jnp.float32) * field[a, rows, cells]
                    term = term[:8] + term[8:]
                    total = term if total is None else total + term
        sums[pl.ds(pl.multiple_of(8 * k, 8), 8), :] = total


def fold(field):
    total = None
    for part in field:
        for r in range(0, part.shape[0], 8):
            for c in range(0, part.shape[1], LANES):
                term = part[r : r + 8, c : c + LANES]
                total = term if total is None else total + term
    return total


def send_sums(sums, turned, out_ref):
    for k in range(SLOTS):
        turned[pl.ds(k, 8, stride=SLOTS), :] = sums[8 * k : 8 * k + 8, :]
    by_slot = turned[:SLOTS]
    for j in range(1, 8):
        by_slot = by_slot + turned[SLOTS * j : SLOTS * (j + 1)]
    row = lax.dot_general(
        jnp.ones((8, LANES), jnp.float32),
        by_slot,
        (((1,), (1,)), ((), ())),
        precision=lax.Precision.HIGHEST,
        preferred_element_type=jnp.float32,
    )
    wide = jnp.concatenate([row[:1], jnp.zeros((1, LANES - SLOTS), jnp.float32)], 1)
    out_ref[...] = jnp.broadcast_to(wide, out_ref.shape)


def pack_copies(out_ref, first_row, rhs_ref, visc_ref, coup_ref, inverse_ref, sems, at_sem):
    rows = pl.ds(pl.multiple_of(first_row, HALO), HALO)
    moves = [(visc_ref.at[rows, :], 0, HALO, None)]
    for a in range(2):
        moves.append((coup_ref.at[a, rows, :], HALO * (1 + a), HALO, None))
        moves.append((rhs_ref.at[a, rows, :], HALO * (3 + a), HALO, None))
    columns = inverse_ref.shape[1]
    at = EDGE_AT + INVERSE_AT
    for c in range(0, columns - 511, 512):
        moves.append((inverse_ref.at[:, pl.ds(c, 512)], at, VECTORS, None))
        at += VECTORS
    if columns % 512:
        half = VECTORS // 2
        last = pl.ds(columns - 256, 256)
        moves.append((inverse_ref.at[pl.ds(0, half), last], at, half, 0))
        moves.append((inverse_ref.at[pl.ds(half, half), last], at, half, 256))
    copies = []
    for n, (source, at, size, lane) in enumerate(moves):
        place = pl.ds(at, size)
        target = out_ref.at[place, :] if lane is None else out_ref.at[place, pl.ds(lane, 256)]
        copies.append(pltpu.make_async_copy(source, target, sems.at[at_sem + n]))
    return copies


def pack_count(columns):
    return 5 + columns // 512 + 2 * (columns % 512 // 256)


def pack_kernel(
    rhs_ref, visc_ref, coup_ref, inverse_ref, basis_ref,
    partner_ref, other_ref,
    groups, group_sems, pack_sems,
):
    odd = lax.axis_index("sub") % 2
    sides = ((partner_ref, 1 - odd), (other_ref, odd))
    group_copies, packs = [], []
    for n, (out_ref, up) in enumerate(sides):
        for a in range(2):
            rows = pl.ds(pl.multiple_of(up * (ROWS - CHUNK), CHUNK), CHUNK)
            group_copies.append(
                pltpu.make_async_copy(
                    basis_ref.at[:, a, rows, :], groups.at[2 * n + a], group_sems.at[2 * n + a]
                )
            )
        packs += pack_copies(
            out_ref, up * (ROWS - HALO), rhs_ref, visc_ref, coup_ref, inverse_ref, pack_sems,
            n * pack_count(inverse_ref.shape[1]),
        )
    for copy in group_copies + packs:
        copy.start()
    for n, (out_ref, up) in enumerate(sides):
        for a in range(2):
            group_copies[2 * n + a].wait()
            for k in range(VECTORS):
                rows = groups[2 * n + a, k].astype(jnp.float32)
                at = EDGE_AT + VECTORS * a + k
                out_ref[at : at + 1] = jnp.where(up == 1, rows[CHUNK - 1 :], rows[:1])
    for copy in packs:
        copy.wait()


def restrict_kernel(rhs_ref, held, sums_ref, sums, turned):
    sums[...] = jnp.zeros_like(sums)
    sums[8 * VECTORS : 8 * VECTORS + 8] = fold([rhs_ref[a] * rhs_ref[a] for a in range(2)])

    def body(i, carry):
        restrict_piece(i, held, rhs_ref, sums)
        return carry

    lax.fori_loop(0, PIECES, body, 0)
    send_sums(sums, turned, sums_ref)


class Neighbour:
    def __init__(self, first_ref, second_ref):
        self.odd = lax.axis_index("sub") % 2 == 1
        self.first, self.second = first_ref, second_ref

    def __getitem__(self, index):
        return jnp.where(self.odd, self.first[index], self.second[index])


def neighbours_of(partner_ref, other_ref):
    return Neighbour(partner_ref, other_ref), Neighbour(other_ref, partner_ref)


def block_rows(ref, index, field):
    columns = []
    for c in range(CELLS // LANES):
        part = field[:, LANES * c : LANES * (c + 1)]
        ref[index, c, :EXT] = part
        ref[index, c, EXT : EXT + STRIP] = part[:STRIP]
        ref[index, c, EXT + STRIP :] = part[EXT - STRIP :]
        tiles = [ref[index, c, pl.ds(t, 8, stride=BLOCK), :] for t in range(BLOCK)]
        columns.append(jnp.stack(tiles))
    return jnp.concatenate(columns, 2)


def solve(
    count, margin_ref, visc_ref, coup_ref, field_ref, low_ref, high_ref, edges, out_ref, stacked
):
    rank = lax.axis_index("sub")
    lower = jnp.where(rank > 0, margin_ref[jnp.maximum(rank - 1, 0)], 0)
    upper = jnp.where(rank < count - 1, margin_ref[rank], 0)
    lower_f, upper_f = lower.astype(jnp.float32), upper.astype(jnp.float32)
    low_scale = 2.0 * jnp.maximum(lower_f, 1.0)
    high_scale = 2.0 * jnp.maximum(upper_f, 1.0)

    shape = (BLOCK, 8, LANES)
    row = lax.broadcasted_iota(jnp.int32, shape, 0)
    row = row + BLOCK * lax.broadcasted_iota(jnp.int32, shape, 1)
    own, below = row < EXT, row < EXT + STRIP
    place = row - jnp.where(own, HALO, jnp.where(below, EXT + HALO, EXT + 2 * STRIP - ROWS - HALO))
    place_f = place.astype(jnp.float32)
    rising = lambda base, scale: (place_f - base + 0.5) / scale
    falling = lambda base, scale: (base - place_f - 0.5) / scale
    own_live = (place >= -lower) & (place < ROWS + upper)
    own_weight = jnp.where(place < lower, rising(-lower_f, low_scale), 1.0)
    own_weight = jnp.where(place >= ROWS - upper, falling(ROWS + upper_f, high_scale), own_weight)
    below_live = place < lower
    below_weight = jnp.where(place >= -lower, falling(lower_f, low_scale), 1.0)
    above_live = place >= ROWS - upper
    above_weight = jnp.where(place < ROWS + upper, rising(ROWS - upper_f, high_scale), 1.0)
    live = (own & own_live) | (~own & below & below_live) | (~below & above_live)
    weight = jnp.where(own, own_weight, jnp.where(below, below_weight, above_weight))
    wide = lambda x: jnp.concatenate([x] * (CELLS // LANES), 2)
    live, weight = wide(live.astype(jnp.float32)), wide(weight)

    def stack(own_rows, at):
        rows = slice(at, at + HALO)
        return jnp.concatenate([low_ref[rows], own_rows, high_ref[rows]], 0)

    viscosity = stack(visc_ref[...], 0)
    first, across, other = [], [], []
    for a in range(2):
        coupling = stack(coup_ref[a], HALO * (1 + a))
        field = jnp.concatenate([edges[a][0], field_ref[a], edges[a][1]], 0)
        scale = RELAX / (10.0 * viscosity + jnp.abs(coupling) + 0.05)
        first.append(live * block_rows(stacked, 3 * a, scale * field))
        across.append(live * block_rows(stacked, 3 * a + 1, scale * viscosity))
        other.append(live * block_rows(stacked, 3 * a + 2, scale * coupling))
    solved = list(first)
    for _ in range(SWEEPS - 1):
        solved = [
            (1.0 - RELAX) * solved[a]
            + first[a]
            + across[a] * neighbours(solved[a], a)
            - other[a] * solved[1 - a]
            for a in range(2)
        ]
    for a in range(2):
        shares = solved[a] * weight
        for c in range(CELLS // LANES):
            cells = slice(LANES * c, LANES * (c + 1))
            for t in range(BLOCK):
                stacked[3 * a, c, pl.ds(t, 8, stride=BLOCK), :] = shares[t, :, cells]
            out_ref[a, :, cells] = stacked[3 * a, c, :EXT]
            out_ref[a, :STRIP, cells] += stacked[3 * a, c, EXT : EXT + STRIP]
            out_ref[a, EXT - STRIP :, cells] += stacked[3 * a, c, EXT + STRIP :]


def line_up(residuals):
    devices = residuals.shape[0]
    lane = lax.broadcasted_iota(jnp.int32, (1, LANES), 1)
    tiles = [jnp.zeros((1, LANES), jnp.float32) for _ in range(devices * VECTORS // LANES)]
    for t in range(devices):
        tile, offset = divmod(VECTORS * t, LANES)
        row = jnp.where(lane < VECTORS, residuals[devices - 1 - t : devices - t], 0.0)
        if offset:
            row = pltpu.roll(row, offset, 1)
        if offset + VECTORS <= LANES:
            tiles[tile] = tiles[tile] + row
        else:
            tiles[tile] = tiles[tile] + jnp.where(lane >= offset, row, 0.0)
            tiles[tile + 1] = tiles[tile + 1] + jnp.where(lane < offset, row, 0.0)
    return jnp.concatenate(tiles, 1)


def rounded(column):
    return column.astype(jnp.bfloat16).astype(jnp.float32)


def lift(inverse_ref, residual):
    return rounded(jnp.sum(inverse_ref[...] * residual, 1, keepdims=True))


def lift_packed(ref, residual):
    columns = residual.shape[1]
    at, total = EDGE_AT + INVERSE_AT, None
    for c in range(0, columns - 511, 512):
        term = jnp.sum(ref[at : at + VECTORS] * residual[:, c : c + 512], 1, keepdims=True)
        total = term if total is None else total + term
        at += VECTORS
    if columns % 512:
        half = VECTORS // 2
        last = residual[:, columns - 256 :]
        rows = ref[at : at + half]
        term = jnp.concatenate(
            [
                jnp.sum(rows[:, :256] * last, 1, keepdims=True),
                jnp.sum(rows[:, 256:] * last, 1, keepdims=True),
            ],
            0,
        )
        total = term if total is None else total + term
    return rounded(total)


def edge_values(ref, lifted):
    starts = [EDGE_AT + VECTORS * a for a in range(2)]
    return [jnp.sum(ref[at : at + VECTORS] * lifted, 0, keepdims=True) for at in starts]


def spread(lifted):
    shape = (VECTORS, CHUNK * VECTORS)
    owner = lax.broadcasted_iota(jnp.int32, shape, 1) // CHUNK
    row = lax.broadcasted_iota(jnp.int32, shape, 0)
    line = jnp.sum(jnp.where(owner == row, lifted, 0.0), 0, keepdims=True)
    shape = (CHUNK, CHUNK * VECTORS)
    place = lax.broadcasted_iota(jnp.int32, shape, 1) % CHUNK
    row = lax.broadcasted_iota(jnp.int32, shape, 0)
    return jnp.where(place == row, line, 0.0).astype(jnp.bfloat16)


def prolong(residual, inverse_ref, held, extended):
    matrix = spread(lift(inverse_ref, residual))
    for a in range(2):
        for r in range(0, ROWS, CHUNK):
            rows = held[:, a, r : r + CHUNK, :].reshape(CHUNK * VECTORS, CELLS)
            extended[a, HALO + r : HALO + r + CHUNK] = jnp.dot(
                matrix, rows, preferred_element_type=jnp.float32
            )


def add_smooth(residual, low, high, smooth, extended):
    low_edge = edge_values(low, lift_packed(low, residual))
    high_edge = edge_values(high, lift_packed(high, residual))
    place = lax.broadcasted_iota(jnp.int32, (HALO, CELLS), 0)
    for a in range(2):
        rows = slice(HALO, HALO + ROWS)
        extended[a, rows] += smooth(a, rows)
        rows = slice(0, HALO)
        extended[a, rows] = smooth(a, rows) + jnp.where(place == HALO - 1, low_edge[a], 0.0)
        rows = slice(EXT - HALO, EXT)
        extended[a, rows] = smooth(a, rows) + jnp.where(place == 0, high_edge[a], 0.0)


def lane_total(received, lane):
    return jnp.sum(received[:, lane : lane + 1], 0, keepdims=True)


def first_turn_kernel(
    count, margin_ref, sums_ref, inverse_ref, partner_ref, other_ref, held, rhs_ref, visc_ref,
    coup_ref,
    direction_ref, image_ref, smooth_ref, partner_rows_ref, other_rows_ref, next_ref,
    extended, sums, turned, stacked,
):
    received = sums_ref[...]
    over_beta = 1.0 / jnp.sqrt(lane_total(received, VECTORS))
    residual = line_up(received) * over_beta
    prolong(residual, inverse_ref, held, extended)
    low, high = neighbours_of(partner_ref, other_ref)
    starts = [HALO * (3 + a) for a in range(2)]
    edges = [(low[at : at + HALO], high[at : at + HALO]) for at in starts]
    solve(count, margin_ref, visc_ref, coup_ref, rhs_ref, low, high, edges, smooth_ref, stacked)
    add_smooth(
        residual, low, high, lambda a, rows: smooth_ref[a, rows] * over_beta, extended
    )
    images = apply_operator(
        [extended[a] for a in range(2)], visc_ref[...], [coup_ref[a] for a in range(2)]
    )
    odd = lax.axis_index("sub") % 2 == 1
    for a in range(2):
        direction_ref[a] = extended[a, HALO : HALO + ROWS]
        image_ref[a] = images[a]
        head, tail = images[a][:HALO], images[a][ROWS - HALO :]
        partner_rows_ref[a] = jnp.where(odd, head, tail)
        other_rows_ref[a] = jnp.where(odd, tail, head)
    sums[...] = jnp.zeros_like(sums)
    at = 8 * VECTORS
    sums[at : at + 8] = fold([rhs_ref[a] * images[a] for a in range(2)])
    sums[at + 8 : at + 16] = fold([images[a] * images[a] for a in range(2)])

    def body(i, carry):
        restrict_piece(i, held, image_ref, sums)
        return carry

    lax.fori_loop(0, PIECES, body, 0)
    send_sums(sums, turned, next_ref)


def first_column(first, second):
    beta = jnp.sqrt(lane_total(first, VECTORS))
    h_00 = lane_total(second, VECTORS) / beta
    h_10 = jnp.sqrt(lane_total(second, VECTORS + 1) - h_00 * h_00)
    return beta, h_00, h_10


def second_turn_kernel(
    count, margin_ref, first_ref, second_ref, inverse_ref, partner_ref, other_ref,
    partner_rows_ref, other_rows_ref, held, smooth_ref, rhs_ref, image_ref, visc_ref, coup_ref,
    direction_ref, next_ref,
    image_smooth, extended, sums, turned, stacked,
):
    first, second = first_ref[...], second_ref[...]
    beta, h_00, h_10 = first_column(first, second)
    ratio = h_00 / beta
    over = 1.0 / h_10
    residual = (line_up(second) - ratio * line_up(first)) * over
    prolong(residual, inverse_ref, held, extended)
    low, high = neighbours_of(partner_ref, other_ref)
    low_rows, high_rows = neighbours_of(partner_rows_ref, other_rows_ref)
    edges = [(low_rows[a], high_rows[a]) for a in range(2)]
    solve(
        count, margin_ref, visc_ref, coup_ref, image_ref, low, high, edges, image_smooth, stacked
    )
    add_smooth(
        residual,
        low,
        high,
        lambda a, rows: (image_smooth[a, rows] - ratio * smooth_ref[a, rows]) * over,
        extended,
    )
    images = apply_operator(
        [extended[a] for a in range(2)], visc_ref[...], [coup_ref[a] for a in range(2)]
    )
    sums[...] = jnp.zeros_like(sums)
    sums[0:8] = fold([rhs_ref[a] * images[a] for a in range(2)])
    sums[8:16] = fold([image_ref[a] * images[a] for a in range(2)])
    sums[16:24] = fold([images[a] * images[a] for a in range(2)])
    for a in range(2):
        direction_ref[a] = extended[a, HALO : HALO + ROWS]
    send_sums(sums, turned, next_ref)


def finish_kernel(
    first_ref, second_ref, third_ref, first_direction_ref, second_direction_ref,
    solution_ref, hessenberg_ref,
):
    third = third_ref[...]
    beta, h_00, h_10 = first_column(first_ref[...], second_ref[...])
    squares = lane_total(third, 2)
    h_01 = lane_total(third, 0) / beta
    h_11 = (lane_total(third, 1) - h_00 * h_01) / h_10
    h_21 = jnp.sqrt(squares - h_01 * h_01 - h_11 * h_11)
    l_00 = jnp.sqrt(h_00 * h_00 + h_10 * h_10)
    l_10 = (h_00 * h_01 + h_10 * h_11) / l_00
    f_0 = beta * h_00 / l_00
    c_1 = (beta * h_01 - l_10 * f_0) / (squares - l_10 * l_10)
    c_0 = (f_0 - l_10 * c_1) / l_00
    for a in range(2):
        solution_ref[a] = c_0 * first_direction_ref[a] + c_1 * second_direction_ref[a]
    shape = hessenberg_ref.shape
    row = lax.broadcasted_iota(jnp.int32, shape, 1)
    column = lax.broadcasted_iota(jnp.int32, shape, 0)
    entries = jnp.zeros(shape, jnp.float32)
    for i, j, value in ((0, 0, h_00), (0, 1, h_01), (1, 0, h_10), (1, 1, h_11), (2, 1, h_21)):
        entries = jnp.where((row == i) & (column == j), value, entries)
    hessenberg_ref[...] = entries


def call(kernel, name, in_specs, outs, flops, scratch=(), traffic=4_000_000):
    return pl.pallas_call(
        kernel,
        name=name,
        in_specs=in_specs,
        out_specs=[VMEM] * len(outs),
        out_shape=outs,
        scratch_shapes=scratch,
        compiler_params=pltpu.CompilerParams(vmem_limit_bytes=16 * 1024 * 1024),
        cost_estimate=pl.CostEstimate(flops=flops, bytes_accessed=traffic, transcendentals=0),
    )


def in_hbm(array):
    return pltpu.with_memory_space_constraint(array, pltpu.HBM)


def from_everyone(rows):
    order = [list(range(lax.axis_size("sub")))[::-1]]
    return lax.all_to_all(rows, "sub", 0, 0, tiled=True, axis_index_groups=order)


def swap(partner, other):
    count = lax.axis_size("sub")
    both = lambda lows: [pair for i in lows for pair in ((i, i + 1), (i + 1, i))]
    other = lax.ppermute(other, "sub", both(range(1, count - 1, 2)))
    return lax.ppermute(partner, "sub", both(range(0, count, 2))), other


def on_device(rhs, viscosity, coupling, margin_rows, coarse_basis, coarse_inverse):
    count = lax.axis_size("sub")
    columns = coarse_inverse.shape[1]
    f32 = lambda *shape: jax.ShapeDtypeStruct(shape, jnp.float32)
    dma = lambda *shape: pltpu.SemaphoreType.DMA(shape)
    extended = pltpu.VMEM((2, EXT, CELLS), jnp.float32)
    stacked = pltpu.VMEM((6, CELLS // LANES, STACKED, LANES), jnp.float32)
    sums = pltpu.VMEM((8 * SLOTS, LANES), jnp.float32)
    row, whole, edge = f32(count, LANES), f32(2, ROWS, CELLS), f32(2, HALO, CELLS)
    packed, smoothed = f32(EDGE_AT + coarse_rows(columns), CELLS), f32(2, EXT, CELLS)
    arguments = (rhs, viscosity, coupling, coarse_inverse, coarse_basis)
    packs = call(
        pack_kernel, "pack", [HBM] * 5, [packed, packed], 5_000_000,
        [pltpu.VMEM((4, VECTORS, CHUNK, CELLS), jnp.bfloat16), dma(4)]
        + [dma(2 * pack_count(columns))],
    )(*map(in_hbm, arguments))
    held, partner, other = lax.optimization_barrier((coarse_basis, *packs))
    partner, other = swap(partner, other)
    (first,) = call(
        restrict_kernel, "restrict", [VMEM] * 2, [row], 10_000_000, [sums, sums]
    )(rhs, held)
    first = from_everyone(first)
    direction, image, smooth, partner_rows, other_rows, second = call(
        functools.partial(first_turn_kernel, count), "first_turn", [SMEM] + [VMEM] * 8,
        [whole, whole, smoothed, edge, edge, row], 20_000_000, [extended, sums, sums, stacked],
    )(margin_rows, first, coarse_inverse, partner, other, held, rhs, viscosity, coupling)
    partner_rows, other_rows = swap(partner_rows, other_rows)
    second = from_everyone(second)
    second_direction, third = call(
        functools.partial(second_turn_kernel, count), "second_turn", [SMEM] + [VMEM] * 13,
        [whole, row], 20_000_000, [extended, extended, sums, sums, stacked],
    )(
        margin_rows, first, second, coarse_inverse, partner, other, partner_rows, other_rows,
        held, smooth, rhs, image, viscosity, coupling,
    )
    third = from_everyone(third)
    result, transposed = call(finish_kernel, "finish", [VMEM] * 5, [whole, f32(2, 3)], 1_000_000)(
        first, second, third, direction, second_direction
    )
    return result, transposed.T


def solution(mesh):
    in_specs = (
        P(None, ("groups", "sub"), None),
        P(("groups", "sub"), None),
        P(None, ("groups", "sub"), None),
        P("groups"),
        P(None, None, ("groups", "sub"), None),
        P(("groups", "sub"), None),
    )
    out_specs = (P(None, ("groups", "sub"), None), P("groups", None))
    return jax.shard_map(
        on_device, mesh=mesh, in_specs=in_specs, out_specs=out_specs, check_vma=False
    )
```

```python
import functools

import jax
import jax.numpy as jnp
from jax import lax
from jax.experimental import pallas as pl
from jax.experimental.pallas import tpu as pltpu
from jax.sharding import PartitionSpec as P

ROWS = 64
CELLS = 512
VECTORS = 48
HALO = 8
EXT = ROWS + 2 * HALO
STRIP = 32
STACKED = EXT + 2 * STRIP
TILE = 8
CHUNK = 16
CHUNKS = 2 * ROWS // CHUNK
PIECE = 6
PIECES = VECTORS // PIECE
LANES = 128
SLOTS = 56
EDGE_AT = 5 * HALO
INVERSE_AT = 2 * VECTORS
SWEEPS = 4
RELAX = 0.7
ROW_FACTOR = (1.0, 4.0)
CELL_FACTOR = (4.0, 1.0)

VMEM = pl.BlockSpec(memory_space=pltpu.VMEM)
SMEM = pl.BlockSpec(memory_space=pltpu.SMEM)
HBM = pl.BlockSpec(memory_space=pltpu.HBM)


def coarse_rows(columns):
    return INVERSE_AT + VECTORS * (columns // 512) + (VECTORS // 2) * (columns % 512 // 256)


def cell_sum(field):
    lane = lax.broadcasted_iota(jnp.int32, (field.shape[0], LANES), 1)
    left, right = pltpu.roll(field, 1, 1), pltpu.roll(field, CELLS - 1, 1)
    inner = left[:, LANES:-LANES] + right[:, LANES:-LANES]
    first = jnp.where(lane == 0, 0.0, left[:, :LANES]) + right[:, :LANES]
    last = left[:, -LANES:] + jnp.where(lane == LANES - 1, 0.0, right[:, -LANES:])
    return jnp.concatenate([first, inner, last], 1)


class Rows:
    def __init__(self, read, first, last):
        self.read, self.first, self.last = read, first, last
        self.tiles, self.down, self.up = {}, {}, {}

    def at(self, t):
        if t not in self.tiles:
            self.tiles[t] = self.read(t)
        return self.tiles[t]

    def moved(self, held, t, by):
        if t not in held:
            held[t] = pltpu.roll(self.at(t), by, 0)
        return held[t]

    def around(self, t):
        row = lax.broadcasted_iota(jnp.int32, (TILE, CELLS), 0)
        below, above = self.moved(self.down, t, 1), self.moved(self.up, t, TILE - 1)
        if t > self.first:
            below = jnp.where(row == 0, self.moved(self.down, t - 1, 1), below)
        if t < self.last:
            above = jnp.where(row == TILE - 1, self.moved(self.up, t + 1, TILE - 1), above)
        return below + above


def neighbours(rows, t, component):
    around, cells = rows.around(t), cell_sum(rows.at(t))
    if component == 0:
        return around + CELL_FACTOR[0] * cells
    return ROW_FACTOR[1] * around + cells


def restrict_piece(i, held, field, sums):
    for n in range(PIECE):
        k = PIECE * i + n
        totals = []
        for c in range(0, CELLS, LANES):
            total = None
            for a in range(2):
                for r in range(0, ROWS, CHUNK):
                    rows, cells = slice(r, r + CHUNK), slice(c, c + LANES)
                    term = held[k, a, rows, cells].astype(jnp.float32) * field[a, rows, cells]
                    total = term if total is None else total + term
            totals.append(total[:8] + total[8:])
        total = (totals[0] + totals[1]) + (totals[2] + totals[3])
        sums[pl.ds(pl.multiple_of(8 * k, 8), 8), :] = total


def fold(row):
    total = row[:, :LANES]
    for c in range(LANES, CELLS, LANES):
        total = total + row[:, c : c + LANES]
    return total


def tile_rows(t):
    return slice(TILE * t, TILE * (t + 1))


def send_sums(sums, turned, out_ref):
    for k in range(SLOTS):
        turned[pl.ds(k, 8, stride=SLOTS), :] = sums[8 * k : 8 * k + 8, :]
    by_slot = turned[:SLOTS]
    for j in range(1, 8):
        by_slot = by_slot + turned[SLOTS * j : SLOTS * (j + 1)]
    row = lax.dot_general(
        jnp.ones((8, LANES), jnp.float32),
        by_slot,
        (((1,), (1,)), ((), ())),
        precision=lax.Precision.HIGHEST,
        preferred_element_type=jnp.float32,
    )
    wide = jnp.concatenate([row[:1], jnp.zeros((1, LANES - SLOTS), jnp.float32)], 1)
    out_ref[...] = jnp.broadcast_to(wide, out_ref.shape)


def pack_copies(out_ref, first_row, rhs_ref, visc_ref, coup_ref, inverse_ref, sems, at_sem):
    rows = pl.ds(pl.multiple_of(first_row, HALO), HALO)
    moves = [(visc_ref.at[rows, :], 0, HALO, None)]
    for a in range(2):
        moves.append((coup_ref.at[a, rows, :], HALO * (1 + a), HALO, None))
        moves.append((rhs_ref.at[a, rows, :], HALO * (3 + a), HALO, None))
    columns = inverse_ref.shape[1]
    at = EDGE_AT + INVERSE_AT
    for c in range(0, columns - 511, 512):
        moves.append((inverse_ref.at[:, pl.ds(c, 512)], at, VECTORS, None))
        at += VECTORS
    if columns % 512:
        half = VECTORS // 2
        last = pl.ds(columns - 256, 256)
        moves.append((inverse_ref.at[pl.ds(0, half), last], at, half, 0))
        moves.append((inverse_ref.at[pl.ds(half, half), last], at, half, 256))
    copies = []
    for n, (source, at, size, lane) in enumerate(moves):
        place = pl.ds(at, size)
        target = out_ref.at[place, :] if lane is None else out_ref.at[place, pl.ds(lane, 256)]
        copies.append(pltpu.make_async_copy(source, target, sems.at[at_sem + n]))
    return copies


def pack_count(columns):
    return 5 + columns // 512 + 2 * (columns % 512 // 256)


def pack_kernel(
    rhs_ref, visc_ref, coup_ref, inverse_ref, basis_ref,
    partner_ref, other_ref,
    groups, group_sems, pack_sems,
):
    odd = lax.axis_index("sub") % 2
    sides = ((partner_ref, 1 - odd), (other_ref, odd))
    group_copies, packs = [], []
    for n, (out_ref, up) in enumerate(sides):
        for a in range(2):
            rows = pl.ds(pl.multiple_of(up * (ROWS - CHUNK), CHUNK), CHUNK)
            group_copies.append(
                pltpu.make_async_copy(
                    basis_ref.at[:, a, rows, :], groups.at[2 * n + a], group_sems.at[2 * n + a]
                )
            )
        packs += pack_copies(
            out_ref, up * (ROWS - HALO), rhs_ref, visc_ref, coup_ref, inverse_ref, pack_sems,
            n * pack_count(inverse_ref.shape[1]),
        )
    for copy in group_copies + packs:
        copy.start()
    for n, (out_ref, up) in enumerate(sides):
        for a in range(2):
            group_copies[2 * n + a].wait()
            for k in range(VECTORS):
                rows = groups[2 * n + a, k].astype(jnp.float32)
                at = EDGE_AT + VECTORS * a + k
                out_ref[at : at + 1] = jnp.where(up == 1, rows[CHUNK - 1 :], rows[:1])
    for copy in packs:
        copy.wait()


def restrict_kernel(rhs_ref, held, sums_ref, sums, turned):
    sums[...] = jnp.zeros_like(sums)
    squares = jnp.zeros((TILE, CELLS), jnp.float32)
    for a in range(2):
        for t in range(ROWS // TILE):
            tile = rhs_ref[a, tile_rows(t)]
            squares = squares + tile * tile
    sums[8 * VECTORS : 8 * VECTORS + 8] = fold(squares)

    def body(i, carry):
        restrict_piece(i, held, rhs_ref, sums)
        return carry

    lax.fori_loop(0, PIECES, body, 0)
    send_sums(sums, turned, sums_ref)


class Neighbour:
    def __init__(self, first_ref, second_ref):
        self.odd = lax.axis_index("sub") % 2 == 1
        self.first, self.second = first_ref, second_ref

    def __getitem__(self, index):
        return jnp.where(self.odd, self.first[index], self.second[index])


def neighbours_of(partner_ref, other_ref):
    return Neighbour(partner_ref, other_ref), Neighbour(other_ref, partner_ref)


def solve(count, margin_ref, visc_ref, coup_ref, field, low, high, out_ref, stacked, solved):
    rank = lax.axis_index("sub")
    lower = jnp.where(rank > 0, margin_ref[jnp.maximum(rank - 1, 0)], 0)
    upper = jnp.where(rank < count - 1, margin_ref[rank], 0)
    lower_f, upper_f = lower.astype(jnp.float32), upper.astype(jnp.float32)
    low_scale = 1.0 / (2.0 * jnp.maximum(lower_f, 1.0))
    high_scale = 1.0 / (2.0 * jnp.maximum(upper_f, 1.0))
    wide = lambda x: jnp.concatenate([x] * (CELLS // LANES), 1)
    own_tiles = ROWS // TILE
    strip_tiles = STRIP // TILE
    last = own_tiles + 1
    segments = (
        (0, 0, last + 1),
        (last + 1, 0, strip_tiles),
        (last + 1 + strip_tiles, last + 1 - strip_tiles, strip_tiles),
    )

    def place_of(e):
        return lax.broadcasted_iota(jnp.int32, (TILE, LANES), 0) + (TILE * e - HALO)

    def live_of(segment, e):
        place = place_of(e)
        if segment == 0:
            live = (place >= -lower) & (place < ROWS + upper)
        elif segment == 1:
            live = place < lower
        else:
            live = place >= ROWS - upper
        return wide(live.astype(jnp.float32))

    def weight_of(segment, e):
        place = place_of(e)
        place_f = place.astype(jnp.float32)
        rising = lambda base, scale: (place_f - base + 0.5) * scale
        falling = lambda base, scale: (base - place_f - 0.5) * scale
        if segment == 0:
            weight = jnp.where(place < lower, rising(-lower_f, low_scale), 1.0)
            weight = jnp.where(
                place >= ROWS - upper, falling(ROWS + upper_f, high_scale), weight
            )
        elif segment == 1:
            weight = jnp.where(place >= -lower, falling(lower_f, low_scale), 1.0)
        else:
            weight = jnp.where(place < ROWS + upper, rising(ROWS - upper_f, high_scale), 1.0)
        return wide(weight)

    def extended(ref, at, e):
        if e == 0:
            return low[at : at + HALO]
        if e == last:
            return high[at : at + HALO]
        return ref[tile_rows(e - 1)]

    for e in range(last + 1):
        viscosity = extended(visc_ref, 0, e)
        for a in range(2):
            coupling = extended(coup_ref.at[a], HALO * (1 + a), e)
            scale = RELAX / (10.0 * viscosity + jnp.abs(coupling) + 0.05)
            parts = (scale * field(a, e - 1), scale * viscosity, scale * coupling)
            for n, (first, begin, size) in enumerate(segments):
                if not begin <= e < begin + size:
                    continue
                rows = tile_rows(first + e - begin)
                always = n == 0 and 0 < e < last
                for m, part in enumerate(parts):
                    stacked[3 * a + m, rows] = part if always else live_of(n, e) * part

    for sweep in range(1, SWEEPS):
        for n, (first, begin, size) in enumerate(segments):
            end = first + size - 1
            if sweep == 1:
                reads = [lambda t, a=a: stacked[3 * a, tile_rows(t)] for a in range(2)]
            else:
                bank = 2 * (sweep % 2)
                reads = [lambda t, a=a: solved[bank + a, tile_rows(t)] for a in range(2)]
            fields = [Rows(read, first, end) for read in reads]
            for t in range(first, end + 1):
                rows = tile_rows(t)
                for a in range(2):
                    value = (
                        ((1.0 - RELAX) * fields[a].at(t) + stacked[3 * a, rows])
                        + stacked[3 * a + 1, rows] * neighbours(fields[a], t, a)
                        - stacked[3 * a + 2, rows] * fields[1 - a].at(t)
                    )
                    e = t - first + begin
                    if sweep < SWEEPS - 1:
                        solved[2 * ((sweep + 1) % 2) + a, rows] = value
                    elif n == 0:
                        out_ref[a, tile_rows(e)] = weight_of(n, e) * value
                    else:
                        out_ref[a, tile_rows(e)] += weight_of(n, e) * value


def line_up(residuals):
    devices = residuals.shape[0]
    lane = lax.broadcasted_iota(jnp.int32, (1, LANES), 1)
    tiles = [jnp.zeros((1, LANES), jnp.float32) for _ in range(devices * VECTORS // LANES)]
    for t in range(devices):
        tile, offset = divmod(VECTORS * t, LANES)
        row = jnp.where(lane < VECTORS, residuals[devices - 1 - t : devices - t], 0.0)
        if offset:
            row = pltpu.roll(row, offset, 1)
        if offset + VECTORS <= LANES:
            tiles[tile] = tiles[tile] + row
        else:
            tiles[tile] = tiles[tile] + jnp.where(lane >= offset, row, 0.0)
            tiles[tile + 1] = tiles[tile + 1] + jnp.where(lane < offset, row, 0.0)
    return jnp.concatenate(tiles, 1)


def rounded(column):
    return column.astype(jnp.bfloat16).astype(jnp.float32)


def lift(inverse_ref, residual):
    return rounded(jnp.sum(inverse_ref[...] * residual, 1, keepdims=True))


def lift_packed(ref, residual):
    columns = residual.shape[1]
    at, total = EDGE_AT + INVERSE_AT, None
    for c in range(0, columns - 511, 512):
        term = jnp.sum(ref[at : at + VECTORS] * residual[:, c : c + 512], 1, keepdims=True)
        total = term if total is None else total + term
        at += VECTORS
    if columns % 512:
        half = VECTORS // 2
        last = residual[:, columns - 256 :]
        rows = ref[at : at + half]
        term = jnp.concatenate(
            [
                jnp.sum(rows[:, :256] * last, 1, keepdims=True),
                jnp.sum(rows[:, 256:] * last, 1, keepdims=True),
            ],
            0,
        )
        total = term if total is None else total + term
    return rounded(total)


def edge_values(ref, lifted):
    starts = [EDGE_AT + VECTORS * a for a in range(2)]
    return [jnp.sum(ref[at : at + VECTORS] * lifted, 0, keepdims=True) for at in starts]


def spread(lifted):
    shape = (VECTORS, CHUNK * VECTORS)
    owner = lax.broadcasted_iota(jnp.int32, shape, 1) // CHUNK
    row = lax.broadcasted_iota(jnp.int32, shape, 0)
    line = jnp.sum(jnp.where(owner == row, lifted, 0.0), 0, keepdims=True)
    shape = (CHUNK, CHUNK * VECTORS)
    place = lax.broadcasted_iota(jnp.int32, shape, 1) % CHUNK
    row = lax.broadcasted_iota(jnp.int32, shape, 0)
    return jnp.where(place == row, line, 0.0).astype(jnp.bfloat16)


def prolong(residual, inverse_ref, held, extended):
    matrix = spread(lift(inverse_ref, residual))
    for a in range(2):
        for r in range(0, ROWS, CHUNK):
            rows = held[:, a, r : r + CHUNK, :].reshape(CHUNK * VECTORS, CELLS)
            extended[a, HALO + r : HALO + r + CHUNK] = jnp.dot(
                matrix, rows, preferred_element_type=jnp.float32
            )


def apply_operator(residual, low, high, smooth, extended, visc_ref, coup_ref, direction_ref):
    edges = [edge_values(side, lift_packed(side, residual)) for side in (low, high)]
    place = lax.broadcasted_iota(jnp.int32, (TILE, CELLS), 0)
    tiles = ROWS // TILE

    def read(t, a):
        if t < 0:
            return smooth(a, 0) + jnp.where(place == TILE - 1, edges[0][a], 0.0)
        if t == tiles:
            return smooth(a, t + 1) + jnp.where(place == 0, edges[1][a], 0.0)
        tile = smooth(a, t + 1) + extended[a, tile_rows(t + 1)]
        direction_ref[a, tile_rows(t)] = tile
        return tile

    fields = [Rows(lambda t, a=a: read(t, a), -1, tiles) for a in range(2)]
    for t in range(tiles):
        rows = tile_rows(t)
        viscosity = visc_ref[rows]
        for a in range(2):
            coupling = coup_ref[a, rows]
            diagonal = 10.0 * viscosity + jnp.abs(coupling) + 0.05
            image = (
                diagonal * fields[a].at(t)
                - viscosity * neighbours(fields[a], t, a)
                + coupling * fields[1 - a].at(t)
            )
            yield t, a, image


def lane_total(received, lane):
    return jnp.sum(received[:, lane : lane + 1], 0, keepdims=True)


def first_turn_kernel(
    count, margin_ref, sums_ref, inverse_ref, partner_ref, other_ref, held, rhs_ref, visc_ref,
    coup_ref,
    direction_ref, image_ref, smooth_ref, partner_rows_ref, other_rows_ref, next_ref,
    extended, sums, turned, stacked, solved,
):
    received = sums_ref[...]
    over_beta = 1.0 / jnp.sqrt(lane_total(received, VECTORS))
    residual = line_up(received) * over_beta
    prolong(residual, inverse_ref, held, extended)
    low, high = neighbours_of(partner_ref, other_ref)

    def field(a, t):
        at = HALO * (3 + a)
        if t < 0:
            return low[at : at + HALO]
        return high[at : at + HALO] if t == ROWS // TILE else rhs_ref[a, tile_rows(t)]

    solve(
        count, margin_ref, visc_ref, coup_ref, field, low, high, smooth_ref, stacked, solved
    )
    smooth = lambda a, t: smooth_ref[a, tile_rows(t)] * over_beta
    images = apply_operator(
        residual, low, high, smooth, extended, visc_ref, coup_ref, direction_ref
    )
    odd = lax.axis_index("sub") % 2 == 1
    products, squares = [jnp.zeros((TILE, CELLS), jnp.float32)] * 2
    heads, tails = [None] * 2, [None] * 2
    for t, a, image in images:
        image_ref[a, tile_rows(t)] = image
        products = products + rhs_ref[a, tile_rows(t)] * image
        squares = squares + image * image
        if t == 0:
            heads[a] = image
        if t == ROWS // TILE - 1:
            tails[a] = image
    for a in range(2):
        partner_rows_ref[a] = jnp.where(odd, heads[a], tails[a])
        other_rows_ref[a] = jnp.where(odd, tails[a], heads[a])
    sums[...] = jnp.zeros_like(sums)
    at = 8 * VECTORS
    sums[at : at + 8] = fold(products)
    sums[at + 8 : at + 16] = fold(squares)

    def body(i, carry):
        restrict_piece(i, held, image_ref, sums)
        return carry

    lax.fori_loop(0, PIECES, body, 0)
    send_sums(sums, turned, next_ref)


def first_column(first, second):
    beta = jnp.sqrt(lane_total(first, VECTORS))
    h_00 = lane_total(second, VECTORS) / beta
    h_10 = jnp.sqrt(lane_total(second, VECTORS + 1) - h_00 * h_00)
    return beta, h_00, h_10


def second_turn_kernel(
    count, margin_ref, first_ref, second_ref, inverse_ref, partner_ref, other_ref,
    partner_rows_ref, other_rows_ref, held, smooth_ref, rhs_ref, image_ref, visc_ref, coup_ref,
    direction_ref, next_ref,
    image_smooth, extended, sums, turned, stacked, solved,
):
    first, second = first_ref[...], second_ref[...]
    beta, h_00, h_10 = first_column(first, second)
    ratio = h_00 / beta
    over = 1.0 / h_10
    residual = (line_up(second) - ratio * line_up(first)) * over
    prolong(residual, inverse_ref, held, extended)
    low, high = neighbours_of(partner_ref, other_ref)
    low_rows, high_rows = neighbours_of(partner_rows_ref, other_rows_ref)

    def field(a, t):
        if t < 0:
            return low_rows[a]
        return high_rows[a] if t == ROWS // TILE else image_ref[a, tile_rows(t)]

    solve(
        count, margin_ref, visc_ref, coup_ref, field, low, high, image_smooth, stacked, solved
    )

    def smooth(a, t):
        rows = tile_rows(t)
        return (image_smooth[a, rows] - ratio * smooth_ref[a, rows]) * over

    images = apply_operator(
        residual, low, high, smooth, extended, visc_ref, coup_ref, direction_ref
    )
    totals = [jnp.zeros((TILE, CELLS), jnp.float32)] * 3
    for t, a, image in images:
        others = (rhs_ref[a, tile_rows(t)], image_ref[a, tile_rows(t)], image)
        totals = [total + x * image for total, x in zip(totals, others)]
    sums[...] = jnp.zeros_like(sums)
    for n, total in enumerate(totals):
        sums[8 * n : 8 * n + 8] = fold(total)
    send_sums(sums, turned, next_ref)


def finish_kernel(
    first_ref, second_ref, third_ref, first_direction_ref, second_direction_ref,
    solution_ref, hessenberg_ref,
):
    third = third_ref[...]
    beta, h_00, h_10 = first_column(first_ref[...], second_ref[...])
    squares = lane_total(third, 2)
    h_01 = lane_total(third, 0) / beta
    h_11 = (lane_total(third, 1) - h_00 * h_01) / h_10
    h_21 = jnp.sqrt(squares - h_01 * h_01 - h_11 * h_11)
    l_00 = jnp.sqrt(h_00 * h_00 + h_10 * h_10)
    l_10 = (h_00 * h_01 + h_10 * h_11) / l_00
    f_0 = beta * h_00 / l_00
    c_1 = (beta * h_01 - l_10 * f_0) / (squares - l_10 * l_10)
    c_0 = (f_0 - l_10 * c_1) / l_00
    for a in range(2):
        solution_ref[a] = c_0 * first_direction_ref[a] + c_1 * second_direction_ref[a]
    shape = hessenberg_ref.shape
    row = lax.broadcasted_iota(jnp.int32, shape, 1)
    column = lax.broadcasted_iota(jnp.int32, shape, 0)
    entries = jnp.zeros(shape, jnp.float32)
    for i, j, value in ((0, 0, h_00), (0, 1, h_01), (1, 0, h_10), (1, 1, h_11), (2, 1, h_21)):
        entries = jnp.where((row == i) & (column == j), value, entries)
    hessenberg_ref[...] = entries


def call(kernel, name, in_specs, outs, flops, scratch=(), traffic=4_000_000):
    return pl.pallas_call(
        kernel,
        name=name,
        in_specs=in_specs,
        out_specs=[VMEM] * len(outs),
        out_shape=outs,
        scratch_shapes=scratch,
        compiler_params=pltpu.CompilerParams(vmem_limit_bytes=16 * 1024 * 1024),
        cost_estimate=pl.CostEstimate(flops=flops, bytes_accessed=traffic, transcendentals=0),
    )


def in_hbm(array):
    return pltpu.with_memory_space_constraint(array, pltpu.HBM)


def from_everyone(rows):
    order = [list(range(lax.axis_size("sub")))[::-1]]
    return lax.all_to_all(rows, "sub", 0, 0, tiled=True, axis_index_groups=order)


def swap(partner, other):
    count = lax.axis_size("sub")
    both = lambda lows: [pair for i in lows for pair in ((i, i + 1), (i + 1, i))]
    return (
        lax.ppermute(partner, "sub", both(range(0, count, 2))),
        lax.ppermute(other, "sub", both(range(1, count - 1, 2))),
    )


def on_device(rhs, viscosity, coupling, margin_rows, coarse_basis, coarse_inverse):
    count = lax.axis_size("sub")
    columns = coarse_inverse.shape[1]
    f32 = lambda *shape: jax.ShapeDtypeStruct(shape, jnp.float32)
    dma = lambda *shape: pltpu.SemaphoreType.DMA(shape)
    extended = pltpu.VMEM((2, EXT, CELLS), jnp.float32)
    stacked = pltpu.VMEM((6, STACKED, CELLS), jnp.float32)
    solved = pltpu.VMEM((4, STACKED, CELLS), jnp.float32)
    sums = pltpu.VMEM((8 * SLOTS, LANES), jnp.float32)
    row, whole, edge = f32(count, LANES), f32(2, ROWS, CELLS), f32(2, HALO, CELLS)
    packed, smoothed = f32(EDGE_AT + coarse_rows(columns), CELLS), f32(2, EXT, CELLS)
    arguments = (rhs, viscosity, coupling, coarse_inverse, coarse_basis)
    packs = call(
        pack_kernel, "pack", [HBM] * 5, [packed, packed], 5_000_000,
        [pltpu.VMEM((4, VECTORS, CHUNK, CELLS), jnp.bfloat16), dma(4)]
        + [dma(2 * pack_count(columns))],
    )(*map(in_hbm, arguments))
    held, partner, other = lax.optimization_barrier((coarse_basis, *packs))
    partner, other = swap(partner, other)
    (first,) = call(
        restrict_kernel, "restrict", [VMEM] * 2, [row], 10_000_000, [sums, sums]
    )(rhs, held)
    first = from_everyone(first)
    direction, image, smooth, partner_rows, other_rows, second = call(
        functools.partial(first_turn_kernel, count), "first_turn", [SMEM] + [VMEM] * 8,
        [whole, whole, smoothed, edge, edge, row], 20_000_000, [extended, sums, sums, stacked, solved],
    )(margin_rows, first, coarse_inverse, partner, other, held, rhs, viscosity, coupling)
    partner_rows, other_rows = swap(partner_rows, other_rows)
    second = from_everyone(second)
    second_direction, third = call(
        functools.partial(second_turn_kernel, count), "second_turn", [SMEM] + [VMEM] * 13,
        [whole, row], 20_000_000, [extended, extended, sums, sums, stacked, solved],
    )(
        margin_rows, first, second, coarse_inverse, partner, other, partner_rows, other_rows,
        held, smooth, rhs, image, viscosity, coupling,
    )
    third = from_everyone(third)
    result, transposed = call(finish_kernel, "finish", [VMEM] * 5, [whole, f32(2, 3)], 1_000_000)(
        first, second, third, direction, second_direction
    )
    return result, transposed.T


def solution(mesh):
    in_specs = (
        P(None, ("groups", "sub"), None),
        P(("groups", "sub"), None),
        P(None, ("groups", "sub"), None),
        P("groups"),
        P(None, None, ("groups", "sub"), None),
        P(("groups", "sub"), None),
    )
    out_specs = (P(None, ("groups", "sub"), None), P("groups", None))
    return jax.shard_map(
        on_device, mesh=mesh, in_specs=in_specs, out_specs=out_specs, check_vma=False
    )
```

```python
import functools

import jax
import jax.numpy as jnp
from jax import lax
from jax.experimental import pallas as pl
from jax.experimental.pallas import tpu as pltpu
from jax.sharding import PartitionSpec as P

ROWS = 64
CELLS = 512
VECTORS = 48
HALO = 8
EXT = ROWS + 2 * HALO
STRIP = 32
STACKED = EXT + 2 * STRIP
TILE = 8
CHUNK = 16
CHUNKS = 2 * ROWS // CHUNK
PIECE = 8
PIECES = VECTORS // PIECE
LANES = 128
SLOTS = 64
EDGE_AT = 5 * HALO
INVERSE_AT = 2 * VECTORS
SWEEPS = 4
RELAX = 0.7
ROW_FACTOR = (1.0, 4.0)
CELL_FACTOR = (4.0, 1.0)

VMEM = pl.BlockSpec(memory_space=pltpu.VMEM)
SMEM = pl.BlockSpec(memory_space=pltpu.SMEM)
HBM = pl.BlockSpec(memory_space=pltpu.HBM)


def coarse_rows(columns):
    return INVERSE_AT + VECTORS * (columns // 512) + (VECTORS // 2) * (columns % 512 // 256)


def cell_sum(field):
    lane = lax.broadcasted_iota(jnp.int32, (field.shape[0], LANES), 1)
    left, right = pltpu.roll(field, 1, 1), pltpu.roll(field, CELLS - 1, 1)
    inner = left[:, LANES:-LANES] + right[:, LANES:-LANES]
    first = jnp.where(lane == 0, 0.0, left[:, :LANES]) + right[:, :LANES]
    last = left[:, -LANES:] + jnp.where(lane == LANES - 1, 0.0, right[:, -LANES:])
    return jnp.concatenate([first, inner, last], 1)


class Rows:
    def __init__(self, read, first, last):
        self.read, self.first, self.last = read, first, last
        self.tiles, self.down, self.up = {}, {}, {}

    def at(self, t):
        if t not in self.tiles:
            self.tiles[t] = self.read(t)
        return self.tiles[t]

    def moved(self, held, t, by):
        if t not in held:
            held[t] = pltpu.roll(self.at(t), by, 0)
        return held[t]

    def around(self, t):
        row = lax.broadcasted_iota(jnp.int32, (TILE, CELLS), 0)
        below, above = self.moved(self.down, t, 1), self.moved(self.up, t, TILE - 1)
        if t > self.first:
            below = jnp.where(row == 0, self.moved(self.down, t - 1, 1), below)
        if t < self.last:
            above = jnp.where(row == TILE - 1, self.moved(self.up, t + 1, TILE - 1), above)
        return below + above


def neighbours(rows, t, component):
    around, cells = rows.around(t), cell_sum(rows.at(t))
    if component == 0:
        return around + CELL_FACTOR[0] * cells
    return ROW_FACTOR[1] * around + cells


def sublane_sum(tile):
    for by in (4, 2, 1):
        tile = tile + pltpu.roll(tile, by, 0)
    return tile


def in_rows(tiles):
    row = lax.broadcasted_iota(jnp.int32, (8, LANES), 0)
    total = jnp.zeros((8, LANES), jnp.float32)
    for n, tile in enumerate(tiles):
        total = jnp.where(row == n, sublane_sum(tile), total)
    return total


def restrict_piece(i, held, field, sums):
    totals = [None] * PIECE
    for a in range(2):
        for r in range(0, ROWS, CHUNK):
            for c in range(0, CELLS, LANES):
                rows, cells = slice(r, r + CHUNK), slice(c, c + LANES)
                tile = field[a, rows, cells]
                for n in range(PIECE):
                    term = held[PIECE * i + n, a, rows, cells].astype(jnp.float32) * tile
                    totals[n] = term if totals[n] is None else totals[n] + term
    tiles = [total[:8] + total[8:] for total in totals]
    sums[pl.ds(pl.multiple_of(PIECE * i, PIECE), PIECE), :] = in_rows(tiles)


def fold(row):
    total = row[:, :LANES]
    for c in range(LANES, CELLS, LANES):
        total = total + row[:, c : c + LANES]
    return total


def tile_rows(t):
    return slice(TILE * t, TILE * (t + 1))


def send_sums(sums, out_ref):
    rest = sums[...]
    parts = []
    for _ in range(3):
        part = rest.astype(jnp.bfloat16)
        parts.append(part)
        rest = rest - part.astype(jnp.float32)
    row = lax.dot_general(
        jnp.ones((CHUNK, 3 * LANES), jnp.bfloat16),
        jnp.concatenate(parts, 1),
        (((1,), (1,)), ((), ())),
        preferred_element_type=jnp.float32,
    )
    wide = jnp.concatenate([row[:1], jnp.zeros((1, LANES - SLOTS), jnp.float32)], 1)
    out_ref[...] = jnp.broadcast_to(wide, out_ref.shape)


def pack_copies(out_ref, first_row, rhs_ref, visc_ref, coup_ref, inverse_ref, sems, at_sem):
    rows = pl.ds(pl.multiple_of(first_row, HALO), HALO)
    moves = [(visc_ref.at[rows, :], 0, HALO, None)]
    for a in range(2):
        moves.append((coup_ref.at[a, rows, :], HALO * (1 + a), HALO, None))
        moves.append((rhs_ref.at[a, rows, :], HALO * (3 + a), HALO, None))
    columns = inverse_ref.shape[1]
    at = EDGE_AT + INVERSE_AT
    for c in range(0, columns - 511, 512):
        moves.append((inverse_ref.at[:, pl.ds(c, 512)], at, VECTORS, None))
        at += VECTORS
    if columns % 512:
        half = VECTORS // 2
        last = pl.ds(columns - 256, 256)
        moves.append((inverse_ref.at[pl.ds(0, half), last], at, half, 0))
        moves.append((inverse_ref.at[pl.ds(half, half), last], at, half, 256))
    copies = []
    for n, (source, at, size, lane) in enumerate(moves):
        place = pl.ds(at, size)
        target = out_ref.at[place, :] if lane is None else out_ref.at[place, pl.ds(lane, 256)]
        copies.append(pltpu.make_async_copy(source, target, sems.at[at_sem + n]))
    return copies


def pack_count(columns):
    return 5 + columns // 512 + 2 * (columns % 512 // 256)


def pack_kernel(
    rhs_ref, visc_ref, coup_ref, inverse_ref, basis_ref,
    partner_ref, other_ref,
    groups, group_sems, pack_sems,
):
    odd = lax.axis_index("sub") % 2
    sides = ((partner_ref, 1 - odd), (other_ref, odd))
    group_copies, packs = [], []
    for n, (out_ref, up) in enumerate(sides):
        for a in range(2):
            rows = pl.ds(pl.multiple_of(up * (ROWS - CHUNK), CHUNK), CHUNK)
            group_copies.append(
                pltpu.make_async_copy(
                    basis_ref.at[:, a, rows, :], groups.at[2 * n + a], group_sems.at[2 * n + a]
                )
            )
        packs += pack_copies(
            out_ref, up * (ROWS - HALO), rhs_ref, visc_ref, coup_ref, inverse_ref, pack_sems,
            n * pack_count(inverse_ref.shape[1]),
        )
    for copy in group_copies + packs:
        copy.start()
    for n, (out_ref, up) in enumerate(sides):
        for a in range(2):
            group_copies[2 * n + a].wait()
            for k in range(VECTORS):
                rows = groups[2 * n + a, k].astype(jnp.float32)
                at = EDGE_AT + VECTORS * a + k
                out_ref[at : at + 1] = jnp.where(up == 1, rows[CHUNK - 1 :], rows[:1])
    for copy in packs:
        copy.wait()


def restrict_kernel(rhs_ref, held, sums_ref, sums):
    sums[...] = jnp.zeros_like(sums)
    squares = jnp.zeros((TILE, CELLS), jnp.float32)
    for a in range(2):
        for t in range(ROWS // TILE):
            tile = rhs_ref[a, tile_rows(t)]
            squares = squares + tile * tile
    sums[VECTORS : VECTORS + 8] = in_rows([fold(squares)])

    def body(i, carry):
        restrict_piece(i, held, rhs_ref, sums)
        return carry

    lax.fori_loop(0, PIECES, body, 0)
    send_sums(sums, sums_ref)


class Neighbour:
    def __init__(self, first_ref, second_ref):
        self.odd = lax.axis_index("sub") % 2 == 1
        self.first, self.second = first_ref, second_ref

    def __getitem__(self, index):
        return jnp.where(self.odd, self.first[index], self.second[index])


def neighbours_of(partner_ref, other_ref):
    return Neighbour(partner_ref, other_ref), Neighbour(other_ref, partner_ref)


def solve(count, margin_ref, visc_ref, coup_ref, field, low, high, out_ref, stacked, solved, steps):
    waiting, done = list(steps), 0
    every = (SWEEPS - 1) * (STACKED // TILE) // len(waiting)
    rank = lax.axis_index("sub")
    lower = jnp.where(rank > 0, margin_ref[jnp.maximum(rank - 1, 0)], 0)
    upper = jnp.where(rank < count - 1, margin_ref[rank], 0)
    lower_f, upper_f = lower.astype(jnp.float32), upper.astype(jnp.float32)
    low_scale = 1.0 / (2.0 * jnp.maximum(lower_f, 1.0))
    high_scale = 1.0 / (2.0 * jnp.maximum(upper_f, 1.0))
    wide = lambda x: jnp.concatenate([x] * (CELLS // LANES), 1)
    own_tiles = ROWS // TILE
    strip_tiles = STRIP // TILE
    last = own_tiles + 1
    segments = (
        (0, 0, last + 1),
        (last + 1, 0, strip_tiles),
        (last + 1 + strip_tiles, last + 1 - strip_tiles, strip_tiles),
    )

    def place_of(e):
        return lax.broadcasted_iota(jnp.int32, (TILE, LANES), 0) + (TILE * e - HALO)

    def live_of(segment, e):
        place = place_of(e)
        if segment == 0:
            live = (place >= -lower) & (place < ROWS + upper)
        elif segment == 1:
            live = place < lower
        else:
            live = place >= ROWS - upper
        return wide(live.astype(jnp.float32))

    def weight_of(segment, e):
        place = place_of(e)
        place_f = place.astype(jnp.float32)
        rising = lambda base, scale: (place_f - base + 0.5) * scale
        falling = lambda base, scale: (base - place_f - 0.5) * scale
        if segment == 0:
            weight = jnp.where(place < lower, rising(-lower_f, low_scale), 1.0)
            weight = jnp.where(
                place >= ROWS - upper, falling(ROWS + upper_f, high_scale), weight
            )
        elif segment == 1:
            weight = jnp.where(place >= -lower, falling(lower_f, low_scale), 1.0)
        else:
            weight = jnp.where(place < ROWS + upper, rising(ROWS - upper_f, high_scale), 1.0)
        return wide(weight)

    def extended(ref, at, e):
        if e == 0:
            return low[at : at + HALO]
        if e == last:
            return high[at : at + HALO]
        return ref[tile_rows(e - 1)]

    for e in range(last + 1):
        viscosity = extended(visc_ref, 0, e)
        for a in range(2):
            coupling = extended(coup_ref.at[a], HALO * (1 + a), e)
            scale = RELAX / (10.0 * viscosity + jnp.abs(coupling) + 0.05)
            parts = (scale * field(a, e - 1), scale * viscosity, scale * coupling)
            for n, (first, begin, size) in enumerate(segments):
                if not begin <= e < begin + size:
                    continue
                rows = tile_rows(first + e - begin)
                always = n == 0 and 0 < e < last
                for m, part in enumerate(parts):
                    stacked[3 * a + m, rows] = part if always else live_of(n, e) * part

    for sweep in range(1, SWEEPS):
        for n, (first, begin, size) in enumerate(segments):
            end = first + size - 1
            if sweep == 1:
                reads = [lambda t, a=a: stacked[3 * a, tile_rows(t)] for a in range(2)]
            else:
                bank = 2 * (sweep % 2)
                reads = [lambda t, a=a: solved[bank + a, tile_rows(t)] for a in range(2)]
            fields = [Rows(read, first, end) for read in reads]
            for t in range(first, end + 1):
                rows = tile_rows(t)
                if done % every == 0 and waiting:
                    waiting.pop(0)()
                done += 1
                for a in range(2):
                    value = (
                        ((1.0 - RELAX) * fields[a].at(t) + stacked[3 * a, rows])
                        + stacked[3 * a + 1, rows] * neighbours(fields[a], t, a)
                        - stacked[3 * a + 2, rows] * fields[1 - a].at(t)
                    )
                    e = t - first + begin
                    if sweep < SWEEPS - 1:
                        solved[2 * ((sweep + 1) % 2) + a, rows] = value
                    elif n == 0:
                        out_ref[a, tile_rows(e)] = weight_of(n, e) * value
                    else:
                        out_ref[a, tile_rows(e)] += weight_of(n, e) * value


def line_up(residuals):
    devices = residuals.shape[0]
    lane = lax.broadcasted_iota(jnp.int32, (1, LANES), 1)
    tiles = [jnp.zeros((1, LANES), jnp.float32) for _ in range(devices * VECTORS // LANES)]
    for t in range(devices):
        tile, offset = divmod(VECTORS * t, LANES)
        row = jnp.where(lane < VECTORS, residuals[devices - 1 - t : devices - t], 0.0)
        if offset:
            row = pltpu.roll(row, offset, 1)
        if offset + VECTORS <= LANES:
            tiles[tile] = tiles[tile] + row
        else:
            tiles[tile] = tiles[tile] + jnp.where(lane >= offset, row, 0.0)
            tiles[tile + 1] = tiles[tile + 1] + jnp.where(lane < offset, row, 0.0)
    return jnp.concatenate(tiles, 1)


def rounded(column):
    return column.astype(jnp.bfloat16).astype(jnp.float32)


def lift(inverse_ref, residual):
    return rounded(jnp.sum(inverse_ref[...] * residual, 1, keepdims=True))


def lift_packed(ref, residual):
    columns = residual.shape[1]
    at, total = EDGE_AT + INVERSE_AT, None
    for c in range(0, columns - 511, 512):
        term = jnp.sum(ref[at : at + VECTORS] * residual[:, c : c + 512], 1, keepdims=True)
        total = term if total is None else total + term
        at += VECTORS
    if columns % 512:
        half = VECTORS // 2
        last = residual[:, columns - 256 :]
        rows = ref[at : at + half]
        term = jnp.concatenate(
            [
                jnp.sum(rows[:, :256] * last, 1, keepdims=True),
                jnp.sum(rows[:, 256:] * last, 1, keepdims=True),
            ],
            0,
        )
        total = term if total is None else total + term
    return rounded(total)


def edge_values(ref, lifted):
    starts = [EDGE_AT + VECTORS * a for a in range(2)]
    return [jnp.sum(ref[at : at + VECTORS] * lifted, 0, keepdims=True) for at in starts]


def spread(lifted):
    shape = (VECTORS, CHUNK * VECTORS)
    owner = lax.broadcasted_iota(jnp.int32, shape, 1) // CHUNK
    row = lax.broadcasted_iota(jnp.int32, shape, 0)
    line = jnp.sum(jnp.where(owner == row, lifted, 0.0), 0, keepdims=True)
    shape = (CHUNK, CHUNK * VECTORS)
    place = lax.broadcasted_iota(jnp.int32, shape, 1) % CHUNK
    row = lax.broadcasted_iota(jnp.int32, shape, 0)
    return jnp.where(place == row, line, 0.0).astype(jnp.bfloat16)


def prolonging(residual, inverse_ref, held, extended):
    matrix = spread(lift(inverse_ref, residual))

    def step(a, r):
        rows = held[:, a, r : r + CHUNK, :].reshape(CHUNK * VECTORS, CELLS)
        extended[a, HALO + r : HALO + r + CHUNK] = jnp.dot(
            matrix, rows, preferred_element_type=jnp.float32
        )

    return [functools.partial(step, a, r) for a in range(2) for r in range(0, ROWS, CHUNK)]


def apply_operator(residual, low, high, smooth, extended, visc_ref, coup_ref, direction_ref):
    edges = [edge_values(side, lift_packed(side, residual)) for side in (low, high)]
    place = lax.broadcasted_iota(jnp.int32, (TILE, CELLS), 0)
    tiles = ROWS // TILE

    def read(t, a):
        if t < 0:
            return smooth(a, 0) + jnp.where(place == TILE - 1, edges[0][a], 0.0)
        if t == tiles:
            return smooth(a, t + 1) + jnp.where(place == 0, edges[1][a], 0.0)
        tile = smooth(a, t + 1) + extended[a, tile_rows(t + 1)]
        direction_ref[a, tile_rows(t)] = tile
        return tile

    fields = [Rows(lambda t, a=a: read(t, a), -1, tiles) for a in range(2)]
    for t in range(tiles):
        rows = tile_rows(t)
        viscosity = visc_ref[rows]
        for a in range(2):
            coupling = coup_ref[a, rows]
            diagonal = 10.0 * viscosity + jnp.abs(coupling) + 0.05
            image = (
                diagonal * fields[a].at(t)
                - viscosity * neighbours(fields[a], t, a)
                + coupling * fields[1 - a].at(t)
            )
            yield t, a, image


def lane_total(received, lane):
    return jnp.sum(received[:, lane : lane + 1], 0, keepdims=True)


def first_turn_kernel(
    count, margin_ref, sums_ref, inverse_ref, partner_ref, other_ref, held, rhs_ref, visc_ref,
    coup_ref,
    direction_ref, image_ref, smooth_ref, partner_rows_ref, other_rows_ref, next_ref,
    extended, sums, stacked, solved,
):
    received = sums_ref[...]
    over_beta = 1.0 / jnp.sqrt(lane_total(received, VECTORS))
    residual = line_up(received) * over_beta
    steps = prolonging(residual, inverse_ref, held, extended)
    low, high = neighbours_of(partner_ref, other_ref)

    def field(a, t):
        at = HALO * (3 + a)
        if t < 0:
            return low[at : at + HALO]
        return high[at : at + HALO] if t == ROWS // TILE else rhs_ref[a, tile_rows(t)]

    solve(
        count, margin_ref, visc_ref, coup_ref, field, low, high, smooth_ref, stacked, solved,
        steps,
    )
    smooth = lambda a, t: smooth_ref[a, tile_rows(t)] * over_beta
    images = apply_operator(
        residual, low, high, smooth, extended, visc_ref, coup_ref, direction_ref
    )
    odd = lax.axis_index("sub") % 2 == 1
    products, squares = [jnp.zeros((TILE, CELLS), jnp.float32)] * 2
    heads, tails = [None] * 2, [None] * 2
    for t, a, image in images:
        image_ref[a, tile_rows(t)] = image
        products = products + rhs_ref[a, tile_rows(t)] * image
        squares = squares + image * image
        if t == 0:
            heads[a] = image
        if t == ROWS // TILE - 1:
            tails[a] = image
    for a in range(2):
        partner_rows_ref[a] = jnp.where(odd, heads[a], tails[a])
        other_rows_ref[a] = jnp.where(odd, tails[a], heads[a])
    sums[...] = jnp.zeros_like(sums)
    sums[VECTORS : VECTORS + 8] = in_rows([fold(products), fold(squares)])

    def body(i, carry):
        restrict_piece(i, held, image_ref, sums)
        return carry

    lax.fori_loop(0, PIECES, body, 0)
    send_sums(sums, next_ref)


def first_column(first, second):
    beta = jnp.sqrt(lane_total(first, VECTORS))
    h_00 = lane_total(second, VECTORS) / beta
    h_10 = jnp.sqrt(lane_total(second, VECTORS + 1) - h_00 * h_00)
    return beta, h_00, h_10


def second_turn_kernel(
    count, margin_ref, first_ref, second_ref, inverse_ref, partner_ref, other_ref,
    partner_rows_ref, other_rows_ref, held, smooth_ref, rhs_ref, image_ref, visc_ref, coup_ref,
    direction_ref, next_ref,
    image_smooth, extended, sums, stacked, solved,
):
    first, second = first_ref[...], second_ref[...]
    beta, h_00, h_10 = first_column(first, second)
    ratio = h_00 / beta
    over = 1.0 / h_10
    residual = (line_up(second) - ratio * line_up(first)) * over
    steps = prolonging(residual, inverse_ref, held, extended)
    low, high = neighbours_of(partner_ref, other_ref)
    low_rows, high_rows = neighbours_of(partner_rows_ref, other_rows_ref)

    def field(a, t):
        if t < 0:
            return low_rows[a]
        return high_rows[a] if t == ROWS // TILE else image_ref[a, tile_rows(t)]

    solve(
        count, margin_ref, visc_ref, coup_ref, field, low, high, image_smooth, stacked, solved,
        steps,
    )

    def smooth(a, t):
        rows = tile_rows(t)
        return (image_smooth[a, rows] - ratio * smooth_ref[a, rows]) * over

    images = apply_operator(
        residual, low, high, smooth, extended, visc_ref, coup_ref, direction_ref
    )
    totals = [jnp.zeros((TILE, CELLS), jnp.float32)] * 3
    for t, a, image in images:
        others = (rhs_ref[a, tile_rows(t)], image_ref[a, tile_rows(t)], image)
        totals = [total + x * image for total, x in zip(totals, others)]
    sums[...] = jnp.zeros_like(sums)
    sums[:8] = in_rows([fold(total) for total in totals])
    send_sums(sums, next_ref)


def finish_kernel(
    first_ref, second_ref, third_ref, first_direction_ref, second_direction_ref,
    solution_ref, hessenberg_ref,
):
    third = third_ref[...]
    beta, h_00, h_10 = first_column(first_ref[...], second_ref[...])
    squares = lane_total(third, 2)
    h_01 = lane_total(third, 0) / beta
    h_11 = (lane_total(third, 1) - h_00 * h_01) / h_10
    h_21 = jnp.sqrt(squares - h_01 * h_01 - h_11 * h_11)
    l_00 = jnp.sqrt(h_00 * h_00 + h_10 * h_10)
    l_10 = (h_00 * h_01 + h_10 * h_11) / l_00
    f_0 = beta * h_00 / l_00
    c_1 = (beta * h_01 - l_10 * f_0) / (squares - l_10 * l_10)
    c_0 = (f_0 - l_10 * c_1) / l_00
    for a in range(2):
        solution_ref[a] = c_0 * first_direction_ref[a] + c_1 * second_direction_ref[a]
    shape = hessenberg_ref.shape
    row = lax.broadcasted_iota(jnp.int32, shape, 1)
    column = lax.broadcasted_iota(jnp.int32, shape, 0)
    entries = jnp.zeros(shape, jnp.float32)
    for i, j, value in ((0, 0, h_00), (0, 1, h_01), (1, 0, h_10), (1, 1, h_11), (2, 1, h_21)):
        entries = jnp.where((row == i) & (column == j), value, entries)
    hessenberg_ref[...] = entries


def call(kernel, name, in_specs, outs, flops, scratch=(), traffic=4_000_000):
    return pl.pallas_call(
        kernel,
        name=name,
        in_specs=in_specs,
        out_specs=[VMEM] * len(outs),
        out_shape=outs,
        scratch_shapes=scratch,
        compiler_params=pltpu.CompilerParams(vmem_limit_bytes=16 * 1024 * 1024),
        cost_estimate=pl.CostEstimate(flops=flops, bytes_accessed=traffic, transcendentals=0),
    )


def in_hbm(array):
    return pltpu.with_memory_space_constraint(array, pltpu.HBM)


def from_everyone(rows):
    order = [list(range(lax.axis_size("sub")))[::-1]]
    return lax.all_to_all(rows, "sub", 0, 0, tiled=True, axis_index_groups=order)


def swap(partner, other):
    count = lax.axis_size("sub")
    both = lambda lows: [pair for i in lows for pair in ((i, i + 1), (i + 1, i))]
    return (
        lax.ppermute(partner, "sub", both(range(0, count, 2))),
        lax.ppermute(other, "sub", both(range(1, count - 1, 2))),
    )


def on_device(rhs, viscosity, coupling, margin_rows, coarse_basis, coarse_inverse):
    count = lax.axis_size("sub")
    columns = coarse_inverse.shape[1]
    f32 = lambda *shape: jax.ShapeDtypeStruct(shape, jnp.float32)
    dma = lambda *shape: pltpu.SemaphoreType.DMA(shape)
    extended = pltpu.VMEM((2, EXT, CELLS), jnp.float32)
    stacked = pltpu.VMEM((6, STACKED, CELLS), jnp.float32)
    solved = pltpu.VMEM((4, STACKED, CELLS), jnp.float32)
    sums = pltpu.VMEM((SLOTS, LANES), jnp.float32)
    row, whole, edge = f32(count, LANES), f32(2, ROWS, CELLS), f32(2, HALO, CELLS)
    packed, smoothed = f32(EDGE_AT + coarse_rows(columns), CELLS), f32(2, EXT, CELLS)
    arguments = (rhs, viscosity, coupling, coarse_inverse, coarse_basis)
    packs = call(
        pack_kernel, "pack", [HBM] * 5, [packed, packed], 5_000_000,
        [pltpu.VMEM((4, VECTORS, CHUNK, CELLS), jnp.bfloat16), dma(4)]
        + [dma(2 * pack_count(columns))],
    )(*map(in_hbm, arguments))
    held, partner, other = lax.optimization_barrier((coarse_basis, *packs))
    partner, other = swap(partner, other)
    (first,) = call(
        restrict_kernel, "restrict", [VMEM] * 2, [row], 10_000_000, [sums]
    )(rhs, held)
    first = from_everyone(first)
    direction, image, smooth, partner_rows, other_rows, second = call(
        functools.partial(first_turn_kernel, count), "first_turn", [SMEM] + [VMEM] * 8,
        [whole, whole, smoothed, edge, edge, row], 20_000_000, [extended, sums, stacked, solved],
    )(margin_rows, first, coarse_inverse, partner, other, held, rhs, viscosity, coupling)
    partner_rows, other_rows = swap(partner_rows, other_rows)
    second = from_everyone(second)
    second_direction, third = call(
        functools.partial(second_turn_kernel, count), "second_turn", [SMEM] + [VMEM] * 13,
        [whole, row], 20_000_000, [extended, extended, sums, stacked, solved],
    )(
        margin_rows, first, second, coarse_inverse, partner, other, partner_rows, other_rows,
        held, smooth, rhs, image, viscosity, coupling,
    )
    third = from_everyone(third)
    result, transposed = call(finish_kernel, "finish", [VMEM] * 5, [whole, f32(2, 3)], 1_000_000)(
        first, second, third, direction, second_direction
    )
    return result, transposed.T


def solution(mesh):
    in_specs = (
        P(None, ("groups", "sub"), None),
        P(("groups", "sub"), None),
        P(None, ("groups", "sub"), None),
        P("groups"),
        P(None, None, ("groups", "sub"), None),
        P(("groups", "sub"), None),
    )
    out_specs = (P(None, ("groups", "sub"), None), P("groups", None))
    return jax.shard_map(
        on_device, mesh=mesh, in_specs=in_specs, out_specs=out_specs, check_vma=False
    )
```

```python
import functools

import jax
import jax.numpy as jnp
from jax import lax
from jax.experimental import pallas as pl
from jax.experimental.pallas import tpu as pltpu
from jax.sharding import PartitionSpec as P

ROWS = 64
CELLS = 512
VECTORS = 48
HALO = 8
EXT = ROWS + 2 * HALO
STRIP = 32
STACKED = EXT + 2 * STRIP
TILE = 8
CHUNK = 16
CHUNKS = 2 * ROWS // CHUNK
PIECE = 8
PIECES = VECTORS // PIECE
LANES = 128
SLOTS = 64
EDGE_AT = 5 * HALO
INVERSE_AT = 2 * VECTORS
SWEEPS = 4
RELAX = 0.7
ROW_FACTOR = (1.0, 4.0)
CELL_FACTOR = (4.0, 1.0)

VMEM = pl.BlockSpec(memory_space=pltpu.VMEM)
SMEM = pl.BlockSpec(memory_space=pltpu.SMEM)
HBM = pl.BlockSpec(memory_space=pltpu.HBM)
ANY = pl.BlockSpec(memory_space=pl.ANY)


def coarse_rows(columns):
    return INVERSE_AT + VECTORS * (columns // 512) + (VECTORS // 2) * (columns % 512 // 256)


def cell_sum(field):
    lane = lax.broadcasted_iota(jnp.int32, (field.shape[0], LANES), 1)
    left, right = pltpu.roll(field, 1, 1), pltpu.roll(field, CELLS - 1, 1)
    inner = left[:, LANES:-LANES] + right[:, LANES:-LANES]
    first = jnp.where(lane == 0, 0.0, left[:, :LANES]) + right[:, :LANES]
    last = left[:, -LANES:] + jnp.where(lane == LANES - 1, 0.0, right[:, -LANES:])
    return jnp.concatenate([first, inner, last], 1)


class Rows:
    def __init__(self, read, first, last):
        self.read, self.first, self.last = read, first, last
        self.tiles, self.down, self.up = {}, {}, {}

    def at(self, t):
        if t not in self.tiles:
            self.tiles[t] = self.read(t)
        return self.tiles[t]

    def moved(self, held, t, by):
        if t not in held:
            held[t] = pltpu.roll(self.at(t), by, 0)
        return held[t]

    def around(self, t):
        row = lax.broadcasted_iota(jnp.int32, (TILE, CELLS), 0)
        below, above = self.moved(self.down, t, 1), self.moved(self.up, t, TILE - 1)
        if t > self.first:
            below = jnp.where(row == 0, self.moved(self.down, t - 1, 1), below)
        if t < self.last:
            above = jnp.where(row == TILE - 1, self.moved(self.up, t + 1, TILE - 1), above)
        return below + above


def neighbours(rows, t, component):
    around, cells = rows.around(t), cell_sum(rows.at(t))
    if component == 0:
        return around + CELL_FACTOR[0] * cells
    return ROW_FACTOR[1] * around + cells


def sublane_sum(tile):
    for by in (4, 2, 1):
        tile = tile + pltpu.roll(tile, by, 0)
    return tile


def in_rows(tiles):
    row = lax.broadcasted_iota(jnp.int32, (8, LANES), 0)
    total = jnp.zeros((8, LANES), jnp.float32)
    for n, tile in enumerate(tiles):
        total = jnp.where(row == n, sublane_sum(tile), total)
    return total


def restrict_piece(i, held, field, sums):
    totals = [None] * PIECE
    for a in range(2):
        for r in range(0, ROWS, CHUNK):
            for c in range(0, CELLS, LANES):
                rows, cells = slice(r, r + CHUNK), slice(c, c + LANES)
                tile = field[a, rows, cells]
                for n in range(PIECE):
                    term = held[PIECE * i + n, a, rows, cells].astype(jnp.float32) * tile
                    totals[n] = term if totals[n] is None else totals[n] + term
    tiles = [total[:8] + total[8:] for total in totals]
    sums[pl.ds(pl.multiple_of(PIECE * i, PIECE), PIECE), :] = in_rows(tiles)


def fold(row):
    total = row[:, :LANES]
    for c in range(LANES, CELLS, LANES):
        total = total + row[:, c : c + LANES]
    return total


def tile_rows(t):
    return slice(TILE * t, TILE * (t + 1))


def send_sums(sums, out_ref):
    rest = sums[...]
    parts = []
    for _ in range(3):
        part = rest.astype(jnp.bfloat16)
        parts.append(part)
        rest = rest - part.astype(jnp.float32)
    row = lax.dot_general(
        jnp.ones((CHUNK, 3 * LANES), jnp.bfloat16),
        jnp.concatenate(parts, 1),
        (((1,), (1,)), ((), ())),
        preferred_element_type=jnp.float32,
    )
    wide = jnp.concatenate([row[:1], jnp.zeros((1, LANES - SLOTS), jnp.float32)], 1)
    out_ref[...] = jnp.broadcast_to(wide, out_ref.shape)


def pack_copies(out_ref, first_row, rhs_ref, visc_ref, coup_ref, inverse_ref, sems):
    rows = pl.ds(pl.multiple_of(first_row, HALO), HALO)
    moves = [(visc_ref.at[rows, :], 0, HALO, None)]
    for a in range(2):
        moves.append((coup_ref.at[a, rows, :], HALO * (1 + a), HALO, None))
        moves.append((rhs_ref.at[a, rows, :], HALO * (3 + a), HALO, None))
    columns = inverse_ref.shape[1]
    at = EDGE_AT + INVERSE_AT
    for c in range(0, columns - 511, 512):
        moves.append((inverse_ref.at[:, pl.ds(c, 512)], at, VECTORS, None))
        at += VECTORS
    if columns % 512:
        half = VECTORS // 2
        last = pl.ds(columns - 256, 256)
        moves.append((inverse_ref.at[pl.ds(0, half), last], at, half, 0))
        moves.append((inverse_ref.at[pl.ds(half, half), last], at, half, 256))
    copies = []
    for n, (source, at, size, lane) in enumerate(moves):
        place = pl.ds(at, size)
        target = out_ref.at[place, :] if lane is None else out_ref.at[place, pl.ds(lane, 256)]
        copies.append(pltpu.make_async_copy(source, target, sems.at[n]))
    return copies


def pack_count(columns):
    return 5 + columns // 512 + 2 * (columns % 512 // 256)


def pack_kernel(flip, rhs_ref, visc_ref, coup_ref, inverse_ref, basis_ref, *refs):
    out_ref, groups, group_sems, sems = refs[-4:]
    up = (lax.axis_index("sub") + flip + 1) % 2
    rows = pl.ds(pl.multiple_of(up * (ROWS - CHUNK), CHUNK), CHUNK)
    group_copies = [
        pltpu.make_async_copy(basis_ref.at[:, a, rows, :], groups.at[a], group_sems.at[a])
        for a in range(2)
    ]
    packs = pack_copies(
        out_ref, up * (ROWS - HALO), rhs_ref, visc_ref, coup_ref, inverse_ref, sems
    )
    for copy in group_copies + packs:
        copy.start()

    def take(a, row):
        for k in range(0, VECTORS, TILE):
            lines = [
                groups[a, k + n].astype(jnp.float32)[row : row + 1] for n in range(TILE)
            ]
            at = EDGE_AT + VECTORS * a + k
            out_ref[at : at + TILE] = jnp.concatenate(lines, 0)

    for a in range(2):
        group_copies[a].wait()

        @pl.when(up == 1)
        def _():
            take(a, CHUNK - 1)

        @pl.when(up == 0)
        def _():
            take(a, 0)

    for copy in packs:
        copy.wait()


def restrict_kernel(rhs_ref, held, sums_ref, sums):
    sums[...] = jnp.zeros_like(sums)
    squares = jnp.zeros((TILE, CELLS), jnp.float32)
    for a in range(2):
        for t in range(ROWS // TILE):
            tile = rhs_ref[a, tile_rows(t)]
            squares = squares + tile * tile
    sums[VECTORS : VECTORS + 8] = in_rows([fold(squares)])

    def body(i, carry):
        restrict_piece(i, held, rhs_ref, sums)
        return carry

    lax.fori_loop(0, PIECES, body, 0)
    send_sums(sums, sums_ref)


class Neighbour:
    def __init__(self, first_ref, second_ref):
        self.odd = lax.axis_index("sub") % 2 == 1
        self.first, self.second = first_ref, second_ref

    def __getitem__(self, index):
        return jnp.where(self.odd, self.first[index], self.second[index])


def neighbours_of(partner_ref, other_ref):
    return Neighbour(partner_ref, other_ref), Neighbour(other_ref, partner_ref)


def solve(count, margin_ref, visc_ref, coup_ref, field, low, high, out_ref, stacked, solved, steps):
    waiting, done = list(steps), 0
    every = (SWEEPS - 1) * (STACKED // TILE) // len(waiting)
    rank = lax.axis_index("sub")
    lower = jnp.where(rank > 0, margin_ref[jnp.maximum(rank - 1, 0)], 0)
    upper = jnp.where(rank < count - 1, margin_ref[rank], 0)
    lower_f, upper_f = lower.astype(jnp.float32), upper.astype(jnp.float32)
    low_scale = 1.0 / (2.0 * jnp.maximum(lower_f, 1.0))
    high_scale = 1.0 / (2.0 * jnp.maximum(upper_f, 1.0))
    wide = lambda x: jnp.concatenate([x] * (CELLS // LANES), 1)
    own_tiles = ROWS // TILE
    strip_tiles = STRIP // TILE
    last = own_tiles + 1
    segments = (
        (0, 0, last + 1),
        (last + 1, 0, strip_tiles),
        (last + 1 + strip_tiles, last + 1 - strip_tiles, strip_tiles),
    )

    def place_of(e):
        return lax.broadcasted_iota(jnp.int32, (TILE, LANES), 0) + (TILE * e - HALO)

    def live_of(segment, e):
        place = place_of(e)
        if segment == 0:
            live = (place >= -lower) & (place < ROWS + upper)
        elif segment == 1:
            live = place < lower
        else:
            live = place >= ROWS - upper
        return wide(live.astype(jnp.float32))

    def weight_of(segment, e):
        place = place_of(e)
        place_f = place.astype(jnp.float32)
        rising = lambda base, scale: (place_f - base + 0.5) * scale
        falling = lambda base, scale: (base - place_f - 0.5) * scale
        if segment == 0:
            weight = jnp.where(place < lower, rising(-lower_f, low_scale), 1.0)
            weight = jnp.where(
                place >= ROWS - upper, falling(ROWS + upper_f, high_scale), weight
            )
        elif segment == 1:
            weight = jnp.where(place >= -lower, falling(lower_f, low_scale), 1.0)
        else:
            weight = jnp.where(place < ROWS + upper, rising(ROWS - upper_f, high_scale), 1.0)
        return wide(weight)

    def extended(ref, at, e):
        if e == 0:
            return low[at : at + HALO]
        if e == last:
            return high[at : at + HALO]
        return ref[tile_rows(e - 1)]

    for e in range(last + 1):
        viscosity = extended(visc_ref, 0, e)
        for a in range(2):
            coupling = extended(coup_ref.at[a], HALO * (1 + a), e)
            scale = RELAX / (10.0 * viscosity + jnp.abs(coupling) + 0.05)
            parts = (scale * field(a, e - 1), scale * viscosity, scale * coupling)
            for n, (first, begin, size) in enumerate(segments):
                if not begin <= e < begin + size:
                    continue
                rows = tile_rows(first + e - begin)
                always = n == 0 and 0 < e < last
                for m, part in enumerate(parts):
                    stacked[3 * a + m, rows] = part if always else live_of(n, e) * part

    for sweep in range(1, SWEEPS):
        for n, (first, begin, size) in enumerate(segments):
            end = first + size - 1
            if sweep == 1:
                reads = [lambda t, a=a: stacked[3 * a, tile_rows(t)] for a in range(2)]
            else:
                bank = 2 * (sweep % 2)
                reads = [lambda t, a=a: solved[bank + a, tile_rows(t)] for a in range(2)]
            fields = [Rows(read, first, end) for read in reads]
            for t in range(first, end + 1):
                rows = tile_rows(t)
                if done % every == 0 and waiting:
                    waiting.pop(0)()
                done += 1
                for a in range(2):
                    value = (
                        ((1.0 - RELAX) * fields[a].at(t) + stacked[3 * a, rows])
                        + stacked[3 * a + 1, rows] * neighbours(fields[a], t, a)
                        - stacked[3 * a + 2, rows] * fields[1 - a].at(t)
                    )
                    e = t - first + begin
                    if sweep < SWEEPS - 1:
                        solved[2 * ((sweep + 1) % 2) + a, rows] = value
                    elif n == 0:
                        out_ref[a, tile_rows(e)] = weight_of(n, e) * value
                    else:
                        out_ref[a, tile_rows(e)] += weight_of(n, e) * value


def line_up(residuals):
    devices = residuals.shape[0]
    lane = lax.broadcasted_iota(jnp.int32, (1, LANES), 1)
    tiles = [jnp.zeros((1, LANES), jnp.float32) for _ in range(devices * VECTORS // LANES)]
    for t in range(devices):
        tile, offset = divmod(VECTORS * t, LANES)
        row = jnp.where(lane < VECTORS, residuals[devices - 1 - t : devices - t], 0.0)
        if offset:
            row = pltpu.roll(row, offset, 1)
        if offset + VECTORS <= LANES:
            tiles[tile] = tiles[tile] + row
        else:
            tiles[tile] = tiles[tile] + jnp.where(lane >= offset, row, 0.0)
            tiles[tile + 1] = tiles[tile + 1] + jnp.where(lane < offset, row, 0.0)
    return jnp.concatenate(tiles, 1)


def rounded(column):
    return column.astype(jnp.bfloat16).astype(jnp.float32)


def lift(inverse_ref, residual):
    return rounded(jnp.sum(inverse_ref[...] * residual, 1, keepdims=True))


def lift_packed(ref, residual):
    columns = residual.shape[1]
    at, total = EDGE_AT + INVERSE_AT, None
    for c in range(0, columns - 511, 512):
        term = jnp.sum(ref[at : at + VECTORS] * residual[:, c : c + 512], 1, keepdims=True)
        total = term if total is None else total + term
        at += VECTORS
    if columns % 512:
        half = VECTORS // 2
        last = residual[:, columns - 256 :]
        rows = ref[at : at + half]
        term = jnp.concatenate(
            [
                jnp.sum(rows[:, :256] * last, 1, keepdims=True),
                jnp.sum(rows[:, 256:] * last, 1, keepdims=True),
            ],
            0,
        )
        total = term if total is None else total + term
    return rounded(total)


def edge_values(ref, lifted):
    starts = [EDGE_AT + VECTORS * a for a in range(2)]
    return [jnp.sum(ref[at : at + VECTORS] * lifted, 0, keepdims=True) for at in starts]


def spread(lifted):
    shape = (VECTORS, CHUNK * VECTORS)
    owner = lax.broadcasted_iota(jnp.int32, shape, 1) // CHUNK
    row = lax.broadcasted_iota(jnp.int32, shape, 0)
    line = jnp.sum(jnp.where(owner == row, lifted, 0.0), 0, keepdims=True)
    shape = (CHUNK, CHUNK * VECTORS)
    place = lax.broadcasted_iota(jnp.int32, shape, 1) % CHUNK
    row = lax.broadcasted_iota(jnp.int32, shape, 0)
    return jnp.where(place == row, line, 0.0).astype(jnp.bfloat16)


def prolonging(residual, inverse_ref, held, extended):
    matrix = spread(lift(inverse_ref, residual))

    def step(a, r):
        rows = held[:, a, r : r + CHUNK, :].reshape(CHUNK * VECTORS, CELLS)
        extended[a, HALO + r : HALO + r + CHUNK] = jnp.dot(
            matrix, rows, preferred_element_type=jnp.float32
        )

    return [functools.partial(step, a, r) for a in range(2) for r in range(0, ROWS, CHUNK)]


def apply_operator(residual, low, high, smooth, extended, visc_ref, coup_ref, direction_ref):
    edges = [edge_values(side, lift_packed(side, residual)) for side in (low, high)]
    place = lax.broadcasted_iota(jnp.int32, (TILE, CELLS), 0)
    tiles = ROWS // TILE

    def read(t, a):
        if t < 0:
            return smooth(a, 0) + jnp.where(place == TILE - 1, edges[0][a], 0.0)
        if t == tiles:
            return smooth(a, t + 1) + jnp.where(place == 0, edges[1][a], 0.0)
        tile = smooth(a, t + 1) + extended[a, tile_rows(t + 1)]
        direction_ref[a, tile_rows(t)] = tile
        return tile

    fields = [Rows(lambda t, a=a: read(t, a), -1, tiles) for a in range(2)]
    for t in range(tiles):
        rows = tile_rows(t)
        viscosity = visc_ref[rows]
        for a in range(2):
            coupling = coup_ref[a, rows]
            diagonal = 10.0 * viscosity + jnp.abs(coupling) + 0.05
            image = (
                diagonal * fields[a].at(t)
                - viscosity * neighbours(fields[a], t, a)
                + coupling * fields[1 - a].at(t)
            )
            yield t, a, image


def lane_total(received, lane):
    return jnp.sum(received[:, lane : lane + 1], 0, keepdims=True)


def first_turn_kernel(
    count, margin_ref, sums_ref, inverse_ref, partner_ref, other_ref, held, rhs_ref, visc_ref,
    coup_ref,
    direction_ref, image_ref, smooth_ref, partner_rows_ref, other_rows_ref, next_ref,
    extended, sums, stacked, solved,
):
    received = sums_ref[...]
    over_beta = 1.0 / jnp.sqrt(lane_total(received, VECTORS))
    residual = line_up(received) * over_beta
    steps = prolonging(residual, inverse_ref, held, extended)
    low, high = neighbours_of(partner_ref, other_ref)

    def field(a, t):
        at = HALO * (3 + a)
        if t < 0:
            return low[at : at + HALO]
        return high[at : at + HALO] if t == ROWS // TILE else rhs_ref[a, tile_rows(t)]

    solve(
        count, margin_ref, visc_ref, coup_ref, field, low, high, smooth_ref, stacked, solved,
        steps,
    )
    smooth = lambda a, t: smooth_ref[a, tile_rows(t)] * over_beta
    images = apply_operator(
        residual, low, high, smooth, extended, visc_ref, coup_ref, direction_ref
    )
    odd = lax.axis_index("sub") % 2 == 1
    products, squares = [jnp.zeros((TILE, CELLS), jnp.float32)] * 2
    heads, tails = [None] * 2, [None] * 2
    for t, a, image in images:
        image_ref[a, tile_rows(t)] = image
        products = products + rhs_ref[a, tile_rows(t)] * image
        squares = squares + image * image
        if t == 0:
            heads[a] = image
        if t == ROWS // TILE - 1:
            tails[a] = image
    for a in range(2):
        partner_rows_ref[a] = jnp.where(odd, heads[a], tails[a])
        other_rows_ref[a] = jnp.where(odd, tails[a], heads[a])
    sums[...] = jnp.zeros_like(sums)
    sums[VECTORS : VECTORS + 8] = in_rows([fold(products), fold(squares)])

    def body(i, carry):
        restrict_piece(i, held, image_ref, sums)
        return carry

    lax.fori_loop(0, PIECES, body, 0)
    send_sums(sums, next_ref)


def first_column(first, second):
    beta = jnp.sqrt(lane_total(first, VECTORS))
    h_00 = lane_total(second, VECTORS) / beta
    h_10 = jnp.sqrt(lane_total(second, VECTORS + 1) - h_00 * h_00)
    return beta, h_00, h_10


def second_turn_kernel(
    count, margin_ref, first_ref, second_ref, inverse_ref, partner_ref, other_ref,
    partner_rows_ref, other_rows_ref, held, smooth_ref, rhs_ref, image_ref, visc_ref, coup_ref,
    direction_ref, next_ref,
    image_smooth, extended, sums, stacked, solved,
):
    first, second = first_ref[...], second_ref[...]
    beta, h_00, h_10 = first_column(first, second)
    ratio = h_00 / beta
    over = 1.0 / h_10
    residual = (line_up(second) - ratio * line_up(first)) * over
    steps = prolonging(residual, inverse_ref, held, extended)
    low, high = neighbours_of(partner_ref, other_ref)
    low_rows, high_rows = neighbours_of(partner_rows_ref, other_rows_ref)

    def field(a, t):
        if t < 0:
            return low_rows[a]
        return high_rows[a] if t == ROWS // TILE else image_ref[a, tile_rows(t)]

    solve(
        count, margin_ref, visc_ref, coup_ref, field, low, high, image_smooth, stacked, solved,
        steps,
    )

    def smooth(a, t):
        rows = tile_rows(t)
        return (image_smooth[a, rows] - ratio * smooth_ref[a, rows]) * over

    images = apply_operator(
        residual, low, high, smooth, extended, visc_ref, coup_ref, direction_ref
    )
    totals = [jnp.zeros((TILE, CELLS), jnp.float32)] * 3
    for t, a, image in images:
        others = (rhs_ref[a, tile_rows(t)], image_ref[a, tile_rows(t)], image)
        totals = [total + x * image for total, x in zip(totals, others)]
    sums[...] = jnp.zeros_like(sums)
    sums[:8] = in_rows([fold(total) for total in totals])
    send_sums(sums, next_ref)


def finish_kernel(
    first_ref, second_ref, third_ref, first_direction_ref, second_direction_ref,
    solution_ref, hessenberg_ref,
):
    third = third_ref[...]
    beta, h_00, h_10 = first_column(first_ref[...], second_ref[...])
    squares = lane_total(third, 2)
    h_01 = lane_total(third, 0) / beta
    h_11 = (lane_total(third, 1) - h_00 * h_01) / h_10
    h_21 = jnp.sqrt(squares - h_01 * h_01 - h_11 * h_11)
    l_00 = jnp.sqrt(h_00 * h_00 + h_10 * h_10)
    l_10 = (h_00 * h_01 + h_10 * h_11) / l_00
    f_0 = beta * h_00 / l_00
    c_1 = (beta * h_01 - l_10 * f_0) / (squares - l_10 * l_10)
    c_0 = (f_0 - l_10 * c_1) / l_00
    for a in range(2):
        solution_ref[a] = c_0 * first_direction_ref[a] + c_1 * second_direction_ref[a]
    shape = hessenberg_ref.shape
    row = lax.broadcasted_iota(jnp.int32, shape, 1)
    column = lax.broadcasted_iota(jnp.int32, shape, 0)
    entries = jnp.zeros(shape, jnp.float32)
    for i, j, value in ((0, 0, h_00), (0, 1, h_01), (1, 0, h_10), (1, 1, h_11), (2, 1, h_21)):
        entries = jnp.where((row == i) & (column == j), value, entries)
    hessenberg_ref[...] = entries


def call(kernel, name, in_specs, outs, flops, scratch=(), traffic=4_000_000):
    return pl.pallas_call(
        kernel,
        name=name,
        in_specs=in_specs,
        out_specs=[VMEM] * len(outs),
        out_shape=outs,
        scratch_shapes=scratch,
        compiler_params=pltpu.CompilerParams(vmem_limit_bytes=16 * 1024 * 1024),
        cost_estimate=pl.CostEstimate(flops=flops, bytes_accessed=traffic, transcendentals=0),
    )


def in_hbm(array):
    return pltpu.with_memory_space_constraint(array, pltpu.HBM)


def from_everyone(rows):
    order = [list(range(lax.axis_size("sub")))[::-1]]
    return lax.all_to_all(rows, "sub", 0, 0, tiled=True, axis_index_groups=order)


def swap(partner, other):
    count = lax.axis_size("sub")
    both = lambda lows: [pair for i in lows for pair in ((i, i + 1), (i + 1, i))]
    return (
        lax.ppermute(partner, "sub", both(range(0, count, 2))),
        lax.ppermute(other, "sub", both(range(1, count - 1, 2))),
    )


def on_device(rhs, viscosity, coupling, margin_rows, coarse_basis, coarse_inverse):
    count = lax.axis_size("sub")
    columns = coarse_inverse.shape[1]
    f32 = lambda *shape: jax.ShapeDtypeStruct(shape, jnp.float32)
    dma = lambda *shape: pltpu.SemaphoreType.DMA(shape)
    extended = pltpu.VMEM((2, EXT, CELLS), jnp.float32)
    stacked = pltpu.VMEM((6, STACKED, CELLS), jnp.float32)
    solved = pltpu.VMEM((4, STACKED, CELLS), jnp.float32)
    sums = pltpu.VMEM((SLOTS, LANES), jnp.float32)
    row, whole, edge = f32(count, LANES), f32(2, ROWS, CELLS), f32(2, HALO, CELLS)
    packed, smoothed = f32(EDGE_AT + coarse_rows(columns), CELLS), f32(2, EXT, CELLS)
    arguments = (rhs, viscosity, coupling, coarse_inverse, coarse_basis)
    in_place = [in_hbm(x) for x in arguments]
    scratch = [pltpu.VMEM((2, VECTORS, CHUNK, CELLS), jnp.bfloat16), dma(2)]
    scratch.append(dma(pack_count(columns)))
    pack = lambda flip, name, *before: call(
        functools.partial(pack_kernel, flip), name, [HBM] * 5 + [ANY] * len(before), [packed],
        5_000_000, scratch,
    )(*in_place, *before)[0]
    other = pack(1, "pack_other")
    partner = pack(0, "pack_partner", other)
    partner, other = swap(partner, other)
    (first,) = call(
        restrict_kernel, "restrict", [VMEM] * 2, [row], 10_000_000, [sums]
    )(rhs, coarse_basis)
    first = from_everyone(first)
    direction, image, smooth, partner_rows, other_rows, second = call(
        functools.partial(first_turn_kernel, count), "first_turn", [SMEM] + [VMEM] * 8,
        [whole, whole, smoothed, edge, edge, row], 20_000_000, [extended, sums, stacked, solved],
    )(margin_rows, first, coarse_inverse, partner, other, coarse_basis, rhs, viscosity, coupling)
    partner_rows, other_rows = swap(partner_rows, other_rows)
    second = from_everyone(second)
    second_direction, third = call(
        functools.partial(second_turn_kernel, count), "second_turn", [SMEM] + [VMEM] * 13,
        [whole, row], 20_000_000, [extended, extended, sums, stacked, solved],
    )(
        margin_rows, first, second, coarse_inverse, partner, other, partner_rows, other_rows,
        coarse_basis, smooth, rhs, image, viscosity, coupling,
    )
    third = from_everyone(third)
    result, transposed = call(finish_kernel, "finish", [VMEM] * 5, [whole, f32(2, 3)], 1_000_000)(
        first, second, third, direction, second_direction
    )
    return result, transposed.T


def solution(mesh):
    in_specs = (
        P(None, ("groups", "sub"), None),
        P(("groups", "sub"), None),
        P(None, ("groups", "sub"), None),
        P("groups"),
        P(None, None, ("groups", "sub"), None),
        P(("groups", "sub"), None),
    )
    out_specs = (P(None, ("groups", "sub"), None), P("groups", None))
    return jax.shard_map(
        on_device, mesh=mesh, in_specs=in_specs, out_specs=out_specs, check_vma=False
    )
```

```python
import functools

import jax
import jax.numpy as jnp
from jax import lax
from jax.experimental import pallas as pl
from jax.experimental.pallas import tpu as pltpu
from jax.sharding import PartitionSpec as P

ROWS = 64
CELLS = 512
VECTORS = 48
HALO = 8
EXT = ROWS + 2 * HALO
STRIP = 32
STACKED = EXT + 2 * STRIP
TILE = 8
CHUNK = 16
CHUNKS = 2 * ROWS // CHUNK
PIECE = 8
PIECES = VECTORS // PIECE
LANES = 128
SLOTS = 64
EDGE_AT = 5 * HALO
INVERSE_AT = 2 * VECTORS
SWEEPS = 4
RELAX = 0.7
ROW_FACTOR = (1.0, 4.0)
CELL_FACTOR = (4.0, 1.0)

VMEM = pl.BlockSpec(memory_space=pltpu.VMEM)
SMEM = pl.BlockSpec(memory_space=pltpu.SMEM)
HBM = pl.BlockSpec(memory_space=pltpu.HBM)


def coarse_rows(columns):
    return INVERSE_AT + VECTORS * (columns // 512) + (VECTORS // 2) * (columns % 512 // 256)


def cell_sum(field):
    lane = lax.broadcasted_iota(jnp.int32, (field.shape[0], LANES), 1)
    left, right = pltpu.roll(field, 1, 1), pltpu.roll(field, CELLS - 1, 1)
    inner = left[:, LANES:-LANES] + right[:, LANES:-LANES]
    first = jnp.where(lane == 0, 0.0, left[:, :LANES]) + right[:, :LANES]
    last = left[:, -LANES:] + jnp.where(lane == LANES - 1, 0.0, right[:, -LANES:])
    return jnp.concatenate([first, inner, last], 1)


class Rows:
    def __init__(self, read, first, last):
        self.read, self.first, self.last = read, first, last
        self.tiles, self.down, self.up = {}, {}, {}

    def at(self, t):
        if t not in self.tiles:
            self.tiles[t] = self.read(t)
        return self.tiles[t]

    def moved(self, held, t, by):
        if t not in held:
            held[t] = pltpu.roll(self.at(t), by, 0)
        return held[t]

    def around(self, t):
        row = lax.broadcasted_iota(jnp.int32, (TILE, CELLS), 0)
        below, above = self.moved(self.down, t, 1), self.moved(self.up, t, TILE - 1)
        if t > self.first:
            below = jnp.where(row == 0, self.moved(self.down, t - 1, 1), below)
        if t < self.last:
            above = jnp.where(row == TILE - 1, self.moved(self.up, t + 1, TILE - 1), above)
        return below + above


def neighbours(rows, t, component):
    around, cells = rows.around(t), cell_sum(rows.at(t))
    if component == 0:
        return around + CELL_FACTOR[0] * cells
    return ROW_FACTOR[1] * around + cells


def sublane_sum(tile):
    for by in (4, 2, 1):
        tile = tile + pltpu.roll(tile, by, 0)
    return tile


def in_rows(tiles):
    row = lax.broadcasted_iota(jnp.int32, (8, LANES), 0)
    total = jnp.zeros((8, LANES), jnp.float32)
    for n, tile in enumerate(tiles):
        total = jnp.where(row == n, sublane_sum(tile), total)
    return total


def restrict_piece(i, held, field, sums):
    totals = [None] * PIECE
    for a in range(2):
        for r in range(0, ROWS, CHUNK):
            for c in range(0, CELLS, LANES):
                rows, cells = slice(r, r + CHUNK), slice(c, c + LANES)
                tile = field[a, rows, cells]
                for n in range(PIECE):
                    term = held[PIECE * i + n, a, rows, cells].astype(jnp.float32) * tile
                    totals[n] = term if totals[n] is None else totals[n] + term
    tiles = [total[:8] + total[8:] for total in totals]
    sums[pl.ds(pl.multiple_of(PIECE * i, PIECE), PIECE), :] = in_rows(tiles)


def fold(row):
    total = row[:, :LANES]
    for c in range(LANES, CELLS, LANES):
        total = total + row[:, c : c + LANES]
    return total


def tile_rows(t):
    return slice(TILE * t, TILE * (t + 1))


def send_sums(sums, out_ref):
    rest = sums[...]
    parts = []
    for _ in range(3):
        part = rest.astype(jnp.bfloat16)
        parts.append(part)
        rest = rest - part.astype(jnp.float32)
    row = lax.dot_general(
        jnp.ones((CHUNK, 3 * LANES), jnp.bfloat16),
        jnp.concatenate(parts, 1),
        (((1,), (1,)), ((), ())),
        preferred_element_type=jnp.float32,
    )
    wide = jnp.concatenate([row[:1], jnp.zeros((1, LANES - SLOTS), jnp.float32)], 1)
    out_ref[...] = jnp.broadcast_to(wide, out_ref.shape)


def pack_copies(out_ref, first_row, rhs_ref, visc_ref, coup_ref, inverse_ref, sems, at_sem):
    rows = pl.ds(pl.multiple_of(first_row, HALO), HALO)
    moves = [(visc_ref.at[rows, :], 0, HALO, None)]
    for a in range(2):
        moves.append((coup_ref.at[a, rows, :], HALO * (1 + a), HALO, None))
        moves.append((rhs_ref.at[a, rows, :], HALO * (3 + a), HALO, None))
    columns = inverse_ref.shape[1]
    at = EDGE_AT + INVERSE_AT
    for c in range(0, columns - 511, 512):
        moves.append((inverse_ref.at[:, pl.ds(c, 512)], at, VECTORS, None))
        at += VECTORS
    if columns % 512:
        half = VECTORS // 2
        last = pl.ds(columns - 256, 256)
        moves.append((inverse_ref.at[pl.ds(0, half), last], at, half, 0))
        moves.append((inverse_ref.at[pl.ds(half, half), last], at, half, 256))
    copies = []
    for n, (source, at, size, lane) in enumerate(moves):
        place = pl.ds(at, size)
        target = out_ref.at[place, :] if lane is None else out_ref.at[place, pl.ds(lane, 256)]
        copies.append(pltpu.make_async_copy(source, target, sems.at[at_sem + n]))
    return copies


def pack_count(columns):
    return 5 + columns // 512 + 2 * (columns % 512 // 256)


def pack_kernel(
    rhs_ref, visc_ref, coup_ref, inverse_ref, basis_ref,
    partner_ref, other_ref,
    groups, group_sems, pack_sems,
):
    odd = lax.axis_index("sub") % 2
    sides = ((partner_ref, 1 - odd), (other_ref, odd))
    group_copies, packs = [], []
    for n, (out_ref, up) in enumerate(sides):
        for a in range(2):
            rows = pl.ds(pl.multiple_of(up * (ROWS - CHUNK), CHUNK), CHUNK)
            group_copies.append(
                pltpu.make_async_copy(
                    basis_ref.at[:, a, rows, :], groups.at[2 * n + a], group_sems.at[2 * n + a]
                )
            )
        packs += pack_copies(
            out_ref, up * (ROWS - HALO), rhs_ref, visc_ref, coup_ref, inverse_ref, pack_sems,
            n * pack_count(inverse_ref.shape[1]),
        )
    for copy in group_copies + packs:
        copy.start()

    def take(out_ref, group, a, row):
        for k in range(0, VECTORS, TILE):
            lines = [groups[group, k + n].astype(jnp.float32)[row : row + 1] for n in range(TILE)]
            at = EDGE_AT + VECTORS * a + k
            out_ref[at : at + TILE] = jnp.concatenate(lines, 0)

    for n in range(2):
        for a in range(2):
            group_copies[2 * n + a].wait()

    @pl.when(odd == 0)
    def _():
        for a in range(2):
            take(partner_ref, a, a, CHUNK - 1)
            take(other_ref, 2 + a, a, 0)

    @pl.when(odd == 1)
    def _():
        for a in range(2):
            take(partner_ref, a, a, 0)
            take(other_ref, 2 + a, a, CHUNK - 1)

    for copy in packs:
        copy.wait()


def restrict_kernel(rhs_ref, held, sums_ref, sums):
    sums[...] = jnp.zeros_like(sums)
    squares = jnp.zeros((TILE, CELLS), jnp.float32)
    for a in range(2):
        for t in range(ROWS // TILE):
            tile = rhs_ref[a, tile_rows(t)]
            squares = squares + tile * tile
    sums[VECTORS : VECTORS + 8] = in_rows([fold(squares)])

    def body(i, carry):
        restrict_piece(i, held, rhs_ref, sums)
        return carry

    lax.fori_loop(0, PIECES, body, 0)
    send_sums(sums, sums_ref)


class Neighbour:
    def __init__(self, first_ref, second_ref):
        self.odd = lax.axis_index("sub") % 2 == 1
        self.first, self.second = first_ref, second_ref

    def __getitem__(self, index):
        return jnp.where(self.odd, self.first[index], self.second[index])


def neighbours_of(partner_ref, other_ref):
    return Neighbour(partner_ref, other_ref), Neighbour(other_ref, partner_ref)


def solve(count, margin_ref, visc_ref, coup_ref, field, low, high, out_ref, stacked, solved, steps):
    waiting, done = list(steps), 0
    every = (SWEEPS - 1) * (STACKED // TILE) // len(waiting)
    rank = lax.axis_index("sub")
    lower = jnp.where(rank > 0, margin_ref[jnp.maximum(rank - 1, 0)], 0)
    upper = jnp.where(rank < count - 1, margin_ref[rank], 0)
    lower_f, upper_f = lower.astype(jnp.float32), upper.astype(jnp.float32)
    low_scale = 1.0 / (2.0 * jnp.maximum(lower_f, 1.0))
    high_scale = 1.0 / (2.0 * jnp.maximum(upper_f, 1.0))
    wide = lambda x: jnp.concatenate([x] * (CELLS // LANES), 1)
    own_tiles = ROWS // TILE
    strip_tiles = STRIP // TILE
    last = own_tiles + 1
    segments = (
        (0, 0, last + 1),
        (last + 1, 0, strip_tiles),
        (last + 1 + strip_tiles, last + 1 - strip_tiles, strip_tiles),
    )

    def place_of(e):
        return lax.broadcasted_iota(jnp.int32, (TILE, LANES), 0) + (TILE * e - HALO)

    def live_of(segment, e):
        place = place_of(e)
        if segment == 0:
            live = (place >= -lower) & (place < ROWS + upper)
        elif segment == 1:
            live = place < lower
        else:
            live = place >= ROWS - upper
        return wide(live.astype(jnp.float32))

    def weight_of(segment, e):
        place = place_of(e)
        place_f = place.astype(jnp.float32)
        rising = lambda base, scale: (place_f - base + 0.5) * scale
        falling = lambda base, scale: (base - place_f - 0.5) * scale
        if segment == 0:
            weight = jnp.where(place < lower, rising(-lower_f, low_scale), 1.0)
            weight = jnp.where(
                place >= ROWS - upper, falling(ROWS + upper_f, high_scale), weight
            )
        elif segment == 1:
            weight = jnp.where(place >= -lower, falling(lower_f, low_scale), 1.0)
        else:
            weight = jnp.where(place < ROWS + upper, rising(ROWS - upper_f, high_scale), 1.0)
        return wide(weight)

    def extended(ref, at, e):
        if e == 0:
            return low[at : at + HALO]
        if e == last:
            return high[at : at + HALO]
        return ref[tile_rows(e - 1)]

    for e in range(last + 1):
        viscosity = extended(visc_ref, 0, e)
        for a in range(2):
            coupling = extended(coup_ref.at[a], HALO * (1 + a), e)
            scale = RELAX / (10.0 * viscosity + jnp.abs(coupling) + 0.05)
            parts = (scale * field(a, e - 1), scale * viscosity, scale * coupling)
            for n, (first, begin, size) in enumerate(segments):
                if not begin <= e < begin + size:
                    continue
                rows = tile_rows(first + e - begin)
                always = n == 0 and 0 < e < last
                for m, part in enumerate(parts):
                    stacked[3 * a + m, rows] = part if always else live_of(n, e) * part

    for sweep in range(1, SWEEPS):
        for n, (first, begin, size) in enumerate(segments):
            end = first + size - 1
            if sweep == 1:
                reads = [lambda t, a=a: stacked[3 * a, tile_rows(t)] for a in range(2)]
            else:
                bank = 2 * (sweep % 2)
                reads = [lambda t, a=a: solved[bank + a, tile_rows(t)] for a in range(2)]
            fields = [Rows(read, first, end) for read in reads]
            for t in range(first, end + 1):
                rows = tile_rows(t)
                if done % every == 0 and waiting:
                    waiting.pop(0)()
                done += 1
                for a in range(2):
                    value = (
                        ((1.0 - RELAX) * fields[a].at(t) + stacked[3 * a, rows])
                        + stacked[3 * a + 1, rows] * neighbours(fields[a], t, a)
                        - stacked[3 * a + 2, rows] * fields[1 - a].at(t)
                    )
                    e = t - first + begin
                    if sweep < SWEEPS - 1:
                        solved[2 * ((sweep + 1) % 2) + a, rows] = value
                    elif n == 0:
                        out_ref[a, tile_rows(e)] = weight_of(n, e) * value
                    else:
                        out_ref[a, tile_rows(e)] += weight_of(n, e) * value


def line_up(residuals):
    devices = residuals.shape[0]
    lane = lax.broadcasted_iota(jnp.int32, (1, LANES), 1)
    tiles = [jnp.zeros((1, LANES), jnp.float32) for _ in range(devices * VECTORS // LANES)]
    for t in range(devices):
        tile, offset = divmod(VECTORS * t, LANES)
        row = jnp.where(lane < VECTORS, residuals[devices - 1 - t : devices - t], 0.0)
        if offset:
            row = pltpu.roll(row, offset, 1)
        if offset + VECTORS <= LANES:
            tiles[tile] = tiles[tile] + row
        else:
            tiles[tile] = tiles[tile] + jnp.where(lane >= offset, row, 0.0)
            tiles[tile + 1] = tiles[tile + 1] + jnp.where(lane < offset, row, 0.0)
    return jnp.concatenate(tiles, 1)


def rounded(column):
    return column.astype(jnp.bfloat16).astype(jnp.float32)


def lift(inverse_ref, residual):
    return rounded(jnp.sum(inverse_ref[...] * residual, 1, keepdims=True))


def lift_packed(ref, residual):
    columns = residual.shape[1]
    at, total = EDGE_AT + INVERSE_AT, None
    for c in range(0, columns - 511, 512):
        term = jnp.sum(ref[at : at + VECTORS] * residual[:, c : c + 512], 1, keepdims=True)
        total = term if total is None else total + term
        at += VECTORS
    if columns % 512:
        half = VECTORS // 2
        last = residual[:, columns - 256 :]
        rows = ref[at : at + half]
        term = jnp.concatenate(
            [
                jnp.sum(rows[:, :256] * last, 1, keepdims=True),
                jnp.sum(rows[:, 256:] * last, 1, keepdims=True),
            ],
            0,
        )
        total = term if total is None else total + term
    return rounded(total)


def edge_values(ref, lifted):
    starts = [EDGE_AT + VECTORS * a for a in range(2)]
    return [jnp.sum(ref[at : at + VECTORS] * lifted, 0, keepdims=True) for at in starts]


def spread(lifted):
    shape = (VECTORS, CHUNK * VECTORS)
    owner = lax.broadcasted_iota(jnp.int32, shape, 1) // CHUNK
    row = lax.broadcasted_iota(jnp.int32, shape, 0)
    line = jnp.sum(jnp.where(owner == row, lifted, 0.0), 0, keepdims=True)
    shape = (CHUNK, CHUNK * VECTORS)
    place = lax.broadcasted_iota(jnp.int32, shape, 1) % CHUNK
    row = lax.broadcasted_iota(jnp.int32, shape, 0)
    return jnp.where(place == row, line, 0.0).astype(jnp.bfloat16)


def prolonging(residual, inverse_ref, held, extended):
    matrix = spread(lift(inverse_ref, residual))

    def step(a, r):
        rows = held[:, a, r : r + CHUNK, :].reshape(CHUNK * VECTORS, CELLS)
        extended[a, HALO + r : HALO + r + CHUNK] = jnp.dot(
            matrix, rows, preferred_element_type=jnp.float32
        )

    return [functools.partial(step, a, r) for a in range(2) for r in range(0, ROWS, CHUNK)]


def apply_operator(residual, low, high, smooth, extended, visc_ref, coup_ref, direction_ref):
    edges = [edge_values(side, lift_packed(side, residual)) for side in (low, high)]
    place = lax.broadcasted_iota(jnp.int32, (TILE, CELLS), 0)
    tiles = ROWS // TILE

    def read(t, a):
        if t < 0:
            return smooth(a, 0) + jnp.where(place == TILE - 1, edges[0][a], 0.0)
        if t == tiles:
            return smooth(a, t + 1) + jnp.where(place == 0, edges[1][a], 0.0)
        tile = smooth(a, t + 1) + extended[a, tile_rows(t + 1)]
        direction_ref[a, tile_rows(t)] = tile
        return tile

    fields = [Rows(lambda t, a=a: read(t, a), -1, tiles) for a in range(2)]
    for t in range(tiles):
        rows = tile_rows(t)
        viscosity = visc_ref[rows]
        for a in range(2):
            coupling = coup_ref[a, rows]
            diagonal = 10.0 * viscosity + jnp.abs(coupling) + 0.05
            image = (
                diagonal * fields[a].at(t)
                - viscosity * neighbours(fields[a], t, a)
                + coupling * fields[1 - a].at(t)
            )
            yield t, a, image


def lane_total(received, lane):
    return jnp.sum(received[:, lane : lane + 1], 0, keepdims=True)


def first_turn_kernel(
    count, margin_ref, sums_ref, inverse_ref, other_ref, partner_ref, held, rhs_ref, visc_ref,
    coup_ref,
    direction_ref, image_ref, smooth_ref, partner_rows_ref, other_rows_ref, next_ref,
    extended, sums, stacked, solved,
):
    received = sums_ref[...]
    over_beta = 1.0 / jnp.sqrt(lane_total(received, VECTORS))
    residual = line_up(received) * over_beta
    steps = prolonging(residual, inverse_ref, held, extended)
    low, high = neighbours_of(partner_ref, other_ref)

    def field(a, t):
        at = HALO * (3 + a)
        if t < 0:
            return low[at : at + HALO]
        return high[at : at + HALO] if t == ROWS // TILE else rhs_ref[a, tile_rows(t)]

    solve(
        count, margin_ref, visc_ref, coup_ref, field, low, high, smooth_ref, stacked, solved,
        steps,
    )
    smooth = lambda a, t: smooth_ref[a, tile_rows(t)] * over_beta
    images = apply_operator(
        residual, low, high, smooth, extended, visc_ref, coup_ref, direction_ref
    )
    odd = lax.axis_index("sub") % 2 == 1
    products, squares = [jnp.zeros((TILE, CELLS), jnp.float32)] * 2
    heads, tails = [None] * 2, [None] * 2
    for t, a, image in images:
        image_ref[a, tile_rows(t)] = image
        products = products + rhs_ref[a, tile_rows(t)] * image
        squares = squares + image * image
        if t == 0:
            heads[a] = image
        if t == ROWS // TILE - 1:
            tails[a] = image
    half = lax.broadcasted_iota(jnp.int32, (TILE, CELLS), 0) < TILE // 2
    head = jnp.where(half, heads[0], pltpu.roll(heads[1], TILE // 2, 0))
    tail = jnp.where(half, pltpu.roll(tails[1], TILE // 2, 0), tails[0])
    partner_rows_ref[...] = jnp.where(odd, head, tail)
    other_rows_ref[...] = jnp.where(odd, tail, head)
    sums[...] = jnp.zeros_like(sums)
    sums[VECTORS : VECTORS + 8] = in_rows([fold(products), fold(squares)])

    def body(i, carry):
        restrict_piece(i, held, image_ref, sums)
        return carry

    lax.fori_loop(0, PIECES, body, 0)
    send_sums(sums, next_ref)


def first_column(first, second):
    beta = jnp.sqrt(lane_total(first, VECTORS))
    h_00 = lane_total(second, VECTORS) / beta
    h_10 = jnp.sqrt(lane_total(second, VECTORS + 1) - h_00 * h_00)
    return beta, h_00, h_10


def second_turn_kernel(
    count, margin_ref, first_ref, second_ref, inverse_ref, other_ref, partner_ref,
    other_rows_ref, partner_rows_ref, held, smooth_ref, rhs_ref, image_ref, visc_ref, coup_ref,
    direction_ref, next_ref,
    image_smooth, extended, sums, stacked, solved,
):
    first, second = first_ref[...], second_ref[...]
    beta, h_00, h_10 = first_column(first, second)
    ratio = h_00 / beta
    over = 1.0 / h_10
    residual = (line_up(second) - ratio * line_up(first)) * over
    steps = prolonging(residual, inverse_ref, held, extended)
    low, high = neighbours_of(partner_ref, other_ref)
    low_rows, high_rows = neighbours_of(partner_rows_ref, other_rows_ref)

    def field(a, t):
        if 0 <= t < ROWS // TILE:
            return image_ref[a, tile_rows(t)]
        rows = low_rows[...] if t < 0 else high_rows[...]
        return pltpu.roll(rows, TILE // 2, 0) if a else rows

    solve(
        count, margin_ref, visc_ref, coup_ref, field, low, high, image_smooth, stacked, solved,
        steps,
    )

    def smooth(a, t):
        rows = tile_rows(t)
        return (image_smooth[a, rows] - ratio * smooth_ref[a, rows]) * over

    images = apply_operator(
        residual, low, high, smooth, extended, visc_ref, coup_ref, direction_ref
    )
    totals = [jnp.zeros((TILE, CELLS), jnp.float32)] * 3
    for t, a, image in images:
        others = (rhs_ref[a, tile_rows(t)], image_ref[a, tile_rows(t)], image)
        totals = [total + x * image for total, x in zip(totals, others)]
    sums[...] = jnp.zeros_like(sums)
    sums[:8] = in_rows([fold(total) for total in totals])
    send_sums(sums, next_ref)


def finish_kernel(
    first_ref, second_ref, third_ref, first_direction_ref, second_direction_ref,
    solution_ref, hessenberg_ref,
):
    third = third_ref[...]
    beta, h_00, h_10 = first_column(first_ref[...], second_ref[...])
    squares = lane_total(third, 2)
    h_01 = lane_total(third, 0) / beta
    h_11 = (lane_total(third, 1) - h_00 * h_01) / h_10
    h_21 = jnp.sqrt(squares - h_01 * h_01 - h_11 * h_11)
    l_00 = jnp.sqrt(h_00 * h_00 + h_10 * h_10)
    l_10 = (h_00 * h_01 + h_10 * h_11) / l_00
    f_0 = beta * h_00 / l_00
    c_1 = (beta * h_01 - l_10 * f_0) / (squares - l_10 * l_10)
    c_0 = (f_0 - l_10 * c_1) / l_00
    for a in range(2):
        solution_ref[a] = c_0 * first_direction_ref[a] + c_1 * second_direction_ref[a]
    shape = hessenberg_ref.shape
    row = lax.broadcasted_iota(jnp.int32, shape, 1)
    column = lax.broadcasted_iota(jnp.int32, shape, 0)
    entries = jnp.zeros(shape, jnp.float32)
    for i, j, value in ((0, 0, h_00), (0, 1, h_01), (1, 0, h_10), (1, 1, h_11), (2, 1, h_21)):
        entries = jnp.where((row == i) & (column == j), value, entries)
    hessenberg_ref[...] = entries


def call(kernel, name, in_specs, outs, flops, scratch=(), traffic=4_000_000):
    return pl.pallas_call(
        kernel,
        name=name,
        in_specs=in_specs,
        out_specs=[VMEM] * len(outs),
        out_shape=outs,
        scratch_shapes=scratch,
        compiler_params=pltpu.CompilerParams(vmem_limit_bytes=16 * 1024 * 1024),
        cost_estimate=pl.CostEstimate(flops=flops, bytes_accessed=traffic, transcendentals=0),
    )


def in_hbm(array):
    return pltpu.with_memory_space_constraint(array, pltpu.HBM)


def from_everyone(rows):
    order = [list(range(lax.axis_size("sub")))[::-1]]
    return lax.all_to_all(rows, "sub", 0, 0, tiled=True, axis_index_groups=order)


def swap(partner, other):
    count = lax.axis_size("sub")
    both = lambda lows: [pair for i in lows for pair in ((i, i + 1), (i + 1, i))]
    return (
        lax.ppermute(partner, "sub", both(range(0, count, 2))),
        lax.ppermute(other, "sub", both(range(1, count - 1, 2))),
    )


def on_device(rhs, viscosity, coupling, margin_rows, coarse_basis, coarse_inverse):
    count = lax.axis_size("sub")
    columns = coarse_inverse.shape[1]
    f32 = lambda *shape: jax.ShapeDtypeStruct(shape, jnp.float32)
    dma = lambda *shape: pltpu.SemaphoreType.DMA(shape)
    extended = pltpu.VMEM((2, EXT, CELLS), jnp.float32)
    stacked = pltpu.VMEM((6, STACKED, CELLS), jnp.float32)
    solved = pltpu.VMEM((4, STACKED, CELLS), jnp.float32)
    sums = pltpu.VMEM((SLOTS, LANES), jnp.float32)
    row, whole, edge = f32(count, LANES), f32(2, ROWS, CELLS), f32(TILE, CELLS)
    packed, smoothed = f32(EDGE_AT + coarse_rows(columns), CELLS), f32(2, EXT, CELLS)
    arguments = (rhs, viscosity, coupling, coarse_inverse, coarse_basis)
    packs = call(
        pack_kernel, "pack", [HBM] * 5, [packed, packed], 5_000_000,
        [pltpu.VMEM((4, VECTORS, CHUNK, CELLS), jnp.bfloat16), dma(4)]
        + [dma(2 * pack_count(columns))],
    )(*map(in_hbm, arguments))
    held, partner, other = lax.optimization_barrier((coarse_basis, *packs))
    partner, other = swap(partner, other)
    (first,) = call(
        restrict_kernel, "restrict", [VMEM] * 2, [row], 10_000_000, [sums]
    )(rhs, held)
    first = from_everyone(first)
    direction, image, smooth, partner_rows, other_rows, second = call(
        functools.partial(first_turn_kernel, count), "first_turn", [SMEM] + [VMEM] * 8,
        [whole, whole, smoothed, edge, edge, row], 20_000_000, [extended, sums, stacked, solved],
    )(margin_rows, first, coarse_inverse, other, partner, held, rhs, viscosity, coupling)
    partner_rows, other_rows = swap(partner_rows, other_rows)
    second = from_everyone(second)
    second_direction, third = call(
        functools.partial(second_turn_kernel, count), "second_turn", [SMEM] + [VMEM] * 13,
        [whole, row], 20_000_000, [extended, extended, sums, stacked, solved],
    )(
        margin_rows, first, second, coarse_inverse, other, partner, other_rows, partner_rows,
        held, smooth, rhs, image, viscosity, coupling,
    )
    third = from_everyone(third)
    result, transposed = call(finish_kernel, "finish", [VMEM] * 5, [whole, f32(2, 3)], 1_000_000)(
        first, second, third, direction, second_direction
    )
    return result, transposed.T


def solution(mesh):
    in_specs = (
        P(None, ("groups", "sub"), None),
        P(("groups", "sub"), None),
        P(None, ("groups", "sub"), None),
        P("groups"),
        P(None, None, ("groups", "sub"), None),
        P(("groups", "sub"), None),
    )
    out_specs = (P(None, ("groups", "sub"), None), P("groups", None))
    return jax.shard_map(
        on_device, mesh=mesh, in_specs=in_specs, out_specs=out_specs, check_vma=False
    )
```

```python
import functools

import jax
import jax.numpy as jnp
from jax import lax
from jax.experimental import pallas as pl
from jax.experimental.pallas import tpu as pltpu
from jax.sharding import PartitionSpec as P

ROWS = 64
CELLS = 512
VECTORS = 48
HALO = 8
EXT = ROWS + 2 * HALO
STRIP = 32
GROUP = 16
STACKED = EXT + 2 * STRIP
TILE = 8
CHUNK = 16
CHUNKS = 2 * ROWS // CHUNK
PIECE = 8
PIECES = VECTORS // PIECE
LANES = 128
SLOTS = 64
EDGE_AT = 5 * HALO
INVERSE_AT = 2 * VECTORS
SWEEPS = 4
RELAX = 0.7
ROW_FACTOR = (1.0, 4.0)
CELL_FACTOR = (4.0, 1.0)

VMEM = pl.BlockSpec(memory_space=pltpu.VMEM)
SMEM = pl.BlockSpec(memory_space=pltpu.SMEM)
HBM = pl.BlockSpec(memory_space=pltpu.HBM)


def coarse_rows(columns):
    return INVERSE_AT + VECTORS * (columns // 512) + (VECTORS // 2) * (columns % 512 // 256)


def cell_sum(field):
    lane = lax.broadcasted_iota(jnp.int32, (field.shape[0], LANES), 1)
    left, right = pltpu.roll(field, 1, 1), pltpu.roll(field, CELLS - 1, 1)
    inner = left[:, LANES:-LANES] + right[:, LANES:-LANES]
    first = jnp.where(lane == 0, 0.0, left[:, :LANES]) + right[:, :LANES]
    last = left[:, -LANES:] + jnp.where(lane == LANES - 1, 0.0, right[:, -LANES:])
    return jnp.concatenate([first, inner, last], 1)


class Rows:
    def __init__(self, read, first, last):
        self.read, self.first, self.last = read, first, last
        self.tiles, self.down, self.up = {}, {}, {}

    def at(self, t):
        if t not in self.tiles:
            self.tiles[t] = self.read(t)
        return self.tiles[t]

    def moved(self, held, t, by):
        if t not in held:
            held[t] = pltpu.roll(self.at(t), by, 0)
        return held[t]

    def around(self, t):
        row = lax.broadcasted_iota(jnp.int32, (TILE, CELLS), 0)
        below, above = self.moved(self.down, t, 1), self.moved(self.up, t, TILE - 1)
        if t > self.first:
            below = jnp.where(row == 0, self.moved(self.down, t - 1, 1), below)
        if t < self.last:
            above = jnp.where(row == TILE - 1, self.moved(self.up, t + 1, TILE - 1), above)
        return below + above


def neighbours(rows, t, component):
    around, cells = rows.around(t), cell_sum(rows.at(t))
    if component == 0:
        return around + CELL_FACTOR[0] * cells
    return ROW_FACTOR[1] * around + cells


def sublane_sum(tile):
    for by in (4, 2, 1):
        tile = tile + pltpu.roll(tile, by, 0)
    return tile


def in_rows(tiles):
    row = lax.broadcasted_iota(jnp.int32, (8, LANES), 0)
    total = jnp.zeros((8, LANES), jnp.float32)
    for n, tile in enumerate(tiles):
        total = jnp.where(row == n, sublane_sum(tile), total)
    return total


def restrict_piece(i, held, field, sums):
    totals = [None] * PIECE
    for a in range(2):
        for r in range(0, ROWS, CHUNK):
            for c in range(0, CELLS, LANES):
                rows, cells = slice(r, r + CHUNK), slice(c, c + LANES)
                tile = field[a, rows, cells]
                for n in range(PIECE):
                    term = held[PIECE * i + n, a, rows, cells].astype(jnp.float32) * tile
                    totals[n] = term if totals[n] is None else totals[n] + term
    tiles = [total[:8] + total[8:] for total in totals]
    sums[pl.ds(pl.multiple_of(PIECE * i, PIECE), PIECE), :] = in_rows(tiles)


def fold(row):
    total = row[:, :LANES]
    for c in range(LANES, CELLS, LANES):
        total = total + row[:, c : c + LANES]
    return total


def tile_rows(t):
    return slice(TILE * t, TILE * (t + 1))


def send_sums(sums, out_ref):
    rest = sums[...]
    parts = []
    for _ in range(3):
        part = rest.astype(jnp.bfloat16)
        parts.append(part)
        rest = rest - part.astype(jnp.float32)
    row = lax.dot_general(
        jnp.ones((CHUNK, 3 * LANES), jnp.bfloat16),
        jnp.concatenate(parts, 1),
        (((1,), (1,)), ((), ())),
        preferred_element_type=jnp.float32,
    )
    wide = jnp.concatenate([row[:1], jnp.zeros((1, LANES - SLOTS), jnp.float32)], 1)
    out_ref[...] = jnp.broadcast_to(wide, out_ref.shape)


def pack_copies(out_ref, first_row, rhs_ref, visc_ref, coup_ref, inverse_ref, sems, at_sem):
    rows = pl.ds(pl.multiple_of(first_row, HALO), HALO)
    moves = [(visc_ref.at[rows, :], 0, HALO, None)]
    for a in range(2):
        moves.append((coup_ref.at[a, rows, :], HALO * (1 + a), HALO, None))
        moves.append((rhs_ref.at[a, rows, :], HALO * (3 + a), HALO, None))
    columns = inverse_ref.shape[1]
    at = EDGE_AT + INVERSE_AT
    for c in range(0, columns - 511, 512):
        moves.append((inverse_ref.at[:, pl.ds(c, 512)], at, VECTORS, None))
        at += VECTORS
    if columns % 512:
        half = VECTORS // 2
        last = pl.ds(columns - 256, 256)
        moves.append((inverse_ref.at[pl.ds(0, half), last], at, half, 0))
        moves.append((inverse_ref.at[pl.ds(half, half), last], at, half, 256))
    copies = []
    for n, (source, at, size, lane) in enumerate(moves):
        place = pl.ds(at, size)
        target = out_ref.at[place, :] if lane is None else out_ref.at[place, pl.ds(lane, 256)]
        copies.append(pltpu.make_async_copy(source, target, sems.at[at_sem + n]))
    return copies


def pack_count(columns):
    return 5 + columns // 512 + 2 * (columns % 512 // 256)


def pack_kernel(
    rhs_ref, visc_ref, coup_ref, inverse_ref, basis_ref,
    partner_ref, other_ref,
    groups, group_sems, pack_sems,
):
    odd = lax.axis_index("sub") % 2
    sides = ((partner_ref, 1 - odd), (other_ref, odd))
    group_copies, packs = [], []
    for k in range(0, VECTORS, GROUP):
        for n, (out_ref, up) in enumerate(sides):
            rows = pl.ds(pl.multiple_of(up * (ROWS - CHUNK), CHUNK), CHUNK)
            for a in range(2):
                group_copies.append(
                    pltpu.make_async_copy(
                        basis_ref.at[pl.ds(k, GROUP), a, rows, :],
                        groups.at[2 * n + a, pl.ds(k, GROUP)],
                        group_sems.at[len(group_copies)],
                    )
                )
    for n, (out_ref, up) in enumerate(sides):
        packs += pack_copies(
            out_ref, up * (ROWS - HALO), rhs_ref, visc_ref, coup_ref, inverse_ref, pack_sems,
            n * pack_count(inverse_ref.shape[1]),
        )
    for copy in group_copies + packs:
        copy.start()

    def take(out_ref, group, first, row):
        for k in range(first, first + GROUP, TILE):
            lines = [groups[group, k + n].astype(jnp.float32)[row : row + 1] for n in range(TILE)]
            at = EDGE_AT + VECTORS * (group % 2) + k
            out_ref[at : at + TILE] = jnp.concatenate(lines, 0)

    for first in range(0, VECTORS, GROUP):
        for _ in range(4):
            group_copies.pop(0).wait()

        @pl.when(odd == 0)
        def _():
            for a in range(2):
                take(partner_ref, a, first, CHUNK - 1)
                take(other_ref, 2 + a, first, 0)

        @pl.when(odd == 1)
        def _():
            for a in range(2):
                take(partner_ref, a, first, 0)
                take(other_ref, 2 + a, first, CHUNK - 1)

    for copy in packs:
        copy.wait()


def restrict_kernel(rhs_ref, held, sums_ref, sums):
    sums[...] = jnp.zeros_like(sums)
    squares = jnp.zeros((TILE, CELLS), jnp.float32)
    for a in range(2):
        for t in range(ROWS // TILE):
            tile = rhs_ref[a, tile_rows(t)]
            squares = squares + tile * tile
    sums[VECTORS : VECTORS + 8] = in_rows([fold(squares)])

    def body(i, carry):
        restrict_piece(i, held, rhs_ref, sums)
        return carry

    lax.fori_loop(0, PIECES, body, 0)
    send_sums(sums, sums_ref)


class Neighbour:
    def __init__(self, first_ref, second_ref):
        self.odd = lax.axis_index("sub") % 2 == 1
        self.first, self.second = first_ref, second_ref

    def __getitem__(self, index):
        return jnp.where(self.odd, self.first[index], self.second[index])


def neighbours_of(partner_ref, other_ref):
    return Neighbour(partner_ref, other_ref), Neighbour(other_ref, partner_ref)


def solve(count, margin_ref, visc_ref, coup_ref, field, low, high, out_ref, stacked, solved, steps):
    waiting, done = list(steps), 0
    every = (SWEEPS - 1) * (STACKED // TILE) // len(waiting)
    rank = lax.axis_index("sub")
    lower = jnp.where(rank > 0, margin_ref[jnp.maximum(rank - 1, 0)], 0)
    upper = jnp.where(rank < count - 1, margin_ref[rank], 0)
    lower_f, upper_f = lower.astype(jnp.float32), upper.astype(jnp.float32)
    low_scale = 1.0 / (2.0 * jnp.maximum(lower_f, 1.0))
    high_scale = 1.0 / (2.0 * jnp.maximum(upper_f, 1.0))
    wide = lambda x: jnp.concatenate([x] * (CELLS // LANES), 1)
    own_tiles = ROWS // TILE
    strip_tiles = STRIP // TILE
    last = own_tiles + 1
    segments = (
        (0, 0, last + 1),
        (last + 1, 0, strip_tiles),
        (last + 1 + strip_tiles, last + 1 - strip_tiles, strip_tiles),
    )

    def place_of(e):
        return lax.broadcasted_iota(jnp.int32, (TILE, LANES), 0) + (TILE * e - HALO)

    def live_of(segment, e):
        place = place_of(e)
        if segment == 0:
            live = (place >= -lower) & (place < ROWS + upper)
        elif segment == 1:
            live = place < lower
        else:
            live = place >= ROWS - upper
        return wide(live.astype(jnp.float32))

    def weight_of(segment, e):
        place = place_of(e)
        place_f = place.astype(jnp.float32)
        rising = lambda base, scale: (place_f - base + 0.5) * scale
        falling = lambda base, scale: (base - place_f - 0.5) * scale
        if segment == 0:
            weight = jnp.where(place < lower, rising(-lower_f, low_scale), 1.0)
            weight = jnp.where(
                place >= ROWS - upper, falling(ROWS + upper_f, high_scale), weight
            )
        elif segment == 1:
            weight = jnp.where(place >= -lower, falling(lower_f, low_scale), 1.0)
        else:
            weight = jnp.where(place < ROWS + upper, rising(ROWS - upper_f, high_scale), 1.0)
        return wide(weight)

    def extended(ref, at, e):
        if e == 0:
            return low[at : at + HALO]
        if e == last:
            return high[at : at + HALO]
        return ref[tile_rows(e - 1)]

    for e in range(last + 1):
        viscosity = extended(visc_ref, 0, e)
        for a in range(2):
            coupling = extended(coup_ref.at[a], HALO * (1 + a), e)
            scale = RELAX / (10.0 * viscosity + jnp.abs(coupling) + 0.05)
            parts = (scale * field(a, e - 1), scale * viscosity, scale * coupling)
            for n, (first, begin, size) in enumerate(segments):
                if not begin <= e < begin + size:
                    continue
                rows = tile_rows(first + e - begin)
                always = n == 0 and 0 < e < last
                for m, part in enumerate(parts):
                    stacked[3 * a + m, rows] = part if always else live_of(n, e) * part

    for sweep in range(1, SWEEPS):
        for n, (first, begin, size) in enumerate(segments):
            end = first + size - 1
            if sweep == 1:
                reads = [lambda t, a=a: stacked[3 * a, tile_rows(t)] for a in range(2)]
            else:
                bank = 2 * (sweep % 2)
                reads = [lambda t, a=a: solved[bank + a, tile_rows(t)] for a in range(2)]
            fields = [Rows(read, first, end) for read in reads]
            for t in range(first, end + 1):
                rows = tile_rows(t)
                if done % every == 0 and waiting:
                    waiting.pop(0)()
                done += 1
                for a in range(2):
                    value = (
                        ((1.0 - RELAX) * fields[a].at(t) + stacked[3 * a, rows])
                        + stacked[3 * a + 1, rows] * neighbours(fields[a], t, a)
                        - stacked[3 * a + 2, rows] * fields[1 - a].at(t)
                    )
                    e = t - first + begin
                    if sweep < SWEEPS - 1:
                        solved[2 * ((sweep + 1) % 2) + a, rows] = value
                    elif n == 0:
                        out_ref[a, tile_rows(e)] = weight_of(n, e) * value
                    else:
                        out_ref[a, tile_rows(e)] += weight_of(n, e) * value


def line_up(residuals):
    devices = residuals.shape[0]
    lane = lax.broadcasted_iota(jnp.int32, (1, LANES), 1)
    tiles = [jnp.zeros((1, LANES), jnp.float32) for _ in range(devices * VECTORS // LANES)]
    for t in range(devices):
        tile, offset = divmod(VECTORS * t, LANES)
        row = jnp.where(lane < VECTORS, residuals[devices - 1 - t : devices - t], 0.0)
        if offset:
            row = pltpu.roll(row, offset, 1)
        if offset + VECTORS <= LANES:
            tiles[tile] = tiles[tile] + row
        else:
            tiles[tile] = tiles[tile] + jnp.where(lane >= offset, row, 0.0)
            tiles[tile + 1] = tiles[tile + 1] + jnp.where(lane < offset, row, 0.0)
    return jnp.concatenate(tiles, 1)


def rounded(column):
    return column.astype(jnp.bfloat16).astype(jnp.float32)


def lift(inverse_ref, residual):
    return rounded(jnp.sum(inverse_ref[...] * residual, 1, keepdims=True))


def lift_packed(ref, residual):
    columns = residual.shape[1]
    at, total = EDGE_AT + INVERSE_AT, None
    for c in range(0, columns - 511, 512):
        term = jnp.sum(ref[at : at + VECTORS] * residual[:, c : c + 512], 1, keepdims=True)
        total = term if total is None else total + term
        at += VECTORS
    if columns % 512:
        half = VECTORS // 2
        last = residual[:, columns - 256 :]
        rows = ref[at : at + half]
        term = jnp.concatenate(
            [
                jnp.sum(rows[:, :256] * last, 1, keepdims=True),
                jnp.sum(rows[:, 256:] * last, 1, keepdims=True),
            ],
            0,
        )
        total = term if total is None else total + term
    return rounded(total)


def edge_values(ref, lifted):
    starts = [EDGE_AT + VECTORS * a for a in range(2)]
    return [jnp.sum(ref[at : at + VECTORS] * lifted, 0, keepdims=True) for at in starts]


def spread(lifted):
    shape = (VECTORS, CHUNK * VECTORS)
    owner = lax.broadcasted_iota(jnp.int32, shape, 1) // CHUNK
    row = lax.broadcasted_iota(jnp.int32, shape, 0)
    line = jnp.sum(jnp.where(owner == row, lifted, 0.0), 0, keepdims=True)
    shape = (CHUNK, CHUNK * VECTORS)
    place = lax.broadcasted_iota(jnp.int32, shape, 1) % CHUNK
    row = lax.broadcasted_iota(jnp.int32, shape, 0)
    return jnp.where(place == row, line, 0.0).astype(jnp.bfloat16)


def prolonging(residual, inverse_ref, held, extended):
    matrix = spread(lift(inverse_ref, residual))

    def step(a, r):
        rows = held[:, a, r : r + CHUNK, :].reshape(CHUNK * VECTORS, CELLS)
        extended[a, HALO + r : HALO + r + CHUNK] = jnp.dot(
            matrix, rows, preferred_element_type=jnp.float32
        )

    return [functools.partial(step, a, r) for a in range(2) for r in range(0, ROWS, CHUNK)]


def apply_operator(residual, low, high, smooth, extended, visc_ref, coup_ref, direction_ref):
    edges = [edge_values(side, lift_packed(side, residual)) for side in (low, high)]
    place = lax.broadcasted_iota(jnp.int32, (TILE, CELLS), 0)
    tiles = ROWS // TILE

    def read(t, a):
        if t < 0:
            return smooth(a, 0) + jnp.where(place == TILE - 1, edges[0][a], 0.0)
        if t == tiles:
            return smooth(a, t + 1) + jnp.where(place == 0, edges[1][a], 0.0)
        tile = smooth(a, t + 1) + extended[a, tile_rows(t + 1)]
        direction_ref[a, tile_rows(t)] = tile
        return tile

    fields = [Rows(lambda t, a=a: read(t, a), -1, tiles) for a in range(2)]
    for t in range(tiles):
        rows = tile_rows(t)
        viscosity = visc_ref[rows]
        for a in range(2):
            coupling = coup_ref[a, rows]
            diagonal = 10.0 * viscosity + jnp.abs(coupling) + 0.05
            image = (
                diagonal * fields[a].at(t)
                - viscosity * neighbours(fields[a], t, a)
                + coupling * fields[1 - a].at(t)
            )
            yield t, a, image


def lane_total(received, lane):
    return jnp.sum(received[:, lane : lane + 1], 0, keepdims=True)


def first_turn_kernel(
    count, margin_ref, sums_ref, inverse_ref, partner_ref, other_ref, held, rhs_ref, visc_ref,
    coup_ref,
    direction_ref, image_ref, smooth_ref, partner_rows_ref, other_rows_ref, next_ref,
    extended, sums, stacked, solved,
):
    received = sums_ref[...]
    over_beta = 1.0 / jnp.sqrt(lane_total(received, VECTORS))
    residual = line_up(received) * over_beta
    steps = prolonging(residual, inverse_ref, held, extended)
    low, high = neighbours_of(partner_ref, other_ref)

    def field(a, t):
        at = HALO * (3 + a)
        if t < 0:
            return low[at : at + HALO]
        return high[at : at + HALO] if t == ROWS // TILE else rhs_ref[a, tile_rows(t)]

    solve(
        count, margin_ref, visc_ref, coup_ref, field, low, high, smooth_ref, stacked, solved,
        steps,
    )
    smooth = lambda a, t: smooth_ref[a, tile_rows(t)] * over_beta
    images = apply_operator(
        residual, low, high, smooth, extended, visc_ref, coup_ref, direction_ref
    )
    odd = lax.axis_index("sub") % 2 == 1
    products, squares = [jnp.zeros((TILE, CELLS), jnp.float32)] * 2
    heads, tails = [None] * 2, [None] * 2
    for t, a, image in images:
        image_ref[a, tile_rows(t)] = image
        products = products + rhs_ref[a, tile_rows(t)] * image
        squares = squares + image * image
        if t == 0:
            heads[a] = image
        if t == ROWS // TILE - 1:
            tails[a] = image
    half = lax.broadcasted_iota(jnp.int32, (TILE, CELLS), 0) < TILE // 2
    head = jnp.where(half, heads[0], pltpu.roll(heads[1], TILE // 2, 0))
    tail = jnp.where(half, pltpu.roll(tails[1], TILE // 2, 0), tails[0])
    partner_rows_ref[...] = jnp.where(odd, head, tail)
    other_rows_ref[...] = jnp.where(odd, tail, head)
    sums[...] = jnp.zeros_like(sums)
    sums[VECTORS : VECTORS + 8] = in_rows([fold(products), fold(squares)])

    def body(i, carry):
        restrict_piece(i, held, image_ref, sums)
        return carry

    lax.fori_loop(0, PIECES, body, 0)
    send_sums(sums, next_ref)


def first_column(first, second):
    beta = jnp.sqrt(lane_total(first, VECTORS))
    h_00 = lane_total(second, VECTORS) / beta
    h_10 = jnp.sqrt(lane_total(second, VECTORS + 1) - h_00 * h_00)
    return beta, h_00, h_10


def second_turn_kernel(
    count, margin_ref, first_ref, second_ref, inverse_ref, partner_ref, other_ref,
    partner_rows_ref, other_rows_ref, held, smooth_ref, rhs_ref, image_ref, visc_ref, coup_ref,
    direction_ref, next_ref,
    image_smooth, extended, sums, stacked, solved,
):
    first, second = first_ref[...], second_ref[...]
    beta, h_00, h_10 = first_column(first, second)
    ratio = h_00 / beta
    over = 1.0 / h_10
    residual = (line_up(second) - ratio * line_up(first)) * over
    steps = prolonging(residual, inverse_ref, held, extended)
    low, high = neighbours_of(partner_ref, other_ref)
    low_rows, high_rows = neighbours_of(partner_rows_ref, other_rows_ref)

    def field(a, t):
        if 0 <= t < ROWS // TILE:
            return image_ref[a, tile_rows(t)]
        rows = low_rows[...] if t < 0 else high_rows[...]
        return pltpu.roll(rows, TILE // 2, 0) if a else rows

    solve(
        count, margin_ref, visc_ref, coup_ref, field, low, high, image_smooth, stacked, solved,
        steps,
    )

    def smooth(a, t):
        rows = tile_rows(t)
        return (image_smooth[a, rows] - ratio * smooth_ref[a, rows]) * over

    images = apply_operator(
        residual, low, high, smooth, extended, visc_ref, coup_ref, direction_ref
    )
    totals = [jnp.zeros((TILE, CELLS), jnp.float32)] * 3
    for t, a, image in images:
        others = (rhs_ref[a, tile_rows(t)], image_ref[a, tile_rows(t)], image)
        totals = [total + x * image for total, x in zip(totals, others)]
    sums[...] = jnp.zeros_like(sums)
    sums[:8] = in_rows([fold(total) for total in totals])
    send_sums(sums, next_ref)


def finish_kernel(
    first_ref, second_ref, third_ref, first_direction_ref, second_direction_ref,
    solution_ref, hessenberg_ref,
):
    third = third_ref[...]
    beta, h_00, h_10 = first_column(first_ref[...], second_ref[...])
    squares = lane_total(third, 2)
    h_01 = lane_total(third, 0) / beta
    h_11 = (lane_total(third, 1) - h_00 * h_01) / h_10
    h_21 = jnp.sqrt(squares - h_01 * h_01 - h_11 * h_11)
    l_00 = jnp.sqrt(h_00 * h_00 + h_10 * h_10)
    l_10 = (h_00 * h_01 + h_10 * h_11) / l_00
    f_0 = beta * h_00 / l_00
    c_1 = (beta * h_01 - l_10 * f_0) / (squares - l_10 * l_10)
    c_0 = (f_0 - l_10 * c_1) / l_00
    for a in range(2):
        solution_ref[a] = c_0 * first_direction_ref[a] + c_1 * second_direction_ref[a]
    shape = hessenberg_ref.shape
    row = lax.broadcasted_iota(jnp.int32, shape, 1)
    column = lax.broadcasted_iota(jnp.int32, shape, 0)
    entries = jnp.zeros(shape, jnp.float32)
    for i, j, value in ((0, 0, h_00), (0, 1, h_01), (1, 0, h_10), (1, 1, h_11), (2, 1, h_21)):
        entries = jnp.where((row == i) & (column == j), value, entries)
    hessenberg_ref[...] = entries


def call(kernel, name, in_specs, outs, flops, scratch=(), traffic=4_000_000):
    return pl.pallas_call(
        kernel,
        name=name,
        in_specs=in_specs,
        out_specs=[VMEM] * len(outs),
        out_shape=outs,
        scratch_shapes=scratch,
        compiler_params=pltpu.CompilerParams(vmem_limit_bytes=16 * 1024 * 1024),
        cost_estimate=pl.CostEstimate(flops=flops, bytes_accessed=traffic, transcendentals=0),
    )


def in_hbm(array):
    return pltpu.with_memory_space_constraint(array, pltpu.HBM)


def from_everyone(rows):
    order = [list(range(lax.axis_size("sub")))[::-1]]
    return lax.all_to_all(rows, "sub", 0, 0, tiled=True, axis_index_groups=order)


def swap(partner, other):
    count = lax.axis_size("sub")
    both = lambda lows: [pair for i in lows for pair in ((i, i + 1), (i + 1, i))]
    return (
        lax.ppermute(partner, "sub", both(range(0, count, 2))),
        lax.ppermute(other, "sub", both(range(1, count - 1, 2))),
    )


def on_device(rhs, viscosity, coupling, margin_rows, coarse_basis, coarse_inverse):
    count = lax.axis_size("sub")
    columns = coarse_inverse.shape[1]
    f32 = lambda *shape: jax.ShapeDtypeStruct(shape, jnp.float32)
    dma = lambda *shape: pltpu.SemaphoreType.DMA(shape)
    extended = pltpu.VMEM((2, EXT, CELLS), jnp.float32)
    stacked = pltpu.VMEM((6, STACKED, CELLS), jnp.float32)
    solved = pltpu.VMEM((4, STACKED, CELLS), jnp.float32)
    sums = pltpu.VMEM((SLOTS, LANES), jnp.float32)
    row, whole, edge = f32(count, LANES), f32(2, ROWS, CELLS), f32(TILE, CELLS)
    packed, smoothed = f32(EDGE_AT + coarse_rows(columns), CELLS), f32(2, EXT, CELLS)
    arguments = (rhs, viscosity, coupling, coarse_inverse, coarse_basis)
    packs = call(
        pack_kernel, "pack", [HBM] * 5, [packed, packed], 5_000_000,
        [pltpu.VMEM((4, VECTORS, CHUNK, CELLS), jnp.bfloat16), dma(4 * VECTORS // GROUP)]
        + [dma(2 * pack_count(columns))],
    )(*map(in_hbm, arguments))
    held, partner, other = lax.optimization_barrier((coarse_basis, *packs))
    partner, other = swap(partner, other)
    (first,) = call(
        restrict_kernel, "restrict", [VMEM] * 2, [row], 10_000_000, [sums]
    )(rhs, held)
    first = from_everyone(first)
    direction, image, smooth, partner_rows, other_rows, second = call(
        functools.partial(first_turn_kernel, count), "first_turn", [SMEM] + [VMEM] * 8,
        [whole, whole, smoothed, edge, edge, row], 20_000_000, [extended, sums, stacked, solved],
    )(margin_rows, first, coarse_inverse, partner, other, held, rhs, viscosity, coupling)
    partner_rows, other_rows = swap(partner_rows, other_rows)
    second = from_everyone(second)
    second_direction, third = call(
        functools.partial(second_turn_kernel, count), "second_turn", [SMEM] + [VMEM] * 13,
        [whole, row], 20_000_000, [extended, extended, sums, stacked, solved],
    )(
        margin_rows, first, second, coarse_inverse, partner, other, partner_rows, other_rows,
        held, smooth, rhs, image, viscosity, coupling,
    )
    third = from_everyone(third)
    result, transposed = call(finish_kernel, "finish", [VMEM] * 5, [whole, f32(2, 3)], 1_000_000)(
        first, second, third, direction, second_direction
    )
    return result, transposed.T


def solution(mesh):
    in_specs = (
        P(None, ("groups", "sub"), None),
        P(("groups", "sub"), None),
        P(None, ("groups", "sub"), None),
        P("groups"),
        P(None, None, ("groups", "sub"), None),
        P(("groups", "sub"), None),
    )
    out_specs = (P(None, ("groups", "sub"), None), P("groups", None))
    return jax.shard_map(
        on_device, mesh=mesh, in_specs=in_specs, out_specs=out_specs, check_vma=False
    )
```

```python
import functools

import jax
import jax.numpy as jnp
from jax import lax
from jax.experimental import pallas as pl
from jax.experimental.pallas import tpu as pltpu
from jax.sharding import PartitionSpec as P

ROWS = 64
CELLS = 512
VECTORS = 48
HALO = 8
EXT = ROWS + 2 * HALO
STRIP = 32
GROUP = 16
STACKED = EXT + 2 * STRIP
TILE = 8
CHUNK = 16
CHUNKS = 2 * ROWS // CHUNK
PIECE = 8
LANES = 128
SLOTS = 64
EDGE_AT = 5 * HALO
INVERSE_AT = 2 * VECTORS
SWEEPS = 4
RELAX = 0.7
ROW_FACTOR = (1.0, 4.0)
CELL_FACTOR = (4.0, 1.0)

VMEM = pl.BlockSpec(memory_space=pltpu.VMEM)
SMEM = pl.BlockSpec(memory_space=pltpu.SMEM)
HBM = pl.BlockSpec(memory_space=pltpu.HBM)


def coarse_rows(columns):
    return INVERSE_AT + VECTORS * (columns // 512) + (VECTORS // 2) * (columns % 512 // 256)


def cell_sum(field):
    lane = lax.broadcasted_iota(jnp.int32, (field.shape[0], LANES), 1)
    left, right = pltpu.roll(field, 1, 1), pltpu.roll(field, CELLS - 1, 1)
    inner = left[:, LANES:-LANES] + right[:, LANES:-LANES]
    first = jnp.where(lane == 0, 0.0, left[:, :LANES]) + right[:, :LANES]
    last = left[:, -LANES:] + jnp.where(lane == LANES - 1, 0.0, right[:, -LANES:])
    return jnp.concatenate([first, inner, last], 1)


class Rows:
    def __init__(self, read, first, last):
        self.read, self.first, self.last = read, first, last
        self.tiles, self.down, self.up = {}, {}, {}

    def at(self, t):
        if t not in self.tiles:
            self.tiles[t] = self.read(t)
        return self.tiles[t]

    def moved(self, held, t, by):
        if t not in held:
            held[t] = pltpu.roll(self.at(t), by, 0)
        return held[t]

    def around(self, t):
        row = lax.broadcasted_iota(jnp.int32, (TILE, CELLS), 0)
        below, above = self.moved(self.down, t, 1), self.moved(self.up, t, TILE - 1)
        if t > self.first:
            below = jnp.where(row == 0, self.moved(self.down, t - 1, 1), below)
        if t < self.last:
            above = jnp.where(row == TILE - 1, self.moved(self.up, t + 1, TILE - 1), above)
        return below + above


def neighbours(rows, t, component):
    around, cells = rows.around(t), cell_sum(rows.at(t))
    if component == 0:
        return around + CELL_FACTOR[0] * cells
    return ROW_FACTOR[1] * around + cells


def sublane_sum(tile):
    for by in (4, 2, 1):
        tile = tile + pltpu.roll(tile, by, 0)
    return tile


def in_rows(tiles):
    row = lax.broadcasted_iota(jnp.int32, (8, LANES), 0)
    total = jnp.zeros((8, LANES), jnp.float32)
    for n, tile in enumerate(tiles):
        total = jnp.where(row == n, sublane_sum(tile), total)
    return total


MATRIX_GROUPS = tuple((1, r) for r in range(CHUNK, ROWS, CHUNK))
VECTOR_GROUPS = ((0, 0), (0, 16), (0, 32), (0, 48), (1, 0))


def restrict(held, field, sums, lines):
    lines[2 * CHUNK :] = jnp.zeros((LANES - 2 * CHUNK, lines.shape[1]), jnp.bfloat16)
    blocks = []
    for g, (a, r) in enumerate(MATRIX_GROUPS):
        part, cells = field[a, r : r + CHUNK], slice(CELLS * g, CELLS * (g + 1))
        high = part.astype(jnp.bfloat16)
        lines[:CHUNK, cells] = high
        lines[CHUNK : 2 * CHUNK, cells] = (part - high.astype(jnp.float32)).astype(jnp.bfloat16)
        blocks.append(held[:, a, r : r + CHUNK, :].reshape(CHUNK * VECTORS, CELLS))
    products = lax.dot_general(
        jnp.concatenate(blocks, 1),
        lines[...],
        (((1,), (1,)), ((), ())),
        preferred_element_type=jnp.float32,
    )
    row = lax.broadcasted_iota(jnp.int32, (CHUNK, LANES), 0)
    equal = row == lax.broadcasted_iota(jnp.int32, (CHUNK, LANES), 1) % CHUNK
    for first in range(0, VECTORS, PIECE):
        totals = [
            jnp.where(equal, products[CHUNK * k : CHUNK * (k + 1)], 0.0)
            for k in range(first, first + PIECE)
        ]
        for a, r in VECTOR_GROUPS:
            for c in range(0, CELLS, LANES):
                rows, cells = slice(r, r + CHUNK), slice(c, c + LANES)
                tile = field[a, rows, cells]
                for n in range(PIECE):
                    term = held[first + n, a, rows, cells].astype(jnp.float32) * tile
                    totals[n] = totals[n] + term
        sums[first : first + PIECE] = in_rows([total[:8] + total[8:] for total in totals])


def fold(row):
    total = row[:, :LANES]
    for c in range(LANES, CELLS, LANES):
        total = total + row[:, c : c + LANES]
    return total


def tile_rows(t):
    return slice(TILE * t, TILE * (t + 1))


def send_sums(sums, out_ref):
    rest = sums[...]
    parts = []
    for _ in range(3):
        part = rest.astype(jnp.bfloat16)
        parts.append(part)
        rest = rest - part.astype(jnp.float32)
    row = lax.dot_general(
        jnp.ones((CHUNK, 3 * LANES), jnp.bfloat16),
        jnp.concatenate(parts, 1),
        (((1,), (1,)), ((), ())),
        preferred_element_type=jnp.float32,
    )
    wide = jnp.concatenate([row[:1], jnp.zeros((1, LANES - SLOTS), jnp.float32)], 1)
    out_ref[...] = jnp.broadcast_to(wide, out_ref.shape)


def pack_copies(out_ref, first_row, rhs_ref, visc_ref, coup_ref, inverse_ref, sems, at_sem):
    rows = pl.ds(pl.multiple_of(first_row, HALO), HALO)
    moves = [(visc_ref.at[rows, :], 0, HALO, None)]
    for a in range(2):
        moves.append((coup_ref.at[a, rows, :], HALO * (1 + a), HALO, None))
        moves.append((rhs_ref.at[a, rows, :], HALO * (3 + a), HALO, None))
    columns = inverse_ref.shape[1]
    at = EDGE_AT + INVERSE_AT
    for c in range(0, columns - 511, 512):
        moves.append((inverse_ref.at[:, pl.ds(c, 512)], at, VECTORS, None))
        at += VECTORS
    if columns % 512:
        half = VECTORS // 2
        last = pl.ds(columns - 256, 256)
        moves.append((inverse_ref.at[pl.ds(0, half), last], at, half, 0))
        moves.append((inverse_ref.at[pl.ds(half, half), last], at, half, 256))
    copies = []
    for n, (source, at, size, lane) in enumerate(moves):
        place = pl.ds(at, size)
        target = out_ref.at[place, :] if lane is None else out_ref.at[place, pl.ds(lane, 256)]
        copies.append(pltpu.make_async_copy(source, target, sems.at[at_sem + n]))
    return copies


def pack_count(columns):
    return 5 + columns // 512 + 2 * (columns % 512 // 256)


def pack_kernel(
    rhs_ref, visc_ref, coup_ref, inverse_ref, basis_ref,
    partner_ref, other_ref,
    groups, group_sems, pack_sems,
):
    odd = lax.axis_index("sub") % 2
    sides = ((partner_ref, 1 - odd), (other_ref, odd))
    group_copies, packs = [], []
    for k in range(0, VECTORS, GROUP):
        for n, (out_ref, up) in enumerate(sides):
            rows = pl.ds(pl.multiple_of(up * (ROWS - CHUNK), CHUNK), CHUNK)
            for a in range(2):
                group_copies.append(
                    pltpu.make_async_copy(
                        basis_ref.at[pl.ds(k, GROUP), a, rows, :],
                        groups.at[2 * n + a, pl.ds(k, GROUP)],
                        group_sems.at[len(group_copies)],
                    )
                )
    for n, (out_ref, up) in enumerate(sides):
        packs += pack_copies(
            out_ref, up * (ROWS - HALO), rhs_ref, visc_ref, coup_ref, inverse_ref, pack_sems,
            n * pack_count(inverse_ref.shape[1]),
        )
    for copy in group_copies + packs:
        copy.start()

    def take(out_ref, group, first, row):
        for k in range(first, first + GROUP, TILE):
            lines = [groups[group, k + n].astype(jnp.float32)[row : row + 1] for n in range(TILE)]
            at = EDGE_AT + VECTORS * (group % 2) + k
            out_ref[at : at + TILE] = jnp.concatenate(lines, 0)

    for first in range(0, VECTORS, GROUP):
        for _ in range(4):
            group_copies.pop(0).wait()

        @pl.when(odd == 0)
        def _():
            for a in range(2):
                take(partner_ref, a, first, CHUNK - 1)
                take(other_ref, 2 + a, first, 0)

        @pl.when(odd == 1)
        def _():
            for a in range(2):
                take(partner_ref, a, first, 0)
                take(other_ref, 2 + a, first, CHUNK - 1)

    for copy in packs:
        copy.wait()


def restrict_kernel(rhs_ref, held, sums_ref, sums, lines):
    sums[...] = jnp.zeros_like(sums)
    squares = jnp.zeros((TILE, CELLS), jnp.float32)
    for a in range(2):
        for t in range(ROWS // TILE):
            tile = rhs_ref[a, tile_rows(t)]
            squares = squares + tile * tile
    sums[VECTORS : VECTORS + 8] = in_rows([fold(squares)])

    restrict(held, rhs_ref, sums, lines)
    send_sums(sums, sums_ref)


class Neighbour:
    def __init__(self, first_ref, second_ref):
        self.odd = lax.axis_index("sub") % 2 == 1
        self.first, self.second = first_ref, second_ref

    def __getitem__(self, index):
        return jnp.where(self.odd, self.first[index], self.second[index])


def neighbours_of(partner_ref, other_ref):
    return Neighbour(partner_ref, other_ref), Neighbour(other_ref, partner_ref)


def solve(count, margin_ref, visc_ref, coup_ref, field, low, high, out_ref, stacked, solved, steps):
    waiting, done = list(steps), 0
    every = (SWEEPS - 1) * (STACKED // TILE) // len(waiting)
    rank = lax.axis_index("sub")
    lower = jnp.where(rank > 0, margin_ref[jnp.maximum(rank - 1, 0)], 0)
    upper = jnp.where(rank < count - 1, margin_ref[rank], 0)
    lower_f, upper_f = lower.astype(jnp.float32), upper.astype(jnp.float32)
    low_scale = 1.0 / (2.0 * jnp.maximum(lower_f, 1.0))
    high_scale = 1.0 / (2.0 * jnp.maximum(upper_f, 1.0))
    wide = lambda x: jnp.concatenate([x] * (CELLS // LANES), 1)
    own_tiles = ROWS // TILE
    strip_tiles = STRIP // TILE
    last = own_tiles + 1
    segments = (
        (0, 0, last + 1),
        (last + 1, 0, strip_tiles),
        (last + 1 + strip_tiles, last + 1 - strip_tiles, strip_tiles),
    )

    def place_of(e):
        return lax.broadcasted_iota(jnp.int32, (TILE, LANES), 0) + (TILE * e - HALO)

    def live_of(segment, e):
        place = place_of(e)
        if segment == 0:
            live = (place >= -lower) & (place < ROWS + upper)
        elif segment == 1:
            live = place < lower
        else:
            live = place >= ROWS - upper
        return wide(live.astype(jnp.float32))

    def weight_of(segment, e):
        place = place_of(e)
        place_f = place.astype(jnp.float32)
        rising = lambda base, scale: (place_f - base + 0.5) * scale
        falling = lambda base, scale: (base - place_f - 0.5) * scale
        if segment == 0:
            weight = jnp.where(place < lower, rising(-lower_f, low_scale), 1.0)
            weight = jnp.where(
                place >= ROWS - upper, falling(ROWS + upper_f, high_scale), weight
            )
        elif segment == 1:
            weight = jnp.where(place >= -lower, falling(lower_f, low_scale), 1.0)
        else:
            weight = jnp.where(place < ROWS + upper, rising(ROWS - upper_f, high_scale), 1.0)
        return wide(weight)

    def extended(ref, at, e):
        if e == 0:
            return low[at : at + HALO]
        if e == last:
            return high[at : at + HALO]
        return ref[tile_rows(e - 1)]

    for e in range(last + 1):
        viscosity = extended(visc_ref, 0, e)
        for a in range(2):
            coupling = extended(coup_ref.at[a], HALO * (1 + a), e)
            scale = RELAX / (10.0 * viscosity + jnp.abs(coupling) + 0.05)
            parts = (scale * field(a, e - 1), scale * viscosity, scale * coupling)
            for n, (first, begin, size) in enumerate(segments):
                if not begin <= e < begin + size:
                    continue
                rows = tile_rows(first + e - begin)
                always = n == 0 and 0 < e < last
                for m, part in enumerate(parts):
                    stacked[3 * a + m, rows] = part if always else live_of(n, e) * part

    for sweep in range(1, SWEEPS):
        for n, (first, begin, size) in enumerate(segments):
            end = first + size - 1
            if sweep == 1:
                reads = [lambda t, a=a: stacked[3 * a, tile_rows(t)] for a in range(2)]
            else:
                bank = 2 * (sweep % 2)
                reads = [lambda t, a=a: solved[bank + a, tile_rows(t)] for a in range(2)]
            fields = [Rows(read, first, end) for read in reads]
            for t in range(first, end + 1):
                rows = tile_rows(t)
                if done % every == 0 and waiting:
                    waiting.pop(0)()
                done += 1
                for a in range(2):
                    value = (
                        ((1.0 - RELAX) * fields[a].at(t) + stacked[3 * a, rows])
                        + stacked[3 * a + 1, rows] * neighbours(fields[a], t, a)
                        - stacked[3 * a + 2, rows] * fields[1 - a].at(t)
                    )
                    e = t - first + begin
                    if sweep < SWEEPS - 1:
                        solved[2 * ((sweep + 1) % 2) + a, rows] = value
                    elif n == 0:
                        out_ref[a, tile_rows(e)] = weight_of(n, e) * value
                    else:
                        out_ref[a, tile_rows(e)] += weight_of(n, e) * value


def line_up(residuals):
    devices = residuals.shape[0]
    lane = lax.broadcasted_iota(jnp.int32, (1, LANES), 1)
    tiles = [jnp.zeros((1, LANES), jnp.float32) for _ in range(devices * VECTORS // LANES)]
    for t in range(devices):
        tile, offset = divmod(VECTORS * t, LANES)
        row = jnp.where(lane < VECTORS, residuals[devices - 1 - t : devices - t], 0.0)
        if offset:
            row = pltpu.roll(row, offset, 1)
        if offset + VECTORS <= LANES:
            tiles[tile] = tiles[tile] + row
        else:
            tiles[tile] = tiles[tile] + jnp.where(lane >= offset, row, 0.0)
            tiles[tile + 1] = tiles[tile + 1] + jnp.where(lane < offset, row, 0.0)
    return jnp.concatenate(tiles, 1)


def rounded(column):
    return column.astype(jnp.bfloat16).astype(jnp.float32)


def lift(inverse_ref, residual):
    return rounded(jnp.sum(inverse_ref[...] * residual, 1, keepdims=True))


def lift_packed(ref, residual):
    columns = residual.shape[1]
    at, total = EDGE_AT + INVERSE_AT, None
    for c in range(0, columns - 511, 512):
        term = jnp.sum(ref[at : at + VECTORS] * residual[:, c : c + 512], 1, keepdims=True)
        total = term if total is None else total + term
        at += VECTORS
    if columns % 512:
        half = VECTORS // 2
        last = residual[:, columns - 256 :]
        rows = ref[at : at + half]
        term = jnp.concatenate(
            [
                jnp.sum(rows[:, :256] * last, 1, keepdims=True),
                jnp.sum(rows[:, 256:] * last, 1, keepdims=True),
            ],
            0,
        )
        total = term if total is None else total + term
    return rounded(total)


def edge_values(ref, lifted):
    starts = [EDGE_AT + VECTORS * a for a in range(2)]
    return [jnp.sum(ref[at : at + VECTORS] * lifted, 0, keepdims=True) for at in starts]


def spread(lifted):
    shape = (VECTORS, CHUNK * VECTORS)
    owner = lax.broadcasted_iota(jnp.int32, shape, 1) // CHUNK
    row = lax.broadcasted_iota(jnp.int32, shape, 0)
    line = jnp.sum(jnp.where(owner == row, lifted, 0.0), 0, keepdims=True)
    shape = (CHUNK, CHUNK * VECTORS)
    place = lax.broadcasted_iota(jnp.int32, shape, 1) % CHUNK
    row = lax.broadcasted_iota(jnp.int32, shape, 0)
    return jnp.where(place == row, line, 0.0).astype(jnp.bfloat16)


def prolonging(residual, inverse_ref, held, extended):
    matrix = spread(lift(inverse_ref, residual))

    def step(a, r):
        rows = held[:, a, r : r + CHUNK, :].reshape(CHUNK * VECTORS, CELLS)
        extended[a, HALO + r : HALO + r + CHUNK] = jnp.dot(
            matrix, rows, preferred_element_type=jnp.float32
        )

    return [functools.partial(step, a, r) for a in range(2) for r in range(0, ROWS, CHUNK)]


def apply_operator(residual, low, high, smooth, extended, visc_ref, coup_ref, direction_ref):
    edges = [edge_values(side, lift_packed(side, residual)) for side in (low, high)]
    place = lax.broadcasted_iota(jnp.int32, (TILE, CELLS), 0)
    tiles = ROWS // TILE

    def read(t, a):
        if t < 0:
            return smooth(a, 0) + jnp.where(place == TILE - 1, edges[0][a], 0.0)
        if t == tiles:
            return smooth(a, t + 1) + jnp.where(place == 0, edges[1][a], 0.0)
        tile = smooth(a, t + 1) + extended[a, tile_rows(t + 1)]
        direction_ref[a, tile_rows(t)] = tile
        return tile

    fields = [Rows(lambda t, a=a: read(t, a), -1, tiles) for a in range(2)]
    for t in range(tiles):
        rows = tile_rows(t)
        viscosity = visc_ref[rows]
        for a in range(2):
            coupling = coup_ref[a, rows]
            diagonal = 10.0 * viscosity + jnp.abs(coupling) + 0.05
            image = (
                diagonal * fields[a].at(t)
                - viscosity * neighbours(fields[a], t, a)
                + coupling * fields[1 - a].at(t)
            )
            yield t, a, image


def lane_total(received, lane):
    return jnp.sum(received[:, lane : lane + 1], 0, keepdims=True)


def first_turn_kernel(
    count, margin_ref, sums_ref, inverse_ref, partner_ref, other_ref, held, rhs_ref, visc_ref,
    coup_ref,
    direction_ref, image_ref, smooth_ref, residual_ref, partner_rows_ref, other_rows_ref, next_ref,
    extended, sums, stacked, solved, lines,
):
    received = sums_ref[...]
    over_beta = 1.0 / jnp.sqrt(lane_total(received, VECTORS))
    residual = line_up(received) * over_beta
    residual_ref[...] = residual
    steps = prolonging(residual, inverse_ref, held, extended)
    low, high = neighbours_of(partner_ref, other_ref)

    def field(a, t):
        at = HALO * (3 + a)
        if t < 0:
            return low[at : at + HALO]
        return high[at : at + HALO] if t == ROWS // TILE else rhs_ref[a, tile_rows(t)]

    solve(
        count, margin_ref, visc_ref, coup_ref, field, low, high, smooth_ref, stacked, solved,
        steps,
    )
    smooth = lambda a, t: smooth_ref[a, tile_rows(t)] * over_beta
    images = apply_operator(
        residual, low, high, smooth, extended, visc_ref, coup_ref, direction_ref
    )
    odd = lax.axis_index("sub") % 2 == 1
    products, squares = [jnp.zeros((TILE, CELLS), jnp.float32)] * 2
    heads, tails = [None] * 2, [None] * 2
    for t, a, image in images:
        image_ref[a, tile_rows(t)] = image
        products = products + rhs_ref[a, tile_rows(t)] * image
        squares = squares + image * image
        if t == 0:
            heads[a] = image
        if t == ROWS // TILE - 1:
            tails[a] = image
    half = lax.broadcasted_iota(jnp.int32, (TILE, CELLS), 0) < TILE // 2
    head = jnp.where(half, heads[0], pltpu.roll(heads[1], TILE // 2, 0))
    tail = jnp.where(half, pltpu.roll(tails[1], TILE // 2, 0), tails[0])
    partner_rows_ref[...] = jnp.where(odd, head, tail)
    other_rows_ref[...] = jnp.where(odd, tail, head)
    sums[...] = jnp.zeros_like(sums)
    sums[VECTORS : VECTORS + 8] = in_rows([fold(products), fold(squares)])

    restrict(held, image_ref, sums, lines)
    send_sums(sums, next_ref)


def first_column(first, second):
    beta = jnp.sqrt(lane_total(first, VECTORS))
    h_00 = lane_total(second, VECTORS) / beta
    h_10 = jnp.sqrt(lane_total(second, VECTORS + 1) - h_00 * h_00)
    return beta, h_00, h_10


def second_turn_kernel(
    count, margin_ref, first_ref, second_ref, residual_ref, inverse_ref, partner_ref, other_ref,
    partner_rows_ref, other_rows_ref, held, smooth_ref, rhs_ref, image_ref, visc_ref, coup_ref,
    direction_ref, next_ref,
    image_smooth, extended, sums, stacked, solved,
):
    first, second = first_ref[...], second_ref[...]
    beta, h_00, h_10 = first_column(first, second)
    ratio = h_00 / beta
    over = 1.0 / h_10
    residual = (line_up(second) - h_00 * residual_ref[...]) * over
    steps = prolonging(residual, inverse_ref, held, extended)
    low, high = neighbours_of(partner_ref, other_ref)
    low_rows, high_rows = neighbours_of(partner_rows_ref, other_rows_ref)

    def field(a, t):
        if 0 <= t < ROWS // TILE:
            return image_ref[a, tile_rows(t)]
        rows = low_rows[...] if t < 0 else high_rows[...]
        return pltpu.roll(rows, TILE // 2, 0) if a else rows

    solve(
        count, margin_ref, visc_ref, coup_ref, field, low, high, image_smooth, stacked, solved,
        steps,
    )

    def smooth(a, t):
        rows = tile_rows(t)
        return (image_smooth[a, rows] - ratio * smooth_ref[a, rows]) * over

    images = apply_operator(
        residual, low, high, smooth, extended, visc_ref, coup_ref, direction_ref
    )
    totals = [jnp.zeros((TILE, CELLS), jnp.float32)] * 3
    for t, a, image in images:
        others = (rhs_ref[a, tile_rows(t)], image_ref[a, tile_rows(t)], image)
        totals = [total + x * image for total, x in zip(totals, others)]
    sums[...] = jnp.zeros_like(sums)
    sums[:8] = in_rows([fold(total) for total in totals])
    send_sums(sums, next_ref)


def finish_kernel(
    first_ref, second_ref, third_ref, first_direction_ref, second_direction_ref,
    solution_ref, hessenberg_ref,
):
    third = third_ref[...]
    beta, h_00, h_10 = first_column(first_ref[...], second_ref[...])
    squares = lane_total(third, 2)
    h_01 = lane_total(third, 0) / beta
    h_11 = (lane_total(third, 1) - h_00 * h_01) / h_10
    h_21 = jnp.sqrt(squares - h_01 * h_01 - h_11 * h_11)
    l_00 = jnp.sqrt(h_00 * h_00 + h_10 * h_10)
    l_10 = (h_00 * h_01 + h_10 * h_11) / l_00
    f_0 = beta * h_00 / l_00
    c_1 = (beta * h_01 - l_10 * f_0) / (squares - l_10 * l_10)
    c_0 = (f_0 - l_10 * c_1) / l_00
    for a in range(2):
        solution_ref[a] = c_0 * first_direction_ref[a] + c_1 * second_direction_ref[a]
    shape = hessenberg_ref.shape
    row = lax.broadcasted_iota(jnp.int32, shape, 1)
    column = lax.broadcasted_iota(jnp.int32, shape, 0)
    entries = jnp.zeros(shape, jnp.float32)
    for i, j, value in ((0, 0, h_00), (0, 1, h_01), (1, 0, h_10), (1, 1, h_11), (2, 1, h_21)):
        entries = jnp.where((row == i) & (column == j), value, entries)
    hessenberg_ref[...] = entries


def call(kernel, name, in_specs, outs, flops, scratch=(), traffic=4_000_000):
    return pl.pallas_call(
        kernel,
        name=name,
        in_specs=in_specs,
        out_specs=[VMEM] * len(outs),
        out_shape=outs,
        scratch_shapes=scratch,
        compiler_params=pltpu.CompilerParams(vmem_limit_bytes=16 * 1024 * 1024),
        cost_estimate=pl.CostEstimate(flops=flops, bytes_accessed=traffic, transcendentals=0),
    )


def in_hbm(array):
    return pltpu.with_memory_space_constraint(array, pltpu.HBM)


def from_everyone(rows):
    order = [list(range(lax.axis_size("sub")))[::-1]]
    return lax.all_to_all(rows, "sub", 0, 0, tiled=True, axis_index_groups=order)


def swap(partner, other):
    count = lax.axis_size("sub")
    both = lambda lows: [pair for i in lows for pair in ((i, i + 1), (i + 1, i))]
    return (
        lax.ppermute(partner, "sub", both(range(0, count, 2))),
        lax.ppermute(other, "sub", both(range(1, count - 1, 2))),
    )


def on_device(rhs, viscosity, coupling, margin_rows, coarse_basis, coarse_inverse):
    count = lax.axis_size("sub")
    columns = coarse_inverse.shape[1]
    f32 = lambda *shape: jax.ShapeDtypeStruct(shape, jnp.float32)
    dma = lambda *shape: pltpu.SemaphoreType.DMA(shape)
    extended = pltpu.VMEM((2, EXT, CELLS), jnp.float32)
    stacked = pltpu.VMEM((6, STACKED, CELLS), jnp.float32)
    solved = pltpu.VMEM((4, STACKED, CELLS), jnp.float32)
    sums = pltpu.VMEM((SLOTS, LANES), jnp.float32)
    lines = pltpu.VMEM((LANES, len(MATRIX_GROUPS) * CELLS), jnp.bfloat16)
    row, whole, edge = f32(count, LANES), f32(2, ROWS, CELLS), f32(TILE, CELLS)
    packed, smoothed = f32(EDGE_AT + coarse_rows(columns), CELLS), f32(2, EXT, CELLS)
    arguments = (rhs, viscosity, coupling, coarse_inverse, coarse_basis)
    packs = call(
        pack_kernel, "pack", [HBM] * 5, [packed, packed], 5_000_000,
        [pltpu.VMEM((4, VECTORS, CHUNK, CELLS), jnp.bfloat16), dma(4 * VECTORS // GROUP)]
        + [dma(2 * pack_count(columns))],
    )(*map(in_hbm, arguments))
    held, partner, other = lax.optimization_barrier((coarse_basis, *packs))
    partner, other = swap(partner, other)
    (first,) = call(
        restrict_kernel, "restrict", [VMEM] * 2, [row], 10_000_000, [sums, lines]
    )(rhs, held)
    first = from_everyone(first)
    direction, image, smooth, residual, partner_rows, other_rows, second = call(
        functools.partial(first_turn_kernel, count), "first_turn", [SMEM] + [VMEM] * 8,
        [whole, whole, smoothed, f32(1, columns), edge, edge, row], 20_000_000,
        [extended, sums, stacked, solved, lines],
    )(margin_rows, first, coarse_inverse, partner, other, held, rhs, viscosity, coupling)
    partner_rows, other_rows = swap(partner_rows, other_rows)
    second = from_everyone(second)
    second_direction, third = call(
        functools.partial(second_turn_kernel, count), "second_turn", [SMEM] + [VMEM] * 14,
        [whole, row], 20_000_000, [extended, extended, sums, stacked, solved],
    )(
        margin_rows, first, second, residual, coarse_inverse, partner, other, partner_rows, other_rows,
        held, smooth, rhs, image, viscosity, coupling,
    )
    third = from_everyone(third)
    result, transposed = call(finish_kernel, "finish", [VMEM] * 5, [whole, f32(2, 3)], 1_000_000)(
        first, second, third, direction, second_direction
    )
    return result, transposed.T


def solution(mesh):
    in_specs = (
        P(None, ("groups", "sub"), None),
        P(("groups", "sub"), None),
        P(None, ("groups", "sub"), None),
        P("groups"),
        P(None, None, ("groups", "sub"), None),
        P(("groups", "sub"), None),
    )
    out_specs = (P(None, ("groups", "sub"), None), P("groups", None))
    return jax.shard_map(
        on_device, mesh=mesh, in_specs=in_specs, out_specs=out_specs, check_vma=False
    )
```

```python
import functools

import jax
import jax.numpy as jnp
from jax import lax
from jax.experimental import pallas as pl
from jax.experimental.pallas import tpu as pltpu
from jax.sharding import PartitionSpec as P

ROWS = 64
CELLS = 512
VECTORS = 48
HALO = 8
EXT = ROWS + 2 * HALO
STRIP = 32
GROUP = 16
STACKED = EXT + 2 * STRIP
TILE = 8
CHUNK = 16
CHUNKS = 2 * ROWS // CHUNK
PIECE = 8
LANES = 128
SLOTS = 64
EDGE_AT = 5 * HALO
INVERSE_AT = 2 * VECTORS
SWEEPS = 4
RELAX = 0.7
ROW_FACTOR = (1.0, 4.0)
CELL_FACTOR = (4.0, 1.0)

VMEM = pl.BlockSpec(memory_space=pltpu.VMEM)
SMEM = pl.BlockSpec(memory_space=pltpu.SMEM)
HBM = pl.BlockSpec(memory_space=pltpu.HBM)


def coarse_rows(columns):
    return INVERSE_AT + VECTORS * (columns // 512) + (VECTORS // 2) * (columns % 512 // 256)


def cell_sum(field):
    lane = lax.broadcasted_iota(jnp.int32, (field.shape[0], LANES), 1)
    left, right = pltpu.roll(field, 1, 1), pltpu.roll(field, CELLS - 1, 1)
    inner = left[:, LANES:-LANES] + right[:, LANES:-LANES]
    first = jnp.where(lane == 0, 0.0, left[:, :LANES]) + right[:, :LANES]
    last = left[:, -LANES:] + jnp.where(lane == LANES - 1, 0.0, right[:, -LANES:])
    return jnp.concatenate([first, inner, last], 1)


class Rows:
    def __init__(self, read, first, last):
        self.read, self.first, self.last = read, first, last
        self.tiles, self.down, self.up = {}, {}, {}

    def at(self, t):
        if t not in self.tiles:
            self.tiles[t] = self.read(t)
        return self.tiles[t]

    def moved(self, held, t, by):
        if t not in held:
            held[t] = pltpu.roll(self.at(t), by, 0)
        return held[t]

    def around(self, t):
        row = lax.broadcasted_iota(jnp.int32, (TILE, CELLS), 0)
        below, above = self.moved(self.down, t, 1), self.moved(self.up, t, TILE - 1)
        if t > self.first:
            below = jnp.where(row == 0, self.moved(self.down, t - 1, 1), below)
        if t < self.last:
            above = jnp.where(row == TILE - 1, self.moved(self.up, t + 1, TILE - 1), above)
        return below + above


def neighbours(rows, t, component):
    around, cells = rows.around(t), cell_sum(rows.at(t))
    if component == 0:
        return around + CELL_FACTOR[0] * cells
    return ROW_FACTOR[1] * around + cells


def sublane_sum(tile):
    for by in (4, 2, 1):
        tile = tile + pltpu.roll(tile, by, 0)
    return tile


def in_rows(tiles):
    row = lax.broadcasted_iota(jnp.int32, (8, LANES), 0)
    total = jnp.zeros((8, LANES), jnp.float32)
    for n, tile in enumerate(tiles):
        total = jnp.where(row == n, sublane_sum(tile), total)
    return total


MATRIX_GROUPS = tuple((1, r) for r in range(CHUNK, ROWS, CHUNK))
VECTOR_GROUPS = ((0, 0), (0, 16), (0, 32), (0, 48), (1, 0))


def restrict(held, field, sums, lines):
    lines[2 * CHUNK :] = jnp.zeros((LANES - 2 * CHUNK, lines.shape[1]), jnp.bfloat16)
    blocks = []
    for g, (a, r) in enumerate(MATRIX_GROUPS):
        part, cells = field[a, r : r + CHUNK], slice(CELLS * g, CELLS * (g + 1))
        high = part.astype(jnp.bfloat16)
        lines[:CHUNK, cells] = high
        lines[CHUNK : 2 * CHUNK, cells] = (part - high.astype(jnp.float32)).astype(jnp.bfloat16)
        blocks.append(held[:, a, r : r + CHUNK, :].reshape(CHUNK * VECTORS, CELLS))
    products = lax.dot_general(
        jnp.concatenate(blocks, 1),
        lines[...],
        (((1,), (1,)), ((), ())),
        preferred_element_type=jnp.float32,
    )
    row = lax.broadcasted_iota(jnp.int32, (CHUNK, LANES), 0)
    equal = row == lax.broadcasted_iota(jnp.int32, (CHUNK, LANES), 1) % CHUNK
    for first in range(0, VECTORS, PIECE):
        totals = [None] * PIECE
        for a, r in VECTOR_GROUPS:
            for c in range(0, CELLS, LANES):
                rows, cells = slice(r, r + CHUNK), slice(c, c + LANES)
                tile = field[a, rows, cells]
                for n in range(PIECE):
                    term = held[first + n, a, rows, cells].astype(jnp.float32) * tile
                    totals[n] = term if totals[n] is None else totals[n] + term
        for n in range(PIECE):
            at = CHUNK * (first + n)
            totals[n] = totals[n] + jnp.where(equal, products[at : at + CHUNK], 0.0)
        sums[first : first + PIECE] = in_rows([total[:8] + total[8:] for total in totals])


def fold(row):
    total = row[:, :LANES]
    for c in range(LANES, CELLS, LANES):
        total = total + row[:, c : c + LANES]
    return total


def tile_rows(t):
    return slice(TILE * t, TILE * (t + 1))


def send_sums(sums, out_ref, turn):
    rest = sums[...]
    parts = []
    for _ in range(3):
        part = rest.astype(jnp.bfloat16)
        parts.append(part)
        rest = rest - part.astype(jnp.float32)
    row = lax.dot_general(
        jnp.ones((CHUNK, 3 * LANES), jnp.bfloat16),
        jnp.concatenate(parts, 1),
        (((1,), (1,)), ((), ())),
        preferred_element_type=jnp.float32,
    )
    wide = jnp.concatenate([row[:8], jnp.zeros((8, LANES - SLOTS), jnp.float32)], 1)
    wide = pltpu.roll(wide, turn, 1)
    for r in range(0, out_ref.shape[0], 8):
        out_ref[r : r + 8] = wide


def own_turn():
    return VECTORS * lax.axis_index("sub") % LANES


def pack_copies(out_ref, first_row, rhs_ref, visc_ref, coup_ref, inverse_ref, sems, at_sem):
    rows = pl.ds(pl.multiple_of(first_row, HALO), HALO)
    moves = [(visc_ref.at[rows, :], 0, HALO, None)]
    for a in range(2):
        moves.append((coup_ref.at[a, rows, :], HALO * (1 + a), HALO, None))
        moves.append((rhs_ref.at[a, rows, :], HALO * (3 + a), HALO, None))
    columns = inverse_ref.shape[1]
    at = EDGE_AT + INVERSE_AT
    for c in range(0, columns - 511, 512):
        moves.append((inverse_ref.at[:, pl.ds(c, 512)], at, VECTORS, None))
        at += VECTORS
    if columns % 512:
        half = VECTORS // 2
        last = pl.ds(columns - 256, 256)
        moves.append((inverse_ref.at[pl.ds(0, half), last], at, half, 0))
        moves.append((inverse_ref.at[pl.ds(half, half), last], at, half, 256))
    copies = []
    for n, (source, at, size, lane) in enumerate(moves):
        place = pl.ds(at, size)
        target = out_ref.at[place, :] if lane is None else out_ref.at[place, pl.ds(lane, 256)]
        copies.append(pltpu.make_async_copy(source, target, sems.at[at_sem + n]))
    return copies


def pack_count(columns):
    return 5 + columns // 512 + 2 * (columns % 512 // 256)


def pack_kernel(
    rhs_ref, visc_ref, coup_ref, inverse_ref, basis_ref,
    partner_ref, other_ref,
    groups, group_sems, pack_sems,
):
    odd = lax.axis_index("sub") % 2
    sides = ((partner_ref, 1 - odd), (other_ref, odd))
    group_copies, packs = [], []
    for k in range(0, VECTORS, GROUP):
        for n, (out_ref, up) in enumerate(sides):
            rows = pl.ds(pl.multiple_of(up * (ROWS - CHUNK), CHUNK), CHUNK)
            for a in range(2):
                group_copies.append(
                    pltpu.make_async_copy(
                        basis_ref.at[pl.ds(k, GROUP), a, rows, :],
                        groups.at[2 * n + a, pl.ds(k, GROUP)],
                        group_sems.at[len(group_copies)],
                    )
                )
    for n, (out_ref, up) in enumerate(sides):
        packs += pack_copies(
            out_ref, up * (ROWS - HALO), rhs_ref, visc_ref, coup_ref, inverse_ref, pack_sems,
            n * pack_count(inverse_ref.shape[1]),
        )
    for copy in group_copies + packs:
        copy.start()

    def take(out_ref, group, first, row):
        for k in range(first, first + GROUP, TILE):
            lines = [groups[group, k + n].astype(jnp.float32)[row : row + 1] for n in range(TILE)]
            at = EDGE_AT + VECTORS * (group % 2) + k
            out_ref[at : at + TILE] = jnp.concatenate(lines, 0)

    for first in range(0, VECTORS, GROUP):
        for _ in range(4):
            group_copies.pop(0).wait()

        @pl.when(odd == 0)
        def _():
            for a in range(2):
                take(partner_ref, a, first, CHUNK - 1)
                take(other_ref, 2 + a, first, 0)

        @pl.when(odd == 1)
        def _():
            for a in range(2):
                take(partner_ref, a, first, 0)
                take(other_ref, 2 + a, first, CHUNK - 1)

    for copy in packs:
        copy.wait()


def restrict_kernel(rhs_ref, held, sums_ref, sums, lines):
    sums[...] = jnp.zeros_like(sums)
    squares = jnp.zeros((TILE, CELLS), jnp.float32)
    for a in range(2):
        for t in range(ROWS // TILE):
            tile = rhs_ref[a, tile_rows(t)]
            squares = squares + tile * tile
    sums[VECTORS : VECTORS + 8] = in_rows([fold(squares)])

    restrict(held, rhs_ref, sums, lines)
    send_sums(sums, sums_ref, own_turn())


class Neighbour:
    def __init__(self, first_ref, second_ref):
        self.odd = lax.axis_index("sub") % 2 == 1
        self.first, self.second = first_ref, second_ref

    def __getitem__(self, index):
        return jnp.where(self.odd, self.first[index], self.second[index])


def neighbours_of(partner_ref, other_ref):
    return Neighbour(partner_ref, other_ref), Neighbour(other_ref, partner_ref)


def solve(count, margin_ref, visc_ref, coup_ref, field, low, high, out_ref, stacked, solved, steps):
    waiting, done = list(steps), 0
    every = (SWEEPS - 1) * (STACKED // TILE) // len(waiting)
    rank = lax.axis_index("sub")
    lower = jnp.where(rank > 0, margin_ref[jnp.maximum(rank - 1, 0)], 0)
    upper = jnp.where(rank < count - 1, margin_ref[rank], 0)
    lower_f, upper_f = lower.astype(jnp.float32), upper.astype(jnp.float32)
    low_scale = 1.0 / (2.0 * jnp.maximum(lower_f, 1.0))
    high_scale = 1.0 / (2.0 * jnp.maximum(upper_f, 1.0))
    wide = lambda x: jnp.concatenate([x] * (CELLS // LANES), 1)
    own_tiles = ROWS // TILE
    strip_tiles = STRIP // TILE
    last = own_tiles + 1
    segments = (
        (0, 0, last + 1),
        (last + 1, 0, strip_tiles),
        (last + 1 + strip_tiles, last + 1 - strip_tiles, strip_tiles),
    )

    def place_of(e):
        return lax.broadcasted_iota(jnp.int32, (TILE, LANES), 0) + (TILE * e - HALO)

    def live_of(segment, e):
        place = place_of(e)
        if segment == 0:
            live = (place >= -lower) & (place < ROWS + upper)
        elif segment == 1:
            live = place < lower
        else:
            live = place >= ROWS - upper
        return wide(live.astype(jnp.float32))

    def weight_of(segment, e):
        place = place_of(e)
        place_f = place.astype(jnp.float32)
        rising = lambda base, scale: (place_f - base + 0.5) * scale
        falling = lambda base, scale: (base - place_f - 0.5) * scale
        if segment == 0:
            weight = jnp.where(place < lower, rising(-lower_f, low_scale), 1.0)
            weight = jnp.where(
                place >= ROWS - upper, falling(ROWS + upper_f, high_scale), weight
            )
        elif segment == 1:
            weight = jnp.where(place >= -lower, falling(lower_f, low_scale), 1.0)
        else:
            weight = jnp.where(place < ROWS + upper, rising(ROWS - upper_f, high_scale), 1.0)
        return wide(weight)

    def extended(ref, at, e):
        if e == 0:
            return low[at : at + HALO]
        if e == last:
            return high[at : at + HALO]
        return ref[tile_rows(e - 1)]

    for e in range(last + 1):
        viscosity = extended(visc_ref, 0, e)
        for a in range(2):
            coupling = extended(coup_ref.at[a], HALO * (1 + a), e)
            scale = RELAX / (10.0 * viscosity + jnp.abs(coupling) + 0.05)
            parts = (scale * field(a, e - 1), scale * viscosity, scale * coupling)
            for n, (first, begin, size) in enumerate(segments):
                if not begin <= e < begin + size:
                    continue
                rows = tile_rows(first + e - begin)
                always = n == 0 and 0 < e < last
                for m, part in enumerate(parts):
                    stacked[3 * a + m, rows] = part if always else live_of(n, e) * part

    for sweep in range(1, SWEEPS):
        for n, (first, begin, size) in enumerate(segments):
            end = first + size - 1
            if sweep == 1:
                reads = [lambda t, a=a: stacked[3 * a, tile_rows(t)] for a in range(2)]
            else:
                bank = 2 * (sweep % 2)
                reads = [lambda t, a=a: solved[bank + a, tile_rows(t)] for a in range(2)]
            fields = [Rows(read, first, end) for read in reads]
            for t in range(first, end + 1):
                rows = tile_rows(t)
                if done % every == 0 and waiting:
                    waiting.pop(0)()
                done += 1
                for a in range(2):
                    value = (
                        ((1.0 - RELAX) * fields[a].at(t) + stacked[3 * a, rows])
                        + stacked[3 * a + 1, rows] * neighbours(fields[a], t, a)
                        - stacked[3 * a + 2, rows] * fields[1 - a].at(t)
                    )
                    e = t - first + begin
                    if sweep < SWEEPS - 1:
                        solved[2 * ((sweep + 1) % 2) + a, rows] = value
                    elif n == 0:
                        out_ref[a, tile_rows(e)] = weight_of(n, e) * value
                    else:
                        out_ref[a, tile_rows(e)] += weight_of(n, e) * value


def place_in_line(shape):
    rank = shape[0] - 1 - lax.broadcasted_iota(jnp.int32, shape, 0)
    return rank, lax.broadcasted_iota(jnp.int32, shape, 1)


def add_rows(field):
    total = field[:8]
    for r in range(8, field.shape[0], 8):
        total = total + field[r : r + 8]
    return sublane_sum(total)


def line_up(received):
    rank, lane = place_in_line(received.shape)
    first = lane - VECTORS * rank
    tiles = []
    for at in range(0, VECTORS * received.shape[0], LANES):
        own = (first + at >= 0) & (first + at < VECTORS)
        tiles.append(add_rows(jnp.where(own, received, 0.0)))
    return jnp.concatenate(tiles, 1)


def turned_total(received, slot):
    rank, lane = place_in_line(received.shape)
    own = lane == (VECTORS * rank + slot) % LANES
    return jnp.sum(jnp.where(own, received, 0.0), keepdims=True)


def rounded(column):
    return column.astype(jnp.bfloat16).astype(jnp.float32)


def times(matrix, line):
    tall = matrix.reshape(-1, 8, matrix.shape[1])
    return jnp.sum(tall * line[None], 2, keepdims=True).reshape(-1, 1)


def lift(inverse_ref, residual):
    return rounded(times(inverse_ref[...], residual))


def lift_packed(ref, residual):
    columns = residual.shape[1]
    at, total = EDGE_AT + INVERSE_AT, None
    for c in range(0, columns - 511, 512):
        term = times(ref[at : at + VECTORS], residual[:, c : c + 512])
        total = term if total is None else total + term
        at += VECTORS
    if columns % 512:
        half = VECTORS // 2
        last = residual[:, columns - 256 :]
        rows = ref[at : at + half]
        term = jnp.concatenate([times(rows[:, :256], last), times(rows[:, 256:], last)], 0)
        total = term if total is None else total + term
    return rounded(total)


def edge_values(ref, lifted):
    starts = [EDGE_AT + VECTORS * a for a in range(2)]
    return [jnp.sum(ref[at : at + VECTORS] * lifted, 0, keepdims=True) for at in starts]


def spread(lifted):
    shape = (VECTORS, CHUNK * VECTORS)
    owner = lax.broadcasted_iota(jnp.int32, shape, 1) // CHUNK
    row = lax.broadcasted_iota(jnp.int32, shape, 0)
    line = jnp.sum(jnp.where(owner == row, lifted, 0.0), 0, keepdims=True)
    shape = (CHUNK, CHUNK * VECTORS)
    place = lax.broadcasted_iota(jnp.int32, shape, 1) % CHUNK
    row = lax.broadcasted_iota(jnp.int32, shape, 0)
    return jnp.where(place == row, line, 0.0).astype(jnp.bfloat16)


def prolonging(residual, inverse_ref, held, extended):
    matrix = spread(lift(inverse_ref, residual))

    def step(a, r):
        rows = held[:, a, r : r + CHUNK, :].reshape(CHUNK * VECTORS, CELLS)
        extended[a, HALO + r : HALO + r + CHUNK] = jnp.dot(
            matrix, rows, preferred_element_type=jnp.float32
        )

    return [functools.partial(step, a, r) for a in range(2) for r in range(0, ROWS, CHUNK)]


def apply_operator(residual, low, high, smooth, extended, visc_ref, coup_ref, direction_ref):
    edges = [edge_values(side, lift_packed(side, residual)) for side in (low, high)]
    place = lax.broadcasted_iota(jnp.int32, (TILE, CELLS), 0)
    tiles = ROWS // TILE

    def read(t, a):
        if t < 0:
            return smooth(a, 0) + jnp.where(place == TILE - 1, edges[0][a], 0.0)
        if t == tiles:
            return smooth(a, t + 1) + jnp.where(place == 0, edges[1][a], 0.0)
        tile = smooth(a, t + 1) + extended[a, tile_rows(t + 1)]
        direction_ref[a, tile_rows(t)] = tile
        return tile

    fields = [Rows(lambda t, a=a: read(t, a), -1, tiles) for a in range(2)]
    for t in range(tiles):
        rows = tile_rows(t)
        viscosity = visc_ref[rows]
        for a in range(2):
            coupling = coup_ref[a, rows]
            diagonal = 10.0 * viscosity + jnp.abs(coupling) + 0.05
            image = (
                diagonal * fields[a].at(t)
                - viscosity * neighbours(fields[a], t, a)
                + coupling * fields[1 - a].at(t)
            )
            yield t, a, image


def lane_total(received, lane):
    return jnp.sum(received[:, lane : lane + 1], 0, keepdims=True)


def first_turn_kernel(
    count, margin_ref, sums_ref, inverse_ref, partner_ref, other_ref, held, rhs_ref, visc_ref,
    coup_ref,
    direction_ref, image_ref, smooth_ref, residual_ref, partner_rows_ref, other_rows_ref, next_ref,
    extended, sums, stacked, solved, lines,
):
    received = sums_ref[...]
    over_beta = 1.0 / jnp.sqrt(turned_total(received, VECTORS))
    residual = line_up(received) * over_beta
    residual_ref[...] = residual
    steps = prolonging(residual, inverse_ref, held, extended)
    low, high = neighbours_of(partner_ref, other_ref)

    def field(a, t):
        at = HALO * (3 + a)
        if t < 0:
            return low[at : at + HALO]
        return high[at : at + HALO] if t == ROWS // TILE else rhs_ref[a, tile_rows(t)]

    solve(
        count, margin_ref, visc_ref, coup_ref, field, low, high, smooth_ref, stacked, solved,
        steps,
    )
    smooth = lambda a, t: smooth_ref[a, tile_rows(t)] * over_beta
    images = apply_operator(
        residual, low, high, smooth, extended, visc_ref, coup_ref, direction_ref
    )
    odd = lax.axis_index("sub") % 2 == 1
    products, squares = [jnp.zeros((TILE, CELLS), jnp.float32)] * 2
    heads, tails = [None] * 2, [None] * 2
    for t, a, image in images:
        image_ref[a, tile_rows(t)] = image
        products = products + rhs_ref[a, tile_rows(t)] * image
        squares = squares + image * image
        if t == 0:
            heads[a] = image
        if t == ROWS // TILE - 1:
            tails[a] = image
    half = lax.broadcasted_iota(jnp.int32, (TILE, CELLS), 0) < TILE // 2
    head = jnp.where(half, heads[0], pltpu.roll(heads[1], TILE // 2, 0))
    tail = jnp.where(half, pltpu.roll(tails[1], TILE // 2, 0), tails[0])
    partner_rows_ref[...] = jnp.where(odd, head, tail)
    other_rows_ref[...] = jnp.where(odd, tail, head)
    sums[...] = jnp.zeros_like(sums)
    sums[VECTORS : VECTORS + 8] = in_rows([fold(products), fold(squares)])

    restrict(held, image_ref, sums, lines)
    send_sums(sums, next_ref, own_turn())


def first_column(first, second):
    beta = jnp.sqrt(turned_total(first, VECTORS))
    h_00 = turned_total(second, VECTORS) / beta
    h_10 = jnp.sqrt(turned_total(second, VECTORS + 1) - h_00 * h_00)
    return beta, h_00, h_10


def second_turn_kernel(
    count, margin_ref, first_ref, second_ref, residual_ref, inverse_ref, partner_ref, other_ref,
    partner_rows_ref, other_rows_ref, held, smooth_ref, rhs_ref, image_ref, visc_ref, coup_ref,
    direction_ref, next_ref,
    image_smooth, extended, sums, stacked, solved,
):
    first, second = first_ref[...], second_ref[...]
    beta, h_00, h_10 = first_column(first, second)
    ratio = h_00 / beta
    over = 1.0 / h_10
    residual = (line_up(second) - h_00 * residual_ref[...]) * over
    steps = prolonging(residual, inverse_ref, held, extended)
    low, high = neighbours_of(partner_ref, other_ref)
    low_rows, high_rows = neighbours_of(partner_rows_ref, other_rows_ref)

    def field(a, t):
        if 0 <= t < ROWS // TILE:
            return image_ref[a, tile_rows(t)]
        rows = low_rows[...] if t < 0 else high_rows[...]
        return pltpu.roll(rows, TILE // 2, 0) if a else rows

    solve(
        count, margin_ref, visc_ref, coup_ref, field, low, high, image_smooth, stacked, solved,
        steps,
    )

    def smooth(a, t):
        rows = tile_rows(t)
        return (image_smooth[a, rows] - ratio * smooth_ref[a, rows]) * over

    images = apply_operator(
        residual, low, high, smooth, extended, visc_ref, coup_ref, direction_ref
    )
    totals = [jnp.zeros((TILE, CELLS), jnp.float32)] * 3
    for t, a, image in images:
        others = (rhs_ref[a, tile_rows(t)], image_ref[a, tile_rows(t)], image)
        totals = [total + x * image for total, x in zip(totals, others)]
    sums[...] = jnp.zeros_like(sums)
    sums[:8] = in_rows([fold(total) for total in totals])
    send_sums(sums, next_ref, 0)


def finish_kernel(
    first_ref, second_ref, third_ref, first_direction_ref, second_direction_ref,
    solution_ref, hessenberg_ref,
):
    third = third_ref[...]
    beta, h_00, h_10 = first_column(first_ref[...], second_ref[...])
    squares = lane_total(third, 2)
    h_01 = lane_total(third, 0) / beta
    h_11 = (lane_total(third, 1) - h_00 * h_01) / h_10
    h_21 = jnp.sqrt(squares - h_01 * h_01 - h_11 * h_11)
    l_00 = jnp.sqrt(h_00 * h_00 + h_10 * h_10)
    l_10 = (h_00 * h_01 + h_10 * h_11) / l_00
    f_0 = beta * h_00 / l_00
    c_1 = (beta * h_01 - l_10 * f_0) / (squares - l_10 * l_10)
    c_0 = (f_0 - l_10 * c_1) / l_00
    for a in range(2):
        solution_ref[a] = c_0 * first_direction_ref[a] + c_1 * second_direction_ref[a]
    shape = hessenberg_ref.shape
    row = lax.broadcasted_iota(jnp.int32, shape, 1)
    column = lax.broadcasted_iota(jnp.int32, shape, 0)
    entries = jnp.zeros(shape, jnp.float32)
    for i, j, value in ((0, 0, h_00), (0, 1, h_01), (1, 0, h_10), (1, 1, h_11), (2, 1, h_21)):
        entries = jnp.where((row == i) & (column == j), value, entries)
    hessenberg_ref[...] = entries


def call(kernel, name, in_specs, outs, flops, scratch=(), traffic=4_000_000):
    return pl.pallas_call(
        kernel,
        name=name,
        in_specs=in_specs,
        out_specs=[VMEM] * len(outs),
        out_shape=outs,
        scratch_shapes=scratch,
        compiler_params=pltpu.CompilerParams(vmem_limit_bytes=16 * 1024 * 1024),
        cost_estimate=pl.CostEstimate(flops=flops, bytes_accessed=traffic, transcendentals=0),
    )


def in_hbm(array):
    return pltpu.with_memory_space_constraint(array, pltpu.HBM)


def from_everyone(rows):
    order = [list(range(lax.axis_size("sub")))[::-1]]
    return lax.all_to_all(rows, "sub", 0, 0, tiled=True, axis_index_groups=order)


def swap(partner, other):
    count = lax.axis_size("sub")
    both = lambda lows: [pair for i in lows for pair in ((i, i + 1), (i + 1, i))]
    return (
        lax.ppermute(partner, "sub", both(range(0, count, 2))),
        lax.ppermute(other, "sub", both(range(1, count - 1, 2))),
    )


def on_device(rhs, viscosity, coupling, margin_rows, coarse_basis, coarse_inverse):
    count = lax.axis_size("sub")
    columns = coarse_inverse.shape[1]
    f32 = lambda *shape: jax.ShapeDtypeStruct(shape, jnp.float32)
    dma = lambda *shape: pltpu.SemaphoreType.DMA(shape)
    extended = pltpu.VMEM((2, EXT, CELLS), jnp.float32)
    stacked = pltpu.VMEM((6, STACKED, CELLS), jnp.float32)
    solved = pltpu.VMEM((4, STACKED, CELLS), jnp.float32)
    sums = pltpu.VMEM((SLOTS, LANES), jnp.float32)
    lines = pltpu.VMEM((LANES, len(MATRIX_GROUPS) * CELLS), jnp.bfloat16)
    row, whole, edge = f32(count, LANES), f32(2, ROWS, CELLS), f32(TILE, CELLS)
    packed, smoothed = f32(EDGE_AT + coarse_rows(columns), CELLS), f32(2, EXT, CELLS)
    arguments = (rhs, viscosity, coupling, coarse_inverse, coarse_basis)
    packs = call(
        pack_kernel, "pack", [HBM] * 5, [packed, packed], 5_000_000,
        [pltpu.VMEM((4, VECTORS, CHUNK, CELLS), jnp.bfloat16), dma(4 * VECTORS // GROUP)]
        + [dma(2 * pack_count(columns))],
    )(*map(in_hbm, arguments))
    held, partner, other = lax.optimization_barrier((coarse_basis, *packs))
    partner, other = swap(partner, other)
    (first,) = call(
        restrict_kernel, "restrict", [VMEM] * 2, [row], 10_000_000, [sums, lines]
    )(rhs, held)
    first = from_everyone(first)
    direction, image, smooth, residual, partner_rows, other_rows, second = call(
        functools.partial(first_turn_kernel, count), "first_turn", [SMEM] + [VMEM] * 8,
        [whole, whole, smoothed, f32(8, columns), edge, edge, row], 20_000_000,
        [extended, sums, stacked, solved, lines],
    )(margin_rows, first, coarse_inverse, partner, other, held, rhs, viscosity, coupling)
    partner_rows, other_rows = swap(partner_rows, other_rows)
    second = from_everyone(second)
    second_direction, third = call(
        functools.partial(second_turn_kernel, count), "second_turn", [SMEM] + [VMEM] * 14,
        [whole, row], 20_000_000, [extended, extended, sums, stacked, solved],
    )(
        margin_rows, first, second, residual, coarse_inverse, partner, other, partner_rows, other_rows,
        held, smooth, rhs, image, viscosity, coupling,
    )
    third = from_everyone(third)
    result, transposed = call(finish_kernel, "finish", [VMEM] * 5, [whole, f32(2, 3)], 1_000_000)(
        first, second, third, direction, second_direction
    )
    return result, transposed.T


def solution(mesh):
    in_specs = (
        P(None, ("groups", "sub"), None),
        P(("groups", "sub"), None),
        P(None, ("groups", "sub"), None),
        P("groups"),
        P(None, None, ("groups", "sub"), None),
        P(("groups", "sub"), None),
    )
    out_specs = (P(None, ("groups", "sub"), None), P("groups", None))
    return jax.shard_map(
        on_device, mesh=mesh, in_specs=in_specs, out_specs=out_specs, check_vma=False
    )
```

```python
import functools

import jax
import jax.numpy as jnp
from jax import lax
from jax.experimental import pallas as pl
from jax.experimental.pallas import tpu as pltpu
from jax.sharding import PartitionSpec as P

ROWS = 64
CELLS = 512
VECTORS = 48
HALO = 8
EXT = ROWS + 2 * HALO
STRIP = 32
GROUP = 16
STACKED = EXT + 2 * STRIP
TILE = 8
CHUNK = 16
CHUNKS = 2 * ROWS // CHUNK
PIECE = 8
LANES = 128
SLOTS = 64
EDGE_AT = 5 * HALO
INVERSE_AT = 2 * VECTORS
SWEEPS = 4
RELAX = 0.7
ROW_FACTOR = (1.0, 4.0)
CELL_FACTOR = (4.0, 1.0)

VMEM = pl.BlockSpec(memory_space=pltpu.VMEM)
SMEM = pl.BlockSpec(memory_space=pltpu.SMEM)
HBM = pl.BlockSpec(memory_space=pltpu.HBM)


def coarse_rows(columns):
    return INVERSE_AT + VECTORS * (columns // 512) + (VECTORS // 2) * (columns % 512 // 256)


def cell_sum(field):
    lane = lax.broadcasted_iota(jnp.int32, (field.shape[0], LANES), 1)
    left, right = pltpu.roll(field, 1, 1), pltpu.roll(field, CELLS - 1, 1)
    inner = left[:, LANES:-LANES] + right[:, LANES:-LANES]
    first = jnp.where(lane == 0, 0.0, left[:, :LANES]) + right[:, :LANES]
    last = left[:, -LANES:] + jnp.where(lane == LANES - 1, 0.0, right[:, -LANES:])
    return jnp.concatenate([first, inner, last], 1)


class Rows:
    def __init__(self, read, first, last):
        self.read, self.first, self.last = read, first, last
        self.tiles, self.down, self.up = {}, {}, {}

    def at(self, t):
        if t not in self.tiles:
            self.tiles[t] = self.read(t)
        return self.tiles[t]

    def moved(self, held, t, by):
        if t not in held:
            held[t] = pltpu.roll(self.at(t), by, 0)
        return held[t]

    def around(self, t):
        row = lax.broadcasted_iota(jnp.int32, (TILE, CELLS), 0)
        below, above = self.moved(self.down, t, 1), self.moved(self.up, t, TILE - 1)
        if t > self.first:
            below = jnp.where(row == 0, self.moved(self.down, t - 1, 1), below)
        if t < self.last:
            above = jnp.where(row == TILE - 1, self.moved(self.up, t + 1, TILE - 1), above)
        return below + above


def neighbours(rows, t, component):
    around, cells = rows.around(t), cell_sum(rows.at(t))
    if component == 0:
        return around + CELL_FACTOR[0] * cells
    return ROW_FACTOR[1] * around + cells


def sublane_sum(tile):
    for by in (4, 2, 1):
        tile = tile + pltpu.roll(tile, by, 0)
    return tile


def in_rows(tiles):
    row = lax.broadcasted_iota(jnp.int32, (8, LANES), 0)
    total = jnp.zeros((8, LANES), jnp.float32)
    for n, tile in enumerate(tiles):
        total = jnp.where(row == n, sublane_sum(tile), total)
    return total


def restrict_piece(i, held, field, sums):
    totals = [None] * PIECE
    for a in range(2):
        for r in range(0, ROWS, CHUNK):
            for c in range(0, CELLS, LANES):
                rows, cells = slice(r, r + CHUNK), slice(c, c + LANES)
                tile = field[a, rows, cells]
                for n in range(PIECE):
                    term = held[PIECE * i + n, a, rows, cells].astype(jnp.float32) * tile
                    totals[n] = term if totals[n] is None else totals[n] + term
    tiles = [total[:8] + total[8:] for total in totals]
    sums[pl.ds(pl.multiple_of(PIECE * i, PIECE), PIECE), :] = in_rows(tiles)


MATRIX_GROUPS = tuple((1, r) for r in range(CHUNK, ROWS, CHUNK))
VECTOR_GROUPS = ((0, 0), (0, 16), (0, 32), (0, 48), (1, 0))


def restrict(held, field, sums, lines):
    lines[2 * CHUNK :] = jnp.zeros((LANES - 2 * CHUNK, lines.shape[1]), jnp.bfloat16)
    blocks = []
    for g, (a, r) in enumerate(MATRIX_GROUPS):
        part, cells = field[a, r : r + CHUNK], slice(CELLS * g, CELLS * (g + 1))
        high = part.astype(jnp.bfloat16)
        lines[:CHUNK, cells] = high
        lines[CHUNK : 2 * CHUNK, cells] = (part - high.astype(jnp.float32)).astype(jnp.bfloat16)
        blocks.append(held[:, a, r : r + CHUNK, :].reshape(CHUNK * VECTORS, CELLS))
    products = lax.dot_general(
        jnp.concatenate(blocks, 1),
        lines[...],
        (((1,), (1,)), ((), ())),
        preferred_element_type=jnp.float32,
    )
    row = lax.broadcasted_iota(jnp.int32, (CHUNK, LANES), 0)
    equal = row == lax.broadcasted_iota(jnp.int32, (CHUNK, LANES), 1) % CHUNK
    for first in range(0, VECTORS, PIECE):
        totals = [
            jnp.where(equal, products[CHUNK * k : CHUNK * (k + 1)], 0.0)
            for k in range(first, first + PIECE)
        ]
        for a, r in VECTOR_GROUPS:
            for c in range(0, CELLS, LANES):
                rows, cells = slice(r, r + CHUNK), slice(c, c + LANES)
                tile = field[a, rows, cells]
                for n in range(PIECE):
                    term = held[first + n, a, rows, cells].astype(jnp.float32) * tile
                    totals[n] = totals[n] + term
        sums[first : first + PIECE] = in_rows([total[:8] + total[8:] for total in totals])


def fold(row):
    total = row[:, :LANES]
    for c in range(LANES, CELLS, LANES):
        total = total + row[:, c : c + LANES]
    return total


def tile_rows(t):
    return slice(TILE * t, TILE * (t + 1))


def send_sums(sums, out_ref):
    rest = sums[...]
    parts = []
    for _ in range(3):
        part = rest.astype(jnp.bfloat16)
        parts.append(part)
        rest = rest - part.astype(jnp.float32)
    row = lax.dot_general(
        jnp.ones((CHUNK, 3 * LANES), jnp.bfloat16),
        jnp.concatenate(parts, 1),
        (((1,), (1,)), ((), ())),
        preferred_element_type=jnp.float32,
    )
    wide = jnp.concatenate([row[:1], jnp.zeros((1, LANES - SLOTS), jnp.float32)], 1)
    out_ref[...] = jnp.broadcast_to(wide, out_ref.shape)


def pack_copies(out_ref, first_row, rhs_ref, visc_ref, coup_ref, inverse_ref, sems, at_sem):
    rows = pl.ds(pl.multiple_of(first_row, HALO), HALO)
    moves = [(visc_ref.at[rows, :], 0, HALO, None)]
    for a in range(2):
        moves.append((coup_ref.at[a, rows, :], HALO * (1 + a), HALO, None))
        moves.append((rhs_ref.at[a, rows, :], HALO * (3 + a), HALO, None))
    columns = inverse_ref.shape[1]
    at = EDGE_AT + INVERSE_AT
    for c in range(0, columns - 511, 512):
        moves.append((inverse_ref.at[:, pl.ds(c, 512)], at, VECTORS, None))
        at += VECTORS
    if columns % 512:
        half = VECTORS // 2
        last = pl.ds(columns - 256, 256)
        moves.append((inverse_ref.at[pl.ds(0, half), last], at, half, 0))
        moves.append((inverse_ref.at[pl.ds(half, half), last], at, half, 256))
    copies = []
    for n, (source, at, size, lane) in enumerate(moves):
        place = pl.ds(at, size)
        target = out_ref.at[place, :] if lane is None else out_ref.at[place, pl.ds(lane, 256)]
        copies.append(pltpu.make_async_copy(source, target, sems.at[at_sem + n]))
    return copies


def pack_count(columns):
    return 5 + columns // 512 + 2 * (columns % 512 // 256)


def pack_kernel(
    rhs_ref, visc_ref, coup_ref, inverse_ref, basis_ref,
    partner_ref, other_ref,
    groups, group_sems, pack_sems,
):
    odd = lax.axis_index("sub") % 2
    sides = ((partner_ref, 1 - odd), (other_ref, odd))
    group_copies, packs = [], []
    for k in range(0, VECTORS, GROUP):
        for n, (out_ref, up) in enumerate(sides):
            rows = pl.ds(pl.multiple_of(up * (ROWS - CHUNK), CHUNK), CHUNK)
            for a in range(2):
                group_copies.append(
                    pltpu.make_async_copy(
                        basis_ref.at[pl.ds(k, GROUP), a, rows, :],
                        groups.at[2 * n + a, pl.ds(k, GROUP)],
                        group_sems.at[len(group_copies)],
                    )
                )
    for n, (out_ref, up) in enumerate(sides):
        packs += pack_copies(
            out_ref, up * (ROWS - HALO), rhs_ref, visc_ref, coup_ref, inverse_ref, pack_sems,
            n * pack_count(inverse_ref.shape[1]),
        )
    for copy in group_copies + packs:
        copy.start()

    def take(out_ref, group, first, row):
        for k in range(first, first + GROUP, TILE):
            lines = [groups[group, k + n].astype(jnp.float32)[row : row + 1] for n in range(TILE)]
            at = EDGE_AT + VECTORS * (group % 2) + k
            out_ref[at : at + TILE] = jnp.concatenate(lines, 0)

    for first in range(0, VECTORS, GROUP):
        for _ in range(4):
            group_copies.pop(0).wait()

        @pl.when(odd == 0)
        def _():
            for a in range(2):
                take(partner_ref, a, first, CHUNK - 1)
                take(other_ref, 2 + a, first, 0)

        @pl.when(odd == 1)
        def _():
            for a in range(2):
                take(partner_ref, a, first, 0)
                take(other_ref, 2 + a, first, CHUNK - 1)

    for copy in packs:
        copy.wait()


def restrict_kernel(rhs_ref, held, sums_ref, sums):
    sums[...] = jnp.zeros_like(sums)
    squares = jnp.zeros((TILE, CELLS), jnp.float32)
    for a in range(2):
        for t in range(ROWS // TILE):
            tile = rhs_ref[a, tile_rows(t)]
            squares = squares + tile * tile
    sums[VECTORS : VECTORS + 8] = in_rows([fold(squares)])

    def body(i, carry):
        restrict_piece(i, held, rhs_ref, sums)
        return carry

    lax.fori_loop(0, VECTORS // PIECE, body, 0)
    send_sums(sums, sums_ref)


class Neighbour:
    def __init__(self, first_ref, second_ref):
        self.odd = lax.axis_index("sub") % 2 == 1
        self.first, self.second = first_ref, second_ref

    def __getitem__(self, index):
        return jnp.where(self.odd, self.first[index], self.second[index])


def neighbours_of(partner_ref, other_ref):
    return Neighbour(partner_ref, other_ref), Neighbour(other_ref, partner_ref)


def solve(count, margin_ref, visc_ref, coup_ref, field, low, high, out_ref, stacked, solved, steps):
    waiting, done = list(steps), 0
    every = (SWEEPS - 1) * (STACKED // TILE) // len(waiting)
    rank = lax.axis_index("sub")
    lower = jnp.where(rank > 0, margin_ref[jnp.maximum(rank - 1, 0)], 0)
    upper = jnp.where(rank < count - 1, margin_ref[rank], 0)
    lower_f, upper_f = lower.astype(jnp.float32), upper.astype(jnp.float32)
    low_scale = 1.0 / (2.0 * jnp.maximum(lower_f, 1.0))
    high_scale = 1.0 / (2.0 * jnp.maximum(upper_f, 1.0))
    wide = lambda x: jnp.concatenate([x] * (CELLS // LANES), 1)
    own_tiles = ROWS // TILE
    strip_tiles = STRIP // TILE
    last = own_tiles + 1
    segments = (
        (0, 0, last + 1),
        (last + 1, 0, strip_tiles),
        (last + 1 + strip_tiles, last + 1 - strip_tiles, strip_tiles),
    )

    def place_of(e):
        return lax.broadcasted_iota(jnp.int32, (TILE, LANES), 0) + (TILE * e - HALO)

    def live_of(segment, e):
        place = place_of(e)
        if segment == 0:
            live = (place >= -lower) & (place < ROWS + upper)
        elif segment == 1:
            live = place < lower
        else:
            live = place >= ROWS - upper
        return wide(live.astype(jnp.float32))

    def weight_of(segment, e):
        place = place_of(e)
        place_f = place.astype(jnp.float32)
        rising = lambda base, scale: (place_f - base + 0.5) * scale
        falling = lambda base, scale: (base - place_f - 0.5) * scale
        if segment == 0:
            weight = jnp.where(place < lower, rising(-lower_f, low_scale), 1.0)
            weight = jnp.where(
                place >= ROWS - upper, falling(ROWS + upper_f, high_scale), weight
            )
        elif segment == 1:
            weight = jnp.where(place >= -lower, falling(lower_f, low_scale), 1.0)
        else:
            weight = jnp.where(place < ROWS + upper, rising(ROWS - upper_f, high_scale), 1.0)
        return wide(weight)

    def extended(ref, at, e):
        if e == 0:
            return low[at : at + HALO]
        if e == last:
            return high[at : at + HALO]
        return ref[tile_rows(e - 1)]

    for e in range(last + 1):
        viscosity = extended(visc_ref, 0, e)
        for a in range(2):
            coupling = extended(coup_ref.at[a], HALO * (1 + a), e)
            scale = RELAX / (10.0 * viscosity + jnp.abs(coupling) + 0.05)
            parts = (scale * field(a, e - 1), scale * viscosity, scale * coupling)
            for n, (first, begin, size) in enumerate(segments):
                if not begin <= e < begin + size:
                    continue
                rows = tile_rows(first + e - begin)
                always = n == 0 and 0 < e < last
                for m, part in enumerate(parts):
                    stacked[3 * a + m, rows] = part if always else live_of(n, e) * part

    for sweep in range(1, SWEEPS):
        for n, (first, begin, size) in enumerate(segments):
            end = first + size - 1
            if sweep == 1:
                reads = [lambda t, a=a: stacked[3 * a, tile_rows(t)] for a in range(2)]
            else:
                bank = 2 * (sweep % 2)
                reads = [lambda t, a=a: solved[bank + a, tile_rows(t)] for a in range(2)]
            fields = [Rows(read, first, end) for read in reads]
            for t in range(first, end + 1):
                rows = tile_rows(t)
                if done % every == 0 and waiting:
                    waiting.pop(0)()
                done += 1
                for a in range(2):
                    value = (
                        ((1.0 - RELAX) * fields[a].at(t) + stacked[3 * a, rows])
                        + stacked[3 * a + 1, rows] * neighbours(fields[a], t, a)
                        - stacked[3 * a + 2, rows] * fields[1 - a].at(t)
                    )
                    e = t - first + begin
                    if sweep < SWEEPS - 1:
                        solved[2 * ((sweep + 1) % 2) + a, rows] = value
                    elif n == 0:
                        out_ref[a, tile_rows(e)] = weight_of(n, e) * value
                    else:
                        out_ref[a, tile_rows(e)] += weight_of(n, e) * value


def place_in_line(shape):
    rank = shape[0] - 1 - lax.broadcasted_iota(jnp.int32, shape, 0)
    return rank, lax.broadcasted_iota(jnp.int32, shape, 1)


def line_up(received):
    devices = received.shape[0]
    rank, lane = place_in_line(received.shape)
    turned, by = received, VECTORS * rank % LANES
    for step in (64, 32, 16):
        turned = jnp.where(by & step != 0, pltpu.roll(turned, step, 1), turned)
    first = lane - VECTORS * rank
    tiles = []
    for at in range(0, VECTORS * devices, LANES):
        own = jnp.where((first + at >= 0) & (first + at < VECTORS), turned, 0.0)
        total = own[:8]
        for r in range(8, devices, 8):
            total = total + own[r : r + 8]
        tiles.append(sublane_sum(total))
    return jnp.concatenate(tiles, 1)


def rounded(column):
    return column.astype(jnp.bfloat16).astype(jnp.float32)


def times(matrix, line):
    return jnp.sum(matrix * jnp.concatenate([line] * (matrix.shape[0] // 8), 0), 1, keepdims=True)


def lift(inverse_ref, residual):
    return rounded(times(inverse_ref[...], residual))


def lift_packed(ref, residual):
    columns = residual.shape[1]
    at, total = EDGE_AT + INVERSE_AT, None
    for c in range(0, columns - 511, 512):
        term = times(ref[at : at + VECTORS], residual[:, c : c + 512])
        total = term if total is None else total + term
        at += VECTORS
    if columns % 512:
        half = VECTORS // 2
        last = residual[:, columns - 256 :]
        rows = ref[at : at + half]
        term = jnp.concatenate([times(rows[:, :256], last), times(rows[:, 256:], last)], 0)
        total = term if total is None else total + term
    return rounded(total)


def edge_values(ref, lifted):
    starts = [EDGE_AT + VECTORS * a for a in range(2)]
    return [jnp.sum(ref[at : at + VECTORS] * lifted, 0, keepdims=True) for at in starts]


def spread(lifted):
    shape = (VECTORS, CHUNK * VECTORS)
    owner = lax.broadcasted_iota(jnp.int32, shape, 1) // CHUNK
    row = lax.broadcasted_iota(jnp.int32, shape, 0)
    line = jnp.sum(jnp.where(owner == row, lifted, 0.0), 0, keepdims=True)
    shape = (CHUNK, CHUNK * VECTORS)
    place = lax.broadcasted_iota(jnp.int32, shape, 1) % CHUNK
    row = lax.broadcasted_iota(jnp.int32, shape, 0)
    return jnp.where(place == row, line, 0.0).astype(jnp.bfloat16)


def prolonging(residual, inverse_ref, held, extended):
    matrix = spread(lift(inverse_ref, residual))

    def step(a, r):
        rows = held[:, a, r : r + CHUNK, :].reshape(CHUNK * VECTORS, CELLS)
        extended[a, HALO + r : HALO + r + CHUNK] = jnp.dot(
            matrix, rows, preferred_element_type=jnp.float32
        )

    return [functools.partial(step, a, r) for a in range(2) for r in range(0, ROWS, CHUNK)]


def apply_operator(residual, low, high, smooth, extended, visc_ref, coup_ref, direction_ref):
    edges = [edge_values(side, lift_packed(side, residual)) for side in (low, high)]
    place = lax.broadcasted_iota(jnp.int32, (TILE, CELLS), 0)
    tiles = ROWS // TILE

    def read(t, a):
        if t < 0:
            return smooth(a, 0) + jnp.where(place == TILE - 1, edges[0][a], 0.0)
        if t == tiles:
            return smooth(a, t + 1) + jnp.where(place == 0, edges[1][a], 0.0)
        tile = smooth(a, t + 1) + extended[a, tile_rows(t + 1)]
        direction_ref[a, tile_rows(t)] = tile
        return tile

    fields = [Rows(lambda t, a=a: read(t, a), -1, tiles) for a in range(2)]
    for t in range(tiles):
        rows = tile_rows(t)
        viscosity = visc_ref[rows]
        for a in range(2):
            coupling = coup_ref[a, rows]
            diagonal = 10.0 * viscosity + jnp.abs(coupling) + 0.05
            image = (
                diagonal * fields[a].at(t)
                - viscosity * neighbours(fields[a], t, a)
                + coupling * fields[1 - a].at(t)
            )
            yield t, a, image


def lane_total(received, lane):
    place = lax.broadcasted_iota(jnp.int32, received.shape, 1)
    return jnp.sum(jnp.where(place == lane, received, 0.0), keepdims=True)


def first_turn_kernel(
    count, margin_ref, sums_ref, inverse_ref, partner_ref, other_ref, held, rhs_ref, visc_ref,
    coup_ref,
    direction_ref, image_ref, smooth_ref, residual_ref, partner_rows_ref, other_rows_ref, next_ref,
    extended, sums, stacked, solved, lines,
):
    received = sums_ref[...]
    over_beta = 1.0 / jnp.sqrt(lane_total(received, VECTORS))
    residual = line_up(received) * over_beta
    residual_ref[...] = residual
    steps = prolonging(residual, inverse_ref, held, extended)
    low, high = neighbours_of(partner_ref, other_ref)

    def field(a, t):
        at = HALO * (3 + a)
        if t < 0:
            return low[at : at + HALO]
        return high[at : at + HALO] if t == ROWS // TILE else rhs_ref[a, tile_rows(t)]

    solve(
        count, margin_ref, visc_ref, coup_ref, field, low, high, smooth_ref, stacked, solved,
        steps,
    )
    smooth = lambda a, t: smooth_ref[a, tile_rows(t)] * over_beta
    images = apply_operator(
        residual, low, high, smooth, extended, visc_ref, coup_ref, direction_ref
    )
    odd = lax.axis_index("sub") % 2 == 1
    products, squares = [jnp.zeros((TILE, CELLS), jnp.float32)] * 2
    heads, tails = [None] * 2, [None] * 2
    for t, a, image in images:
        image_ref[a, tile_rows(t)] = image
        products = products + rhs_ref[a, tile_rows(t)] * image
        squares = squares + image * image
        if t == 0:
            heads[a] = image
        if t == ROWS // TILE - 1:
            tails[a] = image
    half = lax.broadcasted_iota(jnp.int32, (TILE, CELLS), 0) < TILE // 2
    head = jnp.where(half, heads[0], pltpu.roll(heads[1], TILE // 2, 0))
    tail = jnp.where(half, pltpu.roll(tails[1], TILE // 2, 0), tails[0])
    partner_rows_ref[...] = jnp.where(odd, head, tail)
    other_rows_ref[...] = jnp.where(odd, tail, head)
    sums[...] = jnp.zeros_like(sums)
    sums[VECTORS : VECTORS + 8] = in_rows([fold(products), fold(squares)])

    restrict(held, image_ref, sums, lines)
    send_sums(sums, next_ref)


def first_column(first, second):
    beta = jnp.sqrt(lane_total(first, VECTORS))
    h_00 = lane_total(second, VECTORS) / beta
    h_10 = jnp.sqrt(lane_total(second, VECTORS + 1) - h_00 * h_00)
    return beta, h_00, h_10


def second_turn_kernel(
    count, margin_ref, first_ref, second_ref, residual_ref, inverse_ref, partner_ref, other_ref,
    partner_rows_ref, other_rows_ref, held, smooth_ref, rhs_ref, image_ref, visc_ref, coup_ref,
    direction_ref, next_ref,
    image_smooth, extended, sums, stacked, solved,
):
    first, second = first_ref[...], second_ref[...]
    beta, h_00, h_10 = first_column(first, second)
    ratio = h_00 / beta
    over = 1.0 / h_10
    residual = (line_up(second) - h_00 * residual_ref[...]) * over
    steps = prolonging(residual, inverse_ref, held, extended)
    low, high = neighbours_of(partner_ref, other_ref)
    low_rows, high_rows = neighbours_of(partner_rows_ref, other_rows_ref)

    def field(a, t):
        if 0 <= t < ROWS // TILE:
            return image_ref[a, tile_rows(t)]
        rows = low_rows[...] if t < 0 else high_rows[...]
        return pltpu.roll(rows, TILE // 2, 0) if a else rows

    solve(
        count, margin_ref, visc_ref, coup_ref, field, low, high, image_smooth, stacked, solved,
        steps,
    )

    def smooth(a, t):
        rows = tile_rows(t)
        return (image_smooth[a, rows] - ratio * smooth_ref[a, rows]) * over

    images = apply_operator(
        residual, low, high, smooth, extended, visc_ref, coup_ref, direction_ref
    )
    totals = [jnp.zeros((TILE, CELLS), jnp.float32)] * 3
    for t, a, image in images:
        others = (rhs_ref[a, tile_rows(t)], image_ref[a, tile_rows(t)], image)
        totals = [total + x * image for total, x in zip(totals, others)]
    sums[...] = jnp.zeros_like(sums)
    sums[:8] = in_rows([fold(total) for total in totals])
    send_sums(sums, next_ref)


def finish_kernel(
    first_ref, second_ref, third_ref, first_direction_ref, second_direction_ref,
    solution_ref, hessenberg_ref,
):
    third = third_ref[...]
    beta, h_00, h_10 = first_column(first_ref[...], second_ref[...])
    squares = lane_total(third, 2)
    h_01 = lane_total(third, 0) / beta
    h_11 = (lane_total(third, 1) - h_00 * h_01) / h_10
    h_21 = jnp.sqrt(squares - h_01 * h_01 - h_11 * h_11)
    l_00 = jnp.sqrt(h_00 * h_00 + h_10 * h_10)
    l_10 = (h_00 * h_01 + h_10 * h_11) / l_00
    f_0 = beta * h_00 / l_00
    c_1 = (beta * h_01 - l_10 * f_0) / (squares - l_10 * l_10)
    c_0 = (f_0 - l_10 * c_1) / l_00
    for a in range(2):
        solution_ref[a] = c_0 * first_direction_ref[a] + c_1 * second_direction_ref[a]
    shape = hessenberg_ref.shape
    row = lax.broadcasted_iota(jnp.int32, shape, 1)
    column = lax.broadcasted_iota(jnp.int32, shape, 0)
    entries = jnp.zeros(shape, jnp.float32)
    for i, j, value in ((0, 0, h_00), (0, 1, h_01), (1, 0, h_10), (1, 1, h_11), (2, 1, h_21)):
        entries = jnp.where((row == i) & (column == j), value, entries)
    hessenberg_ref[...] = entries


def call(kernel, name, in_specs, outs, flops, scratch=(), traffic=4_000_000):
    return pl.pallas_call(
        kernel,
        name=name,
        in_specs=in_specs,
        out_specs=[VMEM] * len(outs),
        out_shape=outs,
        scratch_shapes=scratch,
        compiler_params=pltpu.CompilerParams(vmem_limit_bytes=16 * 1024 * 1024),
        cost_estimate=pl.CostEstimate(flops=flops, bytes_accessed=traffic, transcendentals=0),
    )


def in_hbm(array):
    return pltpu.with_memory_space_constraint(array, pltpu.HBM)


def from_everyone(rows):
    order = [list(range(lax.axis_size("sub")))[::-1]]
    return lax.all_to_all(rows, "sub", 0, 0, tiled=True, axis_index_groups=order)


def swap(partner, other):
    count = lax.axis_size("sub")
    both = lambda lows: [pair for i in lows for pair in ((i, i + 1), (i + 1, i))]
    return (
        lax.ppermute(partner, "sub", both(range(0, count, 2))),
        lax.ppermute(other, "sub", both(range(1, count - 1, 2))),
    )


def on_device(rhs, viscosity, coupling, margin_rows, coarse_basis, coarse_inverse):
    count = lax.axis_size("sub")
    columns = coarse_inverse.shape[1]
    f32 = lambda *shape: jax.ShapeDtypeStruct(shape, jnp.float32)
    dma = lambda *shape: pltpu.SemaphoreType.DMA(shape)
    extended = pltpu.VMEM((2, EXT, CELLS), jnp.float32)
    stacked = pltpu.VMEM((6, STACKED, CELLS), jnp.float32)
    solved = pltpu.VMEM((4, STACKED, CELLS), jnp.float32)
    sums = pltpu.VMEM((SLOTS, LANES), jnp.float32)
    lines = pltpu.VMEM((LANES, len(MATRIX_GROUPS) * CELLS), jnp.bfloat16)
    row, whole, edge = f32(count, LANES), f32(2, ROWS, CELLS), f32(TILE, CELLS)
    packed, smoothed = f32(EDGE_AT + coarse_rows(columns), CELLS), f32(2, EXT, CELLS)
    arguments = (rhs, viscosity, coupling, coarse_inverse, coarse_basis)
    packs = call(
        pack_kernel, "pack", [HBM] * 5, [packed, packed], 5_000_000,
        [pltpu.VMEM((4, VECTORS, CHUNK, CELLS), jnp.bfloat16), dma(4 * VECTORS // GROUP)]
        + [dma(2 * pack_count(columns))],
    )(*map(in_hbm, arguments))
    held, partner, other = lax.optimization_barrier((coarse_basis, *packs))
    partner, other = swap(partner, other)
    (first,) = call(
        restrict_kernel, "restrict", [VMEM] * 2, [row], 10_000_000, [sums]
    )(rhs, held)
    first = from_everyone(first)
    direction, image, smooth, residual, partner_rows, other_rows, second = call(
        functools.partial(first_turn_kernel, count), "first_turn", [SMEM] + [VMEM] * 8,
        [whole, whole, smoothed, f32(8, columns), edge, edge, row], 20_000_000,
        [extended, sums, stacked, solved, lines],
    )(margin_rows, first, coarse_inverse, partner, other, held, rhs, viscosity, coupling)
    partner_rows, other_rows = swap(partner_rows, other_rows)
    second = from_everyone(second)
    second_direction, third = call(
        functools.partial(second_turn_kernel, count), "second_turn", [SMEM] + [VMEM] * 14,
        [whole, row], 20_000_000, [extended, extended, sums, stacked, solved],
    )(
        margin_rows, first, second, residual, coarse_inverse, partner, other, partner_rows, other_rows,
        held, smooth, rhs, image, viscosity, coupling,
    )
    third = from_everyone(third)
    result, transposed = call(finish_kernel, "finish", [VMEM] * 5, [whole, f32(2, 3)], 1_000_000)(
        first, second, third, direction, second_direction
    )
    return result, transposed.T


def solution(mesh):
    in_specs = (
        P(None, ("groups", "sub"), None),
        P(("groups", "sub"), None),
        P(None, ("groups", "sub"), None),
        P("groups"),
        P(None, None, ("groups", "sub"), None),
        P(("groups", "sub"), None),
    )
    out_specs = (P(None, ("groups", "sub"), None), P("groups", None))
    return jax.shard_map(
        on_device, mesh=mesh, in_specs=in_specs, out_specs=out_specs, check_vma=False
    )
```

```python
import functools

import jax
import jax.numpy as jnp
from jax import lax
from jax.experimental import pallas as pl
from jax.experimental.pallas import tpu as pltpu
from jax.sharding import PartitionSpec as P

ROWS = 64
CELLS = 512
VECTORS = 48
HALO = 8
EXT = ROWS + 2 * HALO
STRIP = 32
GROUP = 16
STACKED = EXT + 2 * STRIP
TILE = 8
CHUNK = 16
CHUNKS = 2 * ROWS // CHUNK
PIECE = 8
LANES = 128
SLOTS = 64
EDGE_AT = 5 * HALO
INVERSE_AT = 2 * VECTORS
SWEEPS = 4
RELAX = 0.7
ROW_FACTOR = (1.0, 4.0)
CELL_FACTOR = (4.0, 1.0)

VMEM = pl.BlockSpec(memory_space=pltpu.VMEM)
SMEM = pl.BlockSpec(memory_space=pltpu.SMEM)
HBM = pl.BlockSpec(memory_space=pltpu.HBM)


def coarse_rows(columns):
    return INVERSE_AT + VECTORS * (columns // 512) + (VECTORS // 2) * (columns % 512 // 256)


def cell_sum(field):
    lane = lax.broadcasted_iota(jnp.int32, (field.shape[0], LANES), 1)
    left, right = pltpu.roll(field, 1, 1), pltpu.roll(field, CELLS - 1, 1)
    inner = left[:, LANES:-LANES] + right[:, LANES:-LANES]
    first = jnp.where(lane == 0, 0.0, left[:, :LANES]) + right[:, :LANES]
    last = left[:, -LANES:] + jnp.where(lane == LANES - 1, 0.0, right[:, -LANES:])
    return jnp.concatenate([first, inner, last], 1)


class Rows:
    def __init__(self, read, first, last):
        self.read, self.first, self.last = read, first, last
        self.tiles, self.down, self.up = {}, {}, {}

    def at(self, t):
        if t not in self.tiles:
            self.tiles[t] = self.read(t)
        return self.tiles[t]

    def moved(self, held, t, by):
        if t not in held:
            held[t] = pltpu.roll(self.at(t), by, 0)
        return held[t]

    def around(self, t):
        row = lax.broadcasted_iota(jnp.int32, (TILE, CELLS), 0)
        below, above = self.moved(self.down, t, 1), self.moved(self.up, t, TILE - 1)
        if t > self.first:
            below = jnp.where(row == 0, self.moved(self.down, t - 1, 1), below)
        if t < self.last:
            above = jnp.where(row == TILE - 1, self.moved(self.up, t + 1, TILE - 1), above)
        return below + above


def neighbours(rows, t, component):
    around, cells = rows.around(t), cell_sum(rows.at(t))
    if component == 0:
        return around + CELL_FACTOR[0] * cells
    return ROW_FACTOR[1] * around + cells


def sublane_sum(tile):
    for by in (4, 2, 1):
        tile = tile + pltpu.roll(tile, by, 0)
    return tile


def in_rows(tiles):
    row = lax.broadcasted_iota(jnp.int32, (8, LANES), 0)
    total = jnp.zeros((8, LANES), jnp.float32)
    for n, tile in enumerate(tiles):
        total = jnp.where(row == n, sublane_sum(tile), total)
    return total


def restrict_piece(i, held, field, sums):
    totals = [None] * PIECE
    for a in range(2):
        for r in range(0, ROWS, CHUNK):
            for c in range(0, CELLS, LANES):
                rows, cells = slice(r, r + CHUNK), slice(c, c + LANES)
                tile = field[a, rows, cells]
                for n in range(PIECE):
                    term = held[PIECE * i + n, a, rows, cells].astype(jnp.float32) * tile
                    totals[n] = term if totals[n] is None else totals[n] + term
    tiles = [total[:8] + total[8:] for total in totals]
    sums[pl.ds(pl.multiple_of(PIECE * i, PIECE), PIECE), :] = in_rows(tiles)


MATRIX_GROUPS = tuple((1, r) for r in range(CHUNK, ROWS, CHUNK))
VECTOR_GROUPS = ((0, 0), (0, 16), (0, 32), (0, 48), (1, 0))


def restrict(held, field, sums, lines):
    lines[2 * CHUNK :] = jnp.zeros((LANES - 2 * CHUNK, lines.shape[1]), jnp.bfloat16)
    blocks = []
    for g, (a, r) in enumerate(MATRIX_GROUPS):
        part, cells = field[a, r : r + CHUNK], slice(CELLS * g, CELLS * (g + 1))
        high = part.astype(jnp.bfloat16)
        lines[:CHUNK, cells] = high
        lines[CHUNK : 2 * CHUNK, cells] = (part - high.astype(jnp.float32)).astype(jnp.bfloat16)
        blocks.append(held[:, a, r : r + CHUNK, :].reshape(CHUNK * VECTORS, CELLS))
    products = lax.dot_general(
        jnp.concatenate(blocks, 1),
        lines[...],
        (((1,), (1,)), ((), ())),
        preferred_element_type=jnp.float32,
    )
    row = lax.broadcasted_iota(jnp.int32, (CHUNK, LANES), 0)
    equal = row == lax.broadcasted_iota(jnp.int32, (CHUNK, LANES), 1) % CHUNK
    for first in range(0, VECTORS, PIECE):
        totals = [
            jnp.where(equal, products[CHUNK * k : CHUNK * (k + 1)], 0.0)
            for k in range(first, first + PIECE)
        ]
        for a, r in VECTOR_GROUPS:
            for c in range(0, CELLS, LANES):
                rows, cells = slice(r, r + CHUNK), slice(c, c + LANES)
                tile = field[a, rows, cells]
                for n in range(PIECE):
                    term = held[first + n, a, rows, cells].astype(jnp.float32) * tile
                    totals[n] = totals[n] + term
        sums[first : first + PIECE] = in_rows([total[:8] + total[8:] for total in totals])


def fold(row):
    total = row[:, :LANES]
    for c in range(LANES, CELLS, LANES):
        total = total + row[:, c : c + LANES]
    return total


def tile_rows(t):
    return slice(TILE * t, TILE * (t + 1))


def send_sums(sums, out_ref):
    rest = sums[...]
    parts = []
    for _ in range(3):
        part = rest.astype(jnp.bfloat16)
        parts.append(part)
        rest = rest - part.astype(jnp.float32)
    row = lax.dot_general(
        jnp.ones((CHUNK, 3 * LANES), jnp.bfloat16),
        jnp.concatenate(parts, 1),
        (((1,), (1,)), ((), ())),
        preferred_element_type=jnp.float32,
    )
    wide = jnp.concatenate([row[:1], jnp.zeros((1, LANES - SLOTS), jnp.float32)], 1)
    out_ref[...] = jnp.broadcast_to(wide, out_ref.shape)


def pack_copies(out_ref, first_row, rhs_ref, visc_ref, coup_ref, inverse_ref, sems, at_sem):
    rows = pl.ds(pl.multiple_of(first_row, HALO), HALO)
    moves = [(visc_ref.at[rows, :], 0, HALO, None)]
    for a in range(2):
        moves.append((coup_ref.at[a, rows, :], HALO * (1 + a), HALO, None))
        moves.append((rhs_ref.at[a, rows, :], HALO * (3 + a), HALO, None))
    columns = inverse_ref.shape[1]
    at = EDGE_AT + INVERSE_AT
    for c in range(0, columns - 511, 512):
        moves.append((inverse_ref.at[:, pl.ds(c, 512)], at, VECTORS, None))
        at += VECTORS
    if columns % 512:
        half = VECTORS // 2
        last = pl.ds(columns - 256, 256)
        moves.append((inverse_ref.at[pl.ds(0, half), last], at, half, 0))
        moves.append((inverse_ref.at[pl.ds(half, half), last], at, half, 256))
    copies = []
    for n, (source, at, size, lane) in enumerate(moves):
        place = pl.ds(at, size)
        target = out_ref.at[place, :] if lane is None else out_ref.at[place, pl.ds(lane, 256)]
        copies.append(pltpu.make_async_copy(source, target, sems.at[at_sem + n]))
    return copies


def pack_count(columns):
    return 5 + columns // 512 + 2 * (columns % 512 // 256)


def pack_kernel(
    rhs_ref, visc_ref, coup_ref, inverse_ref, basis_ref,
    partner_ref, other_ref,
    groups, group_sems, pack_sems,
):
    odd = lax.axis_index("sub") % 2
    sides = ((partner_ref, 1 - odd), (other_ref, odd))
    group_copies, packs = [], []
    for k in range(0, VECTORS, GROUP):
        for n, (out_ref, up) in enumerate(sides):
            rows = pl.ds(pl.multiple_of(up * (ROWS - CHUNK), CHUNK), CHUNK)
            for a in range(2):
                group_copies.append(
                    pltpu.make_async_copy(
                        basis_ref.at[pl.ds(k, GROUP), a, rows, :],
                        groups.at[2 * n + a, pl.ds(k, GROUP)],
                        group_sems.at[len(group_copies)],
                    )
                )
    for n, (out_ref, up) in enumerate(sides):
        packs += pack_copies(
            out_ref, up * (ROWS - HALO), rhs_ref, visc_ref, coup_ref, inverse_ref, pack_sems,
            n * pack_count(inverse_ref.shape[1]),
        )
    for copy in group_copies + packs:
        copy.start()

    def take(out_ref, group, first, row):
        for k in range(first, first + GROUP, TILE):
            lines = [groups[group, k + n].astype(jnp.float32)[row : row + 1] for n in range(TILE)]
            at = EDGE_AT + VECTORS * (group % 2) + k
            out_ref[at : at + TILE] = jnp.concatenate(lines, 0)

    for first in range(0, VECTORS, GROUP):
        for _ in range(4):
            group_copies.pop(0).wait()

        @pl.when(odd == 0)
        def _():
            for a in range(2):
                take(partner_ref, a, first, CHUNK - 1)
                take(other_ref, 2 + a, first, 0)

        @pl.when(odd == 1)
        def _():
            for a in range(2):
                take(partner_ref, a, first, 0)
                take(other_ref, 2 + a, first, CHUNK - 1)

    for copy in packs:
        copy.wait()


def restrict_kernel(rhs_ref, held, sums_ref, sums):
    sums[...] = jnp.zeros_like(sums)
    squares = jnp.zeros((TILE, CELLS), jnp.float32)
    for a in range(2):
        for t in range(ROWS // TILE):
            tile = rhs_ref[a, tile_rows(t)]
            squares = squares + tile * tile
    sums[VECTORS : VECTORS + 8] = in_rows([fold(squares)])

    def body(i, carry):
        restrict_piece(i, held, rhs_ref, sums)
        return carry

    lax.fori_loop(0, VECTORS // PIECE, body, 0)
    send_sums(sums, sums_ref)


class Neighbour:
    def __init__(self, first_ref, second_ref):
        self.odd = lax.axis_index("sub") % 2 == 1
        self.first, self.second = first_ref, second_ref

    def __getitem__(self, index):
        return jnp.where(self.odd, self.first[index], self.second[index])


def neighbours_of(partner_ref, other_ref):
    return Neighbour(partner_ref, other_ref), Neighbour(other_ref, partner_ref)


def solve(count, margin_ref, visc_ref, coup_ref, field, low, high, out_ref, stacked, solved, steps):
    waiting, done = list(steps), 0
    every = (SWEEPS - 1) * (STACKED // TILE) // len(waiting)
    assert every > 0
    rank = lax.axis_index("sub")
    lower = jnp.where(rank > 0, margin_ref[jnp.maximum(rank - 1, 0)], 0)
    upper = jnp.where(rank < count - 1, margin_ref[rank], 0)
    lower_f, upper_f = lower.astype(jnp.float32), upper.astype(jnp.float32)
    low_scale = 1.0 / (2.0 * jnp.maximum(lower_f, 1.0))
    high_scale = 1.0 / (2.0 * jnp.maximum(upper_f, 1.0))
    wide = lambda x: jnp.concatenate([x] * (CELLS // LANES), 1)
    own_tiles = ROWS // TILE
    strip_tiles = STRIP // TILE
    last = own_tiles + 1
    segments = (
        (0, 0, last + 1),
        (last + 1, 0, strip_tiles),
        (last + 1 + strip_tiles, last + 1 - strip_tiles, strip_tiles),
    )

    def place_of(e):
        return lax.broadcasted_iota(jnp.int32, (TILE, LANES), 0) + (TILE * e - HALO)

    def live_of(segment, e):
        place = place_of(e)
        if segment == 0:
            live = (place >= -lower) & (place < ROWS + upper)
        elif segment == 1:
            live = place < lower
        else:
            live = place >= ROWS - upper
        return wide(live.astype(jnp.float32))

    def weight_of(segment, e):
        place = place_of(e)
        place_f = place.astype(jnp.float32)
        rising = lambda base, scale: (place_f - base + 0.5) * scale
        falling = lambda base, scale: (base - place_f - 0.5) * scale
        if segment == 0:
            weight = jnp.where(place < lower, rising(-lower_f, low_scale), 1.0)
            weight = jnp.where(
                place >= ROWS - upper, falling(ROWS + upper_f, high_scale), weight
            )
        elif segment == 1:
            weight = jnp.where(place >= -lower, falling(lower_f, low_scale), 1.0)
        else:
            weight = jnp.where(place < ROWS + upper, rising(ROWS - upper_f, high_scale), 1.0)
        return wide(weight)

    def extended(ref, at, e):
        if e == 0:
            return low[at : at + HALO]
        if e == last:
            return high[at : at + HALO]
        return ref[tile_rows(e - 1)]

    for e in range(last + 1):
        viscosity = extended(visc_ref, 0, e)
        for a in range(2):
            coupling = extended(coup_ref.at[a], HALO * (1 + a), e)
            scale = RELAX / (10.0 * viscosity + jnp.abs(coupling) + 0.05)
            parts = (scale * field(a, e - 1), scale * viscosity, scale * coupling)
            for n, (first, begin, size) in enumerate(segments):
                if not begin <= e < begin + size:
                    continue
                rows = tile_rows(first + e - begin)
                always = n == 0 and 0 < e < last
                for m, part in enumerate(parts):
                    stacked[3 * a + m, rows] = part if always else live_of(n, e) * part

    for sweep in range(1, SWEEPS):
        for n, (first, begin, size) in enumerate(segments):
            end = first + size - 1
            if sweep == 1:
                reads = [lambda t, a=a: stacked[3 * a, tile_rows(t)] for a in range(2)]
            else:
                bank = 2 * (sweep % 2)
                reads = [lambda t, a=a: solved[bank + a, tile_rows(t)] for a in range(2)]
            fields = [Rows(read, first, end) for read in reads]
            for t in range(first, end + 1):
                rows = tile_rows(t)
                if done % every == 0 and waiting:
                    waiting.pop(0)()
                done += 1
                for a in range(2):
                    value = (
                        ((1.0 - RELAX) * fields[a].at(t) + stacked[3 * a, rows])
                        + stacked[3 * a + 1, rows] * neighbours(fields[a], t, a)
                        - stacked[3 * a + 2, rows] * fields[1 - a].at(t)
                    )
                    e = t - first + begin
                    if sweep < SWEEPS - 1:
                        solved[2 * ((sweep + 1) % 2) + a, rows] = value
                    elif n == 0:
                        out_ref[a, tile_rows(e)] = weight_of(n, e) * value
                    else:
                        out_ref[a, tile_rows(e)] += weight_of(n, e) * value


def line_up(residuals):
    devices = residuals.shape[0]
    lane = lax.broadcasted_iota(jnp.int32, (1, LANES), 1)
    tiles = [jnp.zeros((1, LANES), jnp.float32) for _ in range(devices * VECTORS // LANES)]
    for t in range(devices):
        tile, offset = divmod(VECTORS * t, LANES)
        row = jnp.where(lane < VECTORS, residuals[devices - 1 - t : devices - t], 0.0)
        if offset:
            row = pltpu.roll(row, offset, 1)
        if offset + VECTORS <= LANES:
            tiles[tile] = tiles[tile] + row
        else:
            tiles[tile] = tiles[tile] + jnp.where(lane >= offset, row, 0.0)
            tiles[tile + 1] = tiles[tile + 1] + jnp.where(lane < offset, row, 0.0)
    return jnp.concatenate(tiles, 1)


def rounded(column):
    return column.astype(jnp.bfloat16).astype(jnp.float32)


def lift(inverse_ref, residual):
    return rounded(jnp.sum(inverse_ref[...] * residual, 1, keepdims=True))


def lift_packed(ref, residual):
    columns = residual.shape[1]
    at, total = EDGE_AT + INVERSE_AT, None
    for c in range(0, columns - 511, 512):
        term = jnp.sum(ref[at : at + VECTORS] * residual[:, c : c + 512], 1, keepdims=True)
        total = term if total is None else total + term
        at += VECTORS
    if columns % 512:
        half = VECTORS // 2
        last = residual[:, columns - 256 :]
        rows = ref[at : at + half]
        term = jnp.concatenate(
            [
                jnp.sum(rows[:, :256] * last, 1, keepdims=True),
                jnp.sum(rows[:, 256:] * last, 1, keepdims=True),
            ],
            0,
        )
        total = term if total is None else total + term
    return rounded(total)


def edge_values(ref, lifted):
    starts = [EDGE_AT + VECTORS * a for a in range(2)]
    return [jnp.sum(ref[at : at + VECTORS] * lifted, 0, keepdims=True) for at in starts]


def spread(lifted):
    shape = (VECTORS, CHUNK * VECTORS)
    owner = lax.broadcasted_iota(jnp.int32, shape, 1) // CHUNK
    row = lax.broadcasted_iota(jnp.int32, shape, 0)
    line = jnp.sum(jnp.where(owner == row, lifted, 0.0), 0, keepdims=True)
    shape = (CHUNK, CHUNK * VECTORS)
    place = lax.broadcasted_iota(jnp.int32, shape, 1) % CHUNK
    row = lax.broadcasted_iota(jnp.int32, shape, 0)
    return jnp.where(place == row, line, 0.0).astype(jnp.bfloat16)


class Coarse:
    def __init__(self, begin, inverse_ref, low, high, held, extended):
        self.inverse, self.sides, self.held, self.extended = inverse_ref, (low, high), held, extended
        self.lifted, self.edges = [None] * 2, [None] * 2
        self.steps = begin(self) + [self.lift_own, self.make_matrix]
        for a in range(2):
            for r in range(0, ROWS, CHUNK):
                self.steps.append(functools.partial(self.prolong, a, r))
        for n in range(2):
            self.steps.insert(len(self.steps) - 6, functools.partial(self.lift_side, n))
            self.steps.append(functools.partial(self.edge, n))

    def lift_own(self):
        self.own = lift(self.inverse, self.residual)

    def make_matrix(self):
        self.matrix = spread(self.own)

    def prolong(self, a, r):
        rows = self.held[:, a, r : r + CHUNK, :].reshape(CHUNK * VECTORS, CELLS)
        self.extended[a, HALO + r : HALO + r + CHUNK] = jnp.dot(
            self.matrix, rows, preferred_element_type=jnp.float32
        )

    def lift_side(self, n):
        self.lifted[n] = lift_packed(self.sides[n], self.residual)

    def edge(self, n):
        self.edges[n] = edge_values(self.sides[n], self.lifted[n])


def apply_operator(edges, smooth, extended, visc_ref, coup_ref, direction_ref):
    place = lax.broadcasted_iota(jnp.int32, (TILE, CELLS), 0)
    tiles = ROWS // TILE

    def read(t, a):
        if t < 0:
            return smooth(a, 0) + jnp.where(place == TILE - 1, edges[0][a], 0.0)
        if t == tiles:
            return smooth(a, t + 1) + jnp.where(place == 0, edges[1][a], 0.0)
        tile = smooth(a, t + 1) + extended[a, tile_rows(t + 1)]
        direction_ref[a, tile_rows(t)] = tile
        return tile

    fields = [Rows(lambda t, a=a: read(t, a), -1, tiles) for a in range(2)]
    for t in range(tiles):
        rows = tile_rows(t)
        viscosity = visc_ref[rows]
        for a in range(2):
            coupling = coup_ref[a, rows]
            diagonal = 10.0 * viscosity + jnp.abs(coupling) + 0.05
            image = (
                diagonal * fields[a].at(t)
                - viscosity * neighbours(fields[a], t, a)
                + coupling * fields[1 - a].at(t)
            )
            yield t, a, image


def lane_total(received, lane):
    place = lax.broadcasted_iota(jnp.int32, received.shape, 1)
    return jnp.sum(jnp.where(place == lane, received, 0.0), keepdims=True)


def first_turn_kernel(
    count, margin_ref, sums_ref, inverse_ref, partner_ref, other_ref, held, rhs_ref, visc_ref,
    coup_ref,
    direction_ref, image_ref, smooth_ref, residual_ref, partner_rows_ref, other_rows_ref, next_ref,
    extended, sums, stacked, solved, lines,
):
    low, high = neighbours_of(partner_ref, other_ref)

    def begin(coarse):
        def scale():
            coarse.over_beta = 1.0 / jnp.sqrt(lane_total(sums_ref[...], VECTORS))

        def line():
            coarse.residual = line_up(sums_ref[...]) * coarse.over_beta
            residual_ref[...] = coarse.residual

        return [scale, line]

    coarse = Coarse(begin, inverse_ref, low, high, held, extended)

    def field(a, t):
        at = HALO * (3 + a)
        if t < 0:
            return low[at : at + HALO]
        return high[at : at + HALO] if t == ROWS // TILE else rhs_ref[a, tile_rows(t)]

    solve(
        count, margin_ref, visc_ref, coup_ref, field, low, high, smooth_ref, stacked, solved,
        coarse.steps,
    )
    smooth = lambda a, t: smooth_ref[a, tile_rows(t)] * coarse.over_beta
    images = apply_operator(
        coarse.edges, smooth, extended, visc_ref, coup_ref, direction_ref
    )
    odd = lax.axis_index("sub") % 2 == 1
    products, squares = [jnp.zeros((TILE, CELLS), jnp.float32)] * 2
    heads, tails = [None] * 2, [None] * 2
    for t, a, image in images:
        image_ref[a, tile_rows(t)] = image
        products = products + rhs_ref[a, tile_rows(t)] * image
        squares = squares + image * image
        if t == 0:
            heads[a] = image
        if t == ROWS // TILE - 1:
            tails[a] = image
    half = lax.broadcasted_iota(jnp.int32, (TILE, CELLS), 0) < TILE // 2
    head = jnp.where(half, heads[0], pltpu.roll(heads[1], TILE // 2, 0))
    tail = jnp.where(half, pltpu.roll(tails[1], TILE // 2, 0), tails[0])
    partner_rows_ref[...] = jnp.where(odd, head, tail)
    other_rows_ref[...] = jnp.where(odd, tail, head)
    sums[...] = jnp.zeros_like(sums)
    sums[VECTORS : VECTORS + 8] = in_rows([fold(products), fold(squares)])

    restrict(held, image_ref, sums, lines)
    send_sums(sums, next_ref)


def first_column(first, second):
    beta = jnp.sqrt(lane_total(first, VECTORS))
    h_00 = lane_total(second, VECTORS) / beta
    h_10 = jnp.sqrt(lane_total(second, VECTORS + 1) - h_00 * h_00)
    return beta, h_00, h_10


def second_turn_kernel(
    count, margin_ref, first_ref, second_ref, residual_ref, inverse_ref, partner_ref, other_ref,
    partner_rows_ref, other_rows_ref, held, smooth_ref, rhs_ref, image_ref, visc_ref, coup_ref,
    direction_ref, next_ref,
    image_smooth, extended, sums, stacked, solved,
):
    low, high = neighbours_of(partner_ref, other_ref)

    def begin(coarse):
        def scale():
            beta, h_00, h_10 = first_column(first_ref[...], second_ref[...])
            coarse.h_00, coarse.ratio, coarse.over = h_00, h_00 / beta, 1.0 / h_10

        def line():
            lined = line_up(second_ref[...])
            coarse.residual = (lined - coarse.h_00 * residual_ref[...]) * coarse.over

        return [scale, line]

    coarse = Coarse(begin, inverse_ref, low, high, held, extended)
    low_rows, high_rows = neighbours_of(partner_rows_ref, other_rows_ref)

    def field(a, t):
        if 0 <= t < ROWS // TILE:
            return image_ref[a, tile_rows(t)]
        rows = low_rows[...] if t < 0 else high_rows[...]
        return pltpu.roll(rows, TILE // 2, 0) if a else rows

    solve(
        count, margin_ref, visc_ref, coup_ref, field, low, high, image_smooth, stacked, solved,
        coarse.steps,
    )

    def smooth(a, t):
        rows = tile_rows(t)
        return (image_smooth[a, rows] - coarse.ratio * smooth_ref[a, rows]) * coarse.over

    images = apply_operator(
        coarse.edges, smooth, extended, visc_ref, coup_ref, direction_ref
    )
    totals = [jnp.zeros((TILE, CELLS), jnp.float32)] * 3
    for t, a, image in images:
        others = (rhs_ref[a, tile_rows(t)], image_ref[a, tile_rows(t)], image)
        totals = [total + x * image for total, x in zip(totals, others)]
    sums[...] = jnp.zeros_like(sums)
    sums[:8] = in_rows([fold(total) for total in totals])
    send_sums(sums, next_ref)


def finish_kernel(
    first_ref, second_ref, third_ref, first_direction_ref, second_direction_ref,
    solution_ref, hessenberg_ref,
):
    third = third_ref[...]
    beta, h_00, h_10 = first_column(first_ref[...], second_ref[...])
    squares = lane_total(third, 2)
    h_01 = lane_total(third, 0) / beta
    h_11 = (lane_total(third, 1) - h_00 * h_01) / h_10
    h_21 = jnp.sqrt(squares - h_01 * h_01 - h_11 * h_11)
    l_00 = jnp.sqrt(h_00 * h_00 + h_10 * h_10)
    l_10 = (h_00 * h_01 + h_10 * h_11) / l_00
    f_0 = beta * h_00 / l_00
    c_1 = (beta * h_01 - l_10 * f_0) / (squares - l_10 * l_10)
    c_0 = (f_0 - l_10 * c_1) / l_00
    for a in range(2):
        solution_ref[a] = c_0 * first_direction_ref[a] + c_1 * second_direction_ref[a]
    shape = hessenberg_ref.shape
    row = lax.broadcasted_iota(jnp.int32, shape, 1)
    column = lax.broadcasted_iota(jnp.int32, shape, 0)
    entries = jnp.zeros(shape, jnp.float32)
    for i, j, value in ((0, 0, h_00), (0, 1, h_01), (1, 0, h_10), (1, 1, h_11), (2, 1, h_21)):
        entries = jnp.where((row == i) & (column == j), value, entries)
    hessenberg_ref[...] = entries


def call(kernel, name, in_specs, outs, flops, scratch=(), traffic=4_000_000):
    return pl.pallas_call(
        kernel,
        name=name,
        in_specs=in_specs,
        out_specs=[VMEM] * len(outs),
        out_shape=outs,
        scratch_shapes=scratch,
        compiler_params=pltpu.CompilerParams(vmem_limit_bytes=16 * 1024 * 1024),
        cost_estimate=pl.CostEstimate(flops=flops, bytes_accessed=traffic, transcendentals=0),
    )


def in_hbm(array):
    return pltpu.with_memory_space_constraint(array, pltpu.HBM)


def from_everyone(rows):
    order = [list(range(lax.axis_size("sub")))[::-1]]
    return lax.all_to_all(rows, "sub", 0, 0, tiled=True, axis_index_groups=order)


def swap(partner, other):
    count = lax.axis_size("sub")
    both = lambda lows: [pair for i in lows for pair in ((i, i + 1), (i + 1, i))]
    return (
        lax.ppermute(partner, "sub", both(range(0, count, 2))),
        lax.ppermute(other, "sub", both(range(1, count - 1, 2))),
    )


def on_device(rhs, viscosity, coupling, margin_rows, coarse_basis, coarse_inverse):
    count = lax.axis_size("sub")
    columns = coarse_inverse.shape[1]
    f32 = lambda *shape: jax.ShapeDtypeStruct(shape, jnp.float32)
    dma = lambda *shape: pltpu.SemaphoreType.DMA(shape)
    extended = pltpu.VMEM((2, EXT, CELLS), jnp.float32)
    stacked = pltpu.VMEM((6, STACKED, CELLS), jnp.float32)
    solved = pltpu.VMEM((4, STACKED, CELLS), jnp.float32)
    sums = pltpu.VMEM((SLOTS, LANES), jnp.float32)
    lines = pltpu.VMEM((LANES, len(MATRIX_GROUPS) * CELLS), jnp.bfloat16)
    row, whole, edge = f32(count, LANES), f32(2, ROWS, CELLS), f32(TILE, CELLS)
    packed, smoothed = f32(EDGE_AT + coarse_rows(columns), CELLS), f32(2, EXT, CELLS)
    arguments = (rhs, viscosity, coupling, coarse_inverse, coarse_basis)
    packs = call(
        pack_kernel, "pack", [HBM] * 5, [packed, packed], 5_000_000,
        [pltpu.VMEM((4, VECTORS, CHUNK, CELLS), jnp.bfloat16), dma(4 * VECTORS // GROUP)]
        + [dma(2 * pack_count(columns))],
    )(*map(in_hbm, arguments))
    held, partner, other = lax.optimization_barrier((coarse_basis, *packs))
    partner, other = swap(partner, other)
    (first,) = call(
        restrict_kernel, "restrict", [VMEM] * 2, [row], 10_000_000, [sums]
    )(rhs, held)
    first = from_everyone(first)
    direction, image, smooth, residual, partner_rows, other_rows, second = call(
        functools.partial(first_turn_kernel, count), "first_turn", [SMEM] + [VMEM] * 8,
        [whole, whole, smoothed, f32(1, columns), edge, edge, row], 20_000_000,
        [extended, sums, stacked, solved, lines],
    )(margin_rows, first, coarse_inverse, partner, other, held, rhs, viscosity, coupling)
    partner_rows, other_rows = swap(partner_rows, other_rows)
    second = from_everyone(second)
    second_direction, third = call(
        functools.partial(second_turn_kernel, count), "second_turn", [SMEM] + [VMEM] * 14,
        [whole, row], 20_000_000, [extended, extended, sums, stacked, solved],
    )(
        margin_rows, first, second, residual, coarse_inverse, partner, other, partner_rows, other_rows,
        held, smooth, rhs, image, viscosity, coupling,
    )
    third = from_everyone(third)
    result, transposed = call(finish_kernel, "finish", [VMEM] * 5, [whole, f32(2, 3)], 1_000_000)(
        first, second, third, direction, second_direction
    )
    return result, transposed.T


def solution(mesh):
    in_specs = (
        P(None, ("groups", "sub"), None),
        P(("groups", "sub"), None),
        P(None, ("groups", "sub"), None),
        P("groups"),
        P(None, None, ("groups", "sub"), None),
        P(("groups", "sub"), None),
    )
    out_specs = (P(None, ("groups", "sub"), None), P("groups", None))
    return jax.shard_map(
        on_device, mesh=mesh, in_specs=in_specs, out_specs=out_specs, check_vma=False
    )
```

```python
import functools

import jax
import jax.numpy as jnp
from jax import lax
from jax.experimental import pallas as pl
from jax.experimental.pallas import tpu as pltpu
from jax.sharding import PartitionSpec as P

ROWS = 64
CELLS = 512
VECTORS = 48
HALO = 8
EXT = ROWS + 2 * HALO
STRIP = 32
GROUP = 16
STACKED = EXT + 2 * STRIP
TILE = 8
CHUNK = 16
CHUNKS = 2 * ROWS // CHUNK
PIECE = 8
LANES = 128
SLOTS = 64
COUPLING_AT = HALO
RHS_AT = 2 * HALO
EDGE_AT = 3 * HALO
INVERSE_AT = 2 * VECTORS
SWEEPS = 4
RELAX = 0.7
ROW_FACTOR = (1.0, 4.0)
CELL_FACTOR = (4.0, 1.0)

VMEM = pl.BlockSpec(memory_space=pltpu.VMEM)
SMEM = pl.BlockSpec(memory_space=pltpu.SMEM)
HBM = pl.BlockSpec(memory_space=pltpu.HBM)


def coarse_rows(columns):
    return INVERSE_AT + VECTORS * (columns // 512) + (VECTORS // 2) * (columns % 512 // 256)


def cell_sum(field):
    lane = lax.broadcasted_iota(jnp.int32, (field.shape[0], LANES), 1)
    left, right = pltpu.roll(field, 1, 1), pltpu.roll(field, CELLS - 1, 1)
    inner = left[:, LANES:-LANES] + right[:, LANES:-LANES]
    first = jnp.where(lane == 0, 0.0, left[:, :LANES]) + right[:, :LANES]
    last = left[:, -LANES:] + jnp.where(lane == LANES - 1, 0.0, right[:, -LANES:])
    return jnp.concatenate([first, inner, last], 1)


class Rows:
    def __init__(self, read, first, last):
        self.read, self.first, self.last = read, first, last
        self.tiles, self.down, self.up = {}, {}, {}

    def at(self, t):
        if t not in self.tiles:
            self.tiles[t] = self.read(t)
        return self.tiles[t]

    def moved(self, held, t, by):
        if t not in held:
            held[t] = pltpu.roll(self.at(t), by, 0)
        return held[t]

    def around(self, t):
        row = lax.broadcasted_iota(jnp.int32, (TILE, CELLS), 0)
        below, above = self.moved(self.down, t, 1), self.moved(self.up, t, TILE - 1)
        if t > self.first:
            below = jnp.where(row == 0, self.moved(self.down, t - 1, 1), below)
        if t < self.last:
            above = jnp.where(row == TILE - 1, self.moved(self.up, t + 1, TILE - 1), above)
        return below + above


def neighbours(rows, t, component):
    around, cells = rows.around(t), cell_sum(rows.at(t))
    if component == 0:
        return around + CELL_FACTOR[0] * cells
    return ROW_FACTOR[1] * around + cells


def sublane_sum(tile):
    for by in (4, 2, 1):
        tile = tile + pltpu.roll(tile, by, 0)
    return tile


def in_rows(tiles):
    row = lax.broadcasted_iota(jnp.int32, (8, LANES), 0)
    total = jnp.zeros((8, LANES), jnp.float32)
    for n, tile in enumerate(tiles):
        total = jnp.where(row == n, sublane_sum(tile), total)
    return total


def restrict_piece(i, held, field, sums):
    totals = [None] * PIECE
    for a in range(2):
        for r in range(0, ROWS, CHUNK):
            for c in range(0, CELLS, LANES):
                rows, cells = slice(r, r + CHUNK), slice(c, c + LANES)
                tile = field[a, rows, cells]
                for n in range(PIECE):
                    term = held[PIECE * i + n, a, rows, cells].astype(jnp.float32) * tile
                    totals[n] = term if totals[n] is None else totals[n] + term
    tiles = [total[:8] + total[8:] for total in totals]
    sums[pl.ds(pl.multiple_of(PIECE * i, PIECE), PIECE), :] = in_rows(tiles)


MATRIX_GROUPS = tuple((1, r) for r in range(CHUNK, ROWS, CHUNK))
VECTOR_GROUPS = ((0, 0), (0, 16), (0, 32), (0, 48), (1, 0))


def restrict(held, field, sums, lines):
    lines[2 * CHUNK :] = jnp.zeros((LANES - 2 * CHUNK, lines.shape[1]), jnp.bfloat16)
    blocks = []
    for g, (a, r) in enumerate(MATRIX_GROUPS):
        part, cells = field[a, r : r + CHUNK], slice(CELLS * g, CELLS * (g + 1))
        high = part.astype(jnp.bfloat16)
        lines[:CHUNK, cells] = high
        lines[CHUNK : 2 * CHUNK, cells] = (part - high.astype(jnp.float32)).astype(jnp.bfloat16)
        blocks.append(held[:, a, r : r + CHUNK, :].reshape(CHUNK * VECTORS, CELLS))
    products = lax.dot_general(
        jnp.concatenate(blocks, 1),
        lines[...],
        (((1,), (1,)), ((), ())),
        preferred_element_type=jnp.float32,
    )
    row = lax.broadcasted_iota(jnp.int32, (CHUNK, LANES), 0)
    equal = row == lax.broadcasted_iota(jnp.int32, (CHUNK, LANES), 1) % CHUNK
    for first in range(0, VECTORS, PIECE):
        totals = [
            jnp.where(equal, products[CHUNK * k : CHUNK * (k + 1)], 0.0)
            for k in range(first, first + PIECE)
        ]
        for a, r in VECTOR_GROUPS:
            for c in range(0, CELLS, LANES):
                rows, cells = slice(r, r + CHUNK), slice(c, c + LANES)
                tile = field[a, rows, cells]
                for n in range(PIECE):
                    term = held[first + n, a, rows, cells].astype(jnp.float32) * tile
                    totals[n] = totals[n] + term
        sums[first : first + PIECE] = in_rows([total[:8] + total[8:] for total in totals])


def fold(row):
    total = row[:, :LANES]
    for c in range(LANES, CELLS, LANES):
        total = total + row[:, c : c + LANES]
    return total


def tile_rows(t):
    return slice(TILE * t, TILE * (t + 1))


def send_sums(sums, out_ref):
    rest = sums[...]
    parts = []
    for _ in range(3):
        part = rest.astype(jnp.bfloat16)
        parts.append(part)
        rest = rest - part.astype(jnp.float32)
    row = lax.dot_general(
        jnp.ones((CHUNK, 3 * LANES), jnp.bfloat16),
        jnp.concatenate(parts, 1),
        (((1,), (1,)), ((), ())),
        preferred_element_type=jnp.float32,
    )
    wide = jnp.concatenate([row[:1], jnp.zeros((1, LANES - SLOTS), jnp.float32)], 1)
    out_ref[...] = jnp.broadcast_to(wide, out_ref.shape)


def pack_copies(out_ref, first_row, visc_ref, inverse_ref, sems, at_sem):
    rows = pl.ds(pl.multiple_of(first_row, HALO), HALO)
    moves = [(visc_ref.at[rows, :], 0, HALO, None)]
    columns = inverse_ref.shape[1]
    at = EDGE_AT + INVERSE_AT
    for c in range(0, columns - 511, 512):
        moves.append((inverse_ref.at[:, pl.ds(c, 512)], at, VECTORS, None))
        at += VECTORS
    if columns % 512:
        half = VECTORS // 2
        last = pl.ds(columns - 256, 256)
        moves.append((inverse_ref.at[pl.ds(0, half), last], at, half, 0))
        moves.append((inverse_ref.at[pl.ds(half, half), last], at, half, 256))
    copies = []
    for n, (source, at, size, lane) in enumerate(moves):
        place = pl.ds(at, size)
        target = out_ref.at[place, :] if lane is None else out_ref.at[place, pl.ds(lane, 256)]
        copies.append(pltpu.make_async_copy(source, target, sems.at[at_sem + n]))
    return copies


def pack_count(columns):
    return 1 + columns // 512 + 2 * (columns % 512 // 256)


def outer_rows(head, tail):
    half = lax.broadcasted_iota(jnp.int32, (TILE, CELLS), 0) < TILE // 2
    return (
        jnp.where(half, head[0], pltpu.roll(head[1], TILE // 2, 0)),
        jnp.where(half, pltpu.roll(tail[1], TILE // 2, 0), tail[0]),
    )


def component(rows, a):
    return pltpu.roll(rows, TILE // 2, 0) if a else rows


def pack_kernel(
    rhs_ref, visc_ref, coup_ref, inverse_ref, basis_ref,
    partner_ref, other_ref,
    groups, staged, group_sems, stage_sems, pack_sems,
):
    odd = lax.axis_index("sub") % 2
    sides = ((partner_ref, 1 - odd), (other_ref, odd))
    group_copies, packs = [], []
    for k in range(0, VECTORS, GROUP):
        for n, (out_ref, up) in enumerate(sides):
            rows = pl.ds(pl.multiple_of(up * (ROWS - CHUNK), CHUNK), CHUNK)
            for a in range(2):
                group_copies.append(
                    pltpu.make_async_copy(
                        basis_ref.at[pl.ds(k, GROUP), a, rows, :],
                        groups.at[2 * n + a, pl.ds(k, GROUP)],
                        group_sems.at[len(group_copies)],
                    )
                )
    for n, (out_ref, up) in enumerate(sides):
        packs += pack_copies(
            out_ref, up * (ROWS - HALO), visc_ref, inverse_ref, pack_sems,
            n * pack_count(inverse_ref.shape[1]),
        )
    stages = []
    for m, ref in enumerate((coup_ref, rhs_ref)):
        for n, first_row in enumerate((0, ROWS - HALO)):
            stages.append(
                pltpu.make_async_copy(
                    ref.at[:, pl.ds(first_row, HALO), :], staged.at[m, n], stage_sems.at[2 * m + n]
                )
            )
    for copy in stages + group_copies + packs:
        copy.start()
    for copy in stages:
        copy.wait()
    for m, at in enumerate((COUPLING_AT, RHS_AT)):
        head, tail = outer_rows(staged[m, 0], staged[m, 1])
        partner_ref[at : at + HALO] = jnp.where(odd == 1, head, tail)
        other_ref[at : at + HALO] = jnp.where(odd == 1, tail, head)

    def take(out_ref, group, first, row):
        for k in range(first, first + GROUP, TILE):
            lines = [groups[group, k + n].astype(jnp.float32)[row : row + 1] for n in range(TILE)]
            at = EDGE_AT + VECTORS * (group % 2) + k
            out_ref[at : at + TILE] = jnp.concatenate(lines, 0)

    for first in range(0, VECTORS, GROUP):
        for _ in range(4):
            group_copies.pop(0).wait()

        @pl.when(odd == 0)
        def _():
            for a in range(2):
                take(partner_ref, a, first, CHUNK - 1)
                take(other_ref, 2 + a, first, 0)

        @pl.when(odd == 1)
        def _():
            for a in range(2):
                take(partner_ref, a, first, 0)
                take(other_ref, 2 + a, first, CHUNK - 1)

    for copy in packs:
        copy.wait()


def restrict_kernel(rhs_ref, held, sums_ref, sums):
    sums[...] = jnp.zeros_like(sums)
    squares = jnp.zeros((TILE, CELLS), jnp.float32)
    for a in range(2):
        for t in range(ROWS // TILE):
            tile = rhs_ref[a, tile_rows(t)]
            squares = squares + tile * tile
    sums[VECTORS : VECTORS + 8] = in_rows([fold(squares)])

    def body(i, carry):
        restrict_piece(i, held, rhs_ref, sums)
        return carry

    lax.fori_loop(0, VECTORS // PIECE, body, 0)
    send_sums(sums, sums_ref)


class Neighbour:
    def __init__(self, first_ref, second_ref):
        self.odd = lax.axis_index("sub") % 2 == 1
        self.first, self.second = first_ref, second_ref

    def __getitem__(self, index):
        return jnp.where(self.odd, self.first[index], self.second[index])


def neighbours_of(partner_ref, other_ref):
    return Neighbour(partner_ref, other_ref), Neighbour(other_ref, partner_ref)


def solve(count, margin_ref, factors_ref, make, field, out_ref, first_ref, solved, steps):
    waiting, done = list(steps), 0
    every = (SWEEPS - 1) * (STACKED // TILE) // len(waiting)
    assert every > 0
    rank = lax.axis_index("sub")
    lower = jnp.where(rank > 0, margin_ref[jnp.maximum(rank - 1, 0)], 0)
    upper = jnp.where(rank < count - 1, margin_ref[rank], 0)
    lower_f, upper_f = lower.astype(jnp.float32), upper.astype(jnp.float32)
    low_scale = 1.0 / (2.0 * jnp.maximum(lower_f, 1.0))
    high_scale = 1.0 / (2.0 * jnp.maximum(upper_f, 1.0))
    wide = lambda x: jnp.concatenate([x] * (CELLS // LANES), 1)
    own_tiles = ROWS // TILE
    strip_tiles = STRIP // TILE
    last = own_tiles + 1
    segments = (
        (0, 0, last + 1),
        (last + 1, 0, strip_tiles),
        (last + 1 + strip_tiles, last + 1 - strip_tiles, strip_tiles),
    )

    def place_of(e):
        return lax.broadcasted_iota(jnp.int32, (TILE, LANES), 0) + (TILE * e - HALO)

    def live_of(segment, e):
        place = place_of(e)
        if segment == 0:
            live = (place >= -lower) & (place < ROWS + upper)
        elif segment == 1:
            live = place < lower
        else:
            live = place >= ROWS - upper
        return wide(live.astype(jnp.float32))

    def weight_of(segment, e):
        place = place_of(e)
        place_f = place.astype(jnp.float32)
        rising = lambda base, scale: (place_f - base + 0.5) * scale
        falling = lambda base, scale: (base - place_f - 0.5) * scale
        if segment == 0:
            weight = jnp.where(place < lower, rising(-lower_f, low_scale), 1.0)
            weight = jnp.where(
                place >= ROWS - upper, falling(ROWS + upper_f, high_scale), weight
            )
        elif segment == 1:
            weight = jnp.where(place >= -lower, falling(lower_f, low_scale), 1.0)
        else:
            weight = jnp.where(place < ROWS + upper, rising(ROWS - upper_f, high_scale), 1.0)
        return wide(weight)

    for e in range(last + 1):
        for a in range(2):
            parts = make(a, e) if make else None
            value = field(a, e - 1)
            for n, (first, begin, size) in enumerate(segments):
                if not begin <= e < begin + size:
                    continue
                rows = tile_rows(first + e - begin)
                if make:
                    always = n == 0 and 0 < e < last
                    live = None if always else live_of(n, e)
                    for m, part in enumerate(parts):
                        factors_ref[3 * a + m, rows] = part if always else live * part
                first_ref[a, rows] = factors_ref[3 * a, rows] * value

    for sweep in range(1, SWEEPS):
        for n, (first, begin, size) in enumerate(segments):
            end = first + size - 1
            if sweep == 1:
                reads = [lambda t, a=a: first_ref[a, tile_rows(t)] for a in range(2)]
            else:
                bank = 2 * (sweep % 2)
                reads = [lambda t, a=a: solved[bank + a, tile_rows(t)] for a in range(2)]
            fields = [Rows(read, first, end) for read in reads]
            for t in range(first, end + 1):
                rows = tile_rows(t)
                if done % every == 0 and waiting:
                    waiting.pop(0)()
                done += 1
                for a in range(2):
                    value = (
                        ((1.0 - RELAX) * fields[a].at(t) + first_ref[a, rows])
                        + factors_ref[3 * a + 1, rows] * neighbours(fields[a], t, a)
                        - factors_ref[3 * a + 2, rows] * fields[1 - a].at(t)
                    )
                    e = t - first + begin
                    if sweep < SWEEPS - 1:
                        solved[2 * ((sweep + 1) % 2) + a, rows] = value
                    elif n == 0:
                        out_ref[a, tile_rows(e)] = weight_of(n, e) * value
                    else:
                        out_ref[a, tile_rows(e)] += weight_of(n, e) * value


def line_up(residuals):
    devices = residuals.shape[0]
    lane = lax.broadcasted_iota(jnp.int32, (1, LANES), 1)
    tiles = [jnp.zeros((1, LANES), jnp.float32) for _ in range(devices * VECTORS // LANES)]
    for t in range(devices):
        tile, offset = divmod(VECTORS * t, LANES)
        row = jnp.where(lane < VECTORS, residuals[devices - 1 - t : devices - t], 0.0)
        if offset:
            row = pltpu.roll(row, offset, 1)
        if offset + VECTORS <= LANES:
            tiles[tile] = tiles[tile] + row
        else:
            tiles[tile] = tiles[tile] + jnp.where(lane >= offset, row, 0.0)
            tiles[tile + 1] = tiles[tile + 1] + jnp.where(lane < offset, row, 0.0)
    return jnp.concatenate(tiles, 1)


def rounded(column):
    return column.astype(jnp.bfloat16).astype(jnp.float32)


def lift(inverse_ref, residual):
    return rounded(jnp.sum(inverse_ref[...] * residual, 1, keepdims=True))


def lift_packed(ref, residual):
    columns = residual.shape[1]
    at, total = EDGE_AT + INVERSE_AT, None
    for c in range(0, columns - 511, 512):
        term = jnp.sum(ref[at : at + VECTORS] * residual[:, c : c + 512], 1, keepdims=True)
        total = term if total is None else total + term
        at += VECTORS
    if columns % 512:
        half = VECTORS // 2
        last = residual[:, columns - 256 :]
        rows = ref[at : at + half]
        term = jnp.concatenate(
            [
                jnp.sum(rows[:, :256] * last, 1, keepdims=True),
                jnp.sum(rows[:, 256:] * last, 1, keepdims=True),
            ],
            0,
        )
        total = term if total is None else total + term
    return rounded(total)


def edge_values(ref, lifted):
    starts = [EDGE_AT + VECTORS * a for a in range(2)]
    return [jnp.sum(ref[at : at + VECTORS] * lifted, 0, keepdims=True) for at in starts]


def spread(lifted):
    shape = (VECTORS, CHUNK * VECTORS)
    owner = lax.broadcasted_iota(jnp.int32, shape, 1) // CHUNK
    row = lax.broadcasted_iota(jnp.int32, shape, 0)
    line = jnp.sum(jnp.where(owner == row, lifted, 0.0), 0, keepdims=True)
    shape = (CHUNK, CHUNK * VECTORS)
    place = lax.broadcasted_iota(jnp.int32, shape, 1) % CHUNK
    row = lax.broadcasted_iota(jnp.int32, shape, 0)
    return jnp.where(place == row, line, 0.0).astype(jnp.bfloat16)


class Coarse:
    def __init__(self, begin, inverse_ref, low, high, held, extended):
        self.inverse, self.sides, self.held, self.extended = inverse_ref, (low, high), held, extended
        self.lifted, self.edges = [None] * 2, [None] * 2
        self.steps = begin(self) + [self.lift_own, self.make_matrix]
        for a in range(2):
            for r in range(0, ROWS, CHUNK):
                self.steps.append(functools.partial(self.prolong, a, r))
        for n in range(2):
            self.steps.insert(len(self.steps) - 6, functools.partial(self.lift_side, n))
            self.steps.append(functools.partial(self.edge, n))

    def lift_own(self):
        self.own = lift(self.inverse, self.residual)

    def make_matrix(self):
        self.matrix = spread(self.own)

    def prolong(self, a, r):
        rows = self.held[:, a, r : r + CHUNK, :].reshape(CHUNK * VECTORS, CELLS)
        self.extended[a, HALO + r : HALO + r + CHUNK] = jnp.dot(
            self.matrix, rows, preferred_element_type=jnp.float32
        )

    def lift_side(self, n):
        self.lifted[n] = lift_packed(self.sides[n], self.residual)

    def edge(self, n):
        self.edges[n] = edge_values(self.sides[n], self.lifted[n])


def apply_operator(edges, smooth, extended, visc_ref, coup_ref, direction_ref):
    place = lax.broadcasted_iota(jnp.int32, (TILE, CELLS), 0)
    tiles = ROWS // TILE

    def read(t, a):
        if t < 0:
            return smooth(a, 0) + jnp.where(place == TILE - 1, edges[0][a], 0.0)
        if t == tiles:
            return smooth(a, t + 1) + jnp.where(place == 0, edges[1][a], 0.0)
        tile = smooth(a, t + 1) + extended[a, tile_rows(t + 1)]
        direction_ref[a, tile_rows(t)] = tile
        return tile

    fields = [Rows(lambda t, a=a: read(t, a), -1, tiles) for a in range(2)]
    for t in range(tiles):
        rows = tile_rows(t)
        viscosity = visc_ref[rows]
        for a in range(2):
            coupling = coup_ref[a, rows]
            diagonal = 10.0 * viscosity + jnp.abs(coupling) + 0.05
            image = (
                diagonal * fields[a].at(t)
                - viscosity * neighbours(fields[a], t, a)
                + coupling * fields[1 - a].at(t)
            )
            yield t, a, image


def lane_total(received, lane):
    place = lax.broadcasted_iota(jnp.int32, received.shape, 1)
    return jnp.sum(jnp.where(place == lane, received, 0.0), keepdims=True)


def first_turn_kernel(
    count, margin_ref, sums_ref, inverse_ref, partner_ref, other_ref, held, rhs_ref, visc_ref,
    coup_ref,
    direction_ref, image_ref, smooth_ref, residual_ref, factors_ref, partner_rows_ref, other_rows_ref,
    next_ref,
    extended, sums, first_ref, solved, lines,
):
    low, high = neighbours_of(partner_ref, other_ref)

    def begin(coarse):
        def scale():
            coarse.over_beta = 1.0 / jnp.sqrt(lane_total(sums_ref[...], VECTORS))

        def line():
            coarse.residual = line_up(sums_ref[...]) * coarse.over_beta
            residual_ref[...] = coarse.residual

        return [scale, line]

    coarse = Coarse(begin, inverse_ref, low, high, held, extended)

    def field(a, t):
        if 0 <= t < ROWS // TILE:
            return rhs_ref[a, tile_rows(t)]
        return component((low if t < 0 else high)[RHS_AT : RHS_AT + HALO], a)

    def make(a, e):
        if 0 < e <= ROWS // TILE:
            viscosity, coupling = visc_ref[tile_rows(e - 1)], coup_ref[a, tile_rows(e - 1)]
        else:
            side = low if e == 0 else high
            viscosity = side[:HALO]
            coupling = component(side[COUPLING_AT : COUPLING_AT + HALO], a)
        scale = RELAX / (10.0 * viscosity + jnp.abs(coupling) + 0.05)
        return scale, scale * viscosity, scale * coupling

    solve(
        count, margin_ref, factors_ref, make, field, smooth_ref, first_ref, solved, coarse.steps
    )
    smooth = lambda a, t: smooth_ref[a, tile_rows(t)] * coarse.over_beta
    images = apply_operator(
        coarse.edges, smooth, extended, visc_ref, coup_ref, direction_ref
    )
    odd = lax.axis_index("sub") % 2 == 1
    products, squares = [jnp.zeros((TILE, CELLS), jnp.float32)] * 2
    heads, tails = [None] * 2, [None] * 2
    for t, a, image in images:
        image_ref[a, tile_rows(t)] = image
        products = products + rhs_ref[a, tile_rows(t)] * image
        squares = squares + image * image
        if t == 0:
            heads[a] = image
        if t == ROWS // TILE - 1:
            tails[a] = image
    head, tail = outer_rows(heads, tails)
    partner_rows_ref[...] = jnp.where(odd, head, tail)
    other_rows_ref[...] = jnp.where(odd, tail, head)
    sums[...] = jnp.zeros_like(sums)
    sums[VECTORS : VECTORS + 8] = in_rows([fold(products), fold(squares)])

    restrict(held, image_ref, sums, lines)
    send_sums(sums, next_ref)


def first_column(first, second):
    beta = jnp.sqrt(lane_total(first, VECTORS))
    h_00 = lane_total(second, VECTORS) / beta
    h_10 = jnp.sqrt(lane_total(second, VECTORS + 1) - h_00 * h_00)
    return beta, h_00, h_10


def second_turn_kernel(
    count, margin_ref, sums_ref, second_ref, residual_ref, factors_ref, inverse_ref, partner_ref, other_ref,
    partner_rows_ref, other_rows_ref, held, smooth_ref, rhs_ref, image_ref, visc_ref, coup_ref,
    direction_ref, next_ref,
    image_smooth, extended, sums, first_ref, solved,
):
    low, high = neighbours_of(partner_ref, other_ref)

    def begin(coarse):
        def scale():
            beta, h_00, h_10 = first_column(sums_ref[...], second_ref[...])
            coarse.h_00, coarse.ratio, coarse.over = h_00, h_00 / beta, 1.0 / h_10

        def line():
            lined = line_up(second_ref[...])
            coarse.residual = (lined - coarse.h_00 * residual_ref[...]) * coarse.over

        return [scale, line]

    coarse = Coarse(begin, inverse_ref, low, high, held, extended)
    low_rows, high_rows = neighbours_of(partner_rows_ref, other_rows_ref)

    def field(a, t):
        if 0 <= t < ROWS // TILE:
            return image_ref[a, tile_rows(t)]
        rows = low_rows[...] if t < 0 else high_rows[...]
        return component(rows, a)

    solve(
        count, margin_ref, factors_ref, None, field, image_smooth, first_ref, solved, coarse.steps
    )

    def smooth(a, t):
        rows = tile_rows(t)
        return (image_smooth[a, rows] - coarse.ratio * smooth_ref[a, rows]) * coarse.over

    images = apply_operator(
        coarse.edges, smooth, extended, visc_ref, coup_ref, direction_ref
    )
    totals = [jnp.zeros((TILE, CELLS), jnp.float32)] * 3
    for t, a, image in images:
        others = (rhs_ref[a, tile_rows(t)], image_ref[a, tile_rows(t)], image)
        totals = [total + x * image for total, x in zip(totals, others)]
    sums[...] = jnp.zeros_like(sums)
    sums[:8] = in_rows([fold(total) for total in totals])
    send_sums(sums, next_ref)


def finish_kernel(
    first_ref, second_ref, third_ref, first_direction_ref, second_direction_ref,
    solution_ref, hessenberg_ref,
):
    third = third_ref[...]
    beta, h_00, h_10 = first_column(first_ref[...], second_ref[...])
    squares = lane_total(third, 2)
    h_01 = lane_total(third, 0) / beta
    h_11 = (lane_total(third, 1) - h_00 * h_01) / h_10
    h_21 = jnp.sqrt(squares - h_01 * h_01 - h_11 * h_11)
    l_00 = jnp.sqrt(h_00 * h_00 + h_10 * h_10)
    l_10 = (h_00 * h_01 + h_10 * h_11) / l_00
    f_0 = beta * h_00 / l_00
    c_1 = (beta * h_01 - l_10 * f_0) / (squares - l_10 * l_10)
    c_0 = (f_0 - l_10 * c_1) / l_00
    for a in range(2):
        solution_ref[a] = c_0 * first_direction_ref[a] + c_1 * second_direction_ref[a]
    shape = hessenberg_ref.shape
    row = lax.broadcasted_iota(jnp.int32, shape, 1)
    column = lax.broadcasted_iota(jnp.int32, shape, 0)
    entries = jnp.zeros(shape, jnp.float32)
    for i, j, value in ((0, 0, h_00), (0, 1, h_01), (1, 0, h_10), (1, 1, h_11), (2, 1, h_21)):
        entries = jnp.where((row == i) & (column == j), value, entries)
    hessenberg_ref[...] = entries


def call(kernel, name, in_specs, outs, flops, scratch=(), traffic=4_000_000):
    return pl.pallas_call(
        kernel,
        name=name,
        in_specs=in_specs,
        out_specs=[VMEM] * len(outs),
        out_shape=outs,
        scratch_shapes=scratch,
        compiler_params=pltpu.CompilerParams(vmem_limit_bytes=16 * 1024 * 1024),
        cost_estimate=pl.CostEstimate(flops=flops, bytes_accessed=traffic, transcendentals=0),
    )


def in_hbm(array):
    return pltpu.with_memory_space_constraint(array, pltpu.HBM)


def from_everyone(rows):
    order = [list(range(lax.axis_size("sub")))[::-1]]
    return lax.all_to_all(rows, "sub", 0, 0, tiled=True, axis_index_groups=order)


def swap(partner, other):
    count = lax.axis_size("sub")
    both = lambda lows: [pair for i in lows for pair in ((i, i + 1), (i + 1, i))]
    return (
        lax.ppermute(partner, "sub", both(range(0, count, 2))),
        lax.ppermute(other, "sub", both(range(1, count - 1, 2))),
    )


def on_device(rhs, viscosity, coupling, margin_rows, coarse_basis, coarse_inverse):
    count = lax.axis_size("sub")
    columns = coarse_inverse.shape[1]
    f32 = lambda *shape: jax.ShapeDtypeStruct(shape, jnp.float32)
    dma = lambda *shape: pltpu.SemaphoreType.DMA(shape)
    extended = pltpu.VMEM((2, EXT, CELLS), jnp.float32)
    stacked = pltpu.VMEM((2, STACKED, CELLS), jnp.float32)
    solved = pltpu.VMEM((4, STACKED, CELLS), jnp.float32)
    sums = pltpu.VMEM((SLOTS, LANES), jnp.float32)
    lines = pltpu.VMEM((LANES, len(MATRIX_GROUPS) * CELLS), jnp.bfloat16)
    row, whole, edge = f32(count, LANES), f32(2, ROWS, CELLS), f32(TILE, CELLS)
    packed, smoothed = f32(EDGE_AT + coarse_rows(columns), CELLS), f32(2, EXT, CELLS)
    arguments = (rhs, viscosity, coupling, coarse_inverse, coarse_basis)
    packs = call(
        pack_kernel, "pack", [HBM] * 5, [packed, packed], 5_000_000,
        [pltpu.VMEM((4, VECTORS, CHUNK, CELLS), jnp.bfloat16)]
        + [pltpu.VMEM((2, 2, 2, HALO, CELLS), jnp.float32), dma(4 * VECTORS // GROUP), dma(4)]
        + [dma(2 * pack_count(columns))],
    )(*map(in_hbm, arguments))
    held, partner, other = lax.optimization_barrier((coarse_basis, *packs))
    partner, other = swap(partner, other)
    (first,) = call(
        restrict_kernel, "restrict", [VMEM] * 2, [row], 10_000_000, [sums]
    )(rhs, held)
    first = from_everyone(first)
    direction, image, smooth, residual, factors, partner_rows, other_rows, second = call(
        functools.partial(first_turn_kernel, count), "first_turn", [SMEM] + [VMEM] * 8,
        [whole, whole, smoothed, f32(1, columns), f32(6, STACKED, CELLS), edge, edge, row], 20_000_000,
        [extended, sums, stacked, solved, lines],
    )(margin_rows, first, coarse_inverse, partner, other, held, rhs, viscosity, coupling)
    partner_rows, other_rows = swap(partner_rows, other_rows)
    second = from_everyone(second)
    second_direction, third = call(
        functools.partial(second_turn_kernel, count), "second_turn", [SMEM] + [VMEM] * 15,
        [whole, row], 20_000_000, [extended, extended, sums, stacked, solved],
    )(
        margin_rows, first, second, residual, factors, coarse_inverse, partner, other, partner_rows, other_rows,
        held, smooth, rhs, image, viscosity, coupling,
    )
    third = from_everyone(third)
    result, transposed = call(finish_kernel, "finish", [VMEM] * 5, [whole, f32(2, 3)], 1_000_000)(
        first, second, third, direction, second_direction
    )
    return result, transposed.T


def solution(mesh):
    in_specs = (
        P(None, ("groups", "sub"), None),
        P(("groups", "sub"), None),
        P(None, ("groups", "sub"), None),
        P("groups"),
        P(None, None, ("groups", "sub"), None),
        P(("groups", "sub"), None),
    )
    out_specs = (P(None, ("groups", "sub"), None), P("groups", None))
    return jax.shard_map(
        on_device, mesh=mesh, in_specs=in_specs, out_specs=out_specs, check_vma=False
    )
```

```python
import functools

import jax
import jax.numpy as jnp
from jax import lax
from jax.experimental import pallas as pl
from jax.experimental.pallas import tpu as pltpu
from jax.sharding import PartitionSpec as P

ROWS = 64
CELLS = 512
VECTORS = 48
HALO = 8
EXT = ROWS + 2 * HALO
STRIP = 32
GROUP = 16
STACKED = EXT + 2 * STRIP
TILE = 8
CHUNK = 16
CHUNKS = 2 * ROWS // CHUNK
PIECE = 8
LANES = 128
SLOTS = 64
COUPLING_AT = HALO
RHS_AT = 2 * HALO
EDGE_AT = 3 * HALO
INVERSE_AT = 2 * VECTORS
SWEEPS = 4
RELAX = 0.7
ROW_FACTOR = (1.0, 4.0)
CELL_FACTOR = (4.0, 1.0)

VMEM = pl.BlockSpec(memory_space=pltpu.VMEM)
SMEM = pl.BlockSpec(memory_space=pltpu.SMEM)
HBM = pl.BlockSpec(memory_space=pltpu.HBM)


def coarse_rows(columns):
    return INVERSE_AT + VECTORS * (columns // 512) + (VECTORS // 2) * (columns % 512 // 256)


def cell_sum(field):
    lane = lax.broadcasted_iota(jnp.int32, (field.shape[0], LANES), 1)
    left, right = pltpu.roll(field, 1, 1), pltpu.roll(field, CELLS - 1, 1)
    inner = left[:, LANES:-LANES] + right[:, LANES:-LANES]
    first = jnp.where(lane == 0, 0.0, left[:, :LANES]) + right[:, :LANES]
    last = left[:, -LANES:] + jnp.where(lane == LANES - 1, 0.0, right[:, -LANES:])
    return jnp.concatenate([first, inner, last], 1)


class Rows:
    def __init__(self, read, first, last):
        self.read, self.first, self.last = read, first, last
        self.tiles, self.down, self.up = {}, {}, {}

    def at(self, t):
        if t not in self.tiles:
            self.tiles[t] = self.read(t)
        return self.tiles[t]

    def moved(self, held, t, by):
        if t not in held:
            held[t] = pltpu.roll(self.at(t), by, 0)
        return held[t]

    def around(self, t):
        row = lax.broadcasted_iota(jnp.int32, (TILE, CELLS), 0)
        below, above = self.moved(self.down, t, 1), self.moved(self.up, t, TILE - 1)
        if t > self.first:
            below = jnp.where(row == 0, self.moved(self.down, t - 1, 1), below)
        if t < self.last:
            above = jnp.where(row == TILE - 1, self.moved(self.up, t + 1, TILE - 1), above)
        return below + above


def neighbours(rows, t, component):
    around, cells = rows.around(t), cell_sum(rows.at(t))
    if component == 0:
        return around + CELL_FACTOR[0] * cells
    return ROW_FACTOR[1] * around + cells


def sublane_sum(tile):
    for by in (4, 2, 1):
        tile = tile + pltpu.roll(tile, by, 0)
    return tile


def in_rows(tiles):
    row = lax.broadcasted_iota(jnp.int32, (8, LANES), 0)
    total = jnp.zeros((8, LANES), jnp.float32)
    for n, tile in enumerate(tiles):
        total = jnp.where(row == n, sublane_sum(tile), total)
    return total


def restrict_piece(i, held, field, sums):
    totals = [None] * PIECE
    for a in range(2):
        for r in range(0, ROWS, CHUNK):
            for c in range(0, CELLS, LANES):
                rows, cells = slice(r, r + CHUNK), slice(c, c + LANES)
                tile = field[a, rows, cells]
                for n in range(PIECE):
                    term = held[PIECE * i + n, a, rows, cells].astype(jnp.float32) * tile
                    totals[n] = term if totals[n] is None else totals[n] + term
    tiles = [total[:8] + total[8:] for total in totals]
    sums[pl.ds(pl.multiple_of(PIECE * i, PIECE), PIECE), :] = in_rows(tiles)


VECTOR_GROUPS = tuple((0, r) for r in range(0, ROWS, CHUNK))
MATRIX_GROUPS = tuple((1, r) for r in range(0, ROWS, CHUNK))


def restrict(held, field, sums, lines):
    lines[2 * CHUNK :] = jnp.zeros((LANES - 2 * CHUNK, lines.shape[1]), jnp.bfloat16)
    blocks = []
    for g, (a, r) in enumerate(MATRIX_GROUPS):
        part, cells = field[a, r : r + CHUNK], slice(CELLS * g, CELLS * (g + 1))
        high = part.astype(jnp.bfloat16)
        lines[:CHUNK, cells] = high
        lines[CHUNK : 2 * CHUNK, cells] = (part - high.astype(jnp.float32)).astype(jnp.bfloat16)
        blocks.append(held[:, a, r : r + CHUNK, :].reshape(CHUNK * VECTORS, CELLS))
    products = lax.dot_general(
        jnp.concatenate(blocks, 1),
        lines[...],
        (((1,), (1,)), ((), ())),
        preferred_element_type=jnp.float32,
    )
    row = lax.broadcasted_iota(jnp.int32, (CHUNK, LANES), 0)
    equal = row == lax.broadcasted_iota(jnp.int32, (CHUNK, LANES), 1) % CHUNK
    for first in range(0, VECTORS, PIECE):
        totals = [
            jnp.where(equal, products[CHUNK * k : CHUNK * (k + 1)], 0.0)
            for k in range(first, first + PIECE)
        ]
        for a, r in VECTOR_GROUPS:
            for c in range(0, CELLS, LANES):
                rows, cells = slice(r, r + CHUNK), slice(c, c + LANES)
                tile = field[a, rows, cells]
                for n in range(PIECE):
                    term = held[first + n, a, rows, cells].astype(jnp.float32) * tile
                    totals[n] = totals[n] + term
        sums[first : first + PIECE] = in_rows([total[:8] + total[8:] for total in totals])


def fold(row):
    total = row[:, :LANES]
    for c in range(LANES, CELLS, LANES):
        total = total + row[:, c : c + LANES]
    return total


def tile_rows(t):
    return slice(TILE * t, TILE * (t + 1))


def send_sums(sums, out_ref):
    rest = sums[...]
    parts = []
    for _ in range(3):
        part = rest.astype(jnp.bfloat16)
        parts.append(part)
        rest = rest - part.astype(jnp.float32)
    row = lax.dot_general(
        jnp.ones((CHUNK, 3 * LANES), jnp.bfloat16),
        jnp.concatenate(parts, 1),
        (((1,), (1,)), ((), ())),
        preferred_element_type=jnp.float32,
    )
    wide = jnp.concatenate([row[:1], jnp.zeros((1, LANES - SLOTS), jnp.float32)], 1)
    out_ref[...] = jnp.broadcast_to(wide, out_ref.shape)


def pack_copies(out_ref, first_row, visc_ref, inverse_ref, sems, at_sem):
    rows = pl.ds(pl.multiple_of(first_row, HALO), HALO)
    moves = [(visc_ref.at[rows, :], 0, HALO, None)]
    columns = inverse_ref.shape[1]
    at = EDGE_AT + INVERSE_AT
    for c in range(0, columns - 511, 512):
        moves.append((inverse_ref.at[:, pl.ds(c, 512)], at, VECTORS, None))
        at += VECTORS
    if columns % 512:
        half = VECTORS // 2
        last = pl.ds(columns - 256, 256)
        moves.append((inverse_ref.at[pl.ds(0, half), last], at, half, 0))
        moves.append((inverse_ref.at[pl.ds(half, half), last], at, half, 256))
    copies = []
    for n, (source, at, size, lane) in enumerate(moves):
        place = pl.ds(at, size)
        target = out_ref.at[place, :] if lane is None else out_ref.at[place, pl.ds(lane, 256)]
        copies.append(pltpu.make_async_copy(source, target, sems.at[at_sem + n]))
    return copies


def pack_count(columns):
    return 1 + columns // 512 + 2 * (columns % 512 // 256)


def outer_rows(head, tail):
    half = lax.broadcasted_iota(jnp.int32, (TILE, CELLS), 0) < TILE // 2
    return (
        jnp.where(half, head[0], pltpu.roll(head[1], TILE // 2, 0)),
        jnp.where(half, pltpu.roll(tail[1], TILE // 2, 0), tail[0]),
    )


def component(rows, a):
    return pltpu.roll(rows, TILE // 2, 0) if a else rows


def pack_kernel(
    rhs_ref, visc_ref, coup_ref, inverse_ref, basis_ref,
    partner_ref, other_ref,
    groups, staged, group_sems, stage_sems, pack_sems,
):
    odd = lax.axis_index("sub") % 2
    sides = ((partner_ref, 1 - odd), (other_ref, odd))
    group_copies, packs = [], []
    for k in range(0, VECTORS, GROUP):
        for n, (out_ref, up) in enumerate(sides):
            rows = pl.ds(pl.multiple_of(up * (ROWS - CHUNK), CHUNK), CHUNK)
            for a in range(2):
                group_copies.append(
                    pltpu.make_async_copy(
                        basis_ref.at[pl.ds(k, GROUP), a, rows, :],
                        groups.at[2 * n + a, pl.ds(k, GROUP)],
                        group_sems.at[len(group_copies)],
                    )
                )
    for n, (out_ref, up) in enumerate(sides):
        packs += pack_copies(
            out_ref, up * (ROWS - HALO), visc_ref, inverse_ref, pack_sems,
            n * pack_count(inverse_ref.shape[1]),
        )
    stages = []
    for m, ref in enumerate((coup_ref, rhs_ref)):
        for n, first_row in enumerate((0, ROWS - HALO)):
            stages.append(
                pltpu.make_async_copy(
                    ref.at[:, pl.ds(first_row, HALO), :], staged.at[m, n], stage_sems.at[2 * m + n]
                )
            )
    for copy in stages + group_copies + packs:
        copy.start(priority=1)
    for copy in stages:
        copy.wait()
    for m, at in enumerate((COUPLING_AT, RHS_AT)):
        head, tail = outer_rows(staged[m, 0], staged[m, 1])
        partner_ref[at : at + HALO] = jnp.where(odd == 1, head, tail)
        other_ref[at : at + HALO] = jnp.where(odd == 1, tail, head)

    def take(out_ref, group, first, row):
        for k in range(first, first + GROUP, TILE):
            lines = [groups[group, k + n].astype(jnp.float32)[row : row + 1] for n in range(TILE)]
            at = EDGE_AT + VECTORS * (group % 2) + k
            out_ref[at : at + TILE] = jnp.concatenate(lines, 0)

    for first in range(0, VECTORS, GROUP):
        for _ in range(4):
            group_copies.pop(0).wait()

        @pl.when(odd == 0)
        def _():
            for a in range(2):
                take(partner_ref, a, first, CHUNK - 1)
                take(other_ref, 2 + a, first, 0)

        @pl.when(odd == 1)
        def _():
            for a in range(2):
                take(partner_ref, a, first, 0)
                take(other_ref, 2 + a, first, CHUNK - 1)

    for copy in packs:
        copy.wait()


def restrict_kernel(rhs_ref, held, sums_ref, sums):
    sums[...] = jnp.zeros_like(sums)
    squares = jnp.zeros((TILE, CELLS), jnp.float32)
    for a in range(2):
        for t in range(ROWS // TILE):
            tile = rhs_ref[a, tile_rows(t)]
            squares = squares + tile * tile
    sums[VECTORS : VECTORS + 8] = in_rows([fold(squares)])

    def body(i, carry):
        restrict_piece(i, held, rhs_ref, sums)
        return carry

    lax.fori_loop(0, VECTORS // PIECE, body, 0)
    send_sums(sums, sums_ref)


class Neighbour:
    def __init__(self, first_ref, second_ref):
        self.odd = lax.axis_index("sub") % 2 == 1
        self.first, self.second = first_ref, second_ref

    def __getitem__(self, index):
        return jnp.where(self.odd, self.first[index], self.second[index])


def neighbours_of(partner_ref, other_ref):
    return Neighbour(partner_ref, other_ref), Neighbour(other_ref, partner_ref)


def solve(count, margin_ref, factors_ref, make, field, out_ref, first_ref, solved, steps):
    waiting, done = list(steps), 0
    every = (SWEEPS - 1) * (STACKED // TILE) // len(waiting)
    assert every > 0
    rank = lax.axis_index("sub")
    lower = jnp.where(rank > 0, margin_ref[jnp.maximum(rank - 1, 0)], 0)
    upper = jnp.where(rank < count - 1, margin_ref[rank], 0)
    lower_f, upper_f = lower.astype(jnp.float32), upper.astype(jnp.float32)
    low_scale = 1.0 / (2.0 * jnp.maximum(lower_f, 1.0))
    high_scale = 1.0 / (2.0 * jnp.maximum(upper_f, 1.0))
    wide = lambda x: jnp.concatenate([x] * (CELLS // LANES), 1)
    own_tiles = ROWS // TILE
    strip_tiles = STRIP // TILE
    last = own_tiles + 1
    segments = (
        (0, 0, last + 1),
        (last + 1, 0, strip_tiles),
        (last + 1 + strip_tiles, last + 1 - strip_tiles, strip_tiles),
    )

    def place_of(e):
        return lax.broadcasted_iota(jnp.int32, (TILE, LANES), 0) + (TILE * e - HALO)

    def live_of(segment, e):
        place = place_of(e)
        if segment == 0:
            live = (place >= -lower) & (place < ROWS + upper)
        elif segment == 1:
            live = place < lower
        else:
            live = place >= ROWS - upper
        return wide(live.astype(jnp.float32))

    def weight_of(segment, e):
        place = place_of(e)
        place_f = place.astype(jnp.float32)
        rising = lambda base, scale: (place_f - base + 0.5) * scale
        falling = lambda base, scale: (base - place_f - 0.5) * scale
        if segment == 0:
            weight = jnp.where(place < lower, rising(-lower_f, low_scale), 1.0)
            weight = jnp.where(
                place >= ROWS - upper, falling(ROWS + upper_f, high_scale), weight
            )
        elif segment == 1:
            weight = jnp.where(place >= -lower, falling(lower_f, low_scale), 1.0)
        else:
            weight = jnp.where(place < ROWS + upper, rising(ROWS - upper_f, high_scale), 1.0)
        return wide(weight)

    for e in range(last + 1):
        for a in range(2):
            parts = make(a, e) if make else None
            value = field(a, e - 1)
            for n, (first, begin, size) in enumerate(segments):
                if not begin <= e < begin + size:
                    continue
                rows = tile_rows(first + e - begin)
                if make:
                    always = n == 0 and 0 < e < last
                    live = None if always else live_of(n, e)
                    for m, part in enumerate(parts):
                        factors_ref[3 * a + m, rows] = part if always else live * part
                first_ref[a, rows] = factors_ref[3 * a, rows] * value

    for sweep in range(1, SWEEPS):
        for n, (first, begin, size) in enumerate(segments):
            end = first + size - 1
            if sweep == 1:
                reads = [lambda t, a=a: first_ref[a, tile_rows(t)] for a in range(2)]
            else:
                bank = 2 * (sweep % 2)
                reads = [lambda t, a=a: solved[bank + a, tile_rows(t)] for a in range(2)]
            fields = [Rows(read, first, end) for read in reads]
            for t in range(first, end + 1):
                rows = tile_rows(t)
                if done % every == 0 and waiting:
                    waiting.pop(0)()
                done += 1
                for a in range(2):
                    value = (
                        ((1.0 - RELAX) * fields[a].at(t) + first_ref[a, rows])
                        + factors_ref[3 * a + 1, rows] * neighbours(fields[a], t, a)
                        - factors_ref[3 * a + 2, rows] * fields[1 - a].at(t)
                    )
                    e = t - first + begin
                    if sweep < SWEEPS - 1:
                        solved[2 * ((sweep + 1) % 2) + a, rows] = value
                    elif n == 0:
                        out_ref[a, tile_rows(e)] = weight_of(n, e) * value
                    else:
                        out_ref[a, tile_rows(e)] += weight_of(n, e) * value


def line_up(residuals):
    devices = residuals.shape[0]
    lane = lax.broadcasted_iota(jnp.int32, (1, LANES), 1)
    tiles = [jnp.zeros((1, LANES), jnp.float32) for _ in range(devices * VECTORS // LANES)]
    for t in range(devices):
        tile, offset = divmod(VECTORS * t, LANES)
        row = jnp.where(lane < VECTORS, residuals[devices - 1 - t : devices - t], 0.0)
        if offset:
            row = pltpu.roll(row, offset, 1)
        if offset + VECTORS <= LANES:
            tiles[tile] = tiles[tile] + row
        else:
            tiles[tile] = tiles[tile] + jnp.where(lane >= offset, row, 0.0)
            tiles[tile + 1] = tiles[tile + 1] + jnp.where(lane < offset, row, 0.0)
    return jnp.concatenate(tiles, 1)


def rounded(column):
    return column.astype(jnp.bfloat16).astype(jnp.float32)


def lift(inverse_ref, residual):
    return rounded(jnp.sum(inverse_ref[...] * residual, 1, keepdims=True))


def lift_packed(ref, residual):
    columns = residual.shape[1]
    at, total = EDGE_AT + INVERSE_AT, None
    for c in range(0, columns - 511, 512):
        term = jnp.sum(ref[at : at + VECTORS] * residual[:, c : c + 512], 1, keepdims=True)
        total = term if total is None else total + term
        at += VECTORS
    if columns % 512:
        half = VECTORS // 2
        last = residual[:, columns - 256 :]
        rows = ref[at : at + half]
        term = jnp.concatenate(
            [
                jnp.sum(rows[:, :256] * last, 1, keepdims=True),
                jnp.sum(rows[:, 256:] * last, 1, keepdims=True),
            ],
            0,
        )
        total = term if total is None else total + term
    return rounded(total)


def edge_values(ref, lifted):
    starts = [EDGE_AT + VECTORS * a for a in range(2)]
    return [jnp.sum(ref[at : at + VECTORS] * lifted, 0, keepdims=True) for at in starts]


def spread(lifted):
    shape = (VECTORS, CHUNK * VECTORS)
    owner = lax.broadcasted_iota(jnp.int32, shape, 1) // CHUNK
    row = lax.broadcasted_iota(jnp.int32, shape, 0)
    line = jnp.sum(jnp.where(owner == row, lifted, 0.0), 0, keepdims=True)
    shape = (CHUNK, CHUNK * VECTORS)
    place = lax.broadcasted_iota(jnp.int32, shape, 1) % CHUNK
    row = lax.broadcasted_iota(jnp.int32, shape, 0)
    return jnp.where(place == row, line, 0.0).astype(jnp.bfloat16)


class Coarse:
    def __init__(self, begin, inverse_ref, low, high, held, extended):
        self.inverse, self.sides, self.held, self.extended = inverse_ref, (low, high), held, extended
        self.lifted, self.edges = [None] * 2, [None] * 2
        self.steps = begin(self) + [self.lift_own, self.make_matrix]
        for a in range(2):
            for r in range(0, ROWS, CHUNK):
                self.steps.append(functools.partial(self.prolong, a, r))
        for n in range(2):
            self.steps.insert(len(self.steps) - 6, functools.partial(self.lift_side, n))
            self.steps.append(functools.partial(self.edge, n))

    def lift_own(self):
        self.own = lift(self.inverse, self.residual)

    def make_matrix(self):
        self.matrix = spread(self.own)

    def prolong(self, a, r):
        rows = self.held[:, a, r : r + CHUNK, :].reshape(CHUNK * VECTORS, CELLS)
        self.extended[a, HALO + r : HALO + r + CHUNK] = jnp.dot(
            self.matrix, rows, preferred_element_type=jnp.float32
        )

    def lift_side(self, n):
        self.lifted[n] = lift_packed(self.sides[n], self.residual)

    def edge(self, n):
        self.edges[n] = edge_values(self.sides[n], self.lifted[n])


def apply_operator(edges, smooth, extended, visc_ref, coup_ref, direction_ref):
    place = lax.broadcasted_iota(jnp.int32, (TILE, CELLS), 0)
    tiles = ROWS // TILE

    def read(t, a):
        if t < 0:
            return smooth(a, 0) + jnp.where(place == TILE - 1, edges[0][a], 0.0)
        if t == tiles:
            return smooth(a, t + 1) + jnp.where(place == 0, edges[1][a], 0.0)
        tile = smooth(a, t + 1) + extended[a, tile_rows(t + 1)]
        direction_ref[a, tile_rows(t)] = tile
        return tile

    fields = [Rows(lambda t, a=a: read(t, a), -1, tiles) for a in range(2)]
    for t in range(tiles):
        rows = tile_rows(t)
        viscosity = visc_ref[rows]
        for a in range(2):
            coupling = coup_ref[a, rows]
            diagonal = 10.0 * viscosity + jnp.abs(coupling) + 0.05
            image = (
                diagonal * fields[a].at(t)
                - viscosity * neighbours(fields[a], t, a)
                + coupling * fields[1 - a].at(t)
            )
            yield t, a, image


def lane_total(received, lane):
    place = lax.broadcasted_iota(jnp.int32, received.shape, 1)
    return jnp.sum(jnp.where(place == lane, received, 0.0), keepdims=True)


def first_turn_kernel(
    count, margin_ref, sums_ref, inverse_ref, partner_ref, other_ref, held, rhs_ref, visc_ref,
    coup_ref,
    direction_ref, image_ref, smooth_ref, residual_ref, factors_ref, partner_rows_ref, other_rows_ref,
    next_ref,
    extended, sums, first_ref, solved, lines,
):
    low, high = neighbours_of(partner_ref, other_ref)

    def begin(coarse):
        def scale():
            coarse.over_beta = 1.0 / jnp.sqrt(lane_total(sums_ref[...], VECTORS))

        def line():
            coarse.residual = line_up(sums_ref[...]) * coarse.over_beta
            residual_ref[...] = coarse.residual

        return [scale, line]

    coarse = Coarse(begin, inverse_ref, low, high, held, extended)

    def field(a, t):
        if 0 <= t < ROWS // TILE:
            return rhs_ref[a, tile_rows(t)]
        return component((low if t < 0 else high)[RHS_AT : RHS_AT + HALO], a)

    def make(a, e):
        if 0 < e <= ROWS // TILE:
            viscosity, coupling = visc_ref[tile_rows(e - 1)], coup_ref[a, tile_rows(e - 1)]
        else:
            side = low if e == 0 else high
            viscosity = side[:HALO]
            coupling = component(side[COUPLING_AT : COUPLING_AT + HALO], a)
        scale = RELAX / (10.0 * viscosity + jnp.abs(coupling) + 0.05)
        return scale, scale * viscosity, scale * coupling

    solve(
        count, margin_ref, factors_ref, make, field, smooth_ref, first_ref, solved, coarse.steps
    )
    smooth = lambda a, t: smooth_ref[a, tile_rows(t)] * coarse.over_beta
    images = apply_operator(
        coarse.edges, smooth, extended, visc_ref, coup_ref, direction_ref
    )
    odd = lax.axis_index("sub") % 2 == 1
    products, squares = [jnp.zeros((TILE, CELLS), jnp.float32)] * 2
    heads, tails = [None] * 2, [None] * 2
    for t, a, image in images:
        image_ref[a, tile_rows(t)] = image
        products = products + rhs_ref[a, tile_rows(t)] * image
        squares = squares + image * image
        if t == 0:
            heads[a] = image
        if t == ROWS // TILE - 1:
            tails[a] = image
    head, tail = outer_rows(heads, tails)
    partner_rows_ref[...] = jnp.where(odd, head, tail)
    other_rows_ref[...] = jnp.where(odd, tail, head)
    sums[...] = jnp.zeros_like(sums)
    sums[VECTORS : VECTORS + 8] = in_rows([fold(products), fold(squares)])

    restrict(held, image_ref, sums, lines)
    send_sums(sums, next_ref)


def first_column(first, second):
    beta = jnp.sqrt(lane_total(first, VECTORS))
    h_00 = lane_total(second, VECTORS) / beta
    h_10 = jnp.sqrt(lane_total(second, VECTORS + 1) - h_00 * h_00)
    return beta, h_00, h_10


def second_turn_kernel(
    count, margin_ref, sums_ref, second_ref, residual_ref, factors_ref, inverse_ref, partner_ref, other_ref,
    partner_rows_ref, other_rows_ref, held, smooth_ref, rhs_ref, image_ref, visc_ref, coup_ref,
    direction_ref, next_ref,
    image_smooth, extended, sums, first_ref, solved,
):
    low, high = neighbours_of(partner_ref, other_ref)

    def begin(coarse):
        def scale():
            beta, h_00, h_10 = first_column(sums_ref[...], second_ref[...])
            coarse.h_00, coarse.ratio, coarse.over = h_00, h_00 / beta, 1.0 / h_10

        def line():
            lined = line_up(second_ref[...])
            coarse.residual = (lined - coarse.h_00 * residual_ref[...]) * coarse.over

        return [scale, line]

    coarse = Coarse(begin, inverse_ref, low, high, held, extended)
    low_rows, high_rows = neighbours_of(partner_rows_ref, other_rows_ref)

    def field(a, t):
        if 0 <= t < ROWS // TILE:
            return image_ref[a, tile_rows(t)]
        rows = low_rows[...] if t < 0 else high_rows[...]
        return component(rows, a)

    solve(
        count, margin_ref, factors_ref, None, field, image_smooth, first_ref, solved, coarse.steps
    )

    def smooth(a, t):
        rows = tile_rows(t)
        return (image_smooth[a, rows] - coarse.ratio * smooth_ref[a, rows]) * coarse.over

    images = apply_operator(
        coarse.edges, smooth, extended, visc_ref, coup_ref, direction_ref
    )
    totals = [jnp.zeros((TILE, CELLS), jnp.float32)] * 3
    for t, a, image in images:
        others = (rhs_ref[a, tile_rows(t)], image_ref[a, tile_rows(t)], image)
        totals = [total + x * image for total, x in zip(totals, others)]
    sums[...] = jnp.zeros_like(sums)
    sums[:8] = in_rows([fold(total) for total in totals])
    send_sums(sums, next_ref)


def finish_kernel(
    first_ref, second_ref, third_ref, first_direction_ref, second_direction_ref,
    solution_ref, hessenberg_ref,
):
    third = third_ref[...]
    beta, h_00, h_10 = first_column(first_ref[...], second_ref[...])
    squares = lane_total(third, 2)
    h_01 = lane_total(third, 0) / beta
    h_11 = (lane_total(third, 1) - h_00 * h_01) / h_10
    h_21 = jnp.sqrt(squares - h_01 * h_01 - h_11 * h_11)
    l_00 = jnp.sqrt(h_00 * h_00 + h_10 * h_10)
    l_10 = (h_00 * h_01 + h_10 * h_11) / l_00
    f_0 = beta * h_00 / l_00
    c_1 = (beta * h_01 - l_10 * f_0) / (squares - l_10 * l_10)
    c_0 = (f_0 - l_10 * c_1) / l_00
    for a in range(2):
        solution_ref[a] = c_0 * first_direction_ref[a] + c_1 * second_direction_ref[a]
    shape = hessenberg_ref.shape
    row = lax.broadcasted_iota(jnp.int32, shape, 1)
    column = lax.broadcasted_iota(jnp.int32, shape, 0)
    entries = jnp.zeros(shape, jnp.float32)
    for i, j, value in ((0, 0, h_00), (0, 1, h_01), (1, 0, h_10), (1, 1, h_11), (2, 1, h_21)):
        entries = jnp.where((row == i) & (column == j), value, entries)
    hessenberg_ref[...] = entries


def call(kernel, name, in_specs, outs, flops, scratch=(), traffic=4_000_000):
    return pl.pallas_call(
        kernel,
        name=name,
        in_specs=in_specs,
        out_specs=[VMEM] * len(outs),
        out_shape=outs,
        scratch_shapes=scratch,
        compiler_params=pltpu.CompilerParams(vmem_limit_bytes=16 * 1024 * 1024),
        cost_estimate=pl.CostEstimate(flops=flops, bytes_accessed=traffic, transcendentals=0),
    )


def in_hbm(array):
    return pltpu.with_memory_space_constraint(array, pltpu.HBM)


def from_everyone(rows):
    order = [list(range(lax.axis_size("sub")))[::-1]]
    return lax.all_to_all(rows, "sub", 0, 0, tiled=True, axis_index_groups=order)


def swap(partner, other):
    count = lax.axis_size("sub")
    both = lambda lows: [pair for i in lows for pair in ((i, i + 1), (i + 1, i))]
    return (
        lax.ppermute(partner, "sub", both(range(0, count, 2))),
        lax.ppermute(other, "sub", both(range(1, count - 1, 2))),
    )


def on_device(rhs, viscosity, coupling, margin_rows, coarse_basis, coarse_inverse):
    count = lax.axis_size("sub")
    columns = coarse_inverse.shape[1]
    f32 = lambda *shape: jax.ShapeDtypeStruct(shape, jnp.float32)
    dma = lambda *shape: pltpu.SemaphoreType.DMA(shape)
    extended = pltpu.VMEM((2, EXT, CELLS), jnp.float32)
    stacked = pltpu.VMEM((2, STACKED, CELLS), jnp.float32)
    solved = pltpu.VMEM((4, STACKED, CELLS), jnp.float32)
    sums = pltpu.VMEM((SLOTS, LANES), jnp.float32)
    lines = pltpu.VMEM((LANES, len(MATRIX_GROUPS) * CELLS), jnp.bfloat16)
    row, whole, edge = f32(count, LANES), f32(2, ROWS, CELLS), f32(TILE, CELLS)
    packed, smoothed = f32(EDGE_AT + coarse_rows(columns), CELLS), f32(2, EXT, CELLS)
    arguments = (rhs, viscosity, coupling, coarse_inverse, coarse_basis)
    packs = call(
        pack_kernel, "pack", [HBM] * 5, [packed, packed], 5_000_000,
        [pltpu.VMEM((4, VECTORS, CHUNK, CELLS), jnp.bfloat16)]
        + [pltpu.VMEM((2, 2, 2, HALO, CELLS), jnp.float32), dma(4 * VECTORS // GROUP), dma(4)]
        + [dma(2 * pack_count(columns))],
    )(*map(in_hbm, arguments))
    held, partner, other = lax.optimization_barrier((coarse_basis, *packs))
    partner, other = swap(partner, other)
    (first,) = call(
        restrict_kernel, "restrict", [VMEM] * 2, [row], 10_000_000, [sums]
    )(rhs, held)
    first = from_everyone(first)
    direction, image, smooth, residual, factors, partner_rows, other_rows, second = call(
        functools.partial(first_turn_kernel, count), "first_turn", [SMEM] + [VMEM] * 8,
        [whole, whole, smoothed, f32(1, columns), f32(6, STACKED, CELLS), edge, edge, row], 20_000_000,
        [extended, sums, stacked, solved, lines],
    )(margin_rows, first, coarse_inverse, partner, other, held, rhs, viscosity, coupling)
    partner_rows, other_rows = swap(partner_rows, other_rows)
    second = from_everyone(second)
    second_direction, third = call(
        functools.partial(second_turn_kernel, count), "second_turn", [SMEM] + [VMEM] * 15,
        [whole, row], 20_000_000, [extended, extended, sums, stacked, solved],
    )(
        margin_rows, first, second, residual, factors, coarse_inverse, partner, other, partner_rows, other_rows,
        held, smooth, rhs, image, viscosity, coupling,
    )
    third = from_everyone(third)
    result, transposed = call(finish_kernel, "finish", [VMEM] * 5, [whole, f32(2, 3)], 1_000_000)(
        first, second, third, direction, second_direction
    )
    return result, transposed.T


def solution(mesh):
    in_specs = (
        P(None, ("groups", "sub"), None),
        P(("groups", "sub"), None),
        P(None, ("groups", "sub"), None),
        P("groups"),
        P(None, None, ("groups", "sub"), None),
        P(("groups", "sub"), None),
    )
    out_specs = (P(None, ("groups", "sub"), None), P("groups", None))
    return jax.shard_map(
        on_device, mesh=mesh, in_specs=in_specs, out_specs=out_specs, check_vma=False
    )
```

```python
import functools

import jax
import jax.numpy as jnp
from jax import lax
from jax.experimental import pallas as pl
from jax.experimental.pallas import tpu as pltpu
from jax.sharding import PartitionSpec as P

ROWS = 64
CELLS = 512
VECTORS = 48
HALO = 8
EXT = ROWS + 2 * HALO
STRIP = 32
GROUP = 16
STACKED = EXT + 2 * STRIP
TILE = 8
CHUNK = 16
CHUNKS = 2 * ROWS // CHUNK
PIECE = 8
LANES = 128
SLOTS = 64
COUPLING_AT = HALO
RHS_AT = 2 * HALO
EDGE_AT = 3 * HALO
INVERSE_AT = 2 * VECTORS
SWEEPS = 4
RELAX = 0.7
ROW_FACTOR = (1.0, 4.0)
CELL_FACTOR = (4.0, 1.0)

VMEM = pl.BlockSpec(memory_space=pltpu.VMEM)
SMEM = pl.BlockSpec(memory_space=pltpu.SMEM)
HBM = pl.BlockSpec(memory_space=pltpu.HBM)


def coarse_rows(columns):
    return INVERSE_AT + VECTORS * (columns // 512) + (VECTORS // 2) * (columns % 512 // 256)


def cell_sum(field):
    lane = lax.broadcasted_iota(jnp.int32, (field.shape[0], LANES), 1)
    left, right = pltpu.roll(field, 1, 1), pltpu.roll(field, CELLS - 1, 1)
    inner = left[:, LANES:-LANES] + right[:, LANES:-LANES]
    first = jnp.where(lane == 0, 0.0, left[:, :LANES]) + right[:, :LANES]
    last = left[:, -LANES:] + jnp.where(lane == LANES - 1, 0.0, right[:, -LANES:])
    return jnp.concatenate([first, inner, last], 1)


class Rows:
    def __init__(self, read, first, last):
        self.read, self.first, self.last = read, first, last
        self.tiles, self.down, self.up = {}, {}, {}

    def at(self, t):
        if t not in self.tiles:
            self.tiles[t] = self.read(t)
        return self.tiles[t]

    def moved(self, held, t, by):
        if t not in held:
            held[t] = pltpu.roll(self.at(t), by, 0)
        return held[t]

    def around(self, t):
        row = lax.broadcasted_iota(jnp.int32, (TILE, CELLS), 0)
        below, above = self.moved(self.down, t, 1), self.moved(self.up, t, TILE - 1)
        if t > self.first:
            below = jnp.where(row == 0, self.moved(self.down, t - 1, 1), below)
        if t < self.last:
            above = jnp.where(row == TILE - 1, self.moved(self.up, t + 1, TILE - 1), above)
        return below + above


def neighbours(rows, t, component):
    around, cells = rows.around(t), cell_sum(rows.at(t))
    if component == 0:
        return around + CELL_FACTOR[0] * cells
    return ROW_FACTOR[1] * around + cells


def sublane_sum(tile):
    for by in (4, 2, 1):
        tile = tile + pltpu.roll(tile, by, 0)
    return tile


def in_rows(tiles):
    row = lax.broadcasted_iota(jnp.int32, (8, LANES), 0)
    total = jnp.zeros((8, LANES), jnp.float32)
    for n, tile in enumerate(tiles):
        total = jnp.where(row == n, sublane_sum(tile), total)
    return total


GROUPS = tuple((a, r) for a in range(2) for r in range(0, ROWS, CHUNK))
VECTOR_GROUPS, MATRIX_GROUPS = GROUPS[:2], GROUPS[2:]


def restrict(held, field, sums, lines):
    lines[2 * CHUNK :] = jnp.zeros((LANES - 2 * CHUNK, lines.shape[1]), jnp.bfloat16)
    blocks = []
    for g, (a, r) in enumerate(MATRIX_GROUPS):
        part, cells = field[a, r : r + CHUNK], slice(CELLS * g, CELLS * (g + 1))
        high = part.astype(jnp.bfloat16)
        lines[:CHUNK, cells] = high
        lines[CHUNK : 2 * CHUNK, cells] = (part - high.astype(jnp.float32)).astype(jnp.bfloat16)
        blocks.append(held[:, a, r : r + CHUNK, :].reshape(CHUNK * VECTORS, CELLS))
    products = lax.dot_general(
        jnp.concatenate(blocks, 1),
        lines[...],
        (((1,), (1,)), ((), ())),
        preferred_element_type=jnp.float32,
    )
    row = lax.broadcasted_iota(jnp.int32, (CHUNK, LANES), 0)
    equal = row == lax.broadcasted_iota(jnp.int32, (CHUNK, LANES), 1) % CHUNK
    for first in range(0, VECTORS, PIECE):
        totals = [
            jnp.where(equal, products[CHUNK * k : CHUNK * (k + 1)], 0.0)
            for k in range(first, first + PIECE)
        ]
        for a, r in VECTOR_GROUPS:
            for c in range(0, CELLS, LANES):
                rows, cells = slice(r, r + CHUNK), slice(c, c + LANES)
                tile = field[a, rows, cells]
                for n in range(PIECE):
                    term = held[first + n, a, rows, cells].astype(jnp.float32) * tile
                    totals[n] = totals[n] + term
        sums[first : first + PIECE] = in_rows([total[:8] + total[8:] for total in totals])


def fold(row):
    total = row[:, :LANES]
    for c in range(LANES, CELLS, LANES):
        total = total + row[:, c : c + LANES]
    return total


def tile_rows(t):
    return slice(TILE * t, TILE * (t + 1))


def send_sums(sums, out_ref):
    rest = sums[...]
    parts = []
    for _ in range(3):
        part = rest.astype(jnp.bfloat16)
        parts.append(part)
        rest = rest - part.astype(jnp.float32)
    row = lax.dot_general(
        jnp.ones((CHUNK, 3 * LANES), jnp.bfloat16),
        jnp.concatenate(parts, 1),
        (((1,), (1,)), ((), ())),
        preferred_element_type=jnp.float32,
    )
    wide = jnp.concatenate([row[:1], jnp.zeros((1, LANES - SLOTS), jnp.float32)], 1)
    out_ref[...] = jnp.broadcast_to(wide, out_ref.shape)


def pack_copies(out_ref, first_row, visc_ref, inverse_ref, sems, at_sem):
    rows = pl.ds(pl.multiple_of(first_row, HALO), HALO)
    moves = [(visc_ref.at[rows, :], 0, HALO, None)]
    columns = inverse_ref.shape[1]
    at = EDGE_AT + INVERSE_AT
    for c in range(0, columns - 511, 512):
        moves.append((inverse_ref.at[:, pl.ds(c, 512)], at, VECTORS, None))
        at += VECTORS
    if columns % 512:
        half = VECTORS // 2
        last = pl.ds(columns - 256, 256)
        moves.append((inverse_ref.at[pl.ds(0, half), last], at, half, 0))
        moves.append((inverse_ref.at[pl.ds(half, half), last], at, half, 256))
    copies = []
    for n, (source, at, size, lane) in enumerate(moves):
        place = pl.ds(at, size)
        target = out_ref.at[place, :] if lane is None else out_ref.at[place, pl.ds(lane, 256)]
        copies.append(pltpu.make_async_copy(source, target, sems.at[at_sem + n]))
    return copies


def pack_count(columns):
    return 1 + columns // 512 + 2 * (columns % 512 // 256)


def outer_rows(head, tail):
    half = lax.broadcasted_iota(jnp.int32, (TILE, CELLS), 0) < TILE // 2
    return (
        jnp.where(half, head[0], pltpu.roll(head[1], TILE // 2, 0)),
        jnp.where(half, pltpu.roll(tail[1], TILE // 2, 0), tail[0]),
    )


def component(rows, a):
    return pltpu.roll(rows, TILE // 2, 0) if a else rows


def pack_kernel(
    rhs_ref, visc_ref, coup_ref, inverse_ref, basis_ref,
    partner_ref, other_ref,
    groups, staged, group_sems, stage_sems, pack_sems,
):
    odd = lax.axis_index("sub") % 2
    sides = ((partner_ref, 1 - odd), (other_ref, odd))
    group_copies, packs = [], []
    for k in range(0, VECTORS, GROUP):
        for n, (out_ref, up) in enumerate(sides):
            rows = pl.ds(pl.multiple_of(up * (ROWS - CHUNK), CHUNK), CHUNK)
            for a in range(2):
                group_copies.append(
                    pltpu.make_async_copy(
                        basis_ref.at[pl.ds(k, GROUP), a, rows, :],
                        groups.at[2 * n + a, pl.ds(k, GROUP)],
                        group_sems.at[len(group_copies)],
                    )
                )
    for n, (out_ref, up) in enumerate(sides):
        packs += pack_copies(
            out_ref, up * (ROWS - HALO), visc_ref, inverse_ref, pack_sems,
            n * pack_count(inverse_ref.shape[1]),
        )
    stages = []
    for m, ref in enumerate((coup_ref, rhs_ref)):
        for n, first_row in enumerate((0, ROWS - HALO)):
            stages.append(
                pltpu.make_async_copy(
                    ref.at[:, pl.ds(first_row, HALO), :], staged.at[m, n], stage_sems.at[2 * m + n]
                )
            )
    for copy in stages + group_copies + packs:
        copy.start(priority=1)
    for copy in stages:
        copy.wait()
    for m, at in enumerate((COUPLING_AT, RHS_AT)):
        head, tail = outer_rows(staged[m, 0], staged[m, 1])
        partner_ref[at : at + HALO] = jnp.where(odd == 1, head, tail)
        other_ref[at : at + HALO] = jnp.where(odd == 1, tail, head)

    def take(out_ref, group, first, row):
        for k in range(first, first + GROUP, TILE):
            lines = [groups[group, k + n].astype(jnp.float32)[row : row + 1] for n in range(TILE)]
            at = EDGE_AT + VECTORS * (group % 2) + k
            out_ref[at : at + TILE] = jnp.concatenate(lines, 0)

    for first in range(0, VECTORS, GROUP):
        for _ in range(4):
            group_copies.pop(0).wait()

        @pl.when(odd == 0)
        def _():
            for a in range(2):
                take(partner_ref, a, first, CHUNK - 1)
                take(other_ref, 2 + a, first, 0)

        @pl.when(odd == 1)
        def _():
            for a in range(2):
                take(partner_ref, a, first, 0)
                take(other_ref, 2 + a, first, CHUNK - 1)

    for copy in packs:
        copy.wait()


def restrict_kernel(rhs_ref, held, sums_ref, sums, lines):
    sums[...] = jnp.zeros_like(sums)
    squares = jnp.zeros((TILE, CELLS), jnp.float32)
    for a in range(2):
        for t in range(ROWS // TILE):
            tile = rhs_ref[a, tile_rows(t)]
            squares = squares + tile * tile
    sums[VECTORS : VECTORS + 8] = in_rows([fold(squares)])

    restrict(held, rhs_ref, sums, lines)
    send_sums(sums, sums_ref)


class Neighbour:
    def __init__(self, first_ref, second_ref):
        self.odd = lax.axis_index("sub") % 2 == 1
        self.first, self.second = first_ref, second_ref

    def __getitem__(self, index):
        return jnp.where(self.odd, self.first[index], self.second[index])


def neighbours_of(partner_ref, other_ref):
    return Neighbour(partner_ref, other_ref), Neighbour(other_ref, partner_ref)


def solve(count, margin_ref, factors_ref, make, field, out_ref, first_ref, solved, steps):
    waiting, done = list(steps), 0
    every = (SWEEPS - 1) * (STACKED // TILE) // len(waiting)
    assert every > 0
    rank = lax.axis_index("sub")
    lower = jnp.where(rank > 0, margin_ref[jnp.maximum(rank - 1, 0)], 0)
    upper = jnp.where(rank < count - 1, margin_ref[rank], 0)
    lower_f, upper_f = lower.astype(jnp.float32), upper.astype(jnp.float32)
    low_scale = 1.0 / (2.0 * jnp.maximum(lower_f, 1.0))
    high_scale = 1.0 / (2.0 * jnp.maximum(upper_f, 1.0))
    wide = lambda x: jnp.concatenate([x] * (CELLS // LANES), 1)
    own_tiles = ROWS // TILE
    strip_tiles = STRIP // TILE
    last = own_tiles + 1
    segments = (
        (0, 0, last + 1),
        (last + 1, 0, strip_tiles),
        (last + 1 + strip_tiles, last + 1 - strip_tiles, strip_tiles),
    )

    def place_of(e):
        return lax.broadcasted_iota(jnp.int32, (TILE, LANES), 0) + (TILE * e - HALO)

    def live_of(segment, e):
        place = place_of(e)
        if segment == 0:
            live = (place >= -lower) & (place < ROWS + upper)
        elif segment == 1:
            live = place < lower
        else:
            live = place >= ROWS - upper
        return wide(live.astype(jnp.float32))

    def weight_of(segment, e):
        place = place_of(e)
        place_f = place.astype(jnp.float32)
        rising = lambda base, scale: (place_f - base + 0.5) * scale
        falling = lambda base, scale: (base - place_f - 0.5) * scale
        if segment == 0:
            weight = jnp.where(place < lower, rising(-lower_f, low_scale), 1.0)
            weight = jnp.where(
                place >= ROWS - upper, falling(ROWS + upper_f, high_scale), weight
            )
        elif segment == 1:
            weight = jnp.where(place >= -lower, falling(lower_f, low_scale), 1.0)
        else:
            weight = jnp.where(place < ROWS + upper, rising(ROWS - upper_f, high_scale), 1.0)
        return wide(weight)

    for e in range(last + 1):
        for a in range(2):
            parts = make(a, e) if make else None
            value = field(a, e - 1)
            for n, (first, begin, size) in enumerate(segments):
                if not begin <= e < begin + size:
                    continue
                rows = tile_rows(first + e - begin)
                if make:
                    always = n == 0 and 0 < e < last
                    live = None if always else live_of(n, e)
                    for m, part in enumerate(parts):
                        factors_ref[3 * a + m, rows] = part if always else live * part
                first_ref[a, rows] = factors_ref[3 * a, rows] * value

    for sweep in range(1, SWEEPS):
        for n, (first, begin, size) in enumerate(segments):
            end = first + size - 1
            if sweep == 1:
                reads = [lambda t, a=a: first_ref[a, tile_rows(t)] for a in range(2)]
            else:
                bank = 2 * (sweep % 2)
                reads = [lambda t, a=a: solved[bank + a, tile_rows(t)] for a in range(2)]
            fields = [Rows(read, first, end) for read in reads]
            for t in range(first, end + 1):
                rows = tile_rows(t)
                if done % every == 0 and waiting:
                    waiting.pop(0)()
                done += 1
                for a in range(2):
                    value = (
                        ((1.0 - RELAX) * fields[a].at(t) + first_ref[a, rows])
                        + factors_ref[3 * a + 1, rows] * neighbours(fields[a], t, a)
                        - factors_ref[3 * a + 2, rows] * fields[1 - a].at(t)
                    )
                    e = t - first + begin
                    if sweep < SWEEPS - 1:
                        solved[2 * ((sweep + 1) % 2) + a, rows] = value
                    elif n == 0:
                        out_ref[a, tile_rows(e)] = weight_of(n, e) * value
                    else:
                        out_ref[a, tile_rows(e)] += weight_of(n, e) * value


def line_up(residuals):
    devices = residuals.shape[0]
    lane = lax.broadcasted_iota(jnp.int32, (1, LANES), 1)
    tiles = [jnp.zeros((1, LANES), jnp.float32) for _ in range(devices * VECTORS // LANES)]
    for t in range(devices):
        tile, offset = divmod(VECTORS * t, LANES)
        row = jnp.where(lane < VECTORS, residuals[devices - 1 - t : devices - t], 0.0)
        if offset:
            row = pltpu.roll(row, offset, 1)
        if offset + VECTORS <= LANES:
            tiles[tile] = tiles[tile] + row
        else:
            tiles[tile] = tiles[tile] + jnp.where(lane >= offset, row, 0.0)
            tiles[tile + 1] = tiles[tile + 1] + jnp.where(lane < offset, row, 0.0)
    return jnp.concatenate(tiles, 1)


def rounded(column):
    return column.astype(jnp.bfloat16).astype(jnp.float32)


def lift(inverse_ref, residual):
    return rounded(jnp.sum(inverse_ref[...] * residual, 1, keepdims=True))


def lift_packed(ref, residual):
    columns = residual.shape[1]
    at, total = EDGE_AT + INVERSE_AT, None
    for c in range(0, columns - 511, 512):
        term = jnp.sum(ref[at : at + VECTORS] * residual[:, c : c + 512], 1, keepdims=True)
        total = term if total is None else total + term
        at += VECTORS
    if columns % 512:
        half = VECTORS // 2
        last = residual[:, columns - 256 :]
        rows = ref[at : at + half]
        term = jnp.concatenate(
            [
                jnp.sum(rows[:, :256] * last, 1, keepdims=True),
                jnp.sum(rows[:, 256:] * last, 1, keepdims=True),
            ],
            0,
        )
        total = term if total is None else total + term
    return rounded(total)


def edge_values(ref, lifted):
    starts = [EDGE_AT + VECTORS * a for a in range(2)]
    return [jnp.sum(ref[at : at + VECTORS] * lifted, 0, keepdims=True) for at in starts]


def spread(lifted):
    shape = (VECTORS, CHUNK * VECTORS)
    owner = lax.broadcasted_iota(jnp.int32, shape, 1) // CHUNK
    row = lax.broadcasted_iota(jnp.int32, shape, 0)
    line = jnp.sum(jnp.where(owner == row, lifted, 0.0), 0, keepdims=True)
    shape = (CHUNK, CHUNK * VECTORS)
    place = lax.broadcasted_iota(jnp.int32, shape, 1) % CHUNK
    row = lax.broadcasted_iota(jnp.int32, shape, 0)
    return jnp.where(place == row, line, 0.0).astype(jnp.bfloat16)


class Coarse:
    def __init__(self, begin, inverse_ref, low, high, held, extended):
        self.inverse, self.sides, self.held, self.extended = inverse_ref, (low, high), held, extended
        self.lifted, self.edges = [None] * 2, [None] * 2
        self.steps = begin(self) + [self.lift_own, self.make_matrix]
        for a in range(2):
            for r in range(0, ROWS, CHUNK):
                self.steps.append(functools.partial(self.prolong, a, r))
        for n in range(2):
            self.steps.insert(len(self.steps) - 6, functools.partial(self.lift_side, n))
            self.steps.append(functools.partial(self.edge, n))

    def lift_own(self):
        self.own = lift(self.inverse, self.residual)

    def make_matrix(self):
        self.matrix = spread(self.own)

    def prolong(self, a, r):
        rows = self.held[:, a, r : r + CHUNK, :].reshape(CHUNK * VECTORS, CELLS)
        self.extended[a, HALO + r : HALO + r + CHUNK] = jnp.dot(
            self.matrix, rows, preferred_element_type=jnp.float32
        )

    def lift_side(self, n):
        self.lifted[n] = lift_packed(self.sides[n], self.residual)

    def edge(self, n):
        self.edges[n] = edge_values(self.sides[n], self.lifted[n])


def apply_operator(edges, smooth, extended, visc_ref, coup_ref, direction_ref):
    place = lax.broadcasted_iota(jnp.int32, (TILE, CELLS), 0)
    tiles = ROWS // TILE

    def read(t, a):
        if t < 0:
            return smooth(a, 0) + jnp.where(place == TILE - 1, edges[0][a], 0.0)
        if t == tiles:
            return smooth(a, t + 1) + jnp.where(place == 0, edges[1][a], 0.0)
        tile = smooth(a, t + 1) + extended[a, tile_rows(t + 1)]
        direction_ref[a, tile_rows(t)] = tile
        return tile

    fields = [Rows(lambda t, a=a: read(t, a), -1, tiles) for a in range(2)]
    for t in range(tiles):
        rows = tile_rows(t)
        viscosity = visc_ref[rows]
        for a in range(2):
            coupling = coup_ref[a, rows]
            diagonal = 10.0 * viscosity + jnp.abs(coupling) + 0.05
            image = (
                diagonal * fields[a].at(t)
                - viscosity * neighbours(fields[a], t, a)
                + coupling * fields[1 - a].at(t)
            )
            yield t, a, image


def lane_total(received, lane):
    place = lax.broadcasted_iota(jnp.int32, received.shape, 1)
    return jnp.sum(jnp.where(place == lane, received, 0.0), keepdims=True)


def first_turn_kernel(
    count, margin_ref, sums_ref, inverse_ref, partner_ref, other_ref, held, rhs_ref, visc_ref,
    coup_ref,
    direction_ref, image_ref, smooth_ref, residual_ref, factors_ref, partner_rows_ref, other_rows_ref,
    next_ref,
    extended, sums, first_ref, solved, lines,
):
    low, high = neighbours_of(partner_ref, other_ref)

    def begin(coarse):
        def scale():
            coarse.over_beta = 1.0 / jnp.sqrt(lane_total(sums_ref[...], VECTORS))

        def line():
            coarse.residual = line_up(sums_ref[...]) * coarse.over_beta
            residual_ref[...] = coarse.residual

        return [scale, line]

    coarse = Coarse(begin, inverse_ref, low, high, held, extended)

    def field(a, t):
        if 0 <= t < ROWS // TILE:
            return rhs_ref[a, tile_rows(t)]
        return component((low if t < 0 else high)[RHS_AT : RHS_AT + HALO], a)

    def make(a, e):
        if 0 < e <= ROWS // TILE:
            viscosity, coupling = visc_ref[tile_rows(e - 1)], coup_ref[a, tile_rows(e - 1)]
        else:
            side = low if e == 0 else high
            viscosity = side[:HALO]
            coupling = component(side[COUPLING_AT : COUPLING_AT + HALO], a)
        scale = RELAX / (10.0 * viscosity + jnp.abs(coupling) + 0.05)
        return scale, scale * viscosity, scale * coupling

    solve(
        count, margin_ref, factors_ref, make, field, smooth_ref, first_ref, solved, coarse.steps
    )
    smooth = lambda a, t: smooth_ref[a, tile_rows(t)] * coarse.over_beta
    images = apply_operator(
        coarse.edges, smooth, extended, visc_ref, coup_ref, direction_ref
    )
    odd = lax.axis_index("sub") % 2 == 1
    products, squares = [jnp.zeros((TILE, CELLS), jnp.float32)] * 2
    heads, tails = [None] * 2, [None] * 2
    for t, a, image in images:
        image_ref[a, tile_rows(t)] = image
        products = products + rhs_ref[a, tile_rows(t)] * image
        squares = squares + image * image
        if t == 0:
            heads[a] = image
        if t == ROWS // TILE - 1:
            tails[a] = image
    head, tail = outer_rows(heads, tails)
    partner_rows_ref[...] = jnp.where(odd, head, tail)
    other_rows_ref[...] = jnp.where(odd, tail, head)
    sums[...] = jnp.zeros_like(sums)
    sums[VECTORS : VECTORS + 8] = in_rows([fold(products), fold(squares)])

    restrict(held, image_ref, sums, lines)
    send_sums(sums, next_ref)


def first_column(first, second):
    beta = jnp.sqrt(lane_total(first, VECTORS))
    h_00 = lane_total(second, VECTORS) / beta
    h_10 = jnp.sqrt(lane_total(second, VECTORS + 1) - h_00 * h_00)
    return beta, h_00, h_10


def second_turn_kernel(
    count, margin_ref, sums_ref, second_ref, residual_ref, factors_ref, inverse_ref, partner_ref, other_ref,
    partner_rows_ref, other_rows_ref, held, smooth_ref, rhs_ref, image_ref, visc_ref, coup_ref,
    direction_ref, next_ref,
    image_smooth, extended, sums, first_ref, solved,
):
    low, high = neighbours_of(partner_ref, other_ref)

    def begin(coarse):
        def scale():
            beta, h_00, h_10 = first_column(sums_ref[...], second_ref[...])
            coarse.h_00, coarse.ratio, coarse.over = h_00, h_00 / beta, 1.0 / h_10

        def line():
            lined = line_up(second_ref[...])
            coarse.residual = (lined - coarse.h_00 * residual_ref[...]) * coarse.over

        return [scale, line]

    coarse = Coarse(begin, inverse_ref, low, high, held, extended)
    low_rows, high_rows = neighbours_of(partner_rows_ref, other_rows_ref)

    def field(a, t):
        if 0 <= t < ROWS // TILE:
            return image_ref[a, tile_rows(t)]
        rows = low_rows[...] if t < 0 else high_rows[...]
        return component(rows, a)

    solve(
        count, margin_ref, factors_ref, None, field, image_smooth, first_ref, solved, coarse.steps
    )

    def smooth(a, t):
        rows = tile_rows(t)
        return (image_smooth[a, rows] - coarse.ratio * smooth_ref[a, rows]) * coarse.over

    images = apply_operator(
        coarse.edges, smooth, extended, visc_ref, coup_ref, direction_ref
    )
    totals = [jnp.zeros((TILE, CELLS), jnp.float32)] * 3
    for t, a, image in images:
        others = (rhs_ref[a, tile_rows(t)], image_ref[a, tile_rows(t)], image)
        totals = [total + x * image for total, x in zip(totals, others)]
    sums[...] = jnp.zeros_like(sums)
    sums[:8] = in_rows([fold(total) for total in totals])
    send_sums(sums, next_ref)


def finish_kernel(
    first_ref, second_ref, third_ref, first_direction_ref, second_direction_ref,
    solution_ref, hessenberg_ref,
):
    third = third_ref[...]
    beta, h_00, h_10 = first_column(first_ref[...], second_ref[...])
    squares = lane_total(third, 2)
    h_01 = lane_total(third, 0) / beta
    h_11 = (lane_total(third, 1) - h_00 * h_01) / h_10
    h_21 = jnp.sqrt(squares - h_01 * h_01 - h_11 * h_11)
    l_00 = jnp.sqrt(h_00 * h_00 + h_10 * h_10)
    l_10 = (h_00 * h_01 + h_10 * h_11) / l_00
    f_0 = beta * h_00 / l_00
    c_1 = (beta * h_01 - l_10 * f_0) / (squares - l_10 * l_10)
    c_0 = (f_0 - l_10 * c_1) / l_00
    for a in range(2):
        solution_ref[a] = c_0 * first_direction_ref[a] + c_1 * second_direction_ref[a]
    shape = hessenberg_ref.shape
    row = lax.broadcasted_iota(jnp.int32, shape, 1)
    column = lax.broadcasted_iota(jnp.int32, shape, 0)
    entries = jnp.zeros(shape, jnp.float32)
    for i, j, value in ((0, 0, h_00), (0, 1, h_01), (1, 0, h_10), (1, 1, h_11), (2, 1, h_21)):
        entries = jnp.where((row == i) & (column == j), value, entries)
    hessenberg_ref[...] = entries


def call(kernel, name, in_specs, outs, flops, scratch=(), traffic=4_000_000):
    return pl.pallas_call(
        kernel,
        name=name,
        in_specs=in_specs,
        out_specs=[VMEM] * len(outs),
        out_shape=outs,
        scratch_shapes=scratch,
        compiler_params=pltpu.CompilerParams(vmem_limit_bytes=16 * 1024 * 1024),
        cost_estimate=pl.CostEstimate(flops=flops, bytes_accessed=traffic, transcendentals=0),
    )


def in_hbm(array):
    return pltpu.with_memory_space_constraint(array, pltpu.HBM)


def from_everyone(rows):
    order = [list(range(lax.axis_size("sub")))[::-1]]
    return lax.all_to_all(rows, "sub", 0, 0, tiled=True, axis_index_groups=order)


def swap(partner, other):
    count = lax.axis_size("sub")
    both = lambda lows: [pair for i in lows for pair in ((i, i + 1), (i + 1, i))]
    return (
        lax.ppermute(partner, "sub", both(range(0, count, 2))),
        lax.ppermute(other, "sub", both(range(1, count - 1, 2))),
    )


def on_device(rhs, viscosity, coupling, margin_rows, coarse_basis, coarse_inverse):
    count = lax.axis_size("sub")
    columns = coarse_inverse.shape[1]
    f32 = lambda *shape: jax.ShapeDtypeStruct(shape, jnp.float32)
    dma = lambda *shape: pltpu.SemaphoreType.DMA(shape)
    extended = pltpu.VMEM((2, EXT, CELLS), jnp.float32)
    stacked = pltpu.VMEM((2, STACKED, CELLS), jnp.float32)
    solved = pltpu.VMEM((4, STACKED, CELLS), jnp.float32)
    sums = pltpu.VMEM((SLOTS, LANES), jnp.float32)
    lines = pltpu.VMEM((LANES, len(MATRIX_GROUPS) * CELLS), jnp.bfloat16)
    row, whole, edge = f32(count, LANES), f32(2, ROWS, CELLS), f32(TILE, CELLS)
    packed, smoothed = f32(EDGE_AT + coarse_rows(columns), CELLS), f32(2, EXT, CELLS)
    arguments = (rhs, viscosity, coupling, coarse_inverse, coarse_basis)
    packs = call(
        pack_kernel, "pack", [HBM] * 5, [packed, packed], 5_000_000,
        [pltpu.VMEM((4, VECTORS, CHUNK, CELLS), jnp.bfloat16)]
        + [pltpu.VMEM((2, 2, 2, HALO, CELLS), jnp.float32), dma(4 * VECTORS // GROUP), dma(4)]
        + [dma(2 * pack_count(columns))],
    )(*map(in_hbm, arguments))
    held, partner, other = lax.optimization_barrier((coarse_basis, *packs))
    partner, other = swap(partner, other)
    (first,) = call(
        restrict_kernel, "restrict", [VMEM] * 2, [row], 10_000_000, [sums, lines]
    )(rhs, held)
    first = from_everyone(first)
    direction, image, smooth, residual, factors, partner_rows, other_rows, second = call(
        functools.partial(first_turn_kernel, count), "first_turn", [SMEM] + [VMEM] * 8,
        [whole, whole, smoothed, f32(1, columns), f32(6, STACKED, CELLS), edge, edge, row], 20_000_000,
        [extended, sums, stacked, solved, lines],
    )(margin_rows, first, coarse_inverse, partner, other, held, rhs, viscosity, coupling)
    partner_rows, other_rows = swap(partner_rows, other_rows)
    second = from_everyone(second)
    second_direction, third = call(
        functools.partial(second_turn_kernel, count), "second_turn", [SMEM] + [VMEM] * 15,
        [whole, row], 20_000_000, [extended, extended, sums, stacked, solved],
    )(
        margin_rows, first, second, residual, factors, coarse_inverse, partner, other, partner_rows, other_rows,
        held, smooth, rhs, image, viscosity, coupling,
    )
    third = from_everyone(third)
    result, transposed = call(finish_kernel, "finish", [VMEM] * 5, [whole, f32(2, 3)], 1_000_000)(
        first, second, third, direction, second_direction
    )
    return result, transposed.T


def solution(mesh):
    in_specs = (
        P(None, ("groups", "sub"), None),
        P(("groups", "sub"), None),
        P(None, ("groups", "sub"), None),
        P("groups"),
        P(None, None, ("groups", "sub"), None),
        P(("groups", "sub"), None),
    )
    out_specs = (P(None, ("groups", "sub"), None), P("groups", None))
    return jax.shard_map(
        on_device, mesh=mesh, in_specs=in_specs, out_specs=out_specs, check_vma=False
    )
```

```python
import functools

import jax
import jax.numpy as jnp
from jax import lax
from jax.experimental import pallas as pl
from jax.experimental.pallas import tpu as pltpu
from jax.sharding import PartitionSpec as P

ROWS = 64
CELLS = 512
VECTORS = 48
HALO = 8
EXT = ROWS + 2 * HALO
STRIP = 32
GROUP = 16
STACKED = EXT + 2 * STRIP
TILE = 8
CHUNK = 16
CHUNKS = 2 * ROWS // CHUNK
PIECE = 8
LANES = 128
SLOTS = 64
COUPLING_AT = HALO
RHS_AT = 2 * HALO
EDGE_AT = 3 * HALO
INVERSE_AT = 2 * VECTORS
SWEEPS = 4
RELAX = 0.7
ROW_FACTOR = (1.0, 4.0)
CELL_FACTOR = (4.0, 1.0)

VMEM = pl.BlockSpec(memory_space=pltpu.VMEM)
SMEM = pl.BlockSpec(memory_space=pltpu.SMEM)
HBM = pl.BlockSpec(memory_space=pltpu.HBM)


def coarse_rows(columns):
    return INVERSE_AT + VECTORS * (columns // 512) + (VECTORS // 2) * (columns % 512 // 256)


def cell_sum(field):
    lane = lax.broadcasted_iota(jnp.int32, (field.shape[0], LANES), 1)
    left, right = pltpu.roll(field, 1, 1), pltpu.roll(field, CELLS - 1, 1)
    inner = left[:, LANES:-LANES] + right[:, LANES:-LANES]
    first = jnp.where(lane == 0, 0.0, left[:, :LANES]) + right[:, :LANES]
    last = left[:, -LANES:] + jnp.where(lane == LANES - 1, 0.0, right[:, -LANES:])
    return jnp.concatenate([first, inner, last], 1)


class Rows:
    def __init__(self, read, first, last):
        self.read, self.first, self.last = read, first, last
        self.tiles, self.down, self.up = {}, {}, {}

    def at(self, t):
        if t not in self.tiles:
            self.tiles[t] = self.read(t)
        return self.tiles[t]

    def moved(self, held, t, by):
        if t not in held:
            held[t] = pltpu.roll(self.at(t), by, 0)
        return held[t]

    def around(self, t):
        row = lax.broadcasted_iota(jnp.int32, (TILE, CELLS), 0)
        below, above = self.moved(self.down, t, 1), self.moved(self.up, t, TILE - 1)
        if t > self.first:
            below = jnp.where(row == 0, self.moved(self.down, t - 1, 1), below)
        if t < self.last:
            above = jnp.where(row == TILE - 1, self.moved(self.up, t + 1, TILE - 1), above)
        return below + above


def neighbours(rows, t, component):
    around, cells = rows.around(t), cell_sum(rows.at(t))
    if component == 0:
        return around + CELL_FACTOR[0] * cells
    return ROW_FACTOR[1] * around + cells


def sublane_sum(tile):
    for by in (4, 2, 1):
        tile = tile + pltpu.roll(tile, by, 0)
    return tile


def in_rows(tiles):
    row = lax.broadcasted_iota(jnp.int32, tiles[0].shape, 0)
    total = jnp.zeros(tiles[0].shape, jnp.float32)
    for n, tile in enumerate(tiles):
        total = jnp.where(row == n, sublane_sum(tile), total)
    return total


VECTOR_GROUPS = tuple((0, r) for r in range(0, ROWS, CHUNK))
MATRIX_GROUPS = tuple((1, r) for r in range(0, ROWS, CHUNK))


def restrict(held, field, sums, lines, others):
    blocks = []
    for g, (a, r) in enumerate(MATRIX_GROUPS):
        part, cells = field[a, r : r + CHUNK], slice(CELLS * g, CELLS * (g + 1))
        high = part.astype(jnp.bfloat16)
        lines[:CHUNK, cells] = high
        lines[CHUNK : 2 * CHUNK, cells] = (part - high.astype(jnp.float32)).astype(jnp.bfloat16)
        blocks.append(held[:, a, r : r + CHUNK, :].reshape(CHUNK * VECTORS, CELLS))
    products = lax.dot_general(
        jnp.concatenate(blocks, 1),
        lines[...],
        (((1,), (1,)), ((), ())),
        preferred_element_type=jnp.float32,
    )
    row = lax.broadcasted_iota(jnp.int32, (CHUNK, 2 * CHUNK), 0)
    equal = row == lax.broadcasted_iota(jnp.int32, (CHUNK, 2 * CHUNK), 1) % CHUNK
    others[...] = jnp.zeros_like(others)
    for first in range(0, VECTORS, PIECE):
        totals = [None] * PIECE
        for a, r in VECTOR_GROUPS:
            for c in range(0, CELLS, LANES):
                rows, cells = slice(r, r + CHUNK), slice(c, c + LANES)
                tile = field[a, rows, cells]
                for n in range(PIECE):
                    term = held[first + n, a, rows, cells].astype(jnp.float32) * tile
                    totals[n] = term if totals[n] is None else totals[n] + term
        sums[first : first + PIECE] = in_rows([total[:8] + total[8:] for total in totals])
        kept = [
            jnp.where(equal, products[CHUNK * k : CHUNK * (k + 1)], 0.0)
            for k in range(first, first + PIECE)
        ]
        others[first : first + PIECE, : 2 * CHUNK] = in_rows([x[:8] + x[8:] for x in kept])
    sums[:VECTORS] += others[...]


def fold(row):
    total = row[:, :LANES]
    for c in range(LANES, CELLS, LANES):
        total = total + row[:, c : c + LANES]
    return total


def tile_rows(t):
    return slice(TILE * t, TILE * (t + 1))


def send_sums(sums, out_ref):
    rest = sums[...]
    parts = []
    for _ in range(3):
        part = rest.astype(jnp.bfloat16)
        parts.append(part)
        rest = rest - part.astype(jnp.float32)
    row = lax.dot_general(
        jnp.ones((CHUNK, 3 * LANES), jnp.bfloat16),
        jnp.concatenate(parts, 1),
        (((1,), (1,)), ((), ())),
        preferred_element_type=jnp.float32,
    )
    wide = jnp.concatenate([row[:1], jnp.zeros((1, LANES - SLOTS), jnp.float32)], 1)
    out_ref[...] = jnp.broadcast_to(wide, out_ref.shape)


def pack_copies(out_ref, first_row, visc_ref, inverse_ref, sems, at_sem):
    rows = pl.ds(pl.multiple_of(first_row, HALO), HALO)
    moves = [(visc_ref.at[rows, :], 0, HALO, None)]
    columns = inverse_ref.shape[1]
    at = EDGE_AT + INVERSE_AT
    for c in range(0, columns - 511, 512):
        moves.append((inverse_ref.at[:, pl.ds(c, 512)], at, VECTORS, None))
        at += VECTORS
    if columns % 512:
        half = VECTORS // 2
        last = pl.ds(columns - 256, 256)
        moves.append((inverse_ref.at[pl.ds(0, half), last], at, half, 0))
        moves.append((inverse_ref.at[pl.ds(half, half), last], at, half, 256))
    copies = []
    for n, (source, at, size, lane) in enumerate(moves):
        place = pl.ds(at, size)
        target = out_ref.at[place, :] if lane is None else out_ref.at[place, pl.ds(lane, 256)]
        copies.append(pltpu.make_async_copy(source, target, sems.at[at_sem + n]))
    return copies


def pack_count(columns):
    return 1 + columns // 512 + 2 * (columns % 512 // 256)


def outer_rows(head, tail):
    half = lax.broadcasted_iota(jnp.int32, (TILE, CELLS), 0) < TILE // 2
    return (
        jnp.where(half, head[0], pltpu.roll(head[1], TILE // 2, 0)),
        jnp.where(half, pltpu.roll(tail[1], TILE // 2, 0), tail[0]),
    )


def component(rows, a):
    return pltpu.roll(rows, TILE // 2, 0) if a else rows


def pack_kernel(
    rhs_ref, visc_ref, coup_ref, inverse_ref, basis_ref,
    partner_ref, other_ref,
    groups, staged, group_sems, stage_sems, pack_sems,
):
    odd = lax.axis_index("sub") % 2
    sides = ((partner_ref, 1 - odd), (other_ref, odd))
    group_copies, packs = [], []
    for k in range(0, VECTORS, GROUP):
        for n, (out_ref, up) in enumerate(sides):
            rows = pl.ds(pl.multiple_of(up * (ROWS - CHUNK), CHUNK), CHUNK)
            for a in range(2):
                group_copies.append(
                    pltpu.make_async_copy(
                        basis_ref.at[pl.ds(k, GROUP), a, rows, :],
                        groups.at[2 * n + a, pl.ds(k, GROUP)],
                        group_sems.at[len(group_copies)],
                    )
                )
    for n, (out_ref, up) in enumerate(sides):
        packs += pack_copies(
            out_ref, up * (ROWS - HALO), visc_ref, inverse_ref, pack_sems,
            n * pack_count(inverse_ref.shape[1]),
        )
    stages = []
    for m, ref in enumerate((coup_ref, rhs_ref)):
        for n, first_row in enumerate((0, ROWS - HALO)):
            stages.append(
                pltpu.make_async_copy(
                    ref.at[:, pl.ds(first_row, HALO), :], staged.at[m, n], stage_sems.at[2 * m + n]
                )
            )
    for copy in stages + group_copies + packs:
        copy.start(priority=1)
    for copy in stages:
        copy.wait()
    for m, at in enumerate((COUPLING_AT, RHS_AT)):
        head, tail = outer_rows(staged[m, 0], staged[m, 1])
        partner_ref[at : at + HALO] = jnp.where(odd == 1, head, tail)
        other_ref[at : at + HALO] = jnp.where(odd == 1, tail, head)

    def take(out_ref, group, first, row):
        for k in range(first, first + GROUP, TILE):
            lines = [groups[group, k + n].astype(jnp.float32)[row : row + 1] for n in range(TILE)]
            at = EDGE_AT + VECTORS * (group % 2) + k
            out_ref[at : at + TILE] = jnp.concatenate(lines, 0)

    for first in range(0, VECTORS, GROUP):
        for _ in range(4):
            group_copies.pop(0).wait()

        @pl.when(odd == 0)
        def _():
            for a in range(2):
                take(partner_ref, a, first, CHUNK - 1)
                take(other_ref, 2 + a, first, 0)

        @pl.when(odd == 1)
        def _():
            for a in range(2):
                take(partner_ref, a, first, 0)
                take(other_ref, 2 + a, first, CHUNK - 1)

    for copy in packs:
        copy.wait()


def restrict_kernel(rhs_ref, held, sums_ref, sums, lines, others):
    sums[...] = jnp.zeros_like(sums)
    squares = jnp.zeros((TILE, CELLS), jnp.float32)
    for a in range(2):
        for t in range(ROWS // TILE):
            tile = rhs_ref[a, tile_rows(t)]
            squares = squares + tile * tile
    sums[VECTORS : VECTORS + 8] = in_rows([fold(squares)])

    restrict(held, rhs_ref, sums, lines, others)
    send_sums(sums, sums_ref)


class Neighbour:
    def __init__(self, first_ref, second_ref):
        self.odd = lax.axis_index("sub") % 2 == 1
        self.first, self.second = first_ref, second_ref

    def __getitem__(self, index):
        return jnp.where(self.odd, self.first[index], self.second[index])


def neighbours_of(partner_ref, other_ref):
    return Neighbour(partner_ref, other_ref), Neighbour(other_ref, partner_ref)


def solve(count, margin_ref, factors_ref, make, field, out_ref, first_ref, solved, steps):
    waiting, done = list(steps), 0
    every = (SWEEPS - 1) * (STACKED // TILE) // len(waiting)
    assert every > 0
    rank = lax.axis_index("sub")
    lower = jnp.where(rank > 0, margin_ref[jnp.maximum(rank - 1, 0)], 0)
    upper = jnp.where(rank < count - 1, margin_ref[rank], 0)
    lower_f, upper_f = lower.astype(jnp.float32), upper.astype(jnp.float32)
    low_scale = 1.0 / (2.0 * jnp.maximum(lower_f, 1.0))
    high_scale = 1.0 / (2.0 * jnp.maximum(upper_f, 1.0))
    wide = lambda x: jnp.concatenate([x] * (CELLS // LANES), 1)
    own_tiles = ROWS // TILE
    strip_tiles = STRIP // TILE
    last = own_tiles + 1
    segments = (
        (0, 0, last + 1),
        (last + 1, 0, strip_tiles),
        (last + 1 + strip_tiles, last + 1 - strip_tiles, strip_tiles),
    )

    def place_of(e):
        return lax.broadcasted_iota(jnp.int32, (TILE, LANES), 0) + (TILE * e - HALO)

    def live_of(segment, e):
        place = place_of(e)
        if segment == 0:
            live = (place >= -lower) & (place < ROWS + upper)
        elif segment == 1:
            live = place < lower
        else:
            live = place >= ROWS - upper
        return wide(live.astype(jnp.float32))

    def weight_of(segment, e):
        place = place_of(e)
        place_f = place.astype(jnp.float32)
        rising = lambda base, scale: (place_f - base + 0.5) * scale
        falling = lambda base, scale: (base - place_f - 0.5) * scale
        if segment == 0:
            weight = jnp.where(place < lower, rising(-lower_f, low_scale), 1.0)
            weight = jnp.where(
                place >= ROWS - upper, falling(ROWS + upper_f, high_scale), weight
            )
        elif segment == 1:
            weight = jnp.where(place >= -lower, falling(lower_f, low_scale), 1.0)
        else:
            weight = jnp.where(place < ROWS + upper, rising(ROWS - upper_f, high_scale), 1.0)
        return wide(weight)

    for e in range(last + 1):
        for a in range(2):
            parts = make(a, e) if make else None
            value = field(a, e - 1)
            for n, (first, begin, size) in enumerate(segments):
                if not begin <= e < begin + size:
                    continue
                rows = tile_rows(first + e - begin)
                if make:
                    always = n == 0 and 0 < e < last
                    live = None if always else live_of(n, e)
                    for m, part in enumerate(parts):
                        factors_ref[3 * a + m, rows] = part if always else live * part
                first_ref[a, rows] = factors_ref[3 * a, rows] * value

    for sweep in range(1, SWEEPS):
        for n, (first, begin, size) in enumerate(segments):
            end = first + size - 1
            if sweep == 1:
                reads = [lambda t, a=a: first_ref[a, tile_rows(t)] for a in range(2)]
            else:
                bank = 2 * (sweep % 2)
                reads = [lambda t, a=a: solved[bank + a, tile_rows(t)] for a in range(2)]
            fields = [Rows(read, first, end) for read in reads]
            for t in range(first, end + 1):
                rows = tile_rows(t)
                if done % every == 0 and waiting:
                    waiting.pop(0)()
                done += 1
                for a in range(2):
                    value = (
                        ((1.0 - RELAX) * fields[a].at(t) + first_ref[a, rows])
                        + factors_ref[3 * a + 1, rows] * neighbours(fields[a], t, a)
                        - factors_ref[3 * a + 2, rows] * fields[1 - a].at(t)
                    )
                    e = t - first + begin
                    if sweep < SWEEPS - 1:
                        solved[2 * ((sweep + 1) % 2) + a, rows] = value
                    elif n == 0:
                        out_ref[a, tile_rows(e)] = weight_of(n, e) * value
                    else:
                        out_ref[a, tile_rows(e)] += weight_of(n, e) * value


def line_up(residuals):
    devices = residuals.shape[0]
    lane = lax.broadcasted_iota(jnp.int32, (1, LANES), 1)
    tiles = [jnp.zeros((1, LANES), jnp.float32) for _ in range(devices * VECTORS // LANES)]
    for t in range(devices):
        tile, offset = divmod(VECTORS * t, LANES)
        row = jnp.where(lane < VECTORS, residuals[devices - 1 - t : devices - t], 0.0)
        if offset:
            row = pltpu.roll(row, offset, 1)
        if offset + VECTORS <= LANES:
            tiles[tile] = tiles[tile] + row
        else:
            tiles[tile] = tiles[tile] + jnp.where(lane >= offset, row, 0.0)
            tiles[tile + 1] = tiles[tile + 1] + jnp.where(lane < offset, row, 0.0)
    return jnp.concatenate(tiles, 1)


def rounded(column):
    return column.astype(jnp.bfloat16).astype(jnp.float32)


def lift(inverse_ref, residual):
    return rounded(jnp.sum(inverse_ref[...] * residual, 1, keepdims=True))


def lift_packed(ref, residual):
    columns = residual.shape[1]
    at, total = EDGE_AT + INVERSE_AT, None
    for c in range(0, columns - 511, 512):
        term = jnp.sum(ref[at : at + VECTORS] * residual[:, c : c + 512], 1, keepdims=True)
        total = term if total is None else total + term
        at += VECTORS
    if columns % 512:
        half = VECTORS // 2
        last = residual[:, columns - 256 :]
        rows = ref[at : at + half]
        term = jnp.concatenate(
            [
                jnp.sum(rows[:, :256] * last, 1, keepdims=True),
                jnp.sum(rows[:, 256:] * last, 1, keepdims=True),
            ],
            0,
        )
        total = term if total is None else total + term
    return rounded(total)


def edge_values(ref, lifted):
    starts = [EDGE_AT + VECTORS * a for a in range(2)]
    return [jnp.sum(ref[at : at + VECTORS] * lifted, 0, keepdims=True) for at in starts]


def spread(lifted):
    shape = (VECTORS, CHUNK * VECTORS)
    owner = lax.broadcasted_iota(jnp.int32, shape, 1) // CHUNK
    row = lax.broadcasted_iota(jnp.int32, shape, 0)
    line = jnp.sum(jnp.where(owner == row, lifted, 0.0), 0, keepdims=True)
    shape = (CHUNK, CHUNK * VECTORS)
    place = lax.broadcasted_iota(jnp.int32, shape, 1) % CHUNK
    row = lax.broadcasted_iota(jnp.int32, shape, 0)
    return jnp.where(place == row, line, 0.0).astype(jnp.bfloat16)


class Coarse:
    def __init__(self, begin, inverse_ref, low, high, held, extended):
        self.inverse, self.sides, self.held, self.extended = inverse_ref, (low, high), held, extended
        self.lifted, self.edges = [None] * 2, [None] * 2
        self.steps = begin(self) + [self.lift_own, self.make_matrix]
        for a in range(2):
            for r in range(0, ROWS, CHUNK):
                self.steps.append(functools.partial(self.prolong, a, r))
        for n in range(2):
            self.steps.insert(len(self.steps) - 6, functools.partial(self.lift_side, n))
            self.steps.append(functools.partial(self.edge, n))

    def lift_own(self):
        self.own = lift(self.inverse, self.residual)

    def make_matrix(self):
        self.matrix = spread(self.own)

    def prolong(self, a, r):
        rows = self.held[:, a, r : r + CHUNK, :].reshape(CHUNK * VECTORS, CELLS)
        self.extended[a, HALO + r : HALO + r + CHUNK] = jnp.dot(
            self.matrix, rows, preferred_element_type=jnp.float32
        )

    def lift_side(self, n):
        self.lifted[n] = lift_packed(self.sides[n], self.residual)

    def edge(self, n):
        self.edges[n] = edge_values(self.sides[n], self.lifted[n])


def apply_operator(edges, smooth, extended, visc_ref, coup_ref, direction_ref):
    place = lax.broadcasted_iota(jnp.int32, (TILE, CELLS), 0)
    tiles = ROWS // TILE

    def read(t, a):
        if t < 0:
            return smooth(a, 0) + jnp.where(place == TILE - 1, edges[0][a], 0.0)
        if t == tiles:
            return smooth(a, t + 1) + jnp.where(place == 0, edges[1][a], 0.0)
        tile = smooth(a, t + 1) + extended[a, tile_rows(t + 1)]
        direction_ref[a, tile_rows(t)] = tile
        return tile

    fields = [Rows(lambda t, a=a: read(t, a), -1, tiles) for a in range(2)]
    for t in range(tiles):
        rows = tile_rows(t)
        viscosity = visc_ref[rows]
        for a in range(2):
            coupling = coup_ref[a, rows]
            diagonal = 10.0 * viscosity + jnp.abs(coupling) + 0.05
            image = (
                diagonal * fields[a].at(t)
                - viscosity * neighbours(fields[a], t, a)
                + coupling * fields[1 - a].at(t)
            )
            yield t, a, image


def lane_total(received, lane):
    place = lax.broadcasted_iota(jnp.int32, received.shape, 1)
    return jnp.sum(jnp.where(place == lane, received, 0.0), keepdims=True)


def first_turn_kernel(
    count, margin_ref, sums_ref, inverse_ref, partner_ref, other_ref, held, rhs_ref, visc_ref,
    coup_ref,
    direction_ref, image_ref, smooth_ref, residual_ref, factors_ref, partner_rows_ref, other_rows_ref,
    next_ref,
    extended, sums, first_ref, solved, lines, others,
):
    low, high = neighbours_of(partner_ref, other_ref)

    def begin(coarse):
        def scale():
            coarse.over_beta = 1.0 / jnp.sqrt(lane_total(sums_ref[...], VECTORS))

        def line():
            coarse.residual = line_up(sums_ref[...]) * coarse.over_beta
            residual_ref[...] = coarse.residual

        return [scale, line]

    coarse = Coarse(begin, inverse_ref, low, high, held, extended)

    def field(a, t):
        if 0 <= t < ROWS // TILE:
            return rhs_ref[a, tile_rows(t)]
        return component((low if t < 0 else high)[RHS_AT : RHS_AT + HALO], a)

    def make(a, e):
        if 0 < e <= ROWS // TILE:
            viscosity, coupling = visc_ref[tile_rows(e - 1)], coup_ref[a, tile_rows(e - 1)]
        else:
            side = low if e == 0 else high
            viscosity = side[:HALO]
            coupling = component(side[COUPLING_AT : COUPLING_AT + HALO], a)
        scale = RELAX / (10.0 * viscosity + jnp.abs(coupling) + 0.05)
        return scale, scale * viscosity, scale * coupling

    solve(
        count, margin_ref, factors_ref, make, field, smooth_ref, first_ref, solved, coarse.steps
    )
    smooth = lambda a, t: smooth_ref[a, tile_rows(t)] * coarse.over_beta
    images = apply_operator(
        coarse.edges, smooth, extended, visc_ref, coup_ref, direction_ref
    )
    odd = lax.axis_index("sub") % 2 == 1
    products, squares = [jnp.zeros((TILE, CELLS), jnp.float32)] * 2
    heads, tails = [None] * 2, [None] * 2
    for t, a, image in images:
        image_ref[a, tile_rows(t)] = image
        products = products + rhs_ref[a, tile_rows(t)] * image
        squares = squares + image * image
        if t == 0:
            heads[a] = image
        if t == ROWS // TILE - 1:
            tails[a] = image
    head, tail = outer_rows(heads, tails)
    partner_rows_ref[...] = jnp.where(odd, head, tail)
    other_rows_ref[...] = jnp.where(odd, tail, head)
    sums[...] = jnp.zeros_like(sums)
    sums[VECTORS : VECTORS + 8] = in_rows([fold(products), fold(squares)])

    restrict(held, image_ref, sums, lines, others)
    send_sums(sums, next_ref)


def first_column(first, second):
    beta = jnp.sqrt(lane_total(first, VECTORS))
    h_00 = lane_total(second, VECTORS) / beta
    h_10 = jnp.sqrt(lane_total(second, VECTORS + 1) - h_00 * h_00)
    return beta, h_00, h_10


def second_turn_kernel(
    count, margin_ref, sums_ref, second_ref, residual_ref, factors_ref, inverse_ref, partner_ref, other_ref,
    partner_rows_ref, other_rows_ref, held, smooth_ref, rhs_ref, image_ref, visc_ref, coup_ref,
    direction_ref, next_ref,
    image_smooth, extended, sums, first_ref, solved,
):
    low, high = neighbours_of(partner_ref, other_ref)

    def begin(coarse):
        def scale():
            beta, h_00, h_10 = first_column(sums_ref[...], second_ref[...])
            coarse.h_00, coarse.ratio, coarse.over = h_00, h_00 / beta, 1.0 / h_10

        def line():
            lined = line_up(second_ref[...])
            coarse.residual = (lined - coarse.h_00 * residual_ref[...]) * coarse.over

        return [scale, line]

    coarse = Coarse(begin, inverse_ref, low, high, held, extended)
    low_rows, high_rows = neighbours_of(partner_rows_ref, other_rows_ref)

    def field(a, t):
        if 0 <= t < ROWS // TILE:
            return image_ref[a, tile_rows(t)]
        rows = low_rows[...] if t < 0 else high_rows[...]
        return component(rows, a)

    solve(
        count, margin_ref, factors_ref, None, field, image_smooth, first_ref, solved, coarse.steps
    )

    def smooth(a, t):
        rows = tile_rows(t)
        return (image_smooth[a, rows] - coarse.ratio * smooth_ref[a, rows]) * coarse.over

    images = apply_operator(
        coarse.edges, smooth, extended, visc_ref, coup_ref, direction_ref
    )
    totals = [jnp.zeros((TILE, CELLS), jnp.float32)] * 3
    for t, a, image in images:
        others = (rhs_ref[a, tile_rows(t)], image_ref[a, tile_rows(t)], image)
        totals = [total + x * image for total, x in zip(totals, others)]
    sums[...] = jnp.zeros_like(sums)
    sums[:8] = in_rows([fold(total) for total in totals])
    send_sums(sums, next_ref)


def finish_kernel(
    first_ref, second_ref, third_ref, first_direction_ref, second_direction_ref,
    solution_ref, hessenberg_ref,
):
    third = third_ref[...]
    beta, h_00, h_10 = first_column(first_ref[...], second_ref[...])
    squares = lane_total(third, 2)
    h_01 = lane_total(third, 0) / beta
    h_11 = (lane_total(third, 1) - h_00 * h_01) / h_10
    h_21 = jnp.sqrt(squares - h_01 * h_01 - h_11 * h_11)
    l_00 = jnp.sqrt(h_00 * h_00 + h_10 * h_10)
    l_10 = (h_00 * h_01 + h_10 * h_11) / l_00
    f_0 = beta * h_00 / l_00
    c_1 = (beta * h_01 - l_10 * f_0) / (squares - l_10 * l_10)
    c_0 = (f_0 - l_10 * c_1) / l_00
    for a in range(2):
        solution_ref[a] = c_0 * first_direction_ref[a] + c_1 * second_direction_ref[a]
    shape = hessenberg_ref.shape
    row = lax.broadcasted_iota(jnp.int32, shape, 1)
    column = lax.broadcasted_iota(jnp.int32, shape, 0)
    entries = jnp.zeros(shape, jnp.float32)
    for i, j, value in ((0, 0, h_00), (0, 1, h_01), (1, 0, h_10), (1, 1, h_11), (2, 1, h_21)):
        entries = jnp.where((row == i) & (column == j), value, entries)
    hessenberg_ref[...] = entries


def call(kernel, name, in_specs, outs, flops, scratch=(), traffic=4_000_000):
    return pl.pallas_call(
        kernel,
        name=name,
        in_specs=in_specs,
        out_specs=[VMEM] * len(outs),
        out_shape=outs,
        scratch_shapes=scratch,
        compiler_params=pltpu.CompilerParams(vmem_limit_bytes=16 * 1024 * 1024),
        cost_estimate=pl.CostEstimate(flops=flops, bytes_accessed=traffic, transcendentals=0),
    )


def in_hbm(array):
    return pltpu.with_memory_space_constraint(array, pltpu.HBM)


def from_everyone(rows):
    order = [list(range(lax.axis_size("sub")))[::-1]]
    return lax.all_to_all(rows, "sub", 0, 0, tiled=True, axis_index_groups=order)


def swap(partner, other):
    count = lax.axis_size("sub")
    both = lambda lows: [pair for i in lows for pair in ((i, i + 1), (i + 1, i))]
    return (
        lax.ppermute(partner, "sub", both(range(0, count, 2))),
        lax.ppermute(other, "sub", both(range(1, count - 1, 2))),
    )


def on_device(rhs, viscosity, coupling, margin_rows, coarse_basis, coarse_inverse):
    count = lax.axis_size("sub")
    columns = coarse_inverse.shape[1]
    f32 = lambda *shape: jax.ShapeDtypeStruct(shape, jnp.float32)
    dma = lambda *shape: pltpu.SemaphoreType.DMA(shape)
    extended = pltpu.VMEM((2, EXT, CELLS), jnp.float32)
    stacked = pltpu.VMEM((2, STACKED, CELLS), jnp.float32)
    solved = pltpu.VMEM((4, STACKED, CELLS), jnp.float32)
    sums = pltpu.VMEM((SLOTS, LANES), jnp.float32)
    lines = pltpu.VMEM((2 * CHUNK, len(MATRIX_GROUPS) * CELLS), jnp.bfloat16)
    others = pltpu.VMEM((VECTORS, LANES), jnp.float32)
    row, whole, edge = f32(count, LANES), f32(2, ROWS, CELLS), f32(TILE, CELLS)
    packed, smoothed = f32(EDGE_AT + coarse_rows(columns), CELLS), f32(2, EXT, CELLS)
    arguments = (rhs, viscosity, coupling, coarse_inverse, coarse_basis)
    packs = call(
        pack_kernel, "pack", [HBM] * 5, [packed, packed], 5_000_000,
        [pltpu.VMEM((4, VECTORS, CHUNK, CELLS), jnp.bfloat16)]
        + [pltpu.VMEM((2, 2, 2, HALO, CELLS), jnp.float32), dma(4 * VECTORS // GROUP), dma(4)]
        + [dma(2 * pack_count(columns))],
    )(*map(in_hbm, arguments))
    held, partner, other = lax.optimization_barrier((coarse_basis, *packs))
    partner, other = swap(partner, other)
    (first,) = call(
        restrict_kernel, "restrict", [VMEM] * 2, [row], 10_000_000, [sums, lines, others]
    )(rhs, held)
    first = from_everyone(first)
    direction, image, smooth, residual, factors, partner_rows, other_rows, second = call(
        functools.partial(first_turn_kernel, count), "first_turn", [SMEM] + [VMEM] * 8,
        [whole, whole, smoothed, f32(1, columns), f32(6, STACKED, CELLS), edge, edge, row], 20_000_000,
        [extended, sums, stacked, solved, lines, others],
    )(margin_rows, first, coarse_inverse, partner, other, held, rhs, viscosity, coupling)
    partner_rows, other_rows = swap(partner_rows, other_rows)
    second = from_everyone(second)
    second_direction, third = call(
        functools.partial(second_turn_kernel, count), "second_turn", [SMEM] + [VMEM] * 15,
        [whole, row], 20_000_000, [extended, extended, sums, stacked, solved],
    )(
        margin_rows, first, second, residual, factors, coarse_inverse, partner, other, partner_rows, other_rows,
        held, smooth, rhs, image, viscosity, coupling,
    )
    third = from_everyone(third)
    result, transposed = call(finish_kernel, "finish", [VMEM] * 5, [whole, f32(2, 3)], 1_000_000)(
        first, second, third, direction, second_direction
    )
    return result, transposed.T


def solution(mesh):
    in_specs = (
        P(None, ("groups", "sub"), None),
        P(("groups", "sub"), None),
        P(None, ("groups", "sub"), None),
        P("groups"),
        P(None, None, ("groups", "sub"), None),
        P(("groups", "sub"), None),
    )
    out_specs = (P(None, ("groups", "sub"), None), P("groups", None))
    return jax.shard_map(
        on_device, mesh=mesh, in_specs=in_specs, out_specs=out_specs, check_vma=False
    )
```

```python
import functools

import jax
import jax.numpy as jnp
from jax import lax
from jax.experimental import pallas as pl
from jax.experimental.pallas import tpu as pltpu
from jax.sharding import PartitionSpec as P

ROWS = 64
CELLS = 512
VECTORS = 48
HALO = 8
EXT = ROWS + 2 * HALO
STRIP = 32
GROUP = 16
STACKED = EXT + 2 * STRIP
TILE = 8
CHUNK = 16
CHUNKS = 2 * ROWS // CHUNK
PIECE = 8
LANES = 128
SLOTS = 64
COUPLING_AT = HALO
RHS_AT = 2 * HALO
EDGE_AT = 3 * HALO
INVERSE_AT = 2 * VECTORS
SWEEPS = 4
RELAX = 0.7
ROW_FACTOR = (1.0, 4.0)
CELL_FACTOR = (4.0, 1.0)

VMEM = pl.BlockSpec(memory_space=pltpu.VMEM)
SMEM = pl.BlockSpec(memory_space=pltpu.SMEM)
HBM = pl.BlockSpec(memory_space=pltpu.HBM)


def coarse_rows(columns):
    return INVERSE_AT + VECTORS * (columns // 512) + (VECTORS // 2) * (columns % 512 // 256)


def cell_sum(field):
    lane = lax.broadcasted_iota(jnp.int32, (field.shape[0], LANES), 1)
    left, right = pltpu.roll(field, 1, 1), pltpu.roll(field, CELLS - 1, 1)
    inner = left[:, LANES:-LANES] + right[:, LANES:-LANES]
    first = jnp.where(lane == 0, 0.0, left[:, :LANES]) + right[:, :LANES]
    last = left[:, -LANES:] + jnp.where(lane == LANES - 1, 0.0, right[:, -LANES:])
    return jnp.concatenate([first, inner, last], 1)


class Rows:
    def __init__(self, read, first, last):
        self.read, self.first, self.last = read, first, last
        self.tiles, self.down, self.up = {}, {}, {}

    def at(self, t):
        if t not in self.tiles:
            self.tiles[t] = self.read(t)
        return self.tiles[t]

    def moved(self, held, t, by):
        if t not in held:
            held[t] = pltpu.roll(self.at(t), by, 0)
        return held[t]

    def around(self, t):
        row = lax.broadcasted_iota(jnp.int32, (TILE, CELLS), 0)
        below, above = self.moved(self.down, t, 1), self.moved(self.up, t, TILE - 1)
        if t > self.first:
            below = jnp.where(row == 0, self.moved(self.down, t - 1, 1), below)
        if t < self.last:
            above = jnp.where(row == TILE - 1, self.moved(self.up, t + 1, TILE - 1), above)
        return below + above


def neighbours(rows, t, component):
    around, cells = rows.around(t), cell_sum(rows.at(t))
    if component == 0:
        return around + CELL_FACTOR[0] * cells
    return ROW_FACTOR[1] * around + cells


def sublane_sum(tile):
    for by in (4, 2, 1):
        tile = tile + pltpu.roll(tile, by, 0)
    return tile


def in_rows(tiles):
    row = lax.broadcasted_iota(jnp.int32, (8, LANES), 0)
    total = jnp.zeros((8, LANES), jnp.float32)
    for n, tile in enumerate(tiles):
        total = jnp.where(row == n, sublane_sum(tile), total)
    return total


def restrict_piece(i, held, field, sums):
    totals = [None] * PIECE
    for a in range(2):
        for r in range(0, ROWS, CHUNK):
            for c in range(0, CELLS, LANES):
                rows, cells = slice(r, r + CHUNK), slice(c, c + LANES)
                tile = field[a, rows, cells]
                for n in range(PIECE):
                    term = held[PIECE * i + n, a, rows, cells].astype(jnp.float32) * tile
                    totals[n] = term if totals[n] is None else totals[n] + term
    tiles = [total[:8] + total[8:] for total in totals]
    sums[pl.ds(pl.multiple_of(PIECE * i, PIECE), PIECE), :] = in_rows(tiles)


VECTOR_GROUPS = tuple((0, r) for r in range(0, ROWS, CHUNK))
MATRIX_GROUPS = tuple((1, r) for r in range(0, ROWS, CHUNK))


def restrict(held, field, sums, lines):
    lines[2 * CHUNK :] = jnp.zeros((LANES - 2 * CHUNK, lines.shape[1]), jnp.bfloat16)
    blocks = []
    for g, (a, r) in enumerate(MATRIX_GROUPS):
        part, cells = field[a, r : r + CHUNK], slice(CELLS * g, CELLS * (g + 1))
        high = part.astype(jnp.bfloat16)
        lines[:CHUNK, cells] = high
        lines[CHUNK : 2 * CHUNK, cells] = (part - high.astype(jnp.float32)).astype(jnp.bfloat16)
        blocks.append(held[:, a, r : r + CHUNK, :].reshape(CHUNK * VECTORS, CELLS))
    products = lax.dot_general(
        jnp.concatenate(blocks, 1),
        lines[...],
        (((1,), (1,)), ((), ())),
        preferred_element_type=jnp.float32,
    )
    row = lax.broadcasted_iota(jnp.int32, (CHUNK, LANES), 0)
    equal = row == lax.broadcasted_iota(jnp.int32, (CHUNK, LANES), 1) % CHUNK
    for first in range(0, VECTORS, PIECE):
        totals = [
            jnp.where(equal, products[CHUNK * k : CHUNK * (k + 1)], 0.0)
            for k in range(first, first + PIECE)
        ]
        for a, r in VECTOR_GROUPS:
            for c in range(0, CELLS, LANES):
                rows, cells = slice(r, r + CHUNK), slice(c, c + LANES)
                tile = field[a, rows, cells]
                for n in range(PIECE):
                    term = held[first + n, a, rows, cells].astype(jnp.float32) * tile
                    totals[n] = totals[n] + term
        sums[first : first + PIECE] = in_rows([total[:8] + total[8:] for total in totals])


def fold(row):
    total = row[:, :LANES]
    for c in range(LANES, CELLS, LANES):
        total = total + row[:, c : c + LANES]
    return total


def tile_rows(t):
    return slice(TILE * t, TILE * (t + 1))


def send_sums(sums, out_ref):
    rest = sums[...]
    parts = []
    for _ in range(3):
        part = rest.astype(jnp.bfloat16)
        parts.append(part)
        rest = rest - part.astype(jnp.float32)
    row = lax.dot_general(
        jnp.ones((CHUNK, 3 * LANES), jnp.bfloat16),
        jnp.concatenate(parts, 1),
        (((1,), (1,)), ((), ())),
        preferred_element_type=jnp.float32,
    )
    wide = jnp.concatenate([row[:1], jnp.zeros((1, LANES - SLOTS), jnp.float32)], 1)
    out_ref[...] = jnp.broadcast_to(wide, out_ref.shape)


def pack_copies(out_ref, first_row, visc_ref, inverse_ref, sems, at_sem):
    rows = pl.ds(pl.multiple_of(first_row, HALO), HALO)
    moves = [(visc_ref.at[rows, :], 0, HALO, None)]
    columns = inverse_ref.shape[1]
    at = EDGE_AT + INVERSE_AT
    for c in range(0, columns - 511, 512):
        moves.append((inverse_ref.at[:, pl.ds(c, 512)], at, VECTORS, None))
        at += VECTORS
    if columns % 512:
        half = VECTORS // 2
        last = pl.ds(columns - 256, 256)
        moves.append((inverse_ref.at[pl.ds(0, half), last], at, half, 0))
        moves.append((inverse_ref.at[pl.ds(half, half), last], at, half, 256))
    copies = []
    for n, (source, at, size, lane) in enumerate(moves):
        place = pl.ds(at, size)
        target = out_ref.at[place, :] if lane is None else out_ref.at[place, pl.ds(lane, 256)]
        copies.append(pltpu.make_async_copy(source, target, sems.at[at_sem + n]))
    return copies


def pack_count(columns):
    return 1 + columns // 512 + 2 * (columns % 512 // 256)


def outer_rows(head, tail):
    half = lax.broadcasted_iota(jnp.int32, (TILE, CELLS), 0) < TILE // 2
    return (
        jnp.where(half, head[0], pltpu.roll(head[1], TILE // 2, 0)),
        jnp.where(half, pltpu.roll(tail[1], TILE // 2, 0), tail[0]),
    )


def component(rows, a):
    return pltpu.roll(rows, TILE // 2, 0) if a else rows


def pack_kernel(
    rhs_ref, visc_ref, coup_ref, inverse_ref, basis_ref,
    partner_ref, other_ref,
    groups, staged, group_sems, stage_sems, pack_sems,
):
    odd = lax.axis_index("sub") % 2
    sides = ((partner_ref, 1 - odd), (other_ref, odd))
    group_copies, packs = [], []
    for k in range(0, VECTORS, GROUP):
        for n, (out_ref, up) in enumerate(sides):
            rows = pl.ds(pl.multiple_of(up * (ROWS - CHUNK), CHUNK), CHUNK)
            for a in range(2):
                group_copies.append(
                    pltpu.make_async_copy(
                        basis_ref.at[pl.ds(k, GROUP), a, rows, :],
                        groups.at[2 * n + a, pl.ds(k, GROUP)],
                        group_sems.at[len(group_copies)],
                    )
                )
    for n, (out_ref, up) in enumerate(sides):
        packs += pack_copies(
            out_ref, up * (ROWS - HALO), visc_ref, inverse_ref, pack_sems,
            n * pack_count(inverse_ref.shape[1]),
        )
    stages = []
    for m, ref in enumerate((coup_ref, rhs_ref)):
        for n, first_row in enumerate((0, ROWS - HALO)):
            stages.append(
                pltpu.make_async_copy(
                    ref.at[:, pl.ds(first_row, HALO), :], staged.at[m, n], stage_sems.at[2 * m + n]
                )
            )
    for copy in stages + group_copies + packs:
        copy.start(priority=1)
    for copy in stages:
        copy.wait()
    for m, at in enumerate((COUPLING_AT, RHS_AT)):
        head, tail = outer_rows(staged[m, 0], staged[m, 1])
        partner_ref[at : at + HALO] = jnp.where(odd == 1, head, tail)
        other_ref[at : at + HALO] = jnp.where(odd == 1, tail, head)

    def take(out_ref, group, first, row):
        for k in range(first, first + GROUP, TILE):
            lines = [groups[group, k + n].astype(jnp.float32)[row : row + 1] for n in range(TILE)]
            at = EDGE_AT + VECTORS * (group % 2) + k
            out_ref[at : at + TILE] = jnp.concatenate(lines, 0)

    for first in range(0, VECTORS, GROUP):
        for _ in range(4):
            group_copies.pop(0).wait()

        @pl.when(odd == 0)
        def _():
            for a in range(2):
                take(partner_ref, a, first, CHUNK - 1)
                take(other_ref, 2 + a, first, 0)

        @pl.when(odd == 1)
        def _():
            for a in range(2):
                take(partner_ref, a, first, 0)
                take(other_ref, 2 + a, first, CHUNK - 1)

    for copy in packs:
        copy.wait()


def restrict_kernel(rhs_ref, held, sums_ref, sums):
    sums[...] = jnp.zeros_like(sums)
    squares = jnp.zeros((TILE, CELLS), jnp.float32)
    for a in range(2):
        for t in range(ROWS // TILE):
            tile = rhs_ref[a, tile_rows(t)]
            squares = squares + tile * tile
    sums[VECTORS : VECTORS + 8] = in_rows([fold(squares)])

    def body(i, carry):
        restrict_piece(i, held, rhs_ref, sums)
        return carry

    lax.fori_loop(0, VECTORS // PIECE, body, 0)
    send_sums(sums, sums_ref)


class Neighbour:
    def __init__(self, first_ref, second_ref):
        self.odd = lax.axis_index("sub") % 2 == 1
        self.first, self.second = first_ref, second_ref

    def __getitem__(self, index):
        return jnp.where(self.odd, self.first[index], self.second[index])


def neighbours_of(partner_ref, other_ref):
    return Neighbour(partner_ref, other_ref), Neighbour(other_ref, partner_ref)


def solve(count, margin_ref, factors_ref, make, field, out_ref, first_ref, solved, steps):
    waiting, done = list(steps), 0
    every = (SWEEPS - 1) * (STACKED // TILE) // len(waiting)
    assert every > 0
    rank = lax.axis_index("sub")
    lower = jnp.where(rank > 0, margin_ref[jnp.maximum(rank - 1, 0)], 0)
    upper = jnp.where(rank < count - 1, margin_ref[rank], 0)
    lower_f, upper_f = lower.astype(jnp.float32), upper.astype(jnp.float32)
    low_scale = 1.0 / (2.0 * jnp.maximum(lower_f, 1.0))
    high_scale = 1.0 / (2.0 * jnp.maximum(upper_f, 1.0))
    wide = lambda x: jnp.concatenate([x] * (CELLS // LANES), 1)
    own_tiles = ROWS // TILE
    strip_tiles = STRIP // TILE
    last = own_tiles + 1
    segments = (
        (0, 0, last + 1),
        (last + 1, 0, strip_tiles),
        (last + 1 + strip_tiles, last + 1 - strip_tiles, strip_tiles),
    )

    def place_of(e):
        return lax.broadcasted_iota(jnp.int32, (TILE, LANES), 0) + (TILE * e - HALO)

    def live_of(segment, e):
        place = place_of(e)
        if segment == 0:
            live = (place >= -lower) & (place < ROWS + upper)
        elif segment == 1:
            live = place < lower
        else:
            live = place >= ROWS - upper
        return wide(live.astype(jnp.float32))

    def weight_of(segment, e):
        place = place_of(e)
        place_f = place.astype(jnp.float32)
        rising = lambda base, scale: (place_f - base + 0.5) * scale
        falling = lambda base, scale: (base - place_f - 0.5) * scale
        if segment == 0:
            weight = jnp.where(place < lower, rising(-lower_f, low_scale), 1.0)
            weight = jnp.where(
                place >= ROWS - upper, falling(ROWS + upper_f, high_scale), weight
            )
        elif segment == 1:
            weight = jnp.where(place >= -lower, falling(lower_f, low_scale), 1.0)
        else:
            weight = jnp.where(place < ROWS + upper, rising(ROWS - upper_f, high_scale), 1.0)
        return wide(weight)

    for e in range(last + 1):
        for a in range(2):
            parts = make(a, e) if make else None
            value = field(a, e - 1)
            for n, (first, begin, size) in enumerate(segments):
                if not begin <= e < begin + size:
                    continue
                rows = tile_rows(first + e - begin)
                if make:
                    always = n == 0 and 0 < e < last
                    live = None if always else live_of(n, e)
                    for m, part in enumerate(parts):
                        factors_ref[3 * a + m, rows] = part if always else live * part
                first_ref[a, rows] = factors_ref[3 * a, rows] * value

    for sweep in range(1, SWEEPS):
        for n, (first, begin, size) in enumerate(segments):
            end = first + size - 1
            if sweep == 1:
                reads = [lambda t, a=a: first_ref[a, tile_rows(t)] for a in range(2)]
            else:
                bank = 2 * (sweep % 2)
                reads = [lambda t, a=a: solved[bank + a, tile_rows(t)] for a in range(2)]
            fields = [Rows(read, first, end) for read in reads]
            for t in range(first, end + 1):
                rows = tile_rows(t)
                if done % every == 0 and waiting:
                    waiting.pop(0)()
                done += 1
                for a in range(2):
                    value = (
                        ((1.0 - RELAX) * fields[a].at(t) + first_ref[a, rows])
                        + factors_ref[3 * a + 1, rows] * neighbours(fields[a], t, a)
                        - factors_ref[3 * a + 2, rows] * fields[1 - a].at(t)
                    )
                    e = t - first + begin
                    if sweep < SWEEPS - 1:
                        solved[2 * ((sweep + 1) % 2) + a, rows] = value
                    elif n == 0:
                        out_ref[a, tile_rows(e)] = weight_of(n, e) * value
                    else:
                        out_ref[a, tile_rows(e)] += weight_of(n, e) * value


def line_up(residuals):
    devices = residuals.shape[0]
    lane = lax.broadcasted_iota(jnp.int32, (1, LANES), 1)
    tiles = [jnp.zeros((1, LANES), jnp.float32) for _ in range(devices * VECTORS // LANES)]
    for t in range(devices):
        tile, offset = divmod(VECTORS * t, LANES)
        row = jnp.where(lane < VECTORS, residuals[devices - 1 - t : devices - t], 0.0)
        if offset:
            row = pltpu.roll(row, offset, 1)
        if offset + VECTORS <= LANES:
            tiles[tile] = tiles[tile] + row
        else:
            tiles[tile] = tiles[tile] + jnp.where(lane >= offset, row, 0.0)
            tiles[tile + 1] = tiles[tile + 1] + jnp.where(lane < offset, row, 0.0)
    return jnp.concatenate(tiles, 1)


def rounded(column):
    return column.astype(jnp.bfloat16).astype(jnp.float32)


def lift(inverse_ref, residual):
    return jnp.sum(inverse_ref[...] * residual, 1, keepdims=True)


def lift_packed(ref, residual):
    columns = residual.shape[1]
    at, total = EDGE_AT + INVERSE_AT, None
    for c in range(0, columns - 511, 512):
        term = jnp.sum(ref[at : at + VECTORS] * residual[:, c : c + 512], 1, keepdims=True)
        total = term if total is None else total + term
        at += VECTORS
    if columns % 512:
        half = VECTORS // 2
        last = residual[:, columns - 256 :]
        rows = ref[at : at + half]
        term = jnp.concatenate(
            [
                jnp.sum(rows[:, :256] * last, 1, keepdims=True),
                jnp.sum(rows[:, 256:] * last, 1, keepdims=True),
            ],
            0,
        )
        total = term if total is None else total + term
    return total


def edge_values(ref, lifted):
    starts = [EDGE_AT + VECTORS * a for a in range(2)]
    return [jnp.sum(ref[at : at + VECTORS] * lifted, 0, keepdims=True) for at in starts]


def spread(lifted):
    shape = (VECTORS, CHUNK * VECTORS)
    owner = lax.broadcasted_iota(jnp.int32, shape, 1) // CHUNK
    row = lax.broadcasted_iota(jnp.int32, shape, 0)
    line = jnp.sum(jnp.where(owner == row, lifted, 0.0), 0, keepdims=True)
    shape = (CHUNK, CHUNK * VECTORS)
    place = lax.broadcasted_iota(jnp.int32, shape, 1) % CHUNK
    row = lax.broadcasted_iota(jnp.int32, shape, 0)
    return jnp.where(place == row, line, 0.0).astype(jnp.bfloat16)


class Coarse:
    def __init__(self, begin, inverse_ref, low, high, held, extended):
        self.inverse, self.sides, self.held, self.extended = inverse_ref, (low, high), held, extended
        self.lifted, self.edges = [None] * 2, [None] * 2
        self.steps = begin(self) + [self.lift_own, self.make_matrix]
        for a in range(2):
            for r in range(0, ROWS, CHUNK):
                self.steps.append(functools.partial(self.prolong, a, r))
        for n in range(2):
            self.steps.insert(len(self.steps) - 6, functools.partial(self.lift_side, n))
            self.steps.append(functools.partial(self.edge, n))

    def lift_own(self):
        self.own = rounded(self.scaled(lift(self.inverse, self.residual), 2))

    def make_matrix(self):
        self.matrix = spread(self.own)

    def prolong(self, a, r):
        rows = self.held[:, a, r : r + CHUNK, :].reshape(CHUNK * VECTORS, CELLS)
        self.extended[a, HALO + r : HALO + r + CHUNK] = jnp.dot(
            self.matrix, rows, preferred_element_type=jnp.float32
        )

    def lift_side(self, n):
        self.lifted[n] = rounded(self.scaled(lift_packed(self.sides[n], self.residual), n))

    def edge(self, n):
        self.edges[n] = edge_values(self.sides[n], self.lifted[n])


def apply_operator(edges, smooth, extended, visc_ref, coup_ref, direction_ref):
    place = lax.broadcasted_iota(jnp.int32, (TILE, CELLS), 0)
    tiles = ROWS // TILE

    def read(t, a):
        if t < 0:
            return smooth(a, 0) + jnp.where(place == TILE - 1, edges[0][a], 0.0)
        if t == tiles:
            return smooth(a, t + 1) + jnp.where(place == 0, edges[1][a], 0.0)
        tile = smooth(a, t + 1) + extended[a, tile_rows(t + 1)]
        direction_ref[a, tile_rows(t)] = tile
        return tile

    fields = [Rows(lambda t, a=a: read(t, a), -1, tiles) for a in range(2)]
    for t in range(tiles):
        rows = tile_rows(t)
        viscosity = visc_ref[rows]
        for a in range(2):
            coupling = coup_ref[a, rows]
            diagonal = 10.0 * viscosity + jnp.abs(coupling) + 0.05
            image = (
                diagonal * fields[a].at(t)
                - viscosity * neighbours(fields[a], t, a)
                + coupling * fields[1 - a].at(t)
            )
            yield t, a, image


def lane_total(received, lane):
    place = lax.broadcasted_iota(jnp.int32, received.shape, 1)
    return jnp.sum(jnp.where(place == lane, received, 0.0), keepdims=True)


def first_turn_kernel(
    count, margin_ref, sums_ref, inverse_ref, partner_ref, other_ref, held, rhs_ref, visc_ref,
    coup_ref,
    direction_ref, image_ref, smooth_ref, columns_ref, factors_ref, partner_rows_ref, other_rows_ref,
    next_ref,
    extended, sums, first_ref, solved, lines,
):
    low, high = neighbours_of(partner_ref, other_ref)

    def begin(coarse):
        def scale():
            coarse.over_beta = 1.0 / jnp.sqrt(lane_total(sums_ref[...], VECTORS))

        def line():
            coarse.residual = line_up(sums_ref[...])

        def scaled(column, n):
            column = column * coarse.over_beta
            columns_ref[n] = jnp.broadcast_to(column, (VECTORS, LANES))
            return column

        coarse.scaled = scaled
        return [line, scale]

    coarse = Coarse(begin, inverse_ref, low, high, held, extended)

    def field(a, t):
        if 0 <= t < ROWS // TILE:
            return rhs_ref[a, tile_rows(t)]
        return component((low if t < 0 else high)[RHS_AT : RHS_AT + HALO], a)

    def make(a, e):
        if 0 < e <= ROWS // TILE:
            viscosity, coupling = visc_ref[tile_rows(e - 1)], coup_ref[a, tile_rows(e - 1)]
        else:
            side = low if e == 0 else high
            viscosity = side[:HALO]
            coupling = component(side[COUPLING_AT : COUPLING_AT + HALO], a)
        scale = RELAX / (10.0 * viscosity + jnp.abs(coupling) + 0.05)
        return scale, scale * viscosity, scale * coupling

    solve(
        count, margin_ref, factors_ref, make, field, smooth_ref, first_ref, solved, coarse.steps
    )
    smooth = lambda a, t: smooth_ref[a, tile_rows(t)] * coarse.over_beta
    images = apply_operator(
        coarse.edges, smooth, extended, visc_ref, coup_ref, direction_ref
    )
    odd = lax.axis_index("sub") % 2 == 1
    products, squares = [jnp.zeros((TILE, CELLS), jnp.float32)] * 2
    heads, tails = [None] * 2, [None] * 2
    for t, a, image in images:
        image_ref[a, tile_rows(t)] = image
        products = products + rhs_ref[a, tile_rows(t)] * image
        squares = squares + image * image
        if t == 0:
            heads[a] = image
        if t == ROWS // TILE - 1:
            tails[a] = image
    head, tail = outer_rows(heads, tails)
    partner_rows_ref[...] = jnp.where(odd, head, tail)
    other_rows_ref[...] = jnp.where(odd, tail, head)
    sums[...] = jnp.zeros_like(sums)
    sums[VECTORS : VECTORS + 8] = in_rows([fold(products), fold(squares)])

    restrict(held, image_ref, sums, lines)
    send_sums(sums, next_ref)


def first_column(first, second):
    beta = jnp.sqrt(lane_total(first, VECTORS))
    h_00 = lane_total(second, VECTORS) / beta
    h_10 = jnp.sqrt(lane_total(second, VECTORS + 1) - h_00 * h_00)
    return beta, h_00, h_10


def second_turn_kernel(
    count, margin_ref, sums_ref, second_ref, columns_ref, factors_ref, inverse_ref, partner_ref, other_ref,
    partner_rows_ref, other_rows_ref, held, smooth_ref, rhs_ref, image_ref, visc_ref, coup_ref,
    direction_ref, next_ref,
    image_smooth, extended, sums, first_ref, solved,
):
    low, high = neighbours_of(partner_ref, other_ref)

    def begin(coarse):
        def scale():
            beta, h_00, h_10 = first_column(sums_ref[...], second_ref[...])
            coarse.h_00, coarse.ratio, coarse.over = h_00, h_00 / beta, 1.0 / h_10

        def line():
            coarse.residual = line_up(second_ref[...])

        coarse.scaled = lambda column, n: (
            (column - coarse.h_00 * columns_ref[n][:, :1]) * coarse.over
        )
        return [line, scale]

    coarse = Coarse(begin, inverse_ref, low, high, held, extended)
    low_rows, high_rows = neighbours_of(partner_rows_ref, other_rows_ref)

    def field(a, t):
        if 0 <= t < ROWS // TILE:
            return image_ref[a, tile_rows(t)]
        rows = low_rows[...] if t < 0 else high_rows[...]
        return component(rows, a)

    solve(
        count, margin_ref, factors_ref, None, field, image_smooth, first_ref, solved, coarse.steps
    )

    def smooth(a, t):
        rows = tile_rows(t)
        return (image_smooth[a, rows] - coarse.ratio * smooth_ref[a, rows]) * coarse.over

    images = apply_operator(
        coarse.edges, smooth, extended, visc_ref, coup_ref, direction_ref
    )
    totals = [jnp.zeros((TILE, CELLS), jnp.float32)] * 3
    for t, a, image in images:
        others = (rhs_ref[a, tile_rows(t)], image_ref[a, tile_rows(t)], image)
        totals = [total + x * image for total, x in zip(totals, others)]
    sums[...] = jnp.zeros_like(sums)
    sums[:8] = in_rows([fold(total) for total in totals])
    send_sums(sums, next_ref)


def finish_kernel(
    first_ref, second_ref, third_ref, first_direction_ref, second_direction_ref,
    solution_ref, hessenberg_ref,
):
    third = third_ref[...]
    beta, h_00, h_10 = first_column(first_ref[...], second_ref[...])
    squares = lane_total(third, 2)
    h_01 = lane_total(third, 0) / beta
    h_11 = (lane_total(third, 1) - h_00 * h_01) / h_10
    h_21 = jnp.sqrt(squares - h_01 * h_01 - h_11 * h_11)
    l_00 = jnp.sqrt(h_00 * h_00 + h_10 * h_10)
    l_10 = (h_00 * h_01 + h_10 * h_11) / l_00
    f_0 = beta * h_00 / l_00
    c_1 = (beta * h_01 - l_10 * f_0) / (squares - l_10 * l_10)
    c_0 = (f_0 - l_10 * c_1) / l_00
    for a in range(2):
        solution_ref[a] = c_0 * first_direction_ref[a] + c_1 * second_direction_ref[a]
    shape = hessenberg_ref.shape
    row = lax.broadcasted_iota(jnp.int32, shape, 1)
    column = lax.broadcasted_iota(jnp.int32, shape, 0)
    entries = jnp.zeros(shape, jnp.float32)
    for i, j, value in ((0, 0, h_00), (0, 1, h_01), (1, 0, h_10), (1, 1, h_11), (2, 1, h_21)):
        entries = jnp.where((row == i) & (column == j), value, entries)
    hessenberg_ref[...] = entries


def call(kernel, name, in_specs, outs, flops, scratch=(), traffic=4_000_000):
    return pl.pallas_call(
        kernel,
        name=name,
        in_specs=in_specs,
        out_specs=[VMEM] * len(outs),
        out_shape=outs,
        scratch_shapes=scratch,
        compiler_params=pltpu.CompilerParams(vmem_limit_bytes=16 * 1024 * 1024),
        cost_estimate=pl.CostEstimate(flops=flops, bytes_accessed=traffic, transcendentals=0),
    )


def in_hbm(array):
    return pltpu.with_memory_space_constraint(array, pltpu.HBM)


def from_everyone(rows):
    order = [list(range(lax.axis_size("sub")))[::-1]]
    return lax.all_to_all(rows, "sub", 0, 0, tiled=True, axis_index_groups=order)


def swap(partner, other):
    count = lax.axis_size("sub")
    both = lambda lows: [pair for i in lows for pair in ((i, i + 1), (i + 1, i))]
    return (
        lax.ppermute(partner, "sub", both(range(0, count, 2))),
        lax.ppermute(other, "sub", both(range(1, count - 1, 2))),
    )


def on_device(rhs, viscosity, coupling, margin_rows, coarse_basis, coarse_inverse):
    count = lax.axis_size("sub")
    columns = coarse_inverse.shape[1]
    f32 = lambda *shape: jax.ShapeDtypeStruct(shape, jnp.float32)
    dma = lambda *shape: pltpu.SemaphoreType.DMA(shape)
    extended = pltpu.VMEM((2, EXT, CELLS), jnp.float32)
    stacked = pltpu.VMEM((2, STACKED, CELLS), jnp.float32)
    solved = pltpu.VMEM((4, STACKED, CELLS), jnp.float32)
    sums = pltpu.VMEM((SLOTS, LANES), jnp.float32)
    lines = pltpu.VMEM((LANES, len(MATRIX_GROUPS) * CELLS), jnp.bfloat16)
    row, whole, edge = f32(count, LANES), f32(2, ROWS, CELLS), f32(TILE, CELLS)
    packed, smoothed = f32(EDGE_AT + coarse_rows(columns), CELLS), f32(2, EXT, CELLS)
    arguments = (rhs, viscosity, coupling, coarse_inverse, coarse_basis)
    packs = call(
        pack_kernel, "pack", [HBM] * 5, [packed, packed], 5_000_000,
        [pltpu.VMEM((4, VECTORS, CHUNK, CELLS), jnp.bfloat16)]
        + [pltpu.VMEM((2, 2, 2, HALO, CELLS), jnp.float32), dma(4 * VECTORS // GROUP), dma(4)]
        + [dma(2 * pack_count(columns))],
    )(*map(in_hbm, arguments))
    held, partner, other = lax.optimization_barrier((coarse_basis, *packs))
    partner, other = swap(partner, other)
    (first,) = call(
        restrict_kernel, "restrict", [VMEM] * 2, [row], 10_000_000, [sums]
    )(rhs, held)
    first = from_everyone(first)
    direction, image, smooth, lifts, factors, partner_rows, other_rows, second = call(
        functools.partial(first_turn_kernel, count), "first_turn", [SMEM] + [VMEM] * 8,
        [whole, whole, smoothed, f32(3, VECTORS, LANES), f32(6, STACKED, CELLS), edge, edge, row], 20_000_000,
        [extended, sums, stacked, solved, lines],
    )(margin_rows, first, coarse_inverse, partner, other, held, rhs, viscosity, coupling)
    partner_rows, other_rows = swap(partner_rows, other_rows)
    second = from_everyone(second)
    second_direction, third = call(
        functools.partial(second_turn_kernel, count), "second_turn", [SMEM] + [VMEM] * 15,
        [whole, row], 20_000_000, [extended, extended, sums, stacked, solved],
    )(
        margin_rows, first, second, lifts, factors, coarse_inverse, partner, other, partner_rows, other_rows,
        held, smooth, rhs, image, viscosity, coupling,
    )
    third = from_everyone(third)
    result, transposed = call(finish_kernel, "finish", [VMEM] * 5, [whole, f32(2, 3)], 1_000_000)(
        first, second, third, direction, second_direction
    )
    return result, transposed.T


def solution(mesh):
    in_specs = (
        P(None, ("groups", "sub"), None),
        P(("groups", "sub"), None),
        P(None, ("groups", "sub"), None),
        P("groups"),
        P(None, None, ("groups", "sub"), None),
        P(("groups", "sub"), None),
    )
    out_specs = (P(None, ("groups", "sub"), None), P("groups", None))
    return jax.shard_map(
        on_device, mesh=mesh, in_specs=in_specs, out_specs=out_specs, check_vma=False
    )
```

```python
import functools

import jax
import jax.numpy as jnp
from jax import lax
from jax.experimental import pallas as pl
from jax.experimental.pallas import tpu as pltpu
from jax.sharding import PartitionSpec as P

ROWS = 64
CELLS = 512
VECTORS = 48
HALO = 8
EXT = ROWS + 2 * HALO
STRIP = 32
GROUP = 16
STACKED = EXT + 2 * STRIP
TILE = 8
CHUNK = 16
CHUNKS = 2 * ROWS // CHUNK
PIECE = 8
LANES = 128
SLOTS = 64
COUPLING_AT = HALO
RHS_AT = 2 * HALO
EDGE_AT = 3 * HALO
INVERSE_AT = 2 * VECTORS
SWEEPS = 4
RELAX = 0.7
ROW_FACTOR = (1.0, 4.0)
CELL_FACTOR = (4.0, 1.0)

VMEM = pl.BlockSpec(memory_space=pltpu.VMEM)
SMEM = pl.BlockSpec(memory_space=pltpu.SMEM)
HBM = pl.BlockSpec(memory_space=pltpu.HBM)


def coarse_rows(columns):
    return INVERSE_AT + VECTORS * (columns // 512) + (VECTORS // 2) * (columns % 512 // 256)


def cell_sum(field):
    lane = lax.broadcasted_iota(jnp.int32, (field.shape[0], LANES), 1)
    left, right = pltpu.roll(field, 1, 1), pltpu.roll(field, CELLS - 1, 1)
    inner = left[:, LANES:-LANES] + right[:, LANES:-LANES]
    first = jnp.where(lane == 0, 0.0, left[:, :LANES]) + right[:, :LANES]
    last = left[:, -LANES:] + jnp.where(lane == LANES - 1, 0.0, right[:, -LANES:])
    return jnp.concatenate([first, inner, last], 1)


class Rows:
    def __init__(self, read, first, last):
        self.read, self.first, self.last = read, first, last
        self.tiles, self.down, self.up = {}, {}, {}

    def at(self, t):
        if t not in self.tiles:
            self.tiles[t] = self.read(t)
        return self.tiles[t]

    def moved(self, held, t, by):
        if t not in held:
            held[t] = pltpu.roll(self.at(t), by, 0)
        return held[t]

    def around(self, t):
        row = lax.broadcasted_iota(jnp.int32, (TILE, CELLS), 0)
        below, above = self.moved(self.down, t, 1), self.moved(self.up, t, TILE - 1)
        if t > self.first:
            below = jnp.where(row == 0, self.moved(self.down, t - 1, 1), below)
        if t < self.last:
            above = jnp.where(row == TILE - 1, self.moved(self.up, t + 1, TILE - 1), above)
        return below + above


def neighbours(rows, t, component):
    around, cells = rows.around(t), cell_sum(rows.at(t))
    if component == 0:
        return around + CELL_FACTOR[0] * cells
    return ROW_FACTOR[1] * around + cells


def sublane_sum(tile):
    for by in (4, 2, 1):
        tile = tile + pltpu.roll(tile, by, 0)
    return tile


def in_rows(tiles):
    row = lax.broadcasted_iota(jnp.int32, (8, LANES), 0)
    total = jnp.zeros((8, LANES), jnp.float32)
    for n, tile in enumerate(tiles):
        total = jnp.where(row == n, sublane_sum(tile), total)
    return total


def restrict_piece(i, held, field, sums):
    totals = [None] * PIECE
    for a in range(2):
        for r in range(0, ROWS, CHUNK):
            for c in range(0, CELLS, LANES):
                rows, cells = slice(r, r + CHUNK), slice(c, c + LANES)
                tile = field[a, rows, cells]
                for n in range(PIECE):
                    term = held[PIECE * i + n, a, rows, cells].astype(jnp.float32) * tile
                    totals[n] = term if totals[n] is None else totals[n] + term
    tiles = [total[:8] + total[8:] for total in totals]
    sums[pl.ds(pl.multiple_of(PIECE * i, PIECE), PIECE), :] = in_rows(tiles)


VECTOR_GROUPS = tuple((0, r) for r in range(0, ROWS, CHUNK))
MATRIX_GROUPS = tuple((1, r) for r in range(0, ROWS, CHUNK))


def restrict(held, field, sums, lines):
    lines[2 * CHUNK :] = jnp.zeros((LANES - 2 * CHUNK, lines.shape[1]), jnp.bfloat16)
    blocks = []
    for g, (a, r) in enumerate(MATRIX_GROUPS):
        part, cells = field[a, r : r + CHUNK], slice(CELLS * g, CELLS * (g + 1))
        high = part.astype(jnp.bfloat16)
        lines[:CHUNK, cells] = high
        lines[CHUNK : 2 * CHUNK, cells] = (part - high.astype(jnp.float32)).astype(jnp.bfloat16)
        blocks.append(held[:, a, r : r + CHUNK, :].reshape(CHUNK * VECTORS, CELLS))
    products = lax.dot_general(
        jnp.concatenate(blocks, 1),
        lines[...],
        (((1,), (1,)), ((), ())),
        preferred_element_type=jnp.float32,
    )
    row = lax.broadcasted_iota(jnp.int32, (CHUNK, LANES), 0)
    equal = row == lax.broadcasted_iota(jnp.int32, (CHUNK, LANES), 1) % CHUNK
    for first in range(0, VECTORS, PIECE):
        totals = [
            jnp.where(equal, products[CHUNK * k : CHUNK * (k + 1)], 0.0)
            for k in range(first, first + PIECE)
        ]
        for a, r in VECTOR_GROUPS:
            for c in range(0, CELLS, LANES):
                rows, cells = slice(r, r + CHUNK), slice(c, c + LANES)
                tile = field[a, rows, cells]
                for n in range(PIECE):
                    term = held[first + n, a, rows, cells].astype(jnp.float32) * tile
                    totals[n] = totals[n] + term
        sums[first : first + PIECE] = in_rows([total[:8] + total[8:] for total in totals])


def fold(row):
    total = row[:, :LANES]
    for c in range(LANES, CELLS, LANES):
        total = total + row[:, c : c + LANES]
    return total


def tile_rows(t):
    return slice(TILE * t, TILE * (t + 1))


def send_sums(sums, out_ref):
    rest = sums[...]
    parts = []
    for _ in range(3):
        part = rest.astype(jnp.bfloat16)
        parts.append(part)
        rest = rest - part.astype(jnp.float32)
    row = lax.dot_general(
        jnp.ones((CHUNK, 3 * LANES), jnp.bfloat16),
        jnp.concatenate(parts, 1),
        (((1,), (1,)), ((), ())),
        preferred_element_type=jnp.float32,
    )
    wide = jnp.concatenate([row[:1], jnp.zeros((1, LANES - SLOTS), jnp.float32)], 1)
    out_ref[...] = jnp.broadcast_to(wide, out_ref.shape)


def pack_copies(out_ref, first_row, visc_ref, inverse_ref, sems, at_sem):
    rows = pl.ds(pl.multiple_of(first_row, HALO), HALO)
    moves = [(visc_ref.at[rows, :], 0, HALO, None)]
    columns = inverse_ref.shape[1]
    at = EDGE_AT + INVERSE_AT
    for c in range(0, columns - 511, 512):
        moves.append((inverse_ref.at[:, pl.ds(c, 512)], at, VECTORS, None))
        at += VECTORS
    if columns % 512:
        half = VECTORS // 2
        last = pl.ds(columns - 256, 256)
        moves.append((inverse_ref.at[pl.ds(0, half), last], at, half, 0))
        moves.append((inverse_ref.at[pl.ds(half, half), last], at, half, 256))
    copies = []
    for n, (source, at, size, lane) in enumerate(moves):
        place = pl.ds(at, size)
        target = out_ref.at[place, :] if lane is None else out_ref.at[place, pl.ds(lane, 256)]
        copies.append(pltpu.make_async_copy(source, target, sems.at[at_sem + n]))
    return copies


def pack_count(columns):
    return 1 + columns // 512 + 2 * (columns % 512 // 256)


def outer_rows(head, tail):
    half = lax.broadcasted_iota(jnp.int32, (TILE, CELLS), 0) < TILE // 2
    return (
        jnp.where(half, head[0], pltpu.roll(head[1], TILE // 2, 0)),
        jnp.where(half, pltpu.roll(tail[1], TILE // 2, 0), tail[0]),
    )


def component(rows, a):
    return pltpu.roll(rows, TILE // 2, 0) if a else rows


def pack_kernel(
    rhs_ref, visc_ref, coup_ref, inverse_ref, basis_ref,
    partner_ref, other_ref,
    groups, staged, group_sems, stage_sems, pack_sems,
):
    odd = lax.axis_index("sub") % 2
    sides = ((partner_ref, 1 - odd), (other_ref, odd))
    group_copies, packs = [], []
    for k in range(0, VECTORS, GROUP):
        for n, (out_ref, up) in enumerate(sides):
            rows = pl.ds(pl.multiple_of(up * (ROWS - CHUNK), CHUNK), CHUNK)
            for a in range(2):
                group_copies.append(
                    pltpu.make_async_copy(
                        basis_ref.at[pl.ds(k, GROUP), a, rows, :],
                        groups.at[2 * n + a, pl.ds(k, GROUP)],
                        group_sems.at[len(group_copies)],
                    )
                )
    for n, (out_ref, up) in enumerate(sides):
        packs += pack_copies(
            out_ref, up * (ROWS - HALO), visc_ref, inverse_ref, pack_sems,
            n * pack_count(inverse_ref.shape[1]),
        )
    stages = []
    for m, ref in enumerate((coup_ref, rhs_ref)):
        for n, first_row in enumerate((0, ROWS - HALO)):
            stages.append(
                pltpu.make_async_copy(
                    ref.at[:, pl.ds(first_row, HALO), :], staged.at[m, n], stage_sems.at[2 * m + n]
                )
            )
    for copy in stages + group_copies + packs:
        copy.start(priority=1)
    for copy in stages:
        copy.wait()
    for m, at in enumerate((COUPLING_AT, RHS_AT)):
        head, tail = outer_rows(staged[m, 0], staged[m, 1])
        partner_ref[at : at + HALO] = jnp.where(odd == 1, head, tail)
        other_ref[at : at + HALO] = jnp.where(odd == 1, tail, head)

    def take(out_ref, group, first, row):
        for k in range(first, first + GROUP, TILE):
            lines = [groups[group, k + n].astype(jnp.float32)[row : row + 1] for n in range(TILE)]
            at = EDGE_AT + VECTORS * (group % 2) + k
            out_ref[at : at + TILE] = jnp.concatenate(lines, 0)

    for first in range(0, VECTORS, GROUP):
        for _ in range(4):
            group_copies.pop(0).wait()

        @pl.when(odd == 0)
        def _():
            for a in range(2):
                take(partner_ref, a, first, CHUNK - 1)
                take(other_ref, 2 + a, first, 0)

        @pl.when(odd == 1)
        def _():
            for a in range(2):
                take(partner_ref, a, first, 0)
                take(other_ref, 2 + a, first, CHUNK - 1)

    for copy in packs:
        copy.wait()


def restrict_kernel(rhs_ref, held, sums_ref, sums):
    sums[...] = jnp.zeros_like(sums)
    squares = jnp.zeros((TILE, CELLS), jnp.float32)
    for a in range(2):
        for t in range(ROWS // TILE):
            tile = rhs_ref[a, tile_rows(t)]
            squares = squares + tile * tile
    sums[VECTORS : VECTORS + 8] = in_rows([fold(squares)])

    def body(i, carry):
        restrict_piece(i, held, rhs_ref, sums)
        return carry

    lax.fori_loop(0, VECTORS // PIECE, body, 0)
    send_sums(sums, sums_ref)


class Neighbour:
    def __init__(self, first_ref, second_ref):
        self.odd = lax.axis_index("sub") % 2 == 1
        self.first, self.second = first_ref, second_ref

    def __getitem__(self, index):
        return jnp.where(self.odd, self.first[index], self.second[index])


def neighbours_of(partner_ref, other_ref):
    return Neighbour(partner_ref, other_ref), Neighbour(other_ref, partner_ref)


def solve(count, margin_ref, factors_ref, make, field, out_ref, first_ref, solved, steps):
    waiting, done = list(steps), 0
    every = (SWEEPS - 1) * (STACKED // TILE) // len(waiting)
    assert every > 0
    rank = lax.axis_index("sub")
    lower = jnp.where(rank > 0, margin_ref[jnp.maximum(rank - 1, 0)], 0)
    upper = jnp.where(rank < count - 1, margin_ref[rank], 0)
    lower_f, upper_f = lower.astype(jnp.float32), upper.astype(jnp.float32)
    low_scale = 1.0 / (2.0 * jnp.maximum(lower_f, 1.0))
    high_scale = 1.0 / (2.0 * jnp.maximum(upper_f, 1.0))
    wide = lambda x: jnp.concatenate([x] * (CELLS // LANES), 1)
    own_tiles = ROWS // TILE
    strip_tiles = STRIP // TILE
    last = own_tiles + 1
    segments = (
        (0, 0, last + 1),
        (last + 1, 0, strip_tiles),
        (last + 1 + strip_tiles, last + 1 - strip_tiles, strip_tiles),
    )

    def place_of(e):
        return lax.broadcasted_iota(jnp.int32, (TILE, LANES), 0) + (TILE * e - HALO)

    def live_of(segment, e):
        place = place_of(e)
        if segment == 0:
            live = (place >= -lower) & (place < ROWS + upper)
        elif segment == 1:
            live = place < lower
        else:
            live = place >= ROWS - upper
        return wide(live.astype(jnp.float32))

    def weight_of(segment, e):
        place = place_of(e)
        place_f = place.astype(jnp.float32)
        rising = lambda base, scale: (place_f - base + 0.5) * scale
        falling = lambda base, scale: (base - place_f - 0.5) * scale
        if segment == 0:
            weight = jnp.where(place < lower, rising(-lower_f, low_scale), 1.0)
            weight = jnp.where(
                place >= ROWS - upper, falling(ROWS + upper_f, high_scale), weight
            )
        elif segment == 1:
            weight = jnp.where(place >= -lower, falling(lower_f, low_scale), 1.0)
        else:
            weight = jnp.where(place < ROWS + upper, rising(ROWS - upper_f, high_scale), 1.0)
        return wide(weight)

    for e in range(last + 1):
        for a in range(2):
            parts = make(a, e) if make else None
            value = field(a, e - 1)
            for n, (first, begin, size) in enumerate(segments):
                if not begin <= e < begin + size:
                    continue
                rows = tile_rows(first + e - begin)
                if make:
                    always = n == 0 and 0 < e < last
                    live = None if always else live_of(n, e)
                    for m, part in enumerate(parts):
                        factors_ref[3 * a + m, rows] = part if always else live * part
                first_ref[a, rows] = factors_ref[3 * a, rows] * value

    for sweep in range(1, SWEEPS):
        for n, (first, begin, size) in enumerate(segments):
            end = first + size - 1
            if sweep == 1:
                reads = [lambda t, a=a: first_ref[a, tile_rows(t)] for a in range(2)]
            else:
                bank = 2 * (sweep % 2)
                reads = [lambda t, a=a: solved[bank + a, tile_rows(t)] for a in range(2)]
            fields = [Rows(read, first, end) for read in reads]
            for t in range(first, end + 1):
                rows = tile_rows(t)
                if done % every == 0 and waiting:
                    waiting.pop(0)()
                done += 1
                for a in range(2):
                    value = (
                        ((1.0 - RELAX) * fields[a].at(t) + first_ref[a, rows])
                        + factors_ref[3 * a + 1, rows] * neighbours(fields[a], t, a)
                        - factors_ref[3 * a + 2, rows] * fields[1 - a].at(t)
                    )
                    e = t - first + begin
                    if sweep < SWEEPS - 1:
                        solved[2 * ((sweep + 1) % 2) + a, rows] = value
                    elif n == 0:
                        out_ref[a, tile_rows(e)] = weight_of(n, e) * value
                    else:
                        out_ref[a, tile_rows(e)] += weight_of(n, e) * value


def gather_order(count):
    return sorted(range(count), key=lambda rank: (abs(2 * rank - count + 1), -rank))


def line_up(residuals):
    devices = residuals.shape[0]
    order = gather_order(devices)
    lane = lax.broadcasted_iota(jnp.int32, (1, LANES), 1)
    tiles = [jnp.zeros((1, LANES), jnp.float32) for _ in range(devices * VECTORS // LANES)]
    for t in range(devices):
        tile, offset = divmod(VECTORS * t, LANES)
        at = order.index(t)
        row = jnp.where(lane < VECTORS, residuals[at : at + 1], 0.0)
        if offset:
            row = pltpu.roll(row, offset, 1)
        if offset + VECTORS <= LANES:
            tiles[tile] = tiles[tile] + row
        else:
            tiles[tile] = tiles[tile] + jnp.where(lane >= offset, row, 0.0)
            tiles[tile + 1] = tiles[tile + 1] + jnp.where(lane < offset, row, 0.0)
    return jnp.concatenate(tiles, 1)


def rounded(column):
    return column.astype(jnp.bfloat16).astype(jnp.float32)


def lift(inverse_ref, residual):
    return rounded(jnp.sum(inverse_ref[...] * residual, 1, keepdims=True))


def lift_packed(ref, residual):
    columns = residual.shape[1]
    at, total = EDGE_AT + INVERSE_AT, None
    for c in range(0, columns - 511, 512):
        term = jnp.sum(ref[at : at + VECTORS] * residual[:, c : c + 512], 1, keepdims=True)
        total = term if total is None else total + term
        at += VECTORS
    if columns % 512:
        half = VECTORS // 2
        last = residual[:, columns - 256 :]
        rows = ref[at : at + half]
        term = jnp.concatenate(
            [
                jnp.sum(rows[:, :256] * last, 1, keepdims=True),
                jnp.sum(rows[:, 256:] * last, 1, keepdims=True),
            ],
            0,
        )
        total = term if total is None else total + term
    return rounded(total)


def edge_values(ref, lifted):
    starts = [EDGE_AT + VECTORS * a for a in range(2)]
    return [jnp.sum(ref[at : at + VECTORS] * lifted, 0, keepdims=True) for at in starts]


def spread(lifted):
    shape = (VECTORS, CHUNK * VECTORS)
    owner = lax.broadcasted_iota(jnp.int32, shape, 1) // CHUNK
    row = lax.broadcasted_iota(jnp.int32, shape, 0)
    line = jnp.sum(jnp.where(owner == row, lifted, 0.0), 0, keepdims=True)
    shape = (CHUNK, CHUNK * VECTORS)
    place = lax.broadcasted_iota(jnp.int32, shape, 1) % CHUNK
    row = lax.broadcasted_iota(jnp.int32, shape, 0)
    return jnp.where(place == row, line, 0.0).astype(jnp.bfloat16)


class Coarse:
    def __init__(self, begin, inverse_ref, low, high, held, extended):
        self.inverse, self.sides, self.held, self.extended = inverse_ref, (low, high), held, extended
        self.lifted, self.edges = [None] * 2, [None] * 2
        self.steps = begin(self) + [self.lift_own, self.make_matrix]
        for a in range(2):
            for r in range(0, ROWS, CHUNK):
                self.steps.append(functools.partial(self.prolong, a, r))
        for n in range(2):
            self.steps.insert(len(self.steps) - 6, functools.partial(self.lift_side, n))
            self.steps.append(functools.partial(self.edge, n))

    def lift_own(self):
        self.own = lift(self.inverse, self.residual)

    def make_matrix(self):
        self.matrix = spread(self.own)

    def prolong(self, a, r):
        rows = self.held[:, a, r : r + CHUNK, :].reshape(CHUNK * VECTORS, CELLS)
        self.extended[a, HALO + r : HALO + r + CHUNK] = jnp.dot(
            self.matrix, rows, preferred_element_type=jnp.float32
        )

    def lift_side(self, n):
        self.lifted[n] = lift_packed(self.sides[n], self.residual)

    def edge(self, n):
        self.edges[n] = edge_values(self.sides[n], self.lifted[n])


def apply_operator(edges, smooth, extended, visc_ref, coup_ref, direction_ref):
    place = lax.broadcasted_iota(jnp.int32, (TILE, CELLS), 0)
    tiles = ROWS // TILE

    def read(t, a):
        if t < 0:
            return smooth(a, 0) + jnp.where(place == TILE - 1, edges[0][a], 0.0)
        if t == tiles:
            return smooth(a, t + 1) + jnp.where(place == 0, edges[1][a], 0.0)
        tile = smooth(a, t + 1) + extended[a, tile_rows(t + 1)]
        direction_ref[a, tile_rows(t)] = tile
        return tile

    fields = [Rows(lambda t, a=a: read(t, a), -1, tiles) for a in range(2)]
    for t in range(tiles):
        rows = tile_rows(t)
        viscosity = visc_ref[rows]
        for a in range(2):
            coupling = coup_ref[a, rows]
            diagonal = 10.0 * viscosity + jnp.abs(coupling) + 0.05
            image = (
                diagonal * fields[a].at(t)
                - viscosity * neighbours(fields[a], t, a)
                + coupling * fields[1 - a].at(t)
            )
            yield t, a, image


def lane_total(received, lane):
    place = lax.broadcasted_iota(jnp.int32, received.shape, 1)
    return jnp.sum(jnp.where(place == lane, received, 0.0), keepdims=True)


def first_turn_kernel(
    count, margin_ref, sums_ref, inverse_ref, partner_ref, other_ref, held, rhs_ref, visc_ref,
    coup_ref,
    direction_ref, image_ref, smooth_ref, residual_ref, factors_ref, partner_rows_ref, other_rows_ref,
    next_ref,
    extended, sums, first_ref, solved, lines,
):
    low, high = neighbours_of(partner_ref, other_ref)

    def begin(coarse):
        def scale():
            coarse.over_beta = 1.0 / jnp.sqrt(lane_total(sums_ref[...], VECTORS))

        def line():
            coarse.residual = line_up(sums_ref[...]) * coarse.over_beta
            residual_ref[...] = coarse.residual

        return [scale, line]

    coarse = Coarse(begin, inverse_ref, low, high, held, extended)

    def field(a, t):
        if 0 <= t < ROWS // TILE:
            return rhs_ref[a, tile_rows(t)]
        return component((low if t < 0 else high)[RHS_AT : RHS_AT + HALO], a)

    def make(a, e):
        if 0 < e <= ROWS // TILE:
            viscosity, coupling = visc_ref[tile_rows(e - 1)], coup_ref[a, tile_rows(e - 1)]
        else:
            side = low if e == 0 else high
            viscosity = side[:HALO]
            coupling = component(side[COUPLING_AT : COUPLING_AT + HALO], a)
        scale = RELAX / (10.0 * viscosity + jnp.abs(coupling) + 0.05)
        return scale, scale * viscosity, scale * coupling

    solve(
        count, margin_ref, factors_ref, make, field, smooth_ref, first_ref, solved, coarse.steps
    )
    smooth = lambda a, t: smooth_ref[a, tile_rows(t)] * coarse.over_beta
    images = apply_operator(
        coarse.edges, smooth, extended, visc_ref, coup_ref, direction_ref
    )
    odd = lax.axis_index("sub") % 2 == 1
    products, squares = [jnp.zeros((TILE, CELLS), jnp.float32)] * 2
    heads, tails = [None] * 2, [None] * 2
    for t, a, image in images:
        image_ref[a, tile_rows(t)] = image
        products = products + rhs_ref[a, tile_rows(t)] * image
        squares = squares + image * image
        if t == 0:
            heads[a] = image
        if t == ROWS // TILE - 1:
            tails[a] = image
    head, tail = outer_rows(heads, tails)
    partner_rows_ref[...] = jnp.where(odd, head, tail)
    other_rows_ref[...] = jnp.where(odd, tail, head)
    sums[...] = jnp.zeros_like(sums)
    sums[VECTORS : VECTORS + 8] = in_rows([fold(products), fold(squares)])

    restrict(held, image_ref, sums, lines)
    send_sums(sums, next_ref)


def first_column(first, second):
    beta = jnp.sqrt(lane_total(first, VECTORS))
    h_00 = lane_total(second, VECTORS) / beta
    h_10 = jnp.sqrt(lane_total(second, VECTORS + 1) - h_00 * h_00)
    return beta, h_00, h_10


def second_turn_kernel(
    count, margin_ref, sums_ref, second_ref, residual_ref, factors_ref, inverse_ref, partner_ref, other_ref,
    partner_rows_ref, other_rows_ref, held, smooth_ref, rhs_ref, image_ref, visc_ref, coup_ref,
    direction_ref, next_ref,
    image_smooth, extended, sums, first_ref, solved,
):
    low, high = neighbours_of(partner_ref, other_ref)

    def begin(coarse):
        def scale():
            beta, h_00, h_10 = first_column(sums_ref[...], second_ref[...])
            coarse.h_00, coarse.ratio, coarse.over = h_00, h_00 / beta, 1.0 / h_10

        def line():
            lined = line_up(second_ref[...])
            coarse.residual = (lined - coarse.h_00 * residual_ref[...]) * coarse.over

        return [scale, line]

    coarse = Coarse(begin, inverse_ref, low, high, held, extended)
    low_rows, high_rows = neighbours_of(partner_rows_ref, other_rows_ref)

    def field(a, t):
        if 0 <= t < ROWS // TILE:
            return image_ref[a, tile_rows(t)]
        rows = low_rows[...] if t < 0 else high_rows[...]
        return component(rows, a)

    solve(
        count, margin_ref, factors_ref, None, field, image_smooth, first_ref, solved, coarse.steps
    )

    def smooth(a, t):
        rows = tile_rows(t)
        return (image_smooth[a, rows] - coarse.ratio * smooth_ref[a, rows]) * coarse.over

    images = apply_operator(
        coarse.edges, smooth, extended, visc_ref, coup_ref, direction_ref
    )
    totals = [jnp.zeros((TILE, CELLS), jnp.float32)] * 3
    for t, a, image in images:
        others = (rhs_ref[a, tile_rows(t)], image_ref[a, tile_rows(t)], image)
        totals = [total + x * image for total, x in zip(totals, others)]
    sums[...] = jnp.zeros_like(sums)
    sums[:8] = in_rows([fold(total) for total in totals])
    send_sums(sums, next_ref)


def finish_kernel(
    first_ref, second_ref, third_ref, first_direction_ref, second_direction_ref,
    solution_ref, hessenberg_ref,
):
    third = third_ref[...]
    beta, h_00, h_10 = first_column(first_ref[...], second_ref[...])
    squares = lane_total(third, 2)
    h_01 = lane_total(third, 0) / beta
    h_11 = (lane_total(third, 1) - h_00 * h_01) / h_10
    h_21 = jnp.sqrt(squares - h_01 * h_01 - h_11 * h_11)
    l_00 = jnp.sqrt(h_00 * h_00 + h_10 * h_10)
    l_10 = (h_00 * h_01 + h_10 * h_11) / l_00
    f_0 = beta * h_00 / l_00
    c_1 = (beta * h_01 - l_10 * f_0) / (squares - l_10 * l_10)
    c_0 = (f_0 - l_10 * c_1) / l_00
    for a in range(2):
        solution_ref[a] = c_0 * first_direction_ref[a] + c_1 * second_direction_ref[a]
    shape = hessenberg_ref.shape
    row = lax.broadcasted_iota(jnp.int32, shape, 1)
    column = lax.broadcasted_iota(jnp.int32, shape, 0)
    entries = jnp.zeros(shape, jnp.float32)
    for i, j, value in ((0, 0, h_00), (0, 1, h_01), (1, 0, h_10), (1, 1, h_11), (2, 1, h_21)):
        entries = jnp.where((row == i) & (column == j), value, entries)
    hessenberg_ref[...] = entries


def call(kernel, name, in_specs, outs, flops, scratch=(), traffic=4_000_000):
    return pl.pallas_call(
        kernel,
        name=name,
        in_specs=in_specs,
        out_specs=[VMEM] * len(outs),
        out_shape=outs,
        scratch_shapes=scratch,
        compiler_params=pltpu.CompilerParams(vmem_limit_bytes=16 * 1024 * 1024),
        cost_estimate=pl.CostEstimate(flops=flops, bytes_accessed=traffic, transcendentals=0),
    )


def in_hbm(array):
    return pltpu.with_memory_space_constraint(array, pltpu.HBM)


def from_everyone(rows):
    order = [gather_order(lax.axis_size("sub"))]
    return lax.all_to_all(rows, "sub", 0, 0, tiled=True, axis_index_groups=order)


def swap(partner, other):
    count = lax.axis_size("sub")
    both = lambda lows: [pair for i in lows for pair in ((i, i + 1), (i + 1, i))]
    return (
        lax.ppermute(partner, "sub", both(range(0, count, 2))),
        lax.ppermute(other, "sub", both(range(1, count - 1, 2))),
    )


def on_device(rhs, viscosity, coupling, margin_rows, coarse_basis, coarse_inverse):
    count = lax.axis_size("sub")
    columns = coarse_inverse.shape[1]
    f32 = lambda *shape: jax.ShapeDtypeStruct(shape, jnp.float32)
    dma = lambda *shape: pltpu.SemaphoreType.DMA(shape)
    extended = pltpu.VMEM((2, EXT, CELLS), jnp.float32)
    stacked = pltpu.VMEM((2, STACKED, CELLS), jnp.float32)
    solved = pltpu.VMEM((4, STACKED, CELLS), jnp.float32)
    sums = pltpu.VMEM((SLOTS, LANES), jnp.float32)
    lines = pltpu.VMEM((LANES, len(MATRIX_GROUPS) * CELLS), jnp.bfloat16)
    row, whole, edge = f32(count, LANES), f32(2, ROWS, CELLS), f32(TILE, CELLS)
    packed, smoothed = f32(EDGE_AT + coarse_rows(columns), CELLS), f32(2, EXT, CELLS)
    arguments = (rhs, viscosity, coupling, coarse_inverse, coarse_basis)
    packs = call(
        pack_kernel, "pack", [HBM] * 5, [packed, packed], 5_000_000,
        [pltpu.VMEM((4, VECTORS, CHUNK, CELLS), jnp.bfloat16)]
        + [pltpu.VMEM((2, 2, 2, HALO, CELLS), jnp.float32), dma(4 * VECTORS // GROUP), dma(4)]
        + [dma(2 * pack_count(columns))],
    )(*map(in_hbm, arguments))
    held, partner, other = lax.optimization_barrier((coarse_basis, *packs))
    partner, other = swap(partner, other)
    (first,) = call(
        restrict_kernel, "restrict", [VMEM] * 2, [row], 10_000_000, [sums]
    )(rhs, held)
    first = from_everyone(first)
    direction, image, smooth, residual, factors, partner_rows, other_rows, second = call(
        functools.partial(first_turn_kernel, count), "first_turn", [SMEM] + [VMEM] * 8,
        [whole, whole, smoothed, f32(1, columns), f32(6, STACKED, CELLS), edge, edge, row], 20_000_000,
        [extended, sums, stacked, solved, lines],
    )(margin_rows, first, coarse_inverse, partner, other, held, rhs, viscosity, coupling)
    partner_rows, other_rows = swap(partner_rows, other_rows)
    second = from_everyone(second)
    second_direction, third = call(
        functools.partial(second_turn_kernel, count), "second_turn", [SMEM] + [VMEM] * 15,
        [whole, row], 20_000_000, [extended, extended, sums, stacked, solved],
    )(
        margin_rows, first, second, residual, factors, coarse_inverse, partner, other, partner_rows, other_rows,
        held, smooth, rhs, image, viscosity, coupling,
    )
    third = from_everyone(third)
    result, transposed = call(finish_kernel, "finish", [VMEM] * 5, [whole, f32(2, 3)], 1_000_000)(
        first, second, third, direction, second_direction
    )
    return result, transposed.T


def solution(mesh):
    in_specs = (
        P(None, ("groups", "sub"), None),
        P(("groups", "sub"), None),
        P(None, ("groups", "sub"), None),
        P("groups"),
        P(None, None, ("groups", "sub"), None),
        P(("groups", "sub"), None),
    )
    out_specs = (P(None, ("groups", "sub"), None), P("groups", None))
    return jax.shard_map(
        on_device, mesh=mesh, in_specs=in_specs, out_specs=out_specs, check_vma=False
    )
```

```python
import functools

import jax
import jax.numpy as jnp
from jax import lax
from jax.experimental import pallas as pl
from jax.experimental.pallas import tpu as pltpu
from jax.sharding import PartitionSpec as P

ROWS = 64
CELLS = 512
VECTORS = 48
HALO = 8
EXT = ROWS + 2 * HALO
STRIP = 32
GROUP = 16
STACKED = EXT + 2 * STRIP
TILE = 8
CHUNK = 16
CHUNKS = 2 * ROWS // CHUNK
PIECE = 8
LANES = 128
SLOTS = 64
COUPLING_AT = HALO
RHS_AT = 2 * HALO
EDGE_AT = 3 * HALO
INVERSE_AT = 2 * VECTORS
SWEEPS = 4
RELAX = 0.7
ROW_FACTOR = (1.0, 4.0)
CELL_FACTOR = (4.0, 1.0)

VMEM = pl.BlockSpec(memory_space=pltpu.VMEM)
SMEM = pl.BlockSpec(memory_space=pltpu.SMEM)
HBM = pl.BlockSpec(memory_space=pltpu.HBM)


def coarse_rows(columns):
    return INVERSE_AT + VECTORS * (columns // 512) + (VECTORS // 2) * (columns % 512 // 256)


def cell_sum(field):
    lane = lax.broadcasted_iota(jnp.int32, (field.shape[0], LANES), 1)
    left, right = pltpu.roll(field, 1, 1), pltpu.roll(field, CELLS - 1, 1)
    inner = left[:, LANES:-LANES] + right[:, LANES:-LANES]
    first = jnp.where(lane == 0, 0.0, left[:, :LANES]) + right[:, :LANES]
    last = left[:, -LANES:] + jnp.where(lane == LANES - 1, 0.0, right[:, -LANES:])
    return jnp.concatenate([first, inner, last], 1)


class Rows:
    def __init__(self, read, first, last):
        self.read, self.first, self.last = read, first, last
        self.tiles, self.down, self.up = {}, {}, {}

    def at(self, t):
        if t not in self.tiles:
            self.tiles[t] = self.read(t)
        return self.tiles[t]

    def moved(self, held, t, by):
        if t not in held:
            held[t] = pltpu.roll(self.at(t), by, 0)
        return held[t]

    def around(self, t):
        row = lax.broadcasted_iota(jnp.int32, (TILE, CELLS), 0)
        below, above = self.moved(self.down, t, 1), self.moved(self.up, t, TILE - 1)
        if t > self.first:
            below = jnp.where(row == 0, self.moved(self.down, t - 1, 1), below)
        if t < self.last:
            above = jnp.where(row == TILE - 1, self.moved(self.up, t + 1, TILE - 1), above)
        return below + above


def neighbours(rows, t, component):
    around, cells = rows.around(t), cell_sum(rows.at(t))
    if component == 0:
        return around + CELL_FACTOR[0] * cells
    return ROW_FACTOR[1] * around + cells


def sublane_sum(tile):
    for by in (4, 2, 1):
        tile = tile + pltpu.roll(tile, by, 0)
    return tile


def in_rows(tiles):
    row = lax.broadcasted_iota(jnp.int32, (8, LANES), 0)
    total = jnp.zeros((8, LANES), jnp.float32)
    for n, tile in enumerate(tiles):
        total = jnp.where(row == n, sublane_sum(tile), total)
    return total


def restrict_piece(i, held, field, sums):
    totals = [None] * PIECE
    for a in range(2):
        for r in range(0, ROWS, CHUNK):
            for c in range(0, CELLS, LANES):
                rows, cells = slice(r, r + CHUNK), slice(c, c + LANES)
                tile = field[a, rows, cells]
                for n in range(PIECE):
                    term = held[PIECE * i + n, a, rows, cells].astype(jnp.float32) * tile
                    totals[n] = term if totals[n] is None else totals[n] + term
    tiles = [total[:8] + total[8:] for total in totals]
    sums[pl.ds(pl.multiple_of(PIECE * i, PIECE), PIECE), :] = in_rows(tiles)


VECTOR_GROUPS = tuple((0, r) for r in range(0, ROWS, CHUNK))
MATRIX_GROUPS = tuple((1, r) for r in range(0, ROWS, CHUNK))


def restrict(held, field, sums, lines):
    lines[2 * CHUNK :] = jnp.zeros((LANES - 2 * CHUNK, lines.shape[1]), jnp.bfloat16)
    blocks = []
    for g, (a, r) in enumerate(MATRIX_GROUPS):
        part, cells = field[a, r : r + CHUNK], slice(CELLS * g, CELLS * (g + 1))
        high = part.astype(jnp.bfloat16)
        lines[:CHUNK, cells] = high
        lines[CHUNK : 2 * CHUNK, cells] = (part - high.astype(jnp.float32)).astype(jnp.bfloat16)
        blocks.append(held[:, a, r : r + CHUNK, :].reshape(CHUNK * VECTORS, CELLS))
    products = lax.dot_general(
        jnp.concatenate(blocks, 1),
        lines[...],
        (((1,), (1,)), ((), ())),
        preferred_element_type=jnp.float32,
    )
    row = lax.broadcasted_iota(jnp.int32, (CHUNK, LANES), 0)
    equal = row == lax.broadcasted_iota(jnp.int32, (CHUNK, LANES), 1) % CHUNK
    for first in range(0, VECTORS, PIECE):
        totals = [
            jnp.where(equal, products[CHUNK * k : CHUNK * (k + 1)], 0.0)
            for k in range(first, first + PIECE)
        ]
        for a, r in VECTOR_GROUPS:
            for c in range(0, CELLS, LANES):
                rows, cells = slice(r, r + CHUNK), slice(c, c + LANES)
                tile = field[a, rows, cells]
                for n in range(PIECE):
                    term = held[first + n, a, rows, cells].astype(jnp.float32) * tile
                    totals[n] = totals[n] + term
        sums[first : first + PIECE] = in_rows([total[:8] + total[8:] for total in totals])


def fold(row):
    total = row[:, :LANES]
    for c in range(LANES, CELLS, LANES):
        total = total + row[:, c : c + LANES]
    return total


def tile_rows(t):
    return slice(TILE * t, TILE * (t + 1))


def send_sums(sums, out_ref):
    rest = sums[...]
    parts = []
    for _ in range(3):
        part = rest.astype(jnp.bfloat16)
        parts.append(part)
        rest = rest - part.astype(jnp.float32)
    row = lax.dot_general(
        jnp.ones((CHUNK, 3 * LANES), jnp.bfloat16),
        jnp.concatenate(parts, 1),
        (((1,), (1,)), ((), ())),
        preferred_element_type=jnp.float32,
    )
    wide = jnp.concatenate([row[:1], jnp.zeros((1, LANES - SLOTS), jnp.float32)], 1)
    out_ref[...] = jnp.broadcast_to(wide, out_ref.shape)


def pack_copies(out_ref, first_row, visc_ref, inverse_ref, sems, at_sem):
    rows = pl.ds(pl.multiple_of(first_row, HALO), HALO)
    moves = [(visc_ref.at[rows, :], 0, HALO, None)]
    columns = inverse_ref.shape[1]
    at = EDGE_AT + INVERSE_AT
    for c in range(0, columns - 511, 512):
        moves.append((inverse_ref.at[:, pl.ds(c, 512)], at, VECTORS, None))
        at += VECTORS
    if columns % 512:
        half = VECTORS // 2
        last = pl.ds(columns - 256, 256)
        moves.append((inverse_ref.at[pl.ds(0, half), last], at, half, 0))
        moves.append((inverse_ref.at[pl.ds(half, half), last], at, half, 256))
    copies = []
    for n, (source, at, size, lane) in enumerate(moves):
        place = pl.ds(at, size)
        target = out_ref.at[place, :] if lane is None else out_ref.at[place, pl.ds(lane, 256)]
        copies.append(pltpu.make_async_copy(source, target, sems.at[at_sem + n]))
    return copies


def pack_count(columns):
    return 1 + columns // 512 + 2 * (columns % 512 // 256)


def outer_rows(head, tail):
    half = lax.broadcasted_iota(jnp.int32, (TILE, CELLS), 0) < TILE // 2
    return (
        jnp.where(half, head[0], pltpu.roll(head[1], TILE // 2, 0)),
        jnp.where(half, pltpu.roll(tail[1], TILE // 2, 0), tail[0]),
    )


def component(rows, a):
    return pltpu.roll(rows, TILE // 2, 0) if a else rows


def pack_kernel(
    rhs_ref, visc_ref, coup_ref, inverse_ref, basis_ref,
    partner_ref, other_ref,
    groups, staged, group_sems, stage_sems, pack_sems,
):
    odd = lax.axis_index("sub") % 2
    sides = ((partner_ref, 1 - odd), (other_ref, odd))
    group_copies, packs = [], []
    for k in range(0, VECTORS, GROUP):
        for n, (out_ref, up) in enumerate(sides):
            rows = pl.ds(pl.multiple_of(up * (ROWS - CHUNK), CHUNK), CHUNK)
            for a in range(2):
                group_copies.append(
                    pltpu.make_async_copy(
                        basis_ref.at[pl.ds(k, GROUP), a, rows, :],
                        groups.at[2 * n + a, pl.ds(k, GROUP)],
                        group_sems.at[len(group_copies)],
                    )
                )
    for n, (out_ref, up) in enumerate(sides):
        packs += pack_copies(
            out_ref, up * (ROWS - HALO), visc_ref, inverse_ref, pack_sems,
            n * pack_count(inverse_ref.shape[1]),
        )
    stages = []
    for m, ref in enumerate((coup_ref, rhs_ref)):
        for n, first_row in enumerate((0, ROWS - HALO)):
            stages.append(
                pltpu.make_async_copy(
                    ref.at[:, pl.ds(first_row, HALO), :], staged.at[m, n], stage_sems.at[2 * m + n]
                )
            )
    for copy in stages + group_copies + packs:
        copy.start(priority=1)
    for copy in stages:
        copy.wait()
    for m, at in enumerate((COUPLING_AT, RHS_AT)):
        head, tail = outer_rows(staged[m, 0], staged[m, 1])
        partner_ref[at : at + HALO] = jnp.where(odd == 1, head, tail)
        other_ref[at : at + HALO] = jnp.where(odd == 1, tail, head)

    def take(out_ref, group, first, row):
        for k in range(first, first + GROUP, TILE):
            lines = [groups[group, k + n].astype(jnp.float32)[row : row + 1] for n in range(TILE)]
            at = EDGE_AT + VECTORS * (group % 2) + k
            out_ref[at : at + TILE] = jnp.concatenate(lines, 0)

    for first in range(0, VECTORS, GROUP):
        for _ in range(4):
            group_copies.pop(0).wait()

        @pl.when(odd == 0)
        def _():
            for a in range(2):
                take(partner_ref, a, first, CHUNK - 1)
                take(other_ref, 2 + a, first, 0)

        @pl.when(odd == 1)
        def _():
            for a in range(2):
                take(partner_ref, a, first, 0)
                take(other_ref, 2 + a, first, CHUNK - 1)

    for copy in packs:
        copy.wait()


def restrict_kernel(rhs_ref, held, sums_ref, sums):
    sums[...] = jnp.zeros_like(sums)
    squares = jnp.zeros((TILE, CELLS), jnp.float32)
    for a in range(2):
        for t in range(ROWS // TILE):
            tile = rhs_ref[a, tile_rows(t)]
            squares = squares + tile * tile
    sums[VECTORS : VECTORS + 8] = in_rows([fold(squares)])

    def body(i, carry):
        restrict_piece(i, held, rhs_ref, sums)
        return carry

    lax.fori_loop(0, VECTORS // PIECE, body, 0)
    send_sums(sums, sums_ref)


class Neighbour:
    def __init__(self, first_ref, second_ref):
        self.odd = lax.axis_index("sub") % 2 == 1
        self.first, self.second = first_ref, second_ref

    def __getitem__(self, index):
        return jnp.where(self.odd, self.first[index], self.second[index])


def neighbours_of(partner_ref, other_ref):
    return Neighbour(partner_ref, other_ref), Neighbour(other_ref, partner_ref)


def solve(count, margin_ref, factors_ref, make, field, out_ref, first_ref, solved, steps):
    waiting, done = list(steps), 0
    every = (SWEEPS - 1) * (STACKED // TILE) // len(waiting)
    assert every > 0
    rank = lax.axis_index("sub")
    lower = jnp.where(rank > 0, margin_ref[jnp.maximum(rank - 1, 0)], 0)
    upper = jnp.where(rank < count - 1, margin_ref[rank], 0)
    lower_f, upper_f = lower.astype(jnp.float32), upper.astype(jnp.float32)
    low_scale = 1.0 / (2.0 * jnp.maximum(lower_f, 1.0))
    high_scale = 1.0 / (2.0 * jnp.maximum(upper_f, 1.0))
    wide = lambda x: jnp.concatenate([x] * (CELLS // LANES), 1)
    own_tiles = ROWS // TILE
    strip_tiles = STRIP // TILE
    last = own_tiles + 1
    segments = (
        (0, 0, last + 1),
        (last + 1, 0, strip_tiles),
        (last + 1 + strip_tiles, last + 1 - strip_tiles, strip_tiles),
    )

    def place_of(e):
        return lax.broadcasted_iota(jnp.int32, (TILE, LANES), 0) + (TILE * e - HALO)

    def live_of(segment, e):
        place = place_of(e)
        if segment == 0:
            live = (place >= -lower) & (place < ROWS + upper)
        elif segment == 1:
            live = place < lower
        else:
            live = place >= ROWS - upper
        return wide(live.astype(jnp.float32))

    def weight_of(segment, e):
        place = place_of(e)
        place_f = place.astype(jnp.float32)
        rising = lambda base, scale: (place_f - base + 0.5) * scale
        falling = lambda base, scale: (base - place_f - 0.5) * scale
        if segment == 0:
            weight = jnp.where(place < lower, rising(-lower_f, low_scale), 1.0)
            weight = jnp.where(
                place >= ROWS - upper, falling(ROWS + upper_f, high_scale), weight
            )
        elif segment == 1:
            weight = jnp.where(place >= -lower, falling(lower_f, low_scale), 1.0)
        else:
            weight = jnp.where(place < ROWS + upper, rising(ROWS - upper_f, high_scale), 1.0)
        return wide(weight)

    for e in range(last + 1):
        for a in range(2):
            parts = make(a, e) if make else None
            value = field(a, e - 1)
            for n, (first, begin, size) in enumerate(segments):
                if not begin <= e < begin + size:
                    continue
                rows = tile_rows(first + e - begin)
                if make:
                    always = n == 0 and 0 < e < last
                    live = None if always else live_of(n, e)
                    for m, part in enumerate(parts):
                        factors_ref[3 * a + m, rows] = part if always else live * part
                first_ref[a, rows] = factors_ref[3 * a, rows] * value

    for sweep in range(1, SWEEPS):
        for n, (first, begin, size) in enumerate(segments):
            end = first + size - 1
            if sweep == 1:
                reads = [lambda t, a=a: first_ref[a, tile_rows(t)] for a in range(2)]
            else:
                bank = 2 * (sweep % 2)
                reads = [lambda t, a=a: solved[bank + a, tile_rows(t)] for a in range(2)]
            fields = [Rows(read, first, end) for read in reads]
            for t in range(first, end + 1):
                rows = tile_rows(t)
                if done % every == 0 and waiting:
                    waiting.pop(0)()
                done += 1
                for a in range(2):
                    value = (
                        ((1.0 - RELAX) * fields[a].at(t) + first_ref[a, rows])
                        + factors_ref[3 * a + 1, rows] * neighbours(fields[a], t, a)
                        - factors_ref[3 * a + 2, rows] * fields[1 - a].at(t)
                    )
                    e = t - first + begin
                    if sweep < SWEEPS - 1:
                        solved[2 * ((sweep + 1) % 2) + a, rows] = value
                    elif n == 0:
                        out_ref[a, tile_rows(e)] = weight_of(n, e) * value
                    else:
                        out_ref[a, tile_rows(e)] += weight_of(n, e) * value


def line_up(residuals):
    devices = residuals.shape[0]
    lane = lax.broadcasted_iota(jnp.int32, (1, LANES), 1)
    tiles = [jnp.zeros((1, LANES), jnp.float32) for _ in range(devices * VECTORS // LANES)]
    for t in range(devices):
        tile, offset = divmod(VECTORS * t, LANES)
        row = jnp.where(lane < VECTORS, residuals[devices - 1 - t : devices - t], 0.0)
        if offset:
            row = pltpu.roll(row, offset, 1)
        if offset + VECTORS <= LANES:
            tiles[tile] = tiles[tile] + row
        else:
            tiles[tile] = tiles[tile] + jnp.where(lane >= offset, row, 0.0)
            tiles[tile + 1] = tiles[tile + 1] + jnp.where(lane < offset, row, 0.0)
    return jnp.concatenate(tiles, 1)


def rounded(column):
    return column.astype(jnp.bfloat16).astype(jnp.float32)


def lift(inverse_ref, residual):
    return rounded(jnp.sum(inverse_ref[...] * residual, 1, keepdims=True))


def lift_packed(ref, residual):
    columns = residual.shape[1]
    at, total = EDGE_AT + INVERSE_AT, None
    for c in range(0, columns - 511, 512):
        term = jnp.sum(ref[at : at + VECTORS] * residual[:, c : c + 512], 1, keepdims=True)
        total = term if total is None else total + term
        at += VECTORS
    if columns % 512:
        half = VECTORS // 2
        last = residual[:, columns - 256 :]
        rows = ref[at : at + half]
        term = jnp.concatenate(
            [
                jnp.sum(rows[:, :256] * last, 1, keepdims=True),
                jnp.sum(rows[:, 256:] * last, 1, keepdims=True),
            ],
            0,
        )
        total = term if total is None else total + term
    return rounded(total)


def edge_values(ref, lifted):
    starts = [EDGE_AT + VECTORS * a for a in range(2)]
    return [jnp.sum(ref[at : at + VECTORS] * lifted, 0, keepdims=True) for at in starts]


def spread(lifted):
    shape = (VECTORS, CHUNK * VECTORS)
    owner = lax.broadcasted_iota(jnp.int32, shape, 1) // CHUNK
    row = lax.broadcasted_iota(jnp.int32, shape, 0)
    line = jnp.sum(jnp.where(owner == row, lifted, 0.0), 0, keepdims=True)
    shape = (CHUNK, CHUNK * VECTORS)
    place = lax.broadcasted_iota(jnp.int32, shape, 1) % CHUNK
    row = lax.broadcasted_iota(jnp.int32, shape, 0)
    return jnp.where(place == row, line, 0.0).astype(jnp.bfloat16)


class Coarse:
    def __init__(self, begin, inverse_ref, low, high, held, extended):
        self.inverse, self.sides, self.held, self.extended = inverse_ref, (low, high), held, extended
        self.lifted, self.edges = [None] * 2, [None] * 2
        for step in begin(self) + [self.lift_own, self.make_matrix]:
            step()
        self.steps = [
            functools.partial(self.prolong, a, r) for a in range(2) for r in range(0, ROWS, CHUNK)
        ]

    def finish_sides(self):
        for n in range(2):
            self.lift_side(n)
            self.edge(n)

    def lift_own(self):
        self.own = lift(self.inverse, self.residual)

    def make_matrix(self):
        self.matrix = spread(self.own)

    def prolong(self, a, r):
        rows = self.held[:, a, r : r + CHUNK, :].reshape(CHUNK * VECTORS, CELLS)
        self.extended[a, HALO + r : HALO + r + CHUNK] = jnp.dot(
            self.matrix, rows, preferred_element_type=jnp.float32
        )

    def lift_side(self, n):
        self.lifted[n] = lift_packed(self.sides[n], self.residual)

    def edge(self, n):
        self.edges[n] = edge_values(self.sides[n], self.lifted[n])


def apply_operator(edges, smooth, extended, visc_ref, coup_ref, direction_ref):
    place = lax.broadcasted_iota(jnp.int32, (TILE, CELLS), 0)
    tiles = ROWS // TILE

    def read(t, a):
        if t < 0:
            return smooth(a, 0) + jnp.where(place == TILE - 1, edges[0][a], 0.0)
        if t == tiles:
            return smooth(a, t + 1) + jnp.where(place == 0, edges[1][a], 0.0)
        tile = smooth(a, t + 1) + extended[a, tile_rows(t + 1)]
        direction_ref[a, tile_rows(t)] = tile
        return tile

    fields = [Rows(lambda t, a=a: read(t, a), -1, tiles) for a in range(2)]
    for t in range(tiles):
        rows = tile_rows(t)
        viscosity = visc_ref[rows]
        for a in range(2):
            coupling = coup_ref[a, rows]
            diagonal = 10.0 * viscosity + jnp.abs(coupling) + 0.05
            image = (
                diagonal * fields[a].at(t)
                - viscosity * neighbours(fields[a], t, a)
                + coupling * fields[1 - a].at(t)
            )
            yield t, a, image


def lane_total(received, lane):
    place = lax.broadcasted_iota(jnp.int32, received.shape, 1)
    return jnp.sum(jnp.where(place == lane, received, 0.0), keepdims=True)


def first_turn_kernel(
    count, margin_ref, sums_ref, inverse_ref, partner_ref, other_ref, held, rhs_ref, visc_ref,
    coup_ref,
    direction_ref, image_ref, smooth_ref, residual_ref, factors_ref, partner_rows_ref, other_rows_ref,
    next_ref,
    extended, sums, first_ref, solved, lines,
):
    low, high = neighbours_of(partner_ref, other_ref)

    def begin(coarse):
        def scale():
            coarse.over_beta = 1.0 / jnp.sqrt(lane_total(sums_ref[...], VECTORS))

        def line():
            coarse.residual = line_up(sums_ref[...]) * coarse.over_beta
            residual_ref[...] = coarse.residual

        return [scale, line]

    coarse = Coarse(begin, inverse_ref, low, high, held, extended)

    def field(a, t):
        if 0 <= t < ROWS // TILE:
            return rhs_ref[a, tile_rows(t)]
        return component((low if t < 0 else high)[RHS_AT : RHS_AT + HALO], a)

    def make(a, e):
        if 0 < e <= ROWS // TILE:
            viscosity, coupling = visc_ref[tile_rows(e - 1)], coup_ref[a, tile_rows(e - 1)]
        else:
            side = low if e == 0 else high
            viscosity = side[:HALO]
            coupling = component(side[COUPLING_AT : COUPLING_AT + HALO], a)
        scale = RELAX / (10.0 * viscosity + jnp.abs(coupling) + 0.05)
        return scale, scale * viscosity, scale * coupling

    solve(
        count, margin_ref, factors_ref, make, field, smooth_ref, first_ref, solved, coarse.steps
    )
    smooth = lambda a, t: smooth_ref[a, tile_rows(t)] * coarse.over_beta
    coarse.finish_sides()
    images = apply_operator(
        coarse.edges, smooth, extended, visc_ref, coup_ref, direction_ref
    )
    odd = lax.axis_index("sub") % 2 == 1
    products, squares = [jnp.zeros((TILE, CELLS), jnp.float32)] * 2
    heads, tails = [None] * 2, [None] * 2
    for t, a, image in images:
        image_ref[a, tile_rows(t)] = image
        products = products + rhs_ref[a, tile_rows(t)] * image
        squares = squares + image * image
        if t == 0:
            heads[a] = image
        if t == ROWS // TILE - 1:
            tails[a] = image
    head, tail = outer_rows(heads, tails)
    partner_rows_ref[...] = jnp.where(odd, head, tail)
    other_rows_ref[...] = jnp.where(odd, tail, head)
    sums[...] = jnp.zeros_like(sums)
    sums[VECTORS : VECTORS + 8] = in_rows([fold(products), fold(squares)])

    restrict(held, image_ref, sums, lines)
    send_sums(sums, next_ref)


def first_column(first, second):
    beta = jnp.sqrt(lane_total(first, VECTORS))
    h_00 = lane_total(second, VECTORS) / beta
    h_10 = jnp.sqrt(lane_total(second, VECTORS + 1) - h_00 * h_00)
    return beta, h_00, h_10


def second_turn_kernel(
    count, margin_ref, sums_ref, second_ref, residual_ref, factors_ref, inverse_ref, partner_ref, other_ref,
    partner_rows_ref, other_rows_ref, held, smooth_ref, rhs_ref, image_ref, visc_ref, coup_ref,
    direction_ref, next_ref,
    image_smooth, extended, sums, first_ref, solved,
):
    low, high = neighbours_of(partner_ref, other_ref)

    def begin(coarse):
        def scale():
            beta, h_00, h_10 = first_column(sums_ref[...], second_ref[...])
            coarse.h_00, coarse.ratio, coarse.over = h_00, h_00 / beta, 1.0 / h_10

        def line():
            lined = line_up(second_ref[...])
            coarse.residual = (lined - coarse.h_00 * residual_ref[...]) * coarse.over

        return [scale, line]

    coarse = Coarse(begin, inverse_ref, low, high, held, extended)
    low_rows, high_rows = neighbours_of(partner_rows_ref, other_rows_ref)

    def field(a, t):
        if 0 <= t < ROWS // TILE:
            return image_ref[a, tile_rows(t)]
        rows = low_rows[...] if t < 0 else high_rows[...]
        return component(rows, a)

    solve(
        count, margin_ref, factors_ref, None, field, image_smooth, first_ref, solved, coarse.steps
    )

    def smooth(a, t):
        rows = tile_rows(t)
        return (image_smooth[a, rows] - coarse.ratio * smooth_ref[a, rows]) * coarse.over

    coarse.finish_sides()
    images = apply_operator(
        coarse.edges, smooth, extended, visc_ref, coup_ref, direction_ref
    )
    totals = [jnp.zeros((TILE, CELLS), jnp.float32)] * 3
    for t, a, image in images:
        others = (rhs_ref[a, tile_rows(t)], image_ref[a, tile_rows(t)], image)
        totals = [total + x * image for total, x in zip(totals, others)]
    sums[...] = jnp.zeros_like(sums)
    sums[:8] = in_rows([fold(total) for total in totals])
    send_sums(sums, next_ref)


def finish_kernel(
    first_ref, second_ref, third_ref, first_direction_ref, second_direction_ref,
    solution_ref, hessenberg_ref,
):
    third = third_ref[...]
    beta, h_00, h_10 = first_column(first_ref[...], second_ref[...])
    squares = lane_total(third, 2)
    h_01 = lane_total(third, 0) / beta
    h_11 = (lane_total(third, 1) - h_00 * h_01) / h_10
    h_21 = jnp.sqrt(squares - h_01 * h_01 - h_11 * h_11)
    l_00 = jnp.sqrt(h_00 * h_00 + h_10 * h_10)
    l_10 = (h_00 * h_01 + h_10 * h_11) / l_00
    f_0 = beta * h_00 / l_00
    c_1 = (beta * h_01 - l_10 * f_0) / (squares - l_10 * l_10)
    c_0 = (f_0 - l_10 * c_1) / l_00
    for a in range(2):
        solution_ref[a] = c_0 * first_direction_ref[a] + c_1 * second_direction_ref[a]
    shape = hessenberg_ref.shape
    row = lax.broadcasted_iota(jnp.int32, shape, 1)
    column = lax.broadcasted_iota(jnp.int32, shape, 0)
    entries = jnp.zeros(shape, jnp.float32)
    for i, j, value in ((0, 0, h_00), (0, 1, h_01), (1, 0, h_10), (1, 1, h_11), (2, 1, h_21)):
        entries = jnp.where((row == i) & (column == j), value, entries)
    hessenberg_ref[...] = entries


def call(kernel, name, in_specs, outs, flops, scratch=(), traffic=4_000_000):
    return pl.pallas_call(
        kernel,
        name=name,
        in_specs=in_specs,
        out_specs=[VMEM] * len(outs),
        out_shape=outs,
        scratch_shapes=scratch,
        compiler_params=pltpu.CompilerParams(vmem_limit_bytes=16 * 1024 * 1024),
        cost_estimate=pl.CostEstimate(flops=flops, bytes_accessed=traffic, transcendentals=0),
    )


def in_hbm(array):
    return pltpu.with_memory_space_constraint(array, pltpu.HBM)


def from_everyone(rows):
    order = [list(range(lax.axis_size("sub")))[::-1]]
    return lax.all_to_all(rows, "sub", 0, 0, tiled=True, axis_index_groups=order)


def swap(partner, other):
    count = lax.axis_size("sub")
    both = lambda lows: [pair for i in lows for pair in ((i, i + 1), (i + 1, i))]
    return (
        lax.ppermute(partner, "sub", both(range(0, count, 2))),
        lax.ppermute(other, "sub", both(range(1, count - 1, 2))),
    )


def on_device(rhs, viscosity, coupling, margin_rows, coarse_basis, coarse_inverse):
    count = lax.axis_size("sub")
    columns = coarse_inverse.shape[1]
    f32 = lambda *shape: jax.ShapeDtypeStruct(shape, jnp.float32)
    dma = lambda *shape: pltpu.SemaphoreType.DMA(shape)
    extended = pltpu.VMEM((2, EXT, CELLS), jnp.float32)
    stacked = pltpu.VMEM((2, STACKED, CELLS), jnp.float32)
    solved = pltpu.VMEM((4, STACKED, CELLS), jnp.float32)
    sums = pltpu.VMEM((SLOTS, LANES), jnp.float32)
    lines = pltpu.VMEM((LANES, len(MATRIX_GROUPS) * CELLS), jnp.bfloat16)
    row, whole, edge = f32(count, LANES), f32(2, ROWS, CELLS), f32(TILE, CELLS)
    packed, smoothed = f32(EDGE_AT + coarse_rows(columns), CELLS), f32(2, EXT, CELLS)
    arguments = (rhs, viscosity, coupling, coarse_inverse, coarse_basis)
    packs = call(
        pack_kernel, "pack", [HBM] * 5, [packed, packed], 5_000_000,
        [pltpu.VMEM((4, VECTORS, CHUNK, CELLS), jnp.bfloat16)]
        + [pltpu.VMEM((2, 2, 2, HALO, CELLS), jnp.float32), dma(4 * VECTORS // GROUP), dma(4)]
        + [dma(2 * pack_count(columns))],
    )(*map(in_hbm, arguments))
    held, partner, other = lax.optimization_barrier((coarse_basis, *packs))
    partner, other = swap(partner, other)
    (first,) = call(
        restrict_kernel, "restrict", [VMEM] * 2, [row], 10_000_000, [sums]
    )(rhs, held)
    first = from_everyone(first)
    direction, image, smooth, residual, factors, partner_rows, other_rows, second = call(
        functools.partial(first_turn_kernel, count), "first_turn", [SMEM] + [VMEM] * 8,
        [whole, whole, smoothed, f32(1, columns), f32(6, STACKED, CELLS), edge, edge, row], 20_000_000,
        [extended, sums, stacked, solved, lines],
    )(margin_rows, first, coarse_inverse, partner, other, held, rhs, viscosity, coupling)
    partner_rows, other_rows = swap(partner_rows, other_rows)
    second = from_everyone(second)
    second_direction, third = call(
        functools.partial(second_turn_kernel, count), "second_turn", [SMEM] + [VMEM] * 15,
        [whole, row], 20_000_000, [extended, extended, sums, stacked, solved],
    )(
        margin_rows, first, second, residual, factors, coarse_inverse, partner, other, partner_rows, other_rows,
        held, smooth, rhs, image, viscosity, coupling,
    )
    third = from_everyone(third)
    result, transposed = call(finish_kernel, "finish", [VMEM] * 5, [whole, f32(2, 3)], 1_000_000)(
        first, second, third, direction, second_direction
    )
    return result, transposed.T


def solution(mesh):
    in_specs = (
        P(None, ("groups", "sub"), None),
        P(("groups", "sub"), None),
        P(None, ("groups", "sub"), None),
        P("groups"),
        P(None, None, ("groups", "sub"), None),
        P(("groups", "sub"), None),
    )
    out_specs = (P(None, ("groups", "sub"), None), P("groups", None))
    return jax.shard_map(
        on_device, mesh=mesh, in_specs=in_specs, out_specs=out_specs, check_vma=False
    )
```

```python
import functools

import jax
import jax.numpy as jnp
from jax import lax
from jax.experimental import pallas as pl
from jax.experimental.pallas import tpu as pltpu
from jax.sharding import PartitionSpec as P

ROWS = 64
CELLS = 512
VECTORS = 48
HALO = 8
EXT = ROWS + 2 * HALO
STRIP = 32
GROUP = 16
STACKED = EXT + 2 * STRIP
TILE = 8
CHUNK = 16
CHUNKS = 2 * ROWS // CHUNK
PIECE = 8
LANES = 128
SLOTS = 64
COUPLING_AT = HALO
RHS_AT = 2 * HALO
EDGE_AT = 3 * HALO
INVERSE_AT = 2 * VECTORS
SWEEPS = 4
RELAX = 0.7
ROW_FACTOR = (1.0, 4.0)
CELL_FACTOR = (4.0, 1.0)

VMEM = pl.BlockSpec(memory_space=pltpu.VMEM)
SMEM = pl.BlockSpec(memory_space=pltpu.SMEM)
HBM = pl.BlockSpec(memory_space=pltpu.HBM)


def coarse_rows(columns):
    return INVERSE_AT + VECTORS * (columns // 512) + (VECTORS // 2) * (columns % 512 // 256)


def cell_sum(field):
    lane = lax.broadcasted_iota(jnp.int32, (field.shape[0], LANES), 1)
    left, right = pltpu.roll(field, 1, 1), pltpu.roll(field, CELLS - 1, 1)
    inner = left[:, LANES:-LANES] + right[:, LANES:-LANES]
    first = jnp.where(lane == 0, 0.0, left[:, :LANES]) + right[:, :LANES]
    last = left[:, -LANES:] + jnp.where(lane == LANES - 1, 0.0, right[:, -LANES:])
    return jnp.concatenate([first, inner, last], 1)


class Rows:
    def __init__(self, read, first, last):
        self.read, self.first, self.last = read, first, last
        self.tiles, self.down, self.up = {}, {}, {}

    def at(self, t):
        if t not in self.tiles:
            self.tiles[t] = self.read(t)
        return self.tiles[t]

    def moved(self, held, t, by):
        if t not in held:
            held[t] = pltpu.roll(self.at(t), by, 0)
        return held[t]

    def around(self, t):
        row = lax.broadcasted_iota(jnp.int32, (TILE, CELLS), 0)
        below, above = self.moved(self.down, t, 1), self.moved(self.up, t, TILE - 1)
        if t > self.first:
            below = jnp.where(row == 0, self.moved(self.down, t - 1, 1), below)
        if t < self.last:
            above = jnp.where(row == TILE - 1, self.moved(self.up, t + 1, TILE - 1), above)
        return below + above


def neighbours(rows, t, component):
    around, cells = rows.around(t), cell_sum(rows.at(t))
    if component == 0:
        return around + CELL_FACTOR[0] * cells
    return ROW_FACTOR[1] * around + cells


def sublane_sum(tile):
    for by in (4, 2, 1):
        tile = tile + pltpu.roll(tile, by, 0)
    return tile


def in_rows(tiles):
    row = lax.broadcasted_iota(jnp.int32, (8, LANES), 0)
    total = jnp.zeros((8, LANES), jnp.float32)
    for n, tile in enumerate(tiles):
        total = jnp.where(row == n, sublane_sum(tile), total)
    return total


def restrict_piece(i, held, field, sums):
    totals = [None] * PIECE
    for a in range(2):
        for r in range(0, ROWS, CHUNK):
            for c in range(0, CELLS, LANES):
                rows, cells = slice(r, r + CHUNK), slice(c, c + LANES)
                tile = field[a, rows, cells]
                for n in range(PIECE):
                    term = held[PIECE * i + n, a, rows, cells].astype(jnp.float32) * tile
                    totals[n] = term if totals[n] is None else totals[n] + term
    tiles = [total[:8] + total[8:] for total in totals]
    sums[pl.ds(pl.multiple_of(PIECE * i, PIECE), PIECE), :] = in_rows(tiles)


VECTOR_GROUPS = tuple((0, r) for r in range(0, ROWS, CHUNK))
MATRIX_GROUPS = tuple((1, r) for r in range(0, ROWS, CHUNK))


def restrict(held, field, sums, lines):
    lines[2 * CHUNK :] = jnp.zeros((LANES - 2 * CHUNK, lines.shape[1]), jnp.bfloat16)
    blocks = []
    for g, (a, r) in enumerate(MATRIX_GROUPS):
        part, cells = field[a, r : r + CHUNK], slice(CELLS * g, CELLS * (g + 1))
        high = part.astype(jnp.bfloat16)
        lines[:CHUNK, cells] = high
        lines[CHUNK : 2 * CHUNK, cells] = (part - high.astype(jnp.float32)).astype(jnp.bfloat16)
        blocks.append(held[:, a, r : r + CHUNK, :].reshape(CHUNK * VECTORS, CELLS))
    products = lax.dot_general(
        jnp.concatenate(blocks, 1),
        lines[...],
        (((1,), (1,)), ((), ())),
        preferred_element_type=jnp.float32,
    )
    row = lax.broadcasted_iota(jnp.int32, (CHUNK, LANES), 0)
    equal = row == lax.broadcasted_iota(jnp.int32, (CHUNK, LANES), 1) % CHUNK
    for first in range(0, VECTORS, PIECE):
        totals = [
            jnp.where(equal, products[CHUNK * k : CHUNK * (k + 1)], 0.0)
            for k in range(first, first + PIECE)
        ]
        for a, r in VECTOR_GROUPS:
            for c in range(0, CELLS, LANES):
                rows, cells = slice(r, r + CHUNK), slice(c, c + LANES)
                tile = field[a, rows, cells]
                for n in range(PIECE):
                    term = held[first + n, a, rows, cells].astype(jnp.float32) * tile
                    totals[n] = totals[n] + term
        sums[first : first + PIECE] = in_rows([total[:8] + total[8:] for total in totals])


def fold(row):
    total = row[:, :LANES]
    for c in range(LANES, CELLS, LANES):
        total = total + row[:, c : c + LANES]
    return total


def tile_rows(t):
    return slice(TILE * t, TILE * (t + 1))


def send_sums(sums, out_ref):
    rest = sums[...]
    parts = []
    for _ in range(3):
        part = rest.astype(jnp.bfloat16)
        parts.append(part)
        rest = rest - part.astype(jnp.float32)
    row = lax.dot_general(
        jnp.ones((CHUNK, 3 * LANES), jnp.bfloat16),
        jnp.concatenate(parts, 1),
        (((1,), (1,)), ((), ())),
        preferred_element_type=jnp.float32,
    )
    wide = jnp.concatenate([row[:1], jnp.zeros((1, LANES - SLOTS), jnp.float32)], 1)
    out_ref[...] = jnp.broadcast_to(wide, out_ref.shape)


def pack_copies(out_ref, first_row, visc_ref, inverse_ref, sems, at_sem):
    rows = pl.ds(pl.multiple_of(first_row, HALO), HALO)
    moves = [(visc_ref.at[rows, :], 0, HALO, None)]
    columns = inverse_ref.shape[1]
    at = EDGE_AT + INVERSE_AT
    for c in range(0, columns - 511, 512):
        moves.append((inverse_ref.at[:, pl.ds(c, 512)], at, VECTORS, None))
        at += VECTORS
    if columns % 512:
        half = VECTORS // 2
        last = pl.ds(columns - 256, 256)
        moves.append((inverse_ref.at[pl.ds(0, half), last], at, half, 0))
        moves.append((inverse_ref.at[pl.ds(half, half), last], at, half, 256))
    copies = []
    for n, (source, at, size, lane) in enumerate(moves):
        place = pl.ds(at, size)
        target = out_ref.at[place, :] if lane is None else out_ref.at[place, pl.ds(lane, 256)]
        copies.append(pltpu.make_async_copy(source, target, sems.at[at_sem + n]))
    return copies


def pack_count(columns):
    return 1 + columns // 512 + 2 * (columns % 512 // 256)


def outer_rows(head, tail):
    half = lax.broadcasted_iota(jnp.int32, (TILE, CELLS), 0) < TILE // 2
    return (
        jnp.where(half, head[0], pltpu.roll(head[1], TILE // 2, 0)),
        jnp.where(half, pltpu.roll(tail[1], TILE // 2, 0), tail[0]),
    )


def component(rows, a):
    return pltpu.roll(rows, TILE // 2, 0) if a else rows


def pack_kernel(
    rhs_ref, visc_ref, coup_ref, inverse_ref, basis_ref,
    partner_ref, other_ref,
    groups, staged, group_sems, stage_sems, pack_sems,
):
    odd = lax.axis_index("sub") % 2
    sides = ((partner_ref, 1 - odd), (other_ref, odd))
    group_copies, packs = [], []
    for k in range(0, VECTORS, GROUP):
        for n, (out_ref, up) in enumerate(sides):
            rows = pl.ds(pl.multiple_of(up * (ROWS - CHUNK), CHUNK), CHUNK)
            for a in range(2):
                group_copies.append(
                    pltpu.make_async_copy(
                        basis_ref.at[pl.ds(k, GROUP), a, rows, :],
                        groups.at[2 * n + a, pl.ds(k, GROUP)],
                        group_sems.at[len(group_copies)],
                    )
                )
    for n, (out_ref, up) in enumerate(sides):
        packs += pack_copies(
            out_ref, up * (ROWS - HALO), visc_ref, inverse_ref, pack_sems,
            n * pack_count(inverse_ref.shape[1]),
        )
    stages = []
    for m, ref in enumerate((coup_ref, rhs_ref)):
        for n, first_row in enumerate((0, ROWS - HALO)):
            stages.append(
                pltpu.make_async_copy(
                    ref.at[:, pl.ds(first_row, HALO), :], staged.at[m, n], stage_sems.at[2 * m + n]
                )
            )
    for copy in stages + group_copies + packs:
        copy.start(priority=1)
    for copy in stages:
        copy.wait()
    for m, at in enumerate((COUPLING_AT, RHS_AT)):
        head, tail = outer_rows(staged[m, 0], staged[m, 1])
        partner_ref[at : at + HALO] = jnp.where(odd == 1, head, tail)
        other_ref[at : at + HALO] = jnp.where(odd == 1, tail, head)

    def take(out_ref, group, first, row):
        for k in range(first, first + GROUP, TILE):
            lines = [groups[group, k + n].astype(jnp.float32)[row : row + 1] for n in range(TILE)]
            at = EDGE_AT + VECTORS * (group % 2) + k
            out_ref[at : at + TILE] = jnp.concatenate(lines, 0)

    for first in range(0, VECTORS, GROUP):
        for _ in range(4):
            group_copies.pop(0).wait()

        @pl.when(odd == 0)
        def _():
            for a in range(2):
                take(partner_ref, a, first, CHUNK - 1)
                take(other_ref, 2 + a, first, 0)

        @pl.when(odd == 1)
        def _():
            for a in range(2):
                take(partner_ref, a, first, 0)
                take(other_ref, 2 + a, first, CHUNK - 1)

    for copy in packs:
        copy.wait()


def restrict_kernel(rhs_ref, held, sums_ref, sums):
    sums[...] = jnp.zeros_like(sums)
    squares = jnp.zeros((TILE, CELLS), jnp.float32)
    for a in range(2):
        for t in range(ROWS // TILE):
            tile = rhs_ref[a, tile_rows(t)]
            squares = squares + tile * tile
    sums[VECTORS : VECTORS + 8] = in_rows([fold(squares)])

    def body(i, carry):
        restrict_piece(i, held, rhs_ref, sums)
        return carry

    lax.fori_loop(0, VECTORS // PIECE, body, 0)
    send_sums(sums, sums_ref)


class Neighbour:
    def __init__(self, first_ref, second_ref):
        self.odd = lax.axis_index("sub") % 2 == 1
        self.first, self.second = first_ref, second_ref

    def __getitem__(self, index):
        return jnp.where(self.odd, self.first[index], self.second[index])


def neighbours_of(partner_ref, other_ref):
    return Neighbour(partner_ref, other_ref), Neighbour(other_ref, partner_ref)


def solve(count, margin_ref, factors_ref, make, field, out_ref, first_ref, solved, steps):
    waiting, done = list(steps), 0
    every = (SWEEPS - 1) * (STACKED // TILE) // len(waiting)
    assert every > 0
    rank = lax.axis_index("sub")
    lower = jnp.where(rank > 0, margin_ref[jnp.maximum(rank - 1, 0)], 0)
    upper = jnp.where(rank < count - 1, margin_ref[rank], 0)
    lower_f, upper_f = lower.astype(jnp.float32), upper.astype(jnp.float32)
    low_scale = 1.0 / (2.0 * jnp.maximum(lower_f, 1.0))
    high_scale = 1.0 / (2.0 * jnp.maximum(upper_f, 1.0))
    wide = lambda x: jnp.concatenate([x] * (CELLS // LANES), 1)
    own_tiles = ROWS // TILE
    strip_tiles = STRIP // TILE
    last = own_tiles + 1
    segments = (
        (0, 0, last + 1),
        (last + 1, 0, strip_tiles),
        (last + 1 + strip_tiles, last + 1 - strip_tiles, strip_tiles),
    )

    def place_of(e):
        return lax.broadcasted_iota(jnp.int32, (TILE, LANES), 0) + (TILE * e - HALO)

    def live_of(segment, e):
        place = place_of(e)
        if segment == 0:
            live = (place >= -lower) & (place < ROWS + upper)
        elif segment == 1:
            live = place < lower
        else:
            live = place >= ROWS - upper
        return wide(live.astype(jnp.float32))

    def weight_of(segment, e):
        place = place_of(e)
        place_f = place.astype(jnp.float32)
        rising = lambda base, scale: (place_f - base + 0.5) * scale
        falling = lambda base, scale: (base - place_f - 0.5) * scale
        if segment == 0:
            weight = jnp.where(place < lower, rising(-lower_f, low_scale), 1.0)
            weight = jnp.where(
                place >= ROWS - upper, falling(ROWS + upper_f, high_scale), weight
            )
        elif segment == 1:
            weight = jnp.where(place >= -lower, falling(lower_f, low_scale), 1.0)
        else:
            weight = jnp.where(place < ROWS + upper, rising(ROWS - upper_f, high_scale), 1.0)
        return wide(weight)

    for e in range(last + 1):
        for a in range(2):
            parts = make(a, e) if make else None
            value = field(a, e - 1)
            for n, (first, begin, size) in enumerate(segments):
                if not begin <= e < begin + size:
                    continue
                rows = tile_rows(first + e - begin)
                if make:
                    always = n == 0 and 0 < e < last
                    live = None if always else live_of(n, e)
                    for m, part in enumerate(parts):
                        factors_ref[3 * a + m, rows] = part if always else live * part
                first_ref[a, rows] = factors_ref[3 * a, rows] * value

    for sweep in range(1, SWEEPS):
        for n, (first, begin, size) in enumerate(segments):
            end = first + size - 1
            if sweep == 1:
                reads = [lambda t, a=a: first_ref[a, tile_rows(t)] for a in range(2)]
            else:
                bank = 2 * (sweep % 2)
                reads = [lambda t, a=a: solved[bank + a, tile_rows(t)] for a in range(2)]
            fields = [Rows(read, first, end) for read in reads]
            for t in range(first, end + 1):
                rows = tile_rows(t)
                if done % every == 0 and waiting:
                    waiting.pop(0)()
                done += 1
                for a in range(2):
                    value = (
                        ((1.0 - RELAX) * fields[a].at(t) + first_ref[a, rows])
                        + factors_ref[3 * a + 1, rows] * neighbours(fields[a], t, a)
                        - factors_ref[3 * a + 2, rows] * fields[1 - a].at(t)
                    )
                    e = t - first + begin
                    if sweep < SWEEPS - 1:
                        solved[2 * ((sweep + 1) % 2) + a, rows] = value
                    elif n == 0:
                        out_ref[a, tile_rows(e)] = weight_of(n, e) * value
                    else:
                        out_ref[a, tile_rows(e)] += weight_of(n, e) * value


def line_up(residuals):
    devices = residuals.shape[0]
    lane = lax.broadcasted_iota(jnp.int32, (1, LANES), 1)
    tiles = [jnp.zeros((1, LANES), jnp.float32) for _ in range(devices * VECTORS // LANES)]
    for t in range(devices):
        tile, offset = divmod(VECTORS * t, LANES)
        row = jnp.where(lane < VECTORS, residuals[devices - 1 - t : devices - t], 0.0)
        if offset:
            row = pltpu.roll(row, offset, 1)
        if offset + VECTORS <= LANES:
            tiles[tile] = tiles[tile] + row
        else:
            tiles[tile] = tiles[tile] + jnp.where(lane >= offset, row, 0.0)
            tiles[tile + 1] = tiles[tile + 1] + jnp.where(lane < offset, row, 0.0)
    return jnp.concatenate(tiles, 1)


def rounded(column):
    return column.astype(jnp.bfloat16).astype(jnp.float32)


def lift(inverse_ref, residual):
    return rounded(jnp.sum(inverse_ref[...] * residual, 1, keepdims=True))


def lift_packed(ref, residual):
    columns = residual.shape[1]
    at, total = EDGE_AT + INVERSE_AT, None
    for c in range(0, columns - 511, 512):
        term = jnp.sum(ref[at : at + VECTORS] * residual[:, c : c + 512], 1, keepdims=True)
        total = term if total is None else total + term
        at += VECTORS
    if columns % 512:
        half = VECTORS // 2
        last = residual[:, columns - 256 :]
        rows = ref[at : at + half]
        term = jnp.concatenate(
            [
                jnp.sum(rows[:, :256] * last, 1, keepdims=True),
                jnp.sum(rows[:, 256:] * last, 1, keepdims=True),
            ],
            0,
        )
        total = term if total is None else total + term
    return rounded(total)


def edge_values(ref, lifted):
    starts = [EDGE_AT + VECTORS * a for a in range(2)]
    return [jnp.sum(ref[at : at + VECTORS] * lifted, 0, keepdims=True) for at in starts]


def spread(lifted):
    shape = (VECTORS, CHUNK * VECTORS)
    owner = lax.broadcasted_iota(jnp.int32, shape, 1) // CHUNK
    row = lax.broadcasted_iota(jnp.int32, shape, 0)
    line = jnp.sum(jnp.where(owner == row, lifted, 0.0), 0, keepdims=True)
    shape = (CHUNK, CHUNK * VECTORS)
    place = lax.broadcasted_iota(jnp.int32, shape, 1) % CHUNK
    row = lax.broadcasted_iota(jnp.int32, shape, 0)
    return jnp.where(place == row, line, 0.0).astype(jnp.bfloat16)


class Coarse:
    def __init__(self, begin, inverse_ref, low, high, held, extended, ahead=0):
        self.inverse, self.sides, self.held, self.extended = inverse_ref, (low, high), held, extended
        self.lifted, self.edges = [None] * 2, [None] * 2
        self.steps = begin(self) + [self.lift_own, self.make_matrix]
        for a in range(2):
            for r in range(0, ROWS, CHUNK):
                self.steps.append(functools.partial(self.prolong, a, r))
        for n in range(2):
            self.steps.insert(len(self.steps) - 6, functools.partial(self.lift_side, n))
            self.steps.append(functools.partial(self.edge, n))
        for _ in range(ahead):
            self.steps.pop(0)()

    def lift_own(self):
        self.own = lift(self.inverse, self.residual)

    def make_matrix(self):
        self.matrix = spread(self.own)

    def prolong(self, a, r):
        rows = self.held[:, a, r : r + CHUNK, :].reshape(CHUNK * VECTORS, CELLS)
        self.extended[a, HALO + r : HALO + r + CHUNK] = jnp.dot(
            self.matrix, rows, preferred_element_type=jnp.float32
        )

    def lift_side(self, n):
        self.lifted[n] = lift_packed(self.sides[n], self.residual)

    def edge(self, n):
        self.edges[n] = edge_values(self.sides[n], self.lifted[n])


def apply_operator(edges, smooth, extended, visc_ref, coup_ref, direction_ref):
    place = lax.broadcasted_iota(jnp.int32, (TILE, CELLS), 0)
    tiles = ROWS // TILE

    def read(t, a):
        if t < 0:
            return smooth(a, 0) + jnp.where(place == TILE - 1, edges[0][a], 0.0)
        if t == tiles:
            return smooth(a, t + 1) + jnp.where(place == 0, edges[1][a], 0.0)
        tile = smooth(a, t + 1) + extended[a, tile_rows(t + 1)]
        direction_ref[a, tile_rows(t)] = tile
        return tile

    fields = [Rows(lambda t, a=a: read(t, a), -1, tiles) for a in range(2)]
    for t in range(tiles):
        rows = tile_rows(t)
        viscosity = visc_ref[rows]
        for a in range(2):
            coupling = coup_ref[a, rows]
            diagonal = 10.0 * viscosity + jnp.abs(coupling) + 0.05
            image = (
                diagonal * fields[a].at(t)
                - viscosity * neighbours(fields[a], t, a)
                + coupling * fields[1 - a].at(t)
            )
            yield t, a, image


def lane_total(received, lane):
    place = lax.broadcasted_iota(jnp.int32, received.shape, 1)
    return jnp.sum(jnp.where(place == lane, received, 0.0), keepdims=True)


def first_turn_kernel(
    count, margin_ref, sums_ref, inverse_ref, partner_ref, other_ref, held, rhs_ref, visc_ref,
    coup_ref,
    direction_ref, image_ref, smooth_ref, residual_ref, factors_ref, partner_rows_ref, other_rows_ref,
    next_ref,
    extended, sums, first_ref, solved, lines,
):
    low, high = neighbours_of(partner_ref, other_ref)

    def begin(coarse):
        def scale():
            coarse.over_beta = 1.0 / jnp.sqrt(lane_total(sums_ref[...], VECTORS))

        def line():
            coarse.residual = line_up(sums_ref[...]) * coarse.over_beta
            residual_ref[...] = coarse.residual

        return [scale, line]

    coarse = Coarse(begin, inverse_ref, low, high, held, extended)

    def field(a, t):
        if 0 <= t < ROWS // TILE:
            return rhs_ref[a, tile_rows(t)]
        return component((low if t < 0 else high)[RHS_AT : RHS_AT + HALO], a)

    def make(a, e):
        if 0 < e <= ROWS // TILE:
            viscosity, coupling = visc_ref[tile_rows(e - 1)], coup_ref[a, tile_rows(e - 1)]
        else:
            side = low if e == 0 else high
            viscosity = side[:HALO]
            coupling = component(side[COUPLING_AT : COUPLING_AT + HALO], a)
        scale = RELAX / (10.0 * viscosity + jnp.abs(coupling) + 0.05)
        return scale, scale * viscosity, scale * coupling

    solve(
        count, margin_ref, factors_ref, make, field, smooth_ref, first_ref, solved, coarse.steps
    )
    smooth = lambda a, t: smooth_ref[a, tile_rows(t)] * coarse.over_beta
    images = apply_operator(
        coarse.edges, smooth, extended, visc_ref, coup_ref, direction_ref
    )
    odd = lax.axis_index("sub") % 2 == 1
    products, squares = [jnp.zeros((TILE, CELLS), jnp.float32)] * 2
    heads, tails = [None] * 2, [None] * 2
    for t, a, image in images:
        image_ref[a, tile_rows(t)] = image
        products = products + rhs_ref[a, tile_rows(t)] * image
        squares = squares + image * image
        if t == 0:
            heads[a] = image
        if t == ROWS // TILE - 1:
            tails[a] = image
    head, tail = outer_rows(heads, tails)
    partner_rows_ref[...] = jnp.where(odd, head, tail)
    other_rows_ref[...] = jnp.where(odd, tail, head)
    sums[...] = jnp.zeros_like(sums)
    sums[VECTORS : VECTORS + 8] = in_rows([fold(products), fold(squares)])

    restrict(held, image_ref, sums, lines)
    send_sums(sums, next_ref)


def first_column(first, second):
    beta = jnp.sqrt(lane_total(first, VECTORS))
    h_00 = lane_total(second, VECTORS) / beta
    h_10 = jnp.sqrt(lane_total(second, VECTORS + 1) - h_00 * h_00)
    return beta, h_00, h_10


def second_turn_kernel(
    count, margin_ref, sums_ref, second_ref, residual_ref, factors_ref, inverse_ref, partner_ref, other_ref,
    partner_rows_ref, other_rows_ref, held, smooth_ref, rhs_ref, image_ref, visc_ref, coup_ref,
    direction_ref, next_ref,
    image_smooth, extended, sums, first_ref, solved,
):
    low, high = neighbours_of(partner_ref, other_ref)

    def begin(coarse):
        def scale():
            beta, h_00, h_10 = first_column(sums_ref[...], second_ref[...])
            coarse.h_00, coarse.ratio, coarse.over = h_00, h_00 / beta, 1.0 / h_10

        def line():
            lined = line_up(second_ref[...])
            coarse.residual = (lined - coarse.h_00 * residual_ref[...]) * coarse.over

        return [scale, line]

    coarse = Coarse(begin, inverse_ref, low, high, held, extended, ahead=4)
    low_rows, high_rows = neighbours_of(partner_rows_ref, other_rows_ref)

    def field(a, t):
        if 0 <= t < ROWS // TILE:
            return image_ref[a, tile_rows(t)]
        rows = low_rows[...] if t < 0 else high_rows[...]
        return component(rows, a)

    solve(
        count, margin_ref, factors_ref, None, field, image_smooth, first_ref, solved, coarse.steps
    )

    def smooth(a, t):
        rows = tile_rows(t)
        return (image_smooth[a, rows] - coarse.ratio * smooth_ref[a, rows]) * coarse.over

    images = apply_operator(
        coarse.edges, smooth, extended, visc_ref, coup_ref, direction_ref
    )
    totals = [jnp.zeros((TILE, CELLS), jnp.float32)] * 3
    for t, a, image in images:
        others = (rhs_ref[a, tile_rows(t)], image_ref[a, tile_rows(t)], image)
        totals = [total + x * image for total, x in zip(totals, others)]
    sums[...] = jnp.zeros_like(sums)
    sums[:8] = in_rows([fold(total) for total in totals])
    send_sums(sums, next_ref)


def finish_kernel(
    first_ref, second_ref, third_ref, first_direction_ref, second_direction_ref,
    solution_ref, hessenberg_ref,
):
    third = third_ref[...]
    beta, h_00, h_10 = first_column(first_ref[...], second_ref[...])
    squares = lane_total(third, 2)
    h_01 = lane_total(third, 0) / beta
    h_11 = (lane_total(third, 1) - h_00 * h_01) / h_10
    h_21 = jnp.sqrt(squares - h_01 * h_01 - h_11 * h_11)
    l_00 = jnp.sqrt(h_00 * h_00 + h_10 * h_10)
    l_10 = (h_00 * h_01 + h_10 * h_11) / l_00
    f_0 = beta * h_00 / l_00
    c_1 = (beta * h_01 - l_10 * f_0) / (squares - l_10 * l_10)
    c_0 = (f_0 - l_10 * c_1) / l_00
    for a in range(2):
        solution_ref[a] = c_0 * first_direction_ref[a] + c_1 * second_direction_ref[a]
    shape = hessenberg_ref.shape
    row = lax.broadcasted_iota(jnp.int32, shape, 1)
    column = lax.broadcasted_iota(jnp.int32, shape, 0)
    entries = jnp.zeros(shape, jnp.float32)
    for i, j, value in ((0, 0, h_00), (0, 1, h_01), (1, 0, h_10), (1, 1, h_11), (2, 1, h_21)):
        entries = jnp.where((row == i) & (column == j), value, entries)
    hessenberg_ref[...] = entries


def call(kernel, name, in_specs, outs, flops, scratch=(), traffic=4_000_000):
    return pl.pallas_call(
        kernel,
        name=name,
        in_specs=in_specs,
        out_specs=[VMEM] * len(outs),
        out_shape=outs,
        scratch_shapes=scratch,
        compiler_params=pltpu.CompilerParams(vmem_limit_bytes=16 * 1024 * 1024),
        cost_estimate=pl.CostEstimate(flops=flops, bytes_accessed=traffic, transcendentals=0),
    )


def in_hbm(array):
    return pltpu.with_memory_space_constraint(array, pltpu.HBM)


def from_everyone(rows):
    order = [list(range(lax.axis_size("sub")))[::-1]]
    return lax.all_to_all(rows, "sub", 0, 0, tiled=True, axis_index_groups=order)


def swap(partner, other):
    count = lax.axis_size("sub")
    both = lambda lows: [pair for i in lows for pair in ((i, i + 1), (i + 1, i))]
    return (
        lax.ppermute(partner, "sub", both(range(0, count, 2))),
        lax.ppermute(other, "sub", both(range(1, count - 1, 2))),
    )


def on_device(rhs, viscosity, coupling, margin_rows, coarse_basis, coarse_inverse):
    count = lax.axis_size("sub")
    columns = coarse_inverse.shape[1]
    f32 = lambda *shape: jax.ShapeDtypeStruct(shape, jnp.float32)
    dma = lambda *shape: pltpu.SemaphoreType.DMA(shape)
    extended = pltpu.VMEM((2, EXT, CELLS), jnp.float32)
    stacked = pltpu.VMEM((2, STACKED, CELLS), jnp.float32)
    solved = pltpu.VMEM((4, STACKED, CELLS), jnp.float32)
    sums = pltpu.VMEM((SLOTS, LANES), jnp.float32)
    lines = pltpu.VMEM((LANES, len(MATRIX_GROUPS) * CELLS), jnp.bfloat16)
    row, whole, edge = f32(count, LANES), f32(2, ROWS, CELLS), f32(TILE, CELLS)
    packed, smoothed = f32(EDGE_AT + coarse_rows(columns), CELLS), f32(2, EXT, CELLS)
    arguments = (rhs, viscosity, coupling, coarse_inverse, coarse_basis)
    packs = call(
        pack_kernel, "pack", [HBM] * 5, [packed, packed], 5_000_000,
        [pltpu.VMEM((4, VECTORS, CHUNK, CELLS), jnp.bfloat16)]
        + [pltpu.VMEM((2, 2, 2, HALO, CELLS), jnp.float32), dma(4 * VECTORS // GROUP), dma(4)]
        + [dma(2 * pack_count(columns))],
    )(*map(in_hbm, arguments))
    held, partner, other = lax.optimization_barrier((coarse_basis, *packs))
    partner, other = swap(partner, other)
    (first,) = call(
        restrict_kernel, "restrict", [VMEM] * 2, [row], 10_000_000, [sums]
    )(rhs, held)
    first = from_everyone(first)
    direction, image, smooth, residual, factors, partner_rows, other_rows, second = call(
        functools.partial(first_turn_kernel, count), "first_turn", [SMEM] + [VMEM] * 8,
        [whole, whole, smoothed, f32(1, columns), f32(6, STACKED, CELLS), edge, edge, row], 20_000_000,
        [extended, sums, stacked, solved, lines],
    )(margin_rows, first, coarse_inverse, partner, other, held, rhs, viscosity, coupling)
    partner_rows, other_rows = swap(partner_rows, other_rows)
    second = from_everyone(second)
    second_direction, third = call(
        functools.partial(second_turn_kernel, count), "second_turn", [SMEM] + [VMEM] * 15,
        [whole, row], 20_000_000, [extended, extended, sums, stacked, solved],
    )(
        margin_rows, first, second, residual, factors, coarse_inverse, partner, other, partner_rows, other_rows,
        held, smooth, rhs, image, viscosity, coupling,
    )
    third = from_everyone(third)
    result, transposed = call(finish_kernel, "finish", [VMEM] * 5, [whole, f32(2, 3)], 1_000_000)(
        first, second, third, direction, second_direction
    )
    return result, transposed.T


def solution(mesh):
    in_specs = (
        P(None, ("groups", "sub"), None),
        P(("groups", "sub"), None),
        P(None, ("groups", "sub"), None),
        P("groups"),
        P(None, None, ("groups", "sub"), None),
        P(("groups", "sub"), None),
    )
    out_specs = (P(None, ("groups", "sub"), None), P("groups", None))
    return jax.shard_map(
        on_device, mesh=mesh, in_specs=in_specs, out_specs=out_specs, check_vma=False
    )
```
